32 devices in a mesh: tile: 8 (over z, x), cuts: 4 (over y, core).
Axes of the slice: x: 2, y: 2, z: 4, core: 2. Of those that a mesh axis runs over, the one named last changes fastest.
Arguments:
- object_slices: bfloat16 [4, 2, 2048, 256], P('cuts', None, 'tile'), may hold values from -5 to 5
- probe: bfloat16 [2, 256, 256], replicated, may hold values from -5 to 5
- fresnel_taps: bfloat16 [2, 63], replicated, may hold values from -0.5 to 0.5
- offsets: int32 [16, 2], P('tile'), may hold values from 128 to 255
- counts: int32 [8], P('tile'), may hold values from 1 to 2, as said below
- measured: float32 [16, 256, 256], P('tile'), may hold values from 0.1 to 3
Outputs:
- object_gradient: float32 [4, 2, 2048, 256], P('cuts', None, 'tile')
The draws below stay inside these ranges and needn't reach their ends.
Inputs may be any that keep to these rules, and one draw needn't show every extreme that they name: Positions of tile t fill its slots 0 to counts[t] - 1; some tile has 2 live slots.
All inputs are finite; a program needn't handle non-finite values.
Results may differ from the reference program's by a relative error of at most 0.02.
Values may be sent and summed in bfloat16 or wider, within the bound.
No kernel may reach another device: no remote copies, remote signals or barrier semaphores. Data moves between devices by JAX's collectives and lax.ppermute only.
A program may use at most 64 MiB of HBM per device.

```python
import math
import jax
import jax.numpy as jnp
from jax import lax

P_SIZE = 256
KTAPS = 63
MAXP = 2
GX = 2
SLICES = 4
TILES = 8
POSITIONS = 16
N_TILE = 8


def draw_counts(key, part):
    key = jax.random.fold_in(key, 11)
    first, second, third = jax.random.split(key, 3)
    extra = jax.random.randint(first, (N_TILE,), 0, MAXP)
    gate = jax.random.randint(second, (N_TILE,), 0, 2)
    base = 1 + extra * gate
    peak = jax.random.randint(third, (), 0, N_TILE)
    return jnp.where(jnp.arange(N_TILE) == peak, MAXP, base).astype(jnp.int32)


def touch_ends(drawn, rng, least, top_value):
    extent = drawn.shape
    spot = [jax.random.randint(jax.random.fold_in(rng, axis), (), 0, extent[axis]) for axis in range(len(extent))]
    drawn = drawn.at[tuple(spot)].set(least)
    longest = extent.index(max(extent))
    spot[longest] = (spot[longest] + 1) % extent[longest]
    return drawn.at[tuple(spot)].set(top_value)


def levels(rng, shape, pieces, low, high):
    def one(axis_at, shards_of):
        heights = jax.random.uniform(jax.random.fold_in(jax.random.fold_in(rng, 6), axis_at), (shards_of,), jnp.float32, low / len(pieces), high / len(pieces))
        return jnp.repeat(jnp.exp(heights), shape[axis_at] // shards_of).reshape((-1,) + (1,) * (len(shape) - axis_at - 1))

    factor_of = one(*pieces[0])
    for cut in pieces[1:]:
        factor_of = factor_of * one(*cut)
    return factor_of


def centred(own_key, dims, scale, limit, cuts=(), held_as=jnp.bfloat16):
    values = scale * jax.random.normal(own_key, dims, jnp.float32)
    if cuts:
        values = values * levels(own_key, dims, cuts, -0.22, 0.18)
    return jnp.clip(values, -limit, limit).astype(held_as)


def setup_inputs(seed: int = 0) -> dict:
    key_list = jax.random.split(jax.random.key(seed), 7)
    object_slices = centred(key_list[0], (SLICES, 2, TILES * P_SIZE, P_SIZE), 0.7, 5.0, ((0, 4), (2, 8)))
    probe = centred(key_list[1], (2, P_SIZE, P_SIZE), 0.7, 5.0)
    fresnel_taps = centred(key_list[2], (2, KTAPS), (2 * KTAPS - KTAPS * KTAPS // (2 * P_SIZE)) ** -0.5, 0.5)
    offsets = touch_ends(jax.random.randint(key_list[3], (POSITIONS, 2), P_SIZE // 2, P_SIZE), jax.random.fold_in(key_list[3], 1), P_SIZE // 2, P_SIZE - 1).astype(jnp.int32)
    counts = draw_counts(jax.random.fold_in(key_list[6], 71), 0)
    measured = jnp.clip(jnp.exp(math.log(3.0) - 3.4011974 * jax.random.uniform(key_list[5], (POSITIONS, P_SIZE, P_SIZE), jnp.float32) ** levels(key_list[5], (POSITIONS, P_SIZE, P_SIZE), ((0, 8),), -0.2, 0.2)), 0.1, 3.0)
    return {"object_slices": object_slices, "probe": probe, "fresnel_taps": fresnel_taps, "offsets": offsets, "counts": counts, "measured": measured}


def band_matrix(taps, width):
    count = taps.shape[1]
    half = count // 2
    filler = jnp.zeros((2, 2 * width - count), taps.dtype)
    wrapped = jnp.concatenate([taps[:, half:], filler, taps[:, :half]], axis=1)
    tiled = jnp.tile(wrapped, (1, width))[:, :width * (2 * width - 1)]
    return tiled.reshape(2, width, 2 * width - 1)[:, :, :width]

def fourier_matrix(width):
    index = jnp.arange(width, dtype=jnp.int32)
    phase = index[:, None] * index[None, :] % width
    angle = 2.0 * jnp.pi * phase.astype(jnp.float32) / width
    scale = 1.0 / jnp.sqrt(jnp.float32(width))
    return jnp.stack([jnp.cos(angle) * scale, -jnp.sin(angle) * scale]).astype(jnp.bfloat16)

def conjugate(field):
    sign = jnp.array([1.0, -1.0], field.dtype)[:, None, None]
    return field * sign

def swapped(matrix):
    return jnp.swapaxes(matrix, 1, 2)

def complex_dot(left_column, right):
    real = jnp.dot(left_column[0], right[0], preferred_element_type=jnp.float32) - jnp.dot(left_column[1], right[1], preferred_element_type=jnp.float32)
    imag = jnp.dot(left_column[0], right[1], preferred_element_type=jnp.float32) + jnp.dot(left_column[1], right[0], preferred_element_type=jnp.float32)
    return jnp.stack([real, imag])

def complex_mul(first, second):
    first = first.astype(jnp.float32)
    second = second.astype(jnp.float32)
    real = first[0] * second[0] - first[1] * second[1]
    imag = first[0] * second[1] + first[1] * second[0]
    return jnp.stack([real, imag])

def sandwich(left_column, field, right):
    inner = complex_dot(left_column, field).astype(jnp.bfloat16)
    return complex_dot(inner, right)

def reference(object_slices, probe, fresnel_taps, offsets, counts, measured):
    band = band_matrix(fresnel_taps, P_SIZE)
    band_t = swapped(band)
    band_c = conjugate(band)
    band_ct = swapped(band_c)
    fourier = fourier_matrix(P_SIZE)
    fourier_c = conjugate(fourier)
    tiles = object_slices.reshape(SLICES, 2, N_TILE, P_SIZE, P_SIZE)
    right = jnp.roll(tiles, -1, axis=2)
    below = jnp.roll(tiles, -GX, axis=2)
    corner = jnp.roll(tiles, -GX - 1, axis=2)
    blocks = jnp.concatenate([jnp.concatenate([tiles, right], axis=4), jnp.concatenate([below, corner], axis=4)], axis=3)
    zero = jnp.zeros((), jnp.int32)

    def position_terms(patches, measured_amplitude, is_active_flag):
        spreads = []
        exit_wave = probe
        for level in range(SLICES):
            if level == 0:
                spread = probe
            else:
                spread = sandwich(band, exit_wave, band_t).astype(jnp.bfloat16)
            spreads.append(spread)
            exit_wave = complex_mul(spread, patches[level]).astype(jnp.bfloat16)
        farfield_wave = sandwich(fourier, exit_wave, fourier)
        wave_intensity = farfield_wave[0] * farfield_wave[0] + farfield_wave[1] * farfield_wave[1]
        amplitude_residual = ((2.0 * is_active_flag * (wave_intensity - measured_amplitude))[None] * farfield_wave).astype(jnp.bfloat16)
        back = sandwich(fourier_c, amplitude_residual, fourier_c).astype(jnp.bfloat16)
        terms = [None] * SLICES
        for level in range(SLICES - 1, -1, -1):
            terms[level] = complex_mul(conjugate(spreads[level]), back)
            if level > 0:
                carried = complex_mul(conjugate(patches[level]), back).astype(jnp.bfloat16)
                back = sandwich(band_ct, carried, band_c).astype(jnp.bfloat16)
        return jnp.stack(terms)

    def one_tile(tile_id):
        block = lax.dynamic_index_in_dim(blocks, tile_id, 2, keepdims=False)
        total = jnp.zeros((SLICES, 2, 2 * P_SIZE, 2 * P_SIZE), jnp.float32)
        for slot in range(MAXP):
            row = tile_id * MAXP + slot
            offset = lax.dynamic_index_in_dim(offsets, row, 0, keepdims=False).astype(jnp.int32)
            measured_amplitude = lax.dynamic_index_in_dim(measured, row, 0, keepdims=False)
            is_active_flag = (slot < counts[tile_id]).astype(jnp.float32)
            start = (zero, zero, offset[0], offset[1])
            patches = lax.dynamic_slice(block, start, (SLICES, 2, P_SIZE, P_SIZE))
            terms = position_terms(patches, measured_amplitude, is_active_flag)
            current = lax.dynamic_slice(total, start, terms.shape)
            total = lax.dynamic_update_slice(total, current + terms, start)
        return total
    sums = lax.map(one_tile, jnp.arange(N_TILE, dtype=jnp.int32))
    gradient = sums[:, :, :, :P_SIZE, :P_SIZE]
    gradient = gradient + jnp.roll(sums[:, :, :, :P_SIZE, P_SIZE:], 1, axis=0)
    gradient = gradient + jnp.roll(sums[:, :, :, P_SIZE:, :P_SIZE], GX, axis=0)
    gradient = gradient + jnp.roll(sums[:, :, :, P_SIZE:, P_SIZE:], GX + 1, axis=0)
    return gradient.transpose(1, 2, 0, 3, 4).reshape(SLICES, 2, N_TILE * P_SIZE, P_SIZE)
```

```python
import jax
import jax.numpy as jnp
import numpy as np
from jax import lax
from jax.experimental import pallas as pl
from jax.experimental.pallas import tpu as pltpu
from jax.sharding import PartitionSpec as P


def passed_along(value, axis, steps):
    count = lax.axis_size(axis)
    pairs = [(source, (source + steps) % count) for source in range(count)]
    return lax.ppermute(value, axis, pairs)


def crossed(value, axis, mask):
    pairs = [(source, source ^ mask) for source in range(lax.axis_size(axis))]
    return lax.ppermute(value, axis, pairs)


def fourier_matrix(width):
    index = np.arange(width)
    angle = 2.0 * np.pi * (index[:, None] * index[None, :] % width) / width
    return np.stack([np.cos(angle), -np.sin(angle)]) / np.sqrt(width)


def dot(left, right):
    return jnp.dot(left, right, preferred_element_type=jnp.float32)


def left_product(real, imag, field):
    top = jnp.concatenate([real, -imag], axis=1)
    bottom = jnp.concatenate([imag, real], axis=1)
    return dot(jnp.concatenate([top, bottom], axis=0), field)


def right_product(field, real, imag):
    width = real.shape[0]
    turned = jnp.concatenate([-field[width:], field[:width]], axis=0)
    return dot(jnp.concatenate([field, turned], axis=1), jnp.concatenate([real, imag], axis=0))


def sandwich(left_real, left_imag, field, right_real, right_imag):
    inner = left_product(left_real, left_imag, field).astype(jnp.bfloat16)
    return right_product(inner, right_real, right_imag)


def complex_mul(first, second, sign):
    width = first.shape[1]
    fr = first[:width].astype(jnp.float32)
    fi = first[width:].astype(jnp.float32) * sign
    sr = second[:width].astype(jnp.float32)
    si = second[width:].astype(jnp.float32)
    return jnp.concatenate([fr * sr - fi * si, fr * si + fi * sr], axis=0)


def cut_kernel(tile_ref, offsets_ref, counts_ref, below_ref, right_ref, own_ref, meta_ref):
    half = right_ref.shape[1]
    below_ref[...] = tile_ref[:, :, half:]
    right_ref[...] = tile_ref[:, half:, :]
    own_ref[...] = tile_ref[:, half:, half:]
    for slot in range(2):
        for axis in range(2):
            meta_ref[slot * 2 + axis] = offsets_ref[slot, axis]
    meta_ref[4] = counts_ref[0]
    for spare in range(5, 8):
        meta_ref[spare] = 0


def band_kernel(taps_ref, band_ref):
    width = band_ref.shape[1]
    half = taps_ref.shape[1] // 2
    rows = lax.broadcasted_iota(jnp.int32, (width, width), 0)
    columns = lax.broadcasted_iota(jnp.int32, (width, width), 1)
    inside = jnp.abs(columns - rows) <= half
    for part in range(2):
        line = taps_ref[part : part + 1, :].astype(jnp.float32)
        filler = jnp.zeros((1, width - line.shape[1]), jnp.float32)
        line = jnp.concatenate([line, filler], axis=1)
        spread = jnp.broadcast_to(line, (width, width))
        turned = pltpu.roll(spread, width - half, 1, stride=1, stride_axis=0)
        band = jnp.where(inside, turned, 0.0)
        band_ref[part] = band.astype(jnp.bfloat16)
        band_ref[part + 2] = band.T.astype(jnp.bfloat16)


def window(meta_ref, slot, width, transposed):
    half = width // 2
    wide = (width, width + half)
    tall = (width + half, width)
    row = meta_ref[2 * slot] - half
    column = meta_ref[2 * slot + 1] - half

    def placed(shape, axis, shift):
        i = lax.broadcasted_iota(jnp.int32, shape, axis)
        j = lax.broadcasted_iota(jnp.int32, shape, 1 - axis)
        return jnp.where(j - i == shift, 1.0, 0.0).astype(jnp.bfloat16)

    if transposed:
        return placed(tall, 1, row), placed(wide, 0, column)
    return placed(wide, 0, row), placed(tall, 1, column)


def patch_kernel(meta_ref, tile_ref, below_ref, right_ref, own_ref, measured_ref, first_ref, second_ref, level_ref):
    width = tile_ref.shape[1]
    core = lax.rem(lax.axis_index("cuts"), 2)
    blocks = []
    for part in range(2):
        upper = jnp.concatenate([own_ref[part], right_ref[part]], axis=1)
        lower = jnp.concatenate([below_ref[part], tile_ref[part]], axis=1)
        blocks.append(jnp.concatenate([upper, lower], axis=0))
    for slot, out_ref in ((core, first_ref), (1 - core, second_ref)):
        rows, columns = window(meta_ref, slot, width, False)
        for part in range(2):
            strip = dot(rows, blocks[part]).astype(jnp.bfloat16)
            out_ref[part * width : (part + 1) * width, :] = dot(strip, columns).astype(jnp.bfloat16)
    level_ref[...] = measured_ref[core].astype(jnp.bfloat16)


def chain_kernel(
    meta_ref, probe_ref, p0_ref, p1_ref, p2_ref, p3_ref, level_ref, band_ref, fourier_ref, mine_ref, other_ref, patch_ref, spread_ref, back_ref
):
    width = level_ref.shape[0]
    cut = lax.axis_index("cuts")
    for mask, ref in enumerate((p0_ref, p1_ref, p2_ref, p3_ref)):
        patch_ref[lax.bitwise_xor(cut, mask)] = ref[...]
    band_r, band_i = band_ref[0], band_ref[1]
    turned_r, turned_i = band_ref[2], band_ref[3]
    fourier_r, fourier_i = fourier_ref[0], fourier_ref[1]
    wave = None
    for level in range(4):
        if level == 0:
            spread = probe_ref[...]
        else:
            spread = sandwich(band_r, band_i, wave, turned_r, turned_i).astype(jnp.bfloat16)
        spread_ref[level] = spread
        wave = complex_mul(spread, patch_ref[level], 1.0).astype(jnp.bfloat16)
    far = sandwich(fourier_r, fourier_i, wave, fourier_r, fourier_i)
    far_r, far_i = far[:width], far[width:]
    live = (lax.rem(cut, 2) < meta_ref[4]).astype(jnp.float32)
    excess = 2.0 * live * (far_r * far_r + far_i * far_i - level_ref[...].astype(jnp.float32))
    residual = jnp.concatenate([excess * far_r, excess * far_i], axis=0).astype(jnp.bfloat16)
    back = sandwich(fourier_r, -fourier_i, residual, fourier_r, -fourier_i).astype(jnp.bfloat16)
    back_ref[...] = back
    for level in range(3, -1, -1):
        if level < 3:
            carried = complex_mul(patch_ref[level + 1], back_ref[...], -1.0).astype(jnp.bfloat16)
            back_ref[...] = sandwich(turned_r, -turned_i, carried, band_r, -band_i).astype(jnp.bfloat16)

        @pl.when(level // 2 == cut // 2)
        def _(level=level):
            term = complex_mul(spread_ref[level], back_ref[...], -1.0).astype(jnp.bfloat16)

            @pl.when(level == cut)
            def _():
                mine_ref[...] = term

            @pl.when(level != cut)
            def _():
                other_ref[...] = term


def scatter_kernel(meta_ref, mine_ref, other_ref, tile_ref, below_ref, right_ref, own_ref):
    width = tile_ref.shape[1]
    half = width // 2
    core = lax.rem(lax.axis_index("cuts"), 2)
    rows, columns = zip(*[window(meta_ref, slot, width, True) for slot in (core, 1 - core)])
    columns = jnp.concatenate(columns, axis=0)
    for part in range(2):
        strips = []
        for slot, ref in enumerate((mine_ref, other_ref)):
            strips.append(dot(rows[slot], ref[part * width : (part + 1) * width, :]).astype(jnp.bfloat16))
        total = dot(jnp.concatenate(strips, axis=1), columns)
        tile_ref[part] = total[half:, half:]
        below_ref[part] = total[half:, :half].astype(jnp.bfloat16)
        right_ref[part] = total[:half, half:].astype(jnp.bfloat16)
        own_ref[part] = total[:half, :half].astype(jnp.bfloat16)


def total_kernel(tile_ref, below_ref, right_ref, own_ref, out_ref):
    half = right_ref.shape[1]
    below = below_ref[...].astype(jnp.float32)
    right = right_ref[...].astype(jnp.float32)
    own = own_ref[...].astype(jnp.float32)
    out_ref[0, :, :half, :half] = tile_ref[:, :half, :half]
    out_ref[0, :, :half, half:] = tile_ref[:, :half, half:] + below[:, :half]
    out_ref[0, :, half:, :half] = tile_ref[:, half:, :half] + right[:, :, :half]
    out_ref[0, :, half:, half:] = tile_ref[:, half:, half:] + below[:, half:] + right[:, :, half:] + own


VMEM = pl.BlockSpec(memory_space=pltpu.VMEM)
SMEM = pl.BlockSpec(memory_space=pltpu.SMEM)
PARAMS = pltpu.CompilerParams(vmem_limit_bytes=48 * 1024 * 1024)


def shaped(*shape, dtype=jnp.bfloat16):
    return jax.ShapeDtypeStruct(shape, dtype)


def local(object_slices, probe, fresnel_taps, offsets, counts, measured):
    width = probe.shape[1]
    half = width // 2
    row_tiles = max(lax.axis_size("tile") // 16, 2)
    tile = object_slices[0]
    below, right, own, meta = pl.pallas_call(
        cut_kernel,
        in_specs=[VMEM, SMEM, SMEM],
        out_specs=[VMEM, VMEM, VMEM, SMEM],
        out_shape=[shaped(2, width, half), shaped(2, half, width), shaped(2, half, half), shaped(8, dtype=jnp.int32)],
        compiler_params=PARAMS,
        name="cut",
    )(tile, offsets, counts)
    below = passed_along(below, "tile", 1)
    right = passed_along(right, "tile", row_tiles)
    own = passed_along(own, "tile", row_tiles + 1)
    meta = passed_along(meta, "tile", row_tiles + 1)
    band = pl.pallas_call(
        band_kernel, in_specs=[VMEM], out_specs=VMEM, out_shape=shaped(4, width, width), compiler_params=PARAMS, name="band"
    )(fresnel_taps)
    first, second, level = pl.pallas_call(
        patch_kernel,
        in_specs=[SMEM] + [VMEM] * 5,
        out_specs=[VMEM] * 3,
        out_shape=[shaped(2 * width, width), shaped(2 * width, width), shaped(width, width)],
        compiler_params=PARAMS,
        name="patch",
    )(meta, tile, below, right, own, measured)
    level = passed_along(level, "tile", row_tiles + 1)
    swapped = crossed(second, "cuts", 1)
    straight = crossed(first, "cuts", 2)
    diagonal = crossed(second, "cuts", 3)
    fourier = jnp.asarray(fourier_matrix(width), jnp.bfloat16)
    mine, other = pl.pallas_call(
        chain_kernel,
        in_specs=[SMEM] + [VMEM] * 8,
        out_specs=[VMEM] * 2,
        out_shape=[shaped(2 * width, width)] * 2,
        scratch_shapes=[
            pltpu.VMEM((4, 2 * width, width), jnp.bfloat16),
            pltpu.VMEM((4, 2 * width, width), jnp.bfloat16),
            pltpu.VMEM((2 * width, width), jnp.bfloat16),
        ],
        compiler_params=PARAMS,
        name="chain",
    )(meta, probe.reshape(2 * width, width), first, swapped, straight, diagonal, level, band, fourier)
    other = crossed(other, "cuts", 1)
    total, below, right, own = pl.pallas_call(
        scatter_kernel,
        in_specs=[SMEM, VMEM, VMEM],
        out_specs=[VMEM] * 4,
        out_shape=[
            shaped(2, width, width, dtype=jnp.float32),
            shaped(2, width, half),
            shaped(2, half, width),
            shaped(2, half, half),
        ],
        compiler_params=PARAMS,
        name="scatter",
    )(meta, mine, other)
    below = passed_along(below, "tile", -1)
    right = passed_along(right, "tile", -row_tiles)
    own = passed_along(own, "tile", -row_tiles - 1)
    return pl.pallas_call(
        total_kernel,
        in_specs=[VMEM] * 4,
        out_specs=VMEM,
        out_shape=shaped(1, 2, width, width, dtype=jnp.float32),
        compiler_params=PARAMS,
        name="total",
    )(total, below, right, own)


def solution(mesh):
    return jax.shard_map(
        local,
        mesh=mesh,
        in_specs=(
            P("cuts", None, "tile", None),
            P(),
            P(),
            P("tile", None),
            P("tile"),
            P("tile", None, None),
        ),
        out_specs=P("cuts", None, "tile", None),
        check_vma=False,
    )
```

```python
import jax
import jax.numpy as jnp
import numpy as np
from jax import lax
from jax.experimental import pallas as pl
from jax.experimental.pallas import tpu as pltpu
from jax.sharding import PartitionSpec as P


def passed_along(value, axis, steps):
    count = lax.axis_size(axis)
    pairs = [(source, (source + steps) % count) for source in range(count)]
    return lax.ppermute(value, axis, pairs)


def crossed(value, axis, mask):
    pairs = [(source, source ^ mask) for source in range(lax.axis_size(axis))]
    return lax.ppermute(value, axis, pairs)


def fourier_matrix(width):
    index = np.arange(width)
    angle = 2.0 * np.pi * (index[:, None] * index[None, :] % width) / width
    return np.stack([np.cos(angle), -np.sin(angle)]) / np.sqrt(width)


def dot(left, right):
    return jnp.dot(left, right, preferred_element_type=jnp.float32)


def left_product(real, imag, field):
    top = jnp.concatenate([real, -imag], axis=1)
    bottom = jnp.concatenate([imag, real], axis=1)
    return dot(jnp.concatenate([top, bottom], axis=0), field)


def right_product(field, real, imag):
    width = real.shape[0]
    turned = jnp.concatenate([-field[width:], field[:width]], axis=0)
    return dot(jnp.concatenate([field, turned], axis=1), jnp.concatenate([real, imag], axis=0))


def sandwich(left_real, left_imag, field, right_real, right_imag):
    inner = left_product(left_real, left_imag, field).astype(jnp.bfloat16)
    return right_product(inner, right_real, right_imag)


def complex_mul(first, second, sign):
    width = first.shape[1]
    fr = first[:width].astype(jnp.float32)
    fi = first[width:].astype(jnp.float32) * sign
    sr = second[:width].astype(jnp.float32)
    si = second[width:].astype(jnp.float32)
    return jnp.concatenate([fr * sr - fi * si, fr * si + fi * sr], axis=0)


def band_kernel(counts_ref, taps_ref, measured_ref, band_ref, level_ref):
    width = band_ref.shape[1]
    half = taps_ref.shape[1] // 2
    core = lax.rem(lax.axis_index("cuts"), 2)
    level_ref[:width, :] = measured_ref[core].astype(jnp.bfloat16)
    live = (core < counts_ref[0]).astype(jnp.float32)
    level_ref[width:, :] = jnp.full((level_ref.shape[0] - width, width), live, jnp.float32).astype(jnp.bfloat16)
    rows = lax.broadcasted_iota(jnp.int32, (width, width), 0)
    columns = lax.broadcasted_iota(jnp.int32, (width, width), 1)
    inside = jnp.abs(columns - rows) <= half
    for part in range(2):
        line = taps_ref[part : part + 1, :].astype(jnp.float32)
        filler = jnp.zeros((1, width - line.shape[1]), jnp.float32)
        line = jnp.concatenate([line, filler], axis=1)
        spread = jnp.broadcast_to(line, (width, width))
        turned = pltpu.roll(spread, width - half, 1, stride=1, stride_axis=0)
        band = jnp.where(inside, turned, 0.0)
        band_ref[part] = band.astype(jnp.bfloat16)
        band_ref[part + 2] = band.T.astype(jnp.bfloat16)


def window_kernel(offsets_ref, rows_ref, columns_ref, rows_back_ref, columns_back_ref):
    half = rows_ref.shape[0] // 2
    width = 2 * half
    core = lax.rem(lax.axis_index("cuts"), 2)

    def placed(shape, axis, shift):
        i = lax.broadcasted_iota(jnp.int32, shape, axis)
        j = lax.broadcasted_iota(jnp.int32, shape, 1 - axis)
        return jnp.where(j - i == shift, 1.0, 0.0).astype(jnp.bfloat16)

    for place, slot in enumerate((core, 1 - core)):
        row = offsets_ref[slot, 0] - half
        column = offsets_ref[slot, 1] - half
        rows_ref[place * half : (place + 1) * half, :] = placed((half, width), 0, row)
        columns_ref[place] = placed((width + half, width), 1, column)
        rows_back_ref[place] = placed((width + half, width), 1, row)
        columns_back_ref[place * width : (place + 1) * width, :] = placed((width, width + half), 0, column)


def extract(rows, columns_ref, blocks, first_ref, second_ref):
    half = rows.shape[0] // 2
    span = blocks[0].shape[1]
    strip = dot(rows, jnp.concatenate(blocks, axis=1)).astype(jnp.bfloat16)
    for place, out_ref in enumerate((first_ref, second_ref)):
        mine = strip[place * half : (place + 1) * half]
        mine = jnp.concatenate([mine[:, :span], mine[:, span:]], axis=0)
        out_ref[...] = dot(mine, columns_ref[place]).astype(jnp.bfloat16)


def lower_kernel(rows_ref, columns_ref, tile_ref, below_ref, first_ref, second_ref, above_ref):
    half = below_ref.shape[2]
    blocks = [jnp.concatenate([below_ref[part], tile_ref[part]], axis=1) for part in range(2)]
    above_ref[:, :, :half] = below_ref[:, half:, :]
    above_ref[:, :, half:] = tile_ref[:, half:, :]
    extract(rows_ref[...], columns_ref, blocks, first_ref, second_ref)


def upper_kernel(rows_ref, columns_ref, tile_ref, below_ref, above_ref, cast_ref, first_ref, second_ref, level_ref):
    half = below_ref.shape[2]
    level_ref[...] = cast_ref[...]
    blocks = []
    for part in range(2):
        lower = jnp.concatenate([below_ref[part, :half], tile_ref[part, :half]], axis=1)
        blocks.append(jnp.concatenate([above_ref[part], lower], axis=0))
    extract(rows_ref[...], columns_ref, blocks, first_ref, second_ref)


def joined(patch_ref, index, upper_ref, lower_ref):
    half = upper_ref.shape[0] // 2
    for part in range(2):
        patch_ref[index, (2 * part) * half : (2 * part + 1) * half, :] = upper_ref[part * half : (part + 1) * half, :]
        patch_ref[index, (2 * part + 1) * half : (2 * part + 2) * half, :] = lower_ref[part * half : (part + 1) * half, :]


def forward(probe_ref, band_ref, patch_ref, spread_ref, first, last):
    for level in range(first, last + 1):
        if level == 0:
            spread_ref[0] = probe_ref[...]
        else:
            wave = complex_mul(spread_ref[level - 1], patch_ref[level - 1], 1.0).astype(jnp.bfloat16)
            spread = sandwich(band_ref[0], band_ref[1], wave, band_ref[2], band_ref[3])
            spread_ref[level] = spread.astype(jnp.bfloat16)


def head_kernel(probe_ref, band_ref, u0_ref, l0_ref, u1_ref, l1_ref, spread_ref, patch_ref):
    cut = lax.axis_index("cuts")

    @pl.when(cut < 2)
    def _():
        joined(patch_ref, cut, u0_ref, l0_ref)
        joined(patch_ref, 1 - cut, u1_ref, l1_ref)
        forward(probe_ref, band_ref, patch_ref, spread_ref, 0, 2)


def chain_kernel(
    probe_ref, u0_ref, l0_ref, u1_ref, l1_ref, u2_ref, l2_ref, u3_ref, l3_ref, level_ref, band_ref, fourier_ref, head_ref,
    mine_ref, other_ref, patch_ref, spread_ref, back_ref
):
    width = probe_ref.shape[1]
    cut = lax.axis_index("cuts")
    for mask, refs in enumerate(((u0_ref, l0_ref), (u1_ref, l1_ref), (u2_ref, l2_ref), (u3_ref, l3_ref))):
        joined(patch_ref, lax.bitwise_xor(cut, mask), *refs)

    @pl.when(cut < 2)
    def _():
        spread_ref[0:3] = head_ref[...]

    @pl.when(cut >= 2)
    def _():
        forward(probe_ref, band_ref, patch_ref, spread_ref, 0, 2)

    forward(probe_ref, band_ref, patch_ref, spread_ref, 3, 3)
    fourier_r, fourier_i = fourier_ref[0], fourier_ref[1]
    wave = complex_mul(spread_ref[3], patch_ref[3], 1.0).astype(jnp.bfloat16)
    far = sandwich(fourier_r, fourier_i, wave, fourier_r, fourier_i)
    far_r, far_i = far[:width], far[width:]
    level = level_ref[:width, :].astype(jnp.float32)
    live = level_ref[width : width + 1, :].astype(jnp.float32)
    excess = 2.0 * live * (far_r * far_r + far_i * far_i - level)
    residual = jnp.concatenate([excess * far_r, excess * far_i], axis=0).astype(jnp.bfloat16)
    back_ref[...] = sandwich(fourier_r, -fourier_i, residual, fourier_r, -fourier_i).astype(jnp.bfloat16)

    def term(level):
        value = complex_mul(spread_ref[level], back_ref[...], -1.0).astype(jnp.bfloat16)

        @pl.when(level == cut)
        def _():
            mine_ref[...] = value

        @pl.when(level != cut)
        def _():
            other_ref[...] = value

    def carry(level):
        carried = complex_mul(patch_ref[level], back_ref[...], -1.0).astype(jnp.bfloat16)
        back = sandwich(band_ref[2], -band_ref[3], carried, band_ref[0], -band_ref[1])
        back_ref[...] = back.astype(jnp.bfloat16)

    @pl.when(cut >= 2)
    def _():
        term(3)

    carry(3)

    @pl.when(cut >= 2)
    def _():
        term(2)

    @pl.when(cut < 2)
    def _():
        carry(2)
        term(1)
        carry(1)
        term(0)


def scatter_kernel(rows_ref, columns_ref, mine_ref, other_ref, tile_ref, below_ref, right_ref, own_ref):
    width = tile_ref.shape[1]
    half = width // 2
    strips = []
    for place, ref in enumerate((mine_ref, other_ref)):
        field = jnp.concatenate([ref[:width, :], ref[width:, :]], axis=1)
        strips.append(dot(rows_ref[place], field).astype(jnp.bfloat16))
    for part in range(2):
        strip = jnp.concatenate([strip[:, part * width : (part + 1) * width] for strip in strips], axis=1)
        total = dot(strip, columns_ref[...])
        tile_ref[part] = total[half:, half:]
        below_ref[part] = total[half:, :half].astype(jnp.bfloat16)
        right_ref[part] = total[:half, half:].astype(jnp.bfloat16)
        own_ref[part] = total[:half, :half].astype(jnp.bfloat16)


def total_kernel(tile_ref, below_ref, right_ref, own_ref, out_ref):
    half = right_ref.shape[1]
    below = below_ref[...].astype(jnp.float32)
    right = right_ref[...].astype(jnp.float32)
    own = own_ref[...].astype(jnp.float32)
    out_ref[0, :, :half, :half] = tile_ref[:, :half, :half]
    out_ref[0, :, :half, half:] = tile_ref[:, :half, half:] + below[:, :half]
    out_ref[0, :, half:, :half] = tile_ref[:, half:, :half] + right[:, :, :half]
    out_ref[0, :, half:, half:] = tile_ref[:, half:, half:] + below[:, half:] + right[:, :, half:] + own


VMEM = pl.BlockSpec(memory_space=pltpu.VMEM)
SMEM = pl.BlockSpec(memory_space=pltpu.SMEM)
PARAMS = pltpu.CompilerParams(vmem_limit_bytes=48 * 1024 * 1024)


def shaped(*shape, dtype=jnp.bfloat16):
    return jax.ShapeDtypeStruct(shape, dtype)


def kernel(body, name, in_specs, out_shape, scratch=()):
    return pl.pallas_call(
        body, in_specs=in_specs, out_specs=[VMEM] * len(out_shape), out_shape=out_shape, scratch_shapes=scratch, compiler_params=PARAMS, name=name
    )


def local(object_slices, probe, fresnel_taps, offsets, counts, measured):
    width = probe.shape[1]
    half = width // 2
    wide = width + half
    full = shaped(2 * width, width)
    part = shaped(width, width)
    row_tiles = max(lax.axis_size("tile") // 16, 2)
    tile = object_slices[0]
    probe = probe.reshape(2 * width, width)
    fourier = jnp.asarray(fourier_matrix(width), jnp.bfloat16)

    below = passed_along(tile[:, :, half:], "tile", 1)
    offsets = passed_along(offsets, "tile", row_tiles + 1)
    level = shaped(width + 16, width)
    band, level = kernel(band_kernel, "band", [SMEM, VMEM, VMEM], [shaped(4, width, width), level])(counts, fresnel_taps, measured)
    rows, columns, rows_back, columns_back = kernel(
        window_kernel,
        "window",
        [SMEM],
        [part, shaped(2, wide, width), shaped(2, wide, width), shaped(2 * width, wide)],
    )(offsets)
    first_l, second_l, above = kernel(lower_kernel, "lower", [VMEM] * 4, [part, part, shaped(2, half, wide)])(rows, columns, tile, below)
    above = passed_along(above, "tile", row_tiles)
    straight_l = crossed(first_l, "cuts", 2)
    diagonal_l = crossed(second_l, "cuts", 3)
    swapped_l = crossed(second_l, "cuts", 1)
    first_u, second_u, level = kernel(upper_kernel, "upper", [VMEM] * 6, [part, part, level])(rows, columns, tile, below, above, level)
    first_u, second_u, straight_l, diagonal_l = lax.optimization_barrier((first_u, second_u, straight_l, diagonal_l))
    straight_u = crossed(first_u, "cuts", 2)
    diagonal_u = crossed(second_u, "cuts", 3)
    swapped_u = crossed(second_u, "cuts", 1)
    level = passed_along(level, "tile", row_tiles + 1)
    (head,) = kernel(head_kernel, "head", [VMEM] * 6, [shaped(3, 2 * width, width)], [pltpu.VMEM((2, 2 * width, width), jnp.bfloat16)])(
        probe, band, first_u, first_l, swapped_u, swapped_l
    )
    mine, other = kernel(
        chain_kernel,
        "chain",
        [VMEM] * 13,
        [full, full],
        [
            pltpu.VMEM((4, 2 * width, width), jnp.bfloat16),
            pltpu.VMEM((4, 2 * width, width), jnp.bfloat16),
            pltpu.VMEM((2 * width, width), jnp.bfloat16),
        ],
    )(probe, first_u, first_l, swapped_u, swapped_l, straight_u, straight_l, diagonal_u, diagonal_l, level, band, fourier, head)
    other = crossed(other, "cuts", 1)
    total, below, right, own = kernel(
        scatter_kernel,
        "scatter",
        [VMEM] * 4,
        [shaped(2, width, width, dtype=jnp.float32), shaped(2, width, half), shaped(2, half, width), shaped(2, half, half)],
    )(rows_back, columns_back, mine, other)
    below = passed_along(below, "tile", -1)
    right = passed_along(right, "tile", -row_tiles)
    own = passed_along(own, "tile", -row_tiles - 1)
    (out,) = kernel(total_kernel, "total", [VMEM] * 4, [shaped(1, 2, width, width, dtype=jnp.float32)])(total, below, right, own)
    return out


def solution(mesh):
    return jax.shard_map(
        local,
        mesh=mesh,
        in_specs=(
            P("cuts", None, "tile", None),
            P(),
            P(),
            P("tile", None),
            P("tile"),
            P("tile", None, None),
        ),
        out_specs=P("cuts", None, "tile", None),
        check_vma=False,
    )
```

```python
import jax
import jax.numpy as jnp
import numpy as np
from jax import lax
from jax.experimental import pallas as pl
from jax.experimental.pallas import tpu as pltpu
from jax.sharding import PartitionSpec as P


def passed_along(value, axis, steps):
    count = lax.axis_size(axis)
    pairs = [(source, (source + steps) % count) for source in range(count)]
    return lax.ppermute(value, axis, pairs)


def crossed(value, axis, mask):
    pairs = [(source, source ^ mask) for source in range(lax.axis_size(axis))]
    return lax.ppermute(value, axis, pairs)


def fourier_matrix(width):
    index = np.arange(width)
    angle = 2.0 * np.pi * (index[:, None] * index[None, :] % width) / width
    return np.stack([np.cos(angle), -np.sin(angle)]) / np.sqrt(width)


def dot(left, right):
    return jnp.dot(left, right, preferred_element_type=jnp.float32)


def left_product(real, imag, field):
    top = jnp.concatenate([real, -imag], axis=1)
    bottom = jnp.concatenate([imag, real], axis=1)
    return dot(jnp.concatenate([top, bottom], axis=0), field)


def right_product(field, real, imag):
    width = real.shape[0]
    turned = jnp.concatenate([-field[width:], field[:width]], axis=0)
    return dot(jnp.concatenate([field, turned], axis=1), jnp.concatenate([real, imag], axis=0))


def sandwich(left_real, left_imag, field, right_real, right_imag):
    inner = left_product(left_real, left_imag, field).astype(jnp.bfloat16)
    return right_product(inner, right_real, right_imag)


def complex_mul(first, second, sign):
    width = first.shape[1]
    fr = first[:width].astype(jnp.float32)
    fi = first[width:].astype(jnp.float32) * sign
    sr = second[:width].astype(jnp.float32)
    si = second[width:].astype(jnp.float32)
    return jnp.concatenate([fr * sr - fi * si, fr * si + fi * sr], axis=0)


def band_kernel(counts_ref, taps_ref, measured_ref, band_ref, level_ref):
    width = band_ref.shape[1]
    half = taps_ref.shape[1] // 2
    core = lax.rem(lax.axis_index("cuts"), 2)
    level_ref[:width, :] = measured_ref[core].astype(jnp.bfloat16)
    live = (core < counts_ref[0]).astype(jnp.float32)
    level_ref[width:, :] = jnp.full((level_ref.shape[0] - width, width), live, jnp.float32).astype(jnp.bfloat16)
    rows = lax.broadcasted_iota(jnp.int32, (width, width), 0)
    columns = lax.broadcasted_iota(jnp.int32, (width, width), 1)
    inside = jnp.abs(columns - rows) <= half
    for part in range(2):
        line = taps_ref[part : part + 1, :].astype(jnp.float32)
        filler = jnp.zeros((1, width - line.shape[1]), jnp.float32)
        line = jnp.concatenate([line, filler], axis=1)
        spread = jnp.broadcast_to(line, (width, width))
        turned = pltpu.roll(spread, width - half, 1, stride=1, stride_axis=0)
        band = jnp.where(inside, turned, 0.0)
        band_ref[part] = band.astype(jnp.bfloat16)
        band_ref[part + 2] = band.T.astype(jnp.bfloat16)


def window_kernel(offsets_ref, rows_ref, columns_ref, rows_back_ref, columns_back_ref):
    half = rows_ref.shape[0] // 2
    width = 2 * half
    core = lax.rem(lax.axis_index("cuts"), 2)

    def placed(shape, axis, shift):
        i = lax.broadcasted_iota(jnp.int32, shape, axis)
        j = lax.broadcasted_iota(jnp.int32, shape, 1 - axis)
        return jnp.where(j - i == shift, 1.0, 0.0).astype(jnp.bfloat16)

    for place, slot in enumerate((core, 1 - core)):
        row = offsets_ref[slot, 0] - half
        column = offsets_ref[slot, 1] - half
        rows_ref[place * half : (place + 1) * half, :] = placed((half, width), 0, row)
        columns_ref[place] = placed((width + half, width), 1, column)
        rows_back_ref[place] = placed((width + half, width), 1, row)
        columns_back_ref[place * width : (place + 1) * width, :] = placed((width, width + half), 0, column)


def extract(rows, columns_ref, blocks, first_ref, second_ref):
    half = rows.shape[0] // 2
    span = blocks[0].shape[1]
    strip = dot(rows, jnp.concatenate(blocks, axis=1)).astype(jnp.bfloat16)
    for place, out_ref in enumerate((first_ref, second_ref)):
        mine = strip[place * half : (place + 1) * half]
        mine = jnp.concatenate([mine[:, :span], mine[:, span:]], axis=0)
        out_ref[...] = dot(mine, columns_ref[place]).astype(jnp.bfloat16)


def pack_kernel(tile_ref, below_ref, above_ref):
    half = below_ref.shape[2]
    above_ref[:, :, :half] = below_ref[:, half:, :]
    above_ref[:, :, half:] = tile_ref[:, half:, :]


def lower_kernel(rows_ref, columns_ref, tile_ref, below_ref, far_tile_ref, far_below_ref, first_ref, far_first_ref, second_ref):
    width = rows_ref.shape[1]
    pairs = (tile_ref, below_ref, first_ref, 0), (far_tile_ref, far_below_ref, far_first_ref, width)
    for here_ref, left_ref, out_ref, row in pairs:
        blocks = [jnp.concatenate([left_ref[part], here_ref[part]], axis=1) for part in range(2)]
        extract(rows_ref[...], columns_ref, blocks, out_ref, second_ref.at[row : row + width])


def upper_kernel(rows_ref, columns_ref, tile_ref, below_ref, above_ref, cast_ref, first_ref, second_ref, level_ref):
    half = below_ref.shape[2]
    level_ref[...] = cast_ref[...]
    blocks = []
    for part in range(2):
        lower = jnp.concatenate([below_ref[part, :half], tile_ref[part, :half]], axis=1)
        blocks.append(jnp.concatenate([above_ref[part], lower], axis=0))
    extract(rows_ref[...], columns_ref, blocks, first_ref, second_ref)


def joined(patch_ref, index, upper_ref, lower_ref):
    half = upper_ref.shape[0] // 2
    for part in range(2):
        patch_ref[index, (2 * part) * half : (2 * part + 1) * half, :] = upper_ref[part * half : (part + 1) * half, :]
        patch_ref[index, (2 * part + 1) * half : (2 * part + 2) * half, :] = lower_ref[part * half : (part + 1) * half, :]


def forward(probe_ref, band_ref, patch_ref, spread_ref, first, last):
    for level in range(first, last + 1):
        if level == 0:
            spread_ref[0] = probe_ref[...]
        else:
            wave = complex_mul(spread_ref[level - 1], patch_ref[level - 1], 1.0).astype(jnp.bfloat16)
            spread = sandwich(band_ref[0], band_ref[1], wave, band_ref[2], band_ref[3])
            spread_ref[level] = spread.astype(jnp.bfloat16)


def head_kernel(probe_ref, band_ref, u0_ref, l0_ref, u1_ref, l13_ref, spread_ref, patch_ref):
    cut = lax.axis_index("cuts")
    l1_ref = l13_ref.at[: probe_ref.shape[1]]

    @pl.when(cut < 2)
    def _():
        joined(patch_ref, cut, u0_ref, l0_ref)
        joined(patch_ref, 1 - cut, u1_ref, l1_ref)
        forward(probe_ref, band_ref, patch_ref, spread_ref, 0, 2)


def chain_kernel(
    probe_ref, u0_ref, l0_ref, u1_ref, l13_ref, u2_ref, l2_ref, u3_ref, level_ref, band_ref, fourier_ref, head_ref,
    mine_ref, other_ref, patch_ref, spread_ref, back_ref
):
    width = probe_ref.shape[1]
    cut = lax.axis_index("cuts")
    l1_ref, l3_ref = l13_ref.at[:width], l13_ref.at[width:]
    for mask, refs in enumerate(((u0_ref, l0_ref), (u1_ref, l1_ref), (u2_ref, l2_ref), (u3_ref, l3_ref))):
        joined(patch_ref, lax.bitwise_xor(cut, mask), *refs)

    @pl.when(cut < 2)
    def _():
        spread_ref[0:3] = head_ref[...]

    @pl.when(cut >= 2)
    def _():
        forward(probe_ref, band_ref, patch_ref, spread_ref, 0, 2)

    forward(probe_ref, band_ref, patch_ref, spread_ref, 3, 3)
    fourier_r, fourier_i = fourier_ref[0], fourier_ref[1]
    wave = complex_mul(spread_ref[3], patch_ref[3], 1.0).astype(jnp.bfloat16)
    far = sandwich(fourier_r, fourier_i, wave, fourier_r, fourier_i)
    far_r, far_i = far[:width], far[width:]
    level = level_ref[:width, :].astype(jnp.float32)
    live = level_ref[width : width + 1, :].astype(jnp.float32)
    excess = 2.0 * live * (far_r * far_r + far_i * far_i - level)
    residual = jnp.concatenate([excess * far_r, excess * far_i], axis=0).astype(jnp.bfloat16)
    back_ref[...] = sandwich(fourier_r, -fourier_i, residual, fourier_r, -fourier_i).astype(jnp.bfloat16)

    def term(level):
        value = complex_mul(spread_ref[level], back_ref[...], -1.0).astype(jnp.bfloat16)

        @pl.when(level == cut)
        def _():
            mine_ref[...] = value

        @pl.when(level != cut)
        def _():
            other_ref[...] = value

    def carry(level):
        carried = complex_mul(patch_ref[level], back_ref[...], -1.0).astype(jnp.bfloat16)
        back = sandwich(band_ref[2], -band_ref[3], carried, band_ref[0], -band_ref[1])
        back_ref[...] = back.astype(jnp.bfloat16)

    @pl.when(cut >= 2)
    def _():
        term(3)

    carry(3)

    @pl.when(cut >= 2)
    def _():
        term(2)

    @pl.when(cut < 2)
    def _():
        carry(2)
        term(1)
        carry(1)
        term(0)


def scatter_kernel(rows_ref, columns_ref, mine_ref, other_ref, tile_ref, below_ref, right_ref, own_ref):
    width = tile_ref.shape[1]
    half = width // 2
    strips = []
    for place, ref in enumerate((mine_ref, other_ref)):
        field = jnp.concatenate([ref[:width, :], ref[width:, :]], axis=1)
        strips.append(dot(rows_ref[place], field).astype(jnp.bfloat16))
    for part in range(2):
        strip = jnp.concatenate([strip[:, part * width : (part + 1) * width] for strip in strips], axis=1)
        total = dot(strip, columns_ref[...])
        tile_ref[part] = total[half:, half:]
        below_ref[part] = total[half:, :half].astype(jnp.bfloat16)
        right_ref[part] = total[:half, half:].astype(jnp.bfloat16)
        own_ref[part] = total[:half, :half].astype(jnp.bfloat16)


def total_kernel(tile_ref, below_ref, right_ref, own_ref, out_ref):
    half = right_ref.shape[1]
    below = below_ref[...].astype(jnp.float32)
    right = right_ref[...].astype(jnp.float32)
    own = own_ref[...].astype(jnp.float32)
    out_ref[0, :, :half, :half] = tile_ref[:, :half, :half]
    out_ref[0, :, :half, half:] = tile_ref[:, :half, half:] + below[:, :half]
    out_ref[0, :, half:, :half] = tile_ref[:, half:, :half] + right[:, :, :half]
    out_ref[0, :, half:, half:] = tile_ref[:, half:, half:] + below[:, half:] + right[:, :, half:] + own


VMEM = pl.BlockSpec(memory_space=pltpu.VMEM)
SMEM = pl.BlockSpec(memory_space=pltpu.SMEM)
PARAMS = pltpu.CompilerParams(vmem_limit_bytes=48 * 1024 * 1024)


def shaped(*shape, dtype=jnp.bfloat16):
    return jax.ShapeDtypeStruct(shape, dtype)


def kernel(body, name, in_specs, out_shape, scratch=()):
    return pl.pallas_call(
        body, in_specs=in_specs, out_specs=[VMEM] * len(out_shape), out_shape=out_shape, scratch_shapes=scratch, compiler_params=PARAMS, name=name
    )


def local(object_slices, probe, fresnel_taps, offsets, counts, measured):
    width = probe.shape[1]
    half = width // 2
    wide = width + half
    full = shaped(2 * width, width)
    part = shaped(width, width)
    row_tiles = max(lax.axis_size("tile") // 16, 2)
    tile = object_slices[0]
    probe = probe.reshape(2 * width, width)
    fourier = jnp.asarray(fourier_matrix(width), jnp.bfloat16)

    below = passed_along(tile[:, :, half:], "tile", 1)
    far_tile = crossed(tile, "cuts", 2)
    offsets = passed_along(offsets, "tile", row_tiles + 1)
    level = shaped(width + 16, width)
    band, level = kernel(band_kernel, "band", [SMEM, VMEM, VMEM], [shaped(4, width, width), level])(counts, fresnel_taps, measured)
    rows, columns, rows_back, columns_back = kernel(
        window_kernel,
        "window",
        [SMEM],
        [part, shaped(2, wide, width), shaped(2, wide, width), shaped(2 * width, wide)],
    )(offsets)
    (above,) = kernel(pack_kernel, "pack", [VMEM] * 2, [shaped(2, half, wide)])(tile, below)
    above = passed_along(above, "tile", row_tiles)
    far_below = crossed(below, "cuts", 2)
    first_u, second_u, level = kernel(upper_kernel, "upper", [VMEM] * 6, [part, part, level])(rows, columns, tile, below, above, level)
    straight_u = crossed(first_u, "cuts", 2)
    diagonal_u = crossed(second_u, "cuts", 3)
    swapped_u = crossed(second_u, "cuts", 1)
    level = passed_along(level, "tile", row_tiles + 1)
    first_l, straight_l, second_l = kernel(lower_kernel, "lower", [VMEM] * 6, [part, part, full])(
        rows, columns, tile, below, far_tile, far_below
    )
    swapped_l = crossed(second_l, "cuts", 1)
    (head,) = kernel(head_kernel, "head", [VMEM] * 6, [shaped(3, 2 * width, width)], [pltpu.VMEM((2, 2 * width, width), jnp.bfloat16)])(
        probe, band, first_u, first_l, swapped_u, swapped_l
    )
    mine, other = kernel(
        chain_kernel,
        "chain",
        [VMEM] * 12,
        [full, full],
        [
            pltpu.VMEM((4, 2 * width, width), jnp.bfloat16),
            pltpu.VMEM((4, 2 * width, width), jnp.bfloat16),
            pltpu.VMEM((2 * width, width), jnp.bfloat16),
        ],
    )(probe, first_u, first_l, swapped_u, swapped_l, straight_u, straight_l, diagonal_u, level, band, fourier, head)
    other = crossed(other, "cuts", 1)
    total, below, right, own = kernel(
        scatter_kernel,
        "scatter",
        [VMEM] * 4,
        [shaped(2, width, width, dtype=jnp.float32), shaped(2, width, half), shaped(2, half, width), shaped(2, half, half)],
    )(rows_back, columns_back, mine, other)
    below = passed_along(below, "tile", -1)
    right = passed_along(right, "tile", -row_tiles)
    own = passed_along(own, "tile", -row_tiles - 1)
    (out,) = kernel(total_kernel, "total", [VMEM] * 4, [shaped(1, 2, width, width, dtype=jnp.float32)])(total, below, right, own)
    return out


def solution(mesh):
    return jax.shard_map(
        local,
        mesh=mesh,
        in_specs=(
            P("cuts", None, "tile", None),
            P(),
            P(),
            P("tile", None),
            P("tile"),
            P("tile", None, None),
        ),
        out_specs=P("cuts", None, "tile", None),
        check_vma=False,
    )
```

```python
import jax
import jax.numpy as jnp
import numpy as np
from jax import lax
from jax.experimental import pallas as pl
from jax.experimental.pallas import tpu as pltpu
from jax.sharding import PartitionSpec as P


def passed_along(value, axis, steps):
    count = lax.axis_size(axis)
    pairs = [(source, (source + steps) % count) for source in range(count)]
    return lax.ppermute(value, axis, pairs)


def crossed(value, axis, mask):
    pairs = [(source, source ^ mask) for source in range(lax.axis_size(axis))]
    return lax.ppermute(value, axis, pairs)


def fourier_matrix(width):
    index = np.arange(width)
    angle = 2.0 * np.pi * (index[:, None] * index[None, :] % width) / width
    return np.stack([np.cos(angle), -np.sin(angle)]) / np.sqrt(width)


def dot(left, right):
    return jnp.dot(left, right, preferred_element_type=jnp.float32)


def left_product(real, imag, field):
    top = jnp.concatenate([real, -imag], axis=1)
    bottom = jnp.concatenate([imag, real], axis=1)
    return dot(jnp.concatenate([top, bottom], axis=0), field)


def right_product(field, real, imag):
    width = real.shape[0]
    turned = jnp.concatenate([-field[width:], field[:width]], axis=0)
    return dot(jnp.concatenate([field, turned], axis=1), jnp.concatenate([real, imag], axis=0))


def sandwich(left_real, left_imag, field, right_real, right_imag):
    inner = left_product(left_real, left_imag, field).astype(jnp.bfloat16)
    return right_product(inner, right_real, right_imag)


def complex_mul(first, second, sign):
    width = first.shape[1]
    fr = first[:width].astype(jnp.float32)
    fi = first[width:].astype(jnp.float32) * sign
    sr = second[:width].astype(jnp.float32)
    si = second[width:].astype(jnp.float32)
    return jnp.concatenate([fr * sr - fi * si, fr * si + fi * sr], axis=0)


def band_kernel(counts_ref, taps_ref, measured_ref, band_ref, level_ref):
    width = band_ref.shape[1]
    half = taps_ref.shape[1] // 2
    core = lax.rem(lax.axis_index("cuts"), 2)
    level_ref[:width, :] = measured_ref[core].astype(jnp.bfloat16)
    live = (core < counts_ref[0]).astype(jnp.float32)
    level_ref[width:, :] = jnp.full((level_ref.shape[0] - width, width), live, jnp.float32).astype(jnp.bfloat16)
    rows = lax.broadcasted_iota(jnp.int32, (width, width), 0)
    columns = lax.broadcasted_iota(jnp.int32, (width, width), 1)
    inside = jnp.abs(columns - rows) <= half
    for part in range(2):
        line = taps_ref[part : part + 1, :].astype(jnp.float32)
        filler = jnp.zeros((1, width - line.shape[1]), jnp.float32)
        line = jnp.concatenate([line, filler], axis=1)
        spread = jnp.broadcast_to(line, (width, width))
        turned = pltpu.roll(spread, width - half, 1, stride=1, stride_axis=0)
        band = jnp.where(inside, turned, 0.0)
        band_ref[part] = band.astype(jnp.bfloat16)
        band_ref[part + 2] = band.T.astype(jnp.bfloat16)


def cut_kernel(tile_ref, offsets_ref, right_ref, own_ref):
    half = right_ref.shape[1]
    right_ref[...] = tile_ref[:, half:, :]
    own_ref[:, :half, :] = tile_ref[:, half:, half:]
    shape = (own_ref.shape[1] - half, half)
    line = lax.broadcasted_iota(jnp.int32, shape, 0)
    lines = jnp.zeros(shape, jnp.float32)
    for index in range(4):
        value = offsets_ref[index // 2 : index // 2 + 1, index % 2 : index % 2 + 1].astype(jnp.float32)
        lines = jnp.where(line == index, value, lines)
    for part in range(2):
        own_ref[part, half:, :] = lines.astype(jnp.bfloat16)


def window_kernel(own_ref, rows_ref, columns_ref, rows_back_ref, columns_back_ref):
    half = own_ref.shape[2]
    width = 2 * half
    core = lax.rem(lax.axis_index("cuts"), 2)
    lines = own_ref[0, half:, :].astype(jnp.float32).astype(jnp.int32) - half

    def placed(shape, axis, shift):
        i = lax.broadcasted_iota(jnp.int32, shape, axis)
        j = lax.broadcasted_iota(jnp.int32, shape, 1 - axis)
        shift = jnp.concatenate([shift] * (shape[1] // half), axis=1)
        return jnp.where(j - i == shift, 1.0, 0.0).astype(jnp.bfloat16)

    for place in range(2):
        second = core != place
        row = jnp.where(second, lines[2:3], lines[0:1])
        column = jnp.where(second, lines[3:4], lines[1:2])
        rows_ref[place * half : (place + 1) * half, :] = placed((half, width), 0, row)
        columns_ref[place] = placed((width + half, width), 1, column)
        rows_back_ref[place] = placed((width + half, width), 1, row)
        columns_back_ref[place * width : (place + 1) * width, :] = placed((width, width + half), 0, column)


def extract_kernel(rows_ref, columns_ref, tile_ref, below_ref, right_ref, own_ref, first_ref, second_ref):
    width = tile_ref.shape[1]
    half = width // 2
    wide = width + half
    blocks = []
    for part in range(2):
        upper = jnp.concatenate([own_ref[part, :half], right_ref[part]], axis=1)
        lower = jnp.concatenate([below_ref[part], tile_ref[part]], axis=1)
        blocks.append(jnp.concatenate([upper, lower], axis=0))
    block = jnp.concatenate(blocks, axis=1)
    strips = [dot(rows_ref[...], block[top : top + width]).astype(jnp.bfloat16) for top in (0, half)]
    for place, out_ref in enumerate((first_ref, second_ref)):
        mine = [strip[place * half : (place + 1) * half, part * wide : (part + 1) * wide] for part in range(2) for strip in strips]
        out_ref[...] = dot(jnp.concatenate(mine, axis=0), columns_ref[place]).astype(jnp.bfloat16)


def forward(probe_ref, band_ref, patch_ref, spread_ref, first, last):
    for level in range(first, last + 1):
        if level == 0:
            spread_ref[0] = probe_ref[...]
        else:
            wave = complex_mul(spread_ref[level - 1], patch_ref[level - 1], 1.0).astype(jnp.bfloat16)
            spread = sandwich(band_ref[0], band_ref[1], wave, band_ref[2], band_ref[3])
            spread_ref[level] = spread.astype(jnp.bfloat16)


def head_kernel(probe_ref, band_ref, p0_ref, p1_ref, spread_ref, patch_ref):
    cut = lax.axis_index("cuts")

    @pl.when(cut < 2)
    def _():
        patch_ref[cut] = p0_ref[...]
        patch_ref[1 - cut] = p1_ref[...]
        forward(probe_ref, band_ref, patch_ref, spread_ref, 0, 2)


def chain_kernel(
    probe_ref, p0_ref, p1_ref, p2_ref, p3_ref, level_ref, band_ref, fourier_ref, head_ref, mine_ref, other_ref, patch_ref, spread_ref, back_ref
):
    width = probe_ref.shape[1]
    cut = lax.axis_index("cuts")
    for mask, ref in enumerate((p0_ref, p1_ref, p2_ref, p3_ref)):
        patch_ref[lax.bitwise_xor(cut, mask)] = ref[...]

    @pl.when(cut < 2)
    def _():
        spread_ref[0:3] = head_ref[...]

    @pl.when(cut >= 2)
    def _():
        forward(probe_ref, band_ref, patch_ref, spread_ref, 0, 2)

    forward(probe_ref, band_ref, patch_ref, spread_ref, 3, 3)
    fourier_r, fourier_i = fourier_ref[0], fourier_ref[1]
    wave = complex_mul(spread_ref[3], patch_ref[3], 1.0).astype(jnp.bfloat16)
    far = sandwich(fourier_r, fourier_i, wave, fourier_r, fourier_i)
    far_r, far_i = far[:width], far[width:]
    level = level_ref[:width, :].astype(jnp.float32)
    live = level_ref[width : width + 1, :].astype(jnp.float32)
    excess = 2.0 * live * (far_r * far_r + far_i * far_i - level)
    residual = jnp.concatenate([excess * far_r, excess * far_i], axis=0).astype(jnp.bfloat16)
    back_ref[...] = sandwich(fourier_r, -fourier_i, residual, fourier_r, -fourier_i).astype(jnp.bfloat16)

    def term(level):
        value = complex_mul(spread_ref[level], back_ref[...], -1.0).astype(jnp.bfloat16)

        @pl.when(level == cut)
        def _():
            mine_ref[...] = value

        @pl.when(level != cut)
        def _():
            other_ref[...] = value

    def carry(level):
        carried = complex_mul(patch_ref[level], back_ref[...], -1.0).astype(jnp.bfloat16)
        back = sandwich(band_ref[2], -band_ref[3], carried, band_ref[0], -band_ref[1])
        back_ref[...] = back.astype(jnp.bfloat16)

    @pl.when(cut >= 2)
    def _():
        term(3)

    carry(3)

    @pl.when(cut >= 2)
    def _():
        term(2)

    @pl.when(cut < 2)
    def _():
        carry(2)
        term(1)
        carry(1)
        term(0)


def scatter_kernel(rows_ref, columns_ref, mine_ref, other_ref, tile_ref, below_ref, right_ref, own_ref):
    width = tile_ref.shape[1]
    half = width // 2
    strips = []
    for place, ref in enumerate((mine_ref, other_ref)):
        field = jnp.concatenate([ref[:width, :], ref[width:, :]], axis=1)
        strips.append(dot(rows_ref[place], field).astype(jnp.bfloat16))
    for part in range(2):
        strip = jnp.concatenate([strip[:, part * width : (part + 1) * width] for strip in strips], axis=1)
        total = dot(strip, columns_ref[...])
        tile_ref[part] = total[half:, half:]
        below_ref[part] = total[half:, :half].astype(jnp.bfloat16)
        right_ref[part] = total[:half, half:].astype(jnp.bfloat16)
        own_ref[part] = total[:half, :half].astype(jnp.bfloat16)


def total_kernel(tile_ref, below_ref, right_ref, own_ref, out_ref):
    half = right_ref.shape[1]
    below = below_ref[...].astype(jnp.float32)
    right = right_ref[...].astype(jnp.float32)
    own = own_ref[...].astype(jnp.float32)
    out_ref[0, :, :half, :half] = tile_ref[:, :half, :half]
    out_ref[0, :, :half, half:] = tile_ref[:, :half, half:] + below[:, :half]
    out_ref[0, :, half:, :half] = tile_ref[:, half:, :half] + right[:, :, :half]
    out_ref[0, :, half:, half:] = tile_ref[:, half:, half:] + below[:, half:] + right[:, :, half:] + own


VMEM = pl.BlockSpec(memory_space=pltpu.VMEM)
SMEM = pl.BlockSpec(memory_space=pltpu.SMEM)
PARAMS = pltpu.CompilerParams(vmem_limit_bytes=48 * 1024 * 1024)


def shaped(*shape, dtype=jnp.bfloat16):
    return jax.ShapeDtypeStruct(shape, dtype)


def kernel(body, name, in_specs, out_shape, scratch=()):
    return pl.pallas_call(
        body, in_specs=in_specs, out_specs=[VMEM] * len(out_shape), out_shape=out_shape, scratch_shapes=scratch, compiler_params=PARAMS, name=name
    )


def local(object_slices, probe, fresnel_taps, offsets, counts, measured):
    width = probe.shape[1]
    half = width // 2
    wide = width + half
    full = shaped(2 * width, width)
    part = shaped(width, width)
    row_tiles = max(lax.axis_size("tile") // 16, 2)
    tile = object_slices[0]
    probe = probe.reshape(2 * width, width)
    fourier = jnp.asarray(fourier_matrix(width), jnp.bfloat16)

    below = passed_along(tile[:, :, half:], "tile", 1)
    far_tile = crossed(tile, "cuts", 2)
    right, own = kernel(cut_kernel, "cut", [VMEM] * 2, [shaped(2, half, width), shaped(2, half + 16, half)])(tile, offsets)
    right = passed_along(right, "tile", row_tiles)
    own = passed_along(own, "tile", row_tiles + 1)
    far_below = crossed(below, "cuts", 2)
    far_right = crossed(right, "cuts", 2)
    far_own = crossed(own, "cuts", 2)
    level = shaped(width + 16, width)
    band, level = kernel(band_kernel, "band", [SMEM, VMEM, VMEM], [shaped(4, width, width), level])(counts, fresnel_taps, measured)
    level, right = lax.optimization_barrier((level, right))
    level = passed_along(level, "tile", row_tiles + 1)
    rows, columns, rows_back, columns_back = kernel(
        window_kernel,
        "window",
        [VMEM],
        [part, shaped(2, wide, width), shaped(2, wide, width), shaped(2 * width, wide)],
    )(own)
    first, second = kernel(extract_kernel, "near", [VMEM] * 6, [full, full])(rows, columns, tile, below, right, own)
    swapped = crossed(second, "cuts", 1)
    far_own, level = lax.optimization_barrier((far_own, level))
    straight, far_second = kernel(extract_kernel, "far", [VMEM] * 6, [full, full])(rows, columns, far_tile, far_below, far_right, far_own)
    diagonal = crossed(far_second, "cuts", 1)
    (head,) = kernel(head_kernel, "head", [VMEM] * 4, [shaped(3, 2 * width, width)], [pltpu.VMEM((2, 2 * width, width), jnp.bfloat16)])(
        probe, band, first, swapped
    )
    mine, other = kernel(
        chain_kernel,
        "chain",
        [VMEM] * 9,
        [full, full],
        [
            pltpu.VMEM((4, 2 * width, width), jnp.bfloat16),
            pltpu.VMEM((4, 2 * width, width), jnp.bfloat16),
            pltpu.VMEM((2 * width, width), jnp.bfloat16),
        ],
    )(probe, first, swapped, straight, diagonal, level, band, fourier, head)
    other = crossed(other, "cuts", 1)
    total, below, right, own = kernel(
        scatter_kernel,
        "scatter",
        [VMEM] * 4,
        [shaped(2, width, width, dtype=jnp.float32), shaped(2, width, half), shaped(2, half, width), shaped(2, half, half)],
    )(rows_back, columns_back, mine, other)
    below = passed_along(below, "tile", -1)
    right = passed_along(right, "tile", -row_tiles)
    own = passed_along(own, "tile", -row_tiles - 1)
    (out,) = kernel(total_kernel, "total", [VMEM] * 4, [shaped(1, 2, width, width, dtype=jnp.float32)])(total, below, right, own)
    return out


def solution(mesh):
    return jax.shard_map(
        local,
        mesh=mesh,
        in_specs=(
            P("cuts", None, "tile", None),
            P(),
            P(),
            P("tile", None),
            P("tile"),
            P("tile", None, None),
        ),
        out_specs=P("cuts", None, "tile", None),
        check_vma=False,
    )
```

```python
import jax
import jax.numpy as jnp
import numpy as np
from jax import lax
from jax.experimental import pallas as pl
from jax.experimental.pallas import tpu as pltpu
from jax.sharding import PartitionSpec as P


def passed_along(value, axis, steps):
    count = lax.axis_size(axis)
    pairs = [(source, (source + steps) % count) for source in range(count)]
    return lax.ppermute(value, axis, pairs)


def crossed(value, axis, mask):
    pairs = [(source, source ^ mask) for source in range(lax.axis_size(axis))]
    return lax.ppermute(value, axis, pairs)


def stepped(value, axis, even, odd):
    count = lax.axis_size(axis)
    pairs = [(source, (source + (odd if source % 2 else even)) % count) for source in range(count)]
    return lax.ppermute(value, axis, pairs)


def fourier_matrix(width):
    index = np.arange(width)
    angle = 2.0 * np.pi * (index[:, None] * index[None, :] % width) / width
    return np.stack([np.cos(angle), -np.sin(angle)]) / np.sqrt(width)


def dot(left, right):
    return jnp.dot(left, right, preferred_element_type=jnp.float32)


def left_product(real, imag, field):
    top = jnp.concatenate([real, -imag], axis=1)
    bottom = jnp.concatenate([imag, real], axis=1)
    return dot(jnp.concatenate([top, bottom], axis=0), field)


def right_product(field, real, imag):
    width = real.shape[0]
    turned = jnp.concatenate([-field[width:], field[:width]], axis=0)
    return dot(jnp.concatenate([field, turned], axis=1), jnp.concatenate([real, imag], axis=0))


def sandwich(left_real, left_imag, field, right_real, right_imag):
    inner = left_product(left_real, left_imag, field).astype(jnp.bfloat16)
    return right_product(inner, right_real, right_imag)


def complex_mul(first, second, sign):
    width = first.shape[1]
    fr = first[:width].astype(jnp.float32)
    fi = first[width:].astype(jnp.float32) * sign
    sr = second[:width].astype(jnp.float32)
    si = second[width:].astype(jnp.float32)
    return jnp.concatenate([fr * sr - fi * si, fr * si + fi * sr], axis=0)


def band_kernel(counts_ref, taps_ref, measured_ref, band_ref, level_ref):
    width = band_ref.shape[1]
    half = taps_ref.shape[1] // 2
    core = lax.rem(lax.axis_index("cuts"), 2)
    level_ref[:width, :] = measured_ref[core].astype(jnp.bfloat16)
    live = (core < counts_ref[0]).astype(jnp.float32)
    level_ref[width:, :] = jnp.full((level_ref.shape[0] - width, width), live, jnp.float32).astype(jnp.bfloat16)
    rows = lax.broadcasted_iota(jnp.int32, (width, width), 0)
    columns = lax.broadcasted_iota(jnp.int32, (width, width), 1)
    inside = jnp.abs(columns - rows) <= half
    for part in range(2):
        line = taps_ref[part : part + 1, :].astype(jnp.float32)
        filler = jnp.zeros((1, width - line.shape[1]), jnp.float32)
        line = jnp.concatenate([line, filler], axis=1)
        spread = jnp.broadcast_to(line, (width, width))
        turned = pltpu.roll(spread, width - half, 1, stride=1, stride_axis=0)
        band = jnp.where(inside, turned, 0.0)
        band_ref[part] = band.astype(jnp.bfloat16)
        band_ref[part + 2] = band.T.astype(jnp.bfloat16)


def cut_kernel(tile_ref, offsets_ref, whole_ref, below_ref, right_ref, own_ref, small_ref, sems):
    half = below_ref.shape[2]
    high = pl.ds(half, half)
    copies = [
        pltpu.make_async_copy(offsets_ref, small_ref, sems.at[0]),
        pltpu.make_async_copy(tile_ref.at[:, :, high], below_ref, sems.at[1]),
        pltpu.make_async_copy(tile_ref.at[:, high, :], right_ref, sems.at[2]),
        pltpu.make_async_copy(tile_ref.at[:, high, high], own_ref.at[:, pl.ds(0, half), :], sems.at[3]),
        pltpu.make_async_copy(tile_ref, whole_ref, sems.at[4]),
    ]
    for copy in copies:
        copy.start()
    copies[0].wait()
    shape = (own_ref.shape[1] - half, half)
    line = lax.broadcasted_iota(jnp.int32, shape, 0)
    lines = jnp.zeros(shape, jnp.float32)
    for index in range(4):
        value = small_ref[index // 2 : index // 2 + 1, index % 2 : index % 2 + 1].astype(jnp.float32)
        lines = jnp.where(line == index, value, lines)
    for part in range(2):
        own_ref[part, half:, :] = lines.astype(jnp.bfloat16)
    for copy in copies[1:]:
        copy.wait()


def window_kernel(own_ref, rows_ref, columns_ref, rows_back_ref, columns_back_ref):
    half = own_ref.shape[2]
    width = 2 * half
    core = lax.rem(lax.axis_index("cuts"), 2)
    lines = own_ref[0, half:, :].astype(jnp.float32).astype(jnp.int32) - half

    def placed(shape, axis, shift):
        i = lax.broadcasted_iota(jnp.int32, shape, axis)
        j = lax.broadcasted_iota(jnp.int32, shape, 1 - axis)
        shift = jnp.concatenate([shift] * (shape[1] // half), axis=1)
        return jnp.where(j - i == shift, 1.0, 0.0).astype(jnp.bfloat16)

    for place in range(2):
        second = core != place
        row = jnp.where(second, lines[2:3], lines[0:1])
        column = jnp.where(second, lines[3:4], lines[1:2])
        rows_ref[place * half : (place + 1) * half, :] = placed((half, width), 0, row)
        columns_ref[place] = placed((width + half, width), 1, column)
        rows_back_ref[place] = placed((width + half, width), 1, row)
        columns_back_ref[place * width : (place + 1) * width, :] = placed((width, width + half), 0, column)


def extract_kernel(rows_ref, columns_ref, tile_ref, below_ref, right_ref, own_ref, first_ref, second_ref):
    width = tile_ref.shape[1]
    half = width // 2
    wide = width + half
    blocks = []
    for part in range(2):
        upper = jnp.concatenate([own_ref[part, :half], right_ref[part]], axis=1)
        lower = jnp.concatenate([below_ref[part], tile_ref[part]], axis=1)
        blocks.append(jnp.concatenate([upper, lower], axis=0))
    block = jnp.concatenate(blocks, axis=1)
    strips = [dot(rows_ref[...], block[top : top + width]).astype(jnp.bfloat16) for top in (0, half)]
    for place, out_ref in enumerate((first_ref, second_ref)):
        mine = [strip[place * half : (place + 1) * half, part * wide : (part + 1) * wide] for part in range(2) for strip in strips]
        out_ref[...] = dot(jnp.concatenate(mine, axis=0), columns_ref[place]).astype(jnp.bfloat16)


def forward(probe_ref, band_ref, patch_ref, spread_ref, first, last):
    for level in range(first, last + 1):
        if level == 0:
            spread_ref[0] = probe_ref[...]
        else:
            wave = complex_mul(spread_ref[level - 1], patch_ref[level - 1], 1.0).astype(jnp.bfloat16)
            spread = sandwich(band_ref[0], band_ref[1], wave, band_ref[2], band_ref[3])
            spread_ref[level] = spread.astype(jnp.bfloat16)


def head_kernel(probe_ref, band_ref, p0_ref, p1_ref, spread_ref, patch_ref):
    cut = lax.axis_index("cuts")

    @pl.when(cut < 2)
    def _():
        patch_ref[cut] = p0_ref[...]
        patch_ref[1 - cut] = p1_ref[...]
        forward(probe_ref, band_ref, patch_ref, spread_ref, 0, 2)


def chain_kernel(
    probe_ref, p0_ref, p1_ref, p2_ref, p3_ref, level_ref, band_ref, fourier_ref, head_ref, mine_ref, other_ref, patch_ref, spread_ref, back_ref
):
    width = probe_ref.shape[1]
    cut = lax.axis_index("cuts")
    for mask, ref in enumerate((p0_ref, p1_ref, p2_ref, p3_ref)):
        patch_ref[lax.bitwise_xor(cut, mask)] = ref[...]

    @pl.when(cut < 2)
    def _():
        spread_ref[0:3] = head_ref[...]

    @pl.when(cut >= 2)
    def _():
        forward(probe_ref, band_ref, patch_ref, spread_ref, 0, 2)

    forward(probe_ref, band_ref, patch_ref, spread_ref, 3, 3)
    fourier_r, fourier_i = fourier_ref[0], fourier_ref[1]
    wave = complex_mul(spread_ref[3], patch_ref[3], 1.0).astype(jnp.bfloat16)
    far = sandwich(fourier_r, fourier_i, wave, fourier_r, fourier_i)
    far_r, far_i = far[:width], far[width:]
    level = level_ref[:width, :].astype(jnp.float32)
    live = level_ref[width : width + 1, :].astype(jnp.float32)
    excess = 2.0 * live * (far_r * far_r + far_i * far_i - level)
    residual = jnp.concatenate([excess * far_r, excess * far_i], axis=0).astype(jnp.bfloat16)
    back_ref[...] = sandwich(fourier_r, -fourier_i, residual, fourier_r, -fourier_i).astype(jnp.bfloat16)

    def term(level):
        value = complex_mul(spread_ref[level], back_ref[...], -1.0).astype(jnp.bfloat16)

        @pl.when(level == cut)
        def _():
            mine_ref[...] = value

        @pl.when(level != cut)
        def _():
            other_ref[...] = value

    def carry(level):
        carried = complex_mul(patch_ref[level], back_ref[...], -1.0).astype(jnp.bfloat16)
        back = sandwich(band_ref[2], -band_ref[3], carried, band_ref[0], -band_ref[1])
        back_ref[...] = back.astype(jnp.bfloat16)

    @pl.when(cut >= 2)
    def _():
        term(3)

    carry(3)

    @pl.when(cut >= 2)
    def _():
        term(2)

    @pl.when(cut < 2)
    def _():
        carry(2)
        term(1)
        carry(1)
        term(0)


def scatter_kernel(rows_ref, columns_ref, mine_ref, other_ref, tile_ref, below_ref, right_ref, own_ref):
    width = tile_ref.shape[1]
    half = width // 2
    strips = []
    for place, ref in enumerate((mine_ref, other_ref)):
        field = jnp.concatenate([ref[:width, :], ref[width:, :]], axis=1)
        strips.append(dot(rows_ref[place], field).astype(jnp.bfloat16))
    for part in range(2):
        strip = jnp.concatenate([strip[:, part * width : (part + 1) * width] for strip in strips], axis=1)
        total = dot(strip, columns_ref[...])
        tile_ref[part] = total[half:, half:]
        below_ref[part] = total[half:, :half].astype(jnp.bfloat16)
        right_ref[part] = total[:half, half:].astype(jnp.bfloat16)
        own_ref[part] = total[:half, :half].astype(jnp.bfloat16)


def total_kernel(tile_ref, below_ref, right_ref, own_ref, out_ref):
    half = right_ref.shape[1]
    below = below_ref[...].astype(jnp.float32)
    right = right_ref[...].astype(jnp.float32)
    own = own_ref[...].astype(jnp.float32)
    out_ref[0, :, :half, :half] = tile_ref[:, :half, :half]
    out_ref[0, :, :half, half:] = tile_ref[:, :half, half:] + below[:, :half]
    out_ref[0, :, half:, :half] = tile_ref[:, half:, :half] + right[:, :, :half]
    out_ref[0, :, half:, half:] = tile_ref[:, half:, half:] + below[:, half:] + right[:, :, half:] + own


VMEM = pl.BlockSpec(memory_space=pltpu.VMEM)
SMEM = pl.BlockSpec(memory_space=pltpu.SMEM)
PARAMS = pltpu.CompilerParams(vmem_limit_bytes=48 * 1024 * 1024)


def shaped(*shape, dtype=jnp.bfloat16):
    return jax.ShapeDtypeStruct(shape, dtype)


def kernel(body, name, in_specs, out_shape, scratch=()):
    return pl.pallas_call(
        body, in_specs=in_specs, out_specs=[VMEM] * len(out_shape), out_shape=out_shape, scratch_shapes=scratch, compiler_params=PARAMS, name=name
    )


def local(object_slices, probe, fresnel_taps, offsets, counts, measured):
    width = probe.shape[1]
    half = width // 2
    wide = width + half
    full = shaped(2 * width, width)
    part = shaped(width, width)
    row_tiles = max(lax.axis_size("tile") // 16, 2)
    probe = probe.reshape(2 * width, width)
    fourier = jnp.asarray(fourier_matrix(width), jnp.bfloat16)

    tile, below, right, own = pl.pallas_call(
        cut_kernel,
        in_specs=[pl.BlockSpec(memory_space=pl.ANY)] * 2,
        out_specs=[VMEM] * 4,
        out_shape=[shaped(2, width, width), shaped(2, width, half), shaped(2, half, width), shaped(2, half + 16, half)],
        scratch_shapes=[pltpu.VMEM((2, 2), jnp.int32), pltpu.SemaphoreType.DMA((5,))],
        compiler_params=PARAMS,
        name="cut",
    )(object_slices[0], offsets)
    below = passed_along(below, "tile", 1)
    far_tile = crossed(tile, "cuts", 2)
    right = passed_along(right, "tile", row_tiles)
    own = passed_along(own, "tile", row_tiles + 1)
    far_below = crossed(below, "cuts", 2)
    far_right = crossed(right, "cuts", 2)
    level = shaped(width + 16, width)
    band, level = kernel(band_kernel, "band", [SMEM, VMEM, VMEM], [shaped(4, width, width), level])(counts, fresnel_taps, measured)
    level = stepped(level, "tile", row_tiles, row_tiles + 2)
    level, own = lax.optimization_barrier((level, own))
    level = stepped(level, "tile", 1, -1)
    far_own = crossed(own, "cuts", 2)
    rows, columns, rows_back, columns_back = kernel(
        window_kernel,
        "window",
        [VMEM],
        [part, shaped(2, wide, width), shaped(2, wide, width), shaped(2 * width, wide)],
    )(own)
    first, second = kernel(extract_kernel, "near", [VMEM] * 6, [full, full])(rows, columns, tile, below, right, own)
    swapped = crossed(second, "cuts", 1)
    straight, far_second = kernel(extract_kernel, "far", [VMEM] * 6, [full, full])(rows, columns, far_tile, far_below, far_right, far_own)
    diagonal = crossed(far_second, "cuts", 1)
    (head,) = kernel(head_kernel, "head", [VMEM] * 4, [shaped(3, 2 * width, width)], [pltpu.VMEM((2, 2 * width, width), jnp.bfloat16)])(
        probe, band, first, swapped
    )
    mine, other = kernel(
        chain_kernel,
        "chain",
        [VMEM] * 9,
        [full, full],
        [
            pltpu.VMEM((4, 2 * width, width), jnp.bfloat16),
            pltpu.VMEM((4, 2 * width, width), jnp.bfloat16),
            pltpu.VMEM((2 * width, width), jnp.bfloat16),
        ],
    )(probe, first, swapped, straight, diagonal, level, band, fourier, head)
    other = crossed(other, "cuts", 1)
    total, below, right, own = kernel(
        scatter_kernel,
        "scatter",
        [VMEM] * 4,
        [shaped(2, width, width, dtype=jnp.float32), shaped(2, width, half), shaped(2, half, width), shaped(2, half, half)],
    )(rows_back, columns_back, mine, other)
    below = passed_along(below, "tile", -1)
    right = passed_along(right, "tile", -row_tiles)
    own = passed_along(own, "tile", -row_tiles - 1)
    (out,) = kernel(total_kernel, "total", [VMEM] * 4, [shaped(1, 2, width, width, dtype=jnp.float32)])(total, below, right, own)
    return out


def solution(mesh):
    return jax.shard_map(
        local,
        mesh=mesh,
        in_specs=(
            P("cuts", None, "tile", None),
            P(),
            P(),
            P("tile", None),
            P("tile"),
            P("tile", None, None),
        ),
        out_specs=P("cuts", None, "tile", None),
        check_vma=False,
    )
```

```python
import jax
import jax.numpy as jnp
import numpy as np
from jax import lax
from jax.experimental import pallas as pl
from jax.experimental.pallas import tpu as pltpu
from jax.sharding import PartitionSpec as P


def passed_along(value, axis, steps):
    count = lax.axis_size(axis)
    pairs = [(source, (source + steps) % count) for source in range(count)]
    return lax.ppermute(value, axis, pairs)


def crossed(value, axis, mask):
    pairs = [(source, source ^ mask) for source in range(lax.axis_size(axis))]
    return lax.ppermute(value, axis, pairs)


def paired(value):
    return lax.all_gather(value, "cuts", axis_index_groups=[[0, 2], [1, 3]])


def fourier_matrix(width):
    index = np.arange(width)
    angle = 2.0 * np.pi * (index[:, None] * index[None, :] % width) / width
    return np.stack([np.cos(angle), -np.sin(angle)]) / np.sqrt(width)


def dot(left, right):
    return jnp.dot(left, right, preferred_element_type=jnp.float32)


def left_product(real, imag, field):
    top = jnp.concatenate([real, -imag], axis=1)
    bottom = jnp.concatenate([imag, real], axis=1)
    return dot(jnp.concatenate([top, bottom], axis=0), field)


def right_product(field, real, imag):
    width = real.shape[0]
    turned = jnp.concatenate([-field[width:], field[:width]], axis=0)
    return dot(jnp.concatenate([field, turned], axis=1), jnp.concatenate([real, imag], axis=0))


def sandwich(left_real, left_imag, field, right_real, right_imag):
    inner = left_product(left_real, left_imag, field).astype(jnp.bfloat16)
    return right_product(inner, right_real, right_imag)


def complex_mul(first, second, sign):
    width = first.shape[1]
    fr = first[:width].astype(jnp.float32)
    fi = first[width:].astype(jnp.float32) * sign
    sr = second[:width].astype(jnp.float32)
    si = second[width:].astype(jnp.float32)
    return jnp.concatenate([fr * sr - fi * si, fr * si + fi * sr], axis=0)


def band_kernel(counts_ref, taps_ref, measured_ref, band_ref, level_ref):
    width = band_ref.shape[1]
    half = taps_ref.shape[1] // 2
    core = lax.rem(lax.axis_index("cuts"), 2)
    level_ref[:width, :] = measured_ref[core].astype(jnp.bfloat16)
    live = (core < counts_ref[0]).astype(jnp.float32)
    level_ref[width:, :] = jnp.full((level_ref.shape[0] - width, width), live, jnp.float32).astype(jnp.bfloat16)
    rows = lax.broadcasted_iota(jnp.int32, (width, width), 0)
    columns = lax.broadcasted_iota(jnp.int32, (width, width), 1)
    inside = jnp.abs(columns - rows) <= half
    for part in range(2):
        line = taps_ref[part : part + 1, :].astype(jnp.float32)
        filler = jnp.zeros((1, width - line.shape[1]), jnp.float32)
        line = jnp.concatenate([line, filler], axis=1)
        spread = jnp.broadcast_to(line, (width, width))
        turned = pltpu.roll(spread, width - half, 1, stride=1, stride_axis=0)
        band = jnp.where(inside, turned, 0.0)
        band_ref[part] = band.astype(jnp.bfloat16)
        band_ref[part + 2] = band.T.astype(jnp.bfloat16)


def cut_kernel(tile_ref, offsets_ref, right_ref, own_ref):
    half = right_ref.shape[1]
    right_ref[...] = tile_ref[:, half:, :]
    own_ref[:, :half, :] = tile_ref[:, half:, half:]
    shape = (own_ref.shape[1] - half, half)
    line = lax.broadcasted_iota(jnp.int32, shape, 0)
    lines = jnp.zeros(shape, jnp.float32)
    for index in range(4):
        value = offsets_ref[index // 2 : index // 2 + 1, index % 2 : index % 2 + 1].astype(jnp.float32)
        lines = jnp.where(line == index, value, lines)
    for part in range(2):
        own_ref[part, half:, :] = lines.astype(jnp.bfloat16)


def window_kernel(own_ref, rows_ref, columns_ref, rows_back_ref, columns_back_ref):
    half = own_ref.shape[2]
    width = 2 * half
    core = lax.rem(lax.axis_index("cuts"), 2)
    lines = own_ref[0, half:, :].astype(jnp.float32).astype(jnp.int32) - half

    def placed(shape, axis, shift):
        i = lax.broadcasted_iota(jnp.int32, shape, axis)
        j = lax.broadcasted_iota(jnp.int32, shape, 1 - axis)
        shift = jnp.concatenate([shift] * (shape[1] // half), axis=1)
        return jnp.where(j - i == shift, 1.0, 0.0).astype(jnp.bfloat16)

    for place in range(2):
        second = core != place
        row = jnp.where(second, lines[2:3], lines[0:1])
        column = jnp.where(second, lines[3:4], lines[1:2])
        rows_ref[place * half : (place + 1) * half, :] = placed((half, width), 0, row)
        columns_ref[place] = placed((width + half, width), 1, column)
        rows_back_ref[place] = placed((width + half, width), 1, row)
        columns_back_ref[place * width : (place + 1) * width, :] = placed((width, width + half), 0, column)


def far_kernel(rows_ref, columns_ref, tile_ref, below_ref, right_ref, own_ref, first_ref, second_ref):
    far = 1 - lax.axis_index("cuts") // 2
    extract_kernel(rows_ref, columns_ref, *(ref.at[far] for ref in (tile_ref, below_ref, right_ref, own_ref)), first_ref, second_ref)


def extract_kernel(rows_ref, columns_ref, tile_ref, below_ref, right_ref, own_ref, first_ref, second_ref):
    width = tile_ref.shape[1]
    half = width // 2
    wide = width + half
    blocks = []
    for part in range(2):
        upper = jnp.concatenate([own_ref[part, :half], right_ref[part]], axis=1)
        lower = jnp.concatenate([below_ref[part], tile_ref[part]], axis=1)
        blocks.append(jnp.concatenate([upper, lower], axis=0))
    block = jnp.concatenate(blocks, axis=1)
    strips = [dot(rows_ref[...], block[top : top + width]).astype(jnp.bfloat16) for top in (0, half)]
    for place, out_ref in enumerate((first_ref, second_ref)):
        mine = [strip[place * half : (place + 1) * half, part * wide : (part + 1) * wide] for part in range(2) for strip in strips]
        out_ref[...] = dot(jnp.concatenate(mine, axis=0), columns_ref[place]).astype(jnp.bfloat16)


def forward(probe_ref, band_ref, patch_ref, spread_ref, first, last):
    for level in range(first, last + 1):
        if level == 0:
            spread_ref[0] = probe_ref[...]
        else:
            wave = complex_mul(spread_ref[level - 1], patch_ref[level - 1], 1.0).astype(jnp.bfloat16)
            spread = sandwich(band_ref[0], band_ref[1], wave, band_ref[2], band_ref[3])
            spread_ref[level] = spread.astype(jnp.bfloat16)


def head_kernel(probe_ref, band_ref, p0_ref, p1_ref, spread_ref, patch_ref):
    cut = lax.axis_index("cuts")

    @pl.when(cut < 2)
    def _():
        patch_ref[cut] = p0_ref[...]
        patch_ref[1 - cut] = p1_ref[...]
        forward(probe_ref, band_ref, patch_ref, spread_ref, 0, 2)


def chain_kernel(
    probe_ref, p0_ref, p1_ref, p2_ref, p3_ref, level_ref, band_ref, fourier_ref, head_ref, mine_ref, other_ref, patch_ref, spread_ref, back_ref
):
    width = probe_ref.shape[1]
    cut = lax.axis_index("cuts")
    for mask, ref in enumerate((p0_ref, p1_ref, p2_ref, p3_ref)):
        patch_ref[lax.bitwise_xor(cut, mask)] = ref[...]

    @pl.when(cut < 2)
    def _():
        spread_ref[0:3] = head_ref[...]

    @pl.when(cut >= 2)
    def _():
        forward(probe_ref, band_ref, patch_ref, spread_ref, 0, 2)

    forward(probe_ref, band_ref, patch_ref, spread_ref, 3, 3)
    fourier_r, fourier_i = fourier_ref[0], fourier_ref[1]
    wave = complex_mul(spread_ref[3], patch_ref[3], 1.0).astype(jnp.bfloat16)
    far = sandwich(fourier_r, fourier_i, wave, fourier_r, fourier_i)
    far_r, far_i = far[:width], far[width:]
    level = level_ref[:width, :].astype(jnp.float32)
    live = level_ref[width : width + 1, :].astype(jnp.float32)
    excess = 2.0 * live * (far_r * far_r + far_i * far_i - level)
    residual = jnp.concatenate([excess * far_r, excess * far_i], axis=0).astype(jnp.bfloat16)
    back_ref[...] = sandwich(fourier_r, -fourier_i, residual, fourier_r, -fourier_i).astype(jnp.bfloat16)

    def term(level):
        value = complex_mul(spread_ref[level], back_ref[...], -1.0).astype(jnp.bfloat16)

        @pl.when(level == cut)
        def _():
            mine_ref[...] = value

        @pl.when(level != cut)
        def _():
            other_ref[...] = value

    def carry(level):
        carried = complex_mul(patch_ref[level], back_ref[...], -1.0).astype(jnp.bfloat16)
        back = sandwich(band_ref[2], -band_ref[3], carried, band_ref[0], -band_ref[1])
        back_ref[...] = back.astype(jnp.bfloat16)

    @pl.when(cut >= 2)
    def _():
        term(3)

    carry(3)

    @pl.when(cut >= 2)
    def _():
        term(2)

    @pl.when(cut < 2)
    def _():
        carry(2)
        term(1)
        carry(1)
        term(0)


def scatter_kernel(rows_ref, columns_ref, mine_ref, other_ref, tile_ref, below_ref, right_ref, own_ref):
    width = tile_ref.shape[1]
    half = width // 2
    strips = []
    for place, ref in enumerate((mine_ref, other_ref)):
        field = jnp.concatenate([ref[:width, :], ref[width:, :]], axis=1)
        strips.append(dot(rows_ref[place], field).astype(jnp.bfloat16))
    for part in range(2):
        strip = jnp.concatenate([strip[:, part * width : (part + 1) * width] for strip in strips], axis=1)
        total = dot(strip, columns_ref[...])
        tile_ref[part] = total[half:, half:]
        below_ref[part] = total[half:, :half].astype(jnp.bfloat16)
        right_ref[part] = total[:half, half:].astype(jnp.bfloat16)
        own_ref[part] = total[:half, :half].astype(jnp.bfloat16)


def total_kernel(tile_ref, below_ref, right_ref, own_ref, out_ref):
    half = right_ref.shape[1]
    below = below_ref[...].astype(jnp.float32)
    right = right_ref[...].astype(jnp.float32)
    own = own_ref[...].astype(jnp.float32)
    out_ref[0, :, :half, :half] = tile_ref[:, :half, :half]
    out_ref[0, :, :half, half:] = tile_ref[:, :half, half:] + below[:, :half]
    out_ref[0, :, half:, :half] = tile_ref[:, half:, :half] + right[:, :, :half]
    out_ref[0, :, half:, half:] = tile_ref[:, half:, half:] + below[:, half:] + right[:, :, half:] + own


VMEM = pl.BlockSpec(memory_space=pltpu.VMEM)
SMEM = pl.BlockSpec(memory_space=pltpu.SMEM)
PARAMS = pltpu.CompilerParams(vmem_limit_bytes=48 * 1024 * 1024)


def shaped(*shape, dtype=jnp.bfloat16):
    return jax.ShapeDtypeStruct(shape, dtype)


def kernel(body, name, in_specs, out_shape, scratch=()):
    return pl.pallas_call(
        body, in_specs=in_specs, out_specs=[VMEM] * len(out_shape), out_shape=out_shape, scratch_shapes=scratch, compiler_params=PARAMS, name=name
    )


def local(object_slices, probe, fresnel_taps, offsets, counts, measured):
    width = probe.shape[1]
    half = width // 2
    wide = width + half
    full = shaped(2 * width, width)
    part = shaped(width, width)
    row_tiles = max(lax.axis_size("tile") // 16, 2)
    tile = object_slices[0]
    probe = probe.reshape(2 * width, width)
    fourier = jnp.asarray(fourier_matrix(width), jnp.bfloat16)

    below = passed_along(tile[:, :, half:], "tile", 1)
    far_tile = paired(tile)
    right, own = kernel(cut_kernel, "cut", [VMEM] * 2, [shaped(2, half, width), shaped(2, half + 16, half)])(tile, offsets)
    right = passed_along(right, "tile", row_tiles)
    own = passed_along(own, "tile", row_tiles + 1)
    far_below = paired(below)
    far_right = paired(right)
    far_own = paired(own)
    level = shaped(width + 16, width)
    band, level = kernel(band_kernel, "band", [SMEM, VMEM, VMEM], [shaped(4, width, width), level])(counts, fresnel_taps, measured)
    level, right = lax.optimization_barrier((level, right))
    level = passed_along(level, "tile", row_tiles + 1)
    rows, columns, rows_back, columns_back = kernel(
        window_kernel,
        "window",
        [VMEM],
        [part, shaped(2, wide, width), shaped(2, wide, width), shaped(2 * width, wide)],
    )(own)
    first, second = kernel(extract_kernel, "near", [VMEM] * 6, [full, full])(rows, columns, tile, below, right, own)
    swapped = crossed(second, "cuts", 1)
    far_own, level = lax.optimization_barrier((far_own, level))
    straight, far_second = kernel(far_kernel, "far", [VMEM] * 6, [full, full])(rows, columns, far_tile, far_below, far_right, far_own)
    diagonal = crossed(far_second, "cuts", 1)
    (head,) = kernel(head_kernel, "head", [VMEM] * 4, [shaped(3, 2 * width, width)], [pltpu.VMEM((2, 2 * width, width), jnp.bfloat16)])(
        probe, band, first, swapped
    )
    mine, other = kernel(
        chain_kernel,
        "chain",
        [VMEM] * 9,
        [full, full],
        [
            pltpu.VMEM((4, 2 * width, width), jnp.bfloat16),
            pltpu.VMEM((4, 2 * width, width), jnp.bfloat16),
            pltpu.VMEM((2 * width, width), jnp.bfloat16),
        ],
    )(probe, first, swapped, straight, diagonal, level, band, fourier, head)
    other = crossed(other, "cuts", 1)
    total, below, right, own = kernel(
        scatter_kernel,
        "scatter",
        [VMEM] * 4,
        [shaped(2, width, width, dtype=jnp.float32), shaped(2, width, half), shaped(2, half, width), shaped(2, half, half)],
    )(rows_back, columns_back, mine, other)
    below = passed_along(below, "tile", -1)
    right = passed_along(right, "tile", -row_tiles)
    own = passed_along(own, "tile", -row_tiles - 1)
    (out,) = kernel(total_kernel, "total", [VMEM] * 4, [shaped(1, 2, width, width, dtype=jnp.float32)])(total, below, right, own)
    return out


def solution(mesh):
    return jax.shard_map(
        local,
        mesh=mesh,
        in_specs=(
            P("cuts", None, "tile", None),
            P(),
            P(),
            P("tile", None),
            P("tile"),
            P("tile", None, None),
        ),
        out_specs=P("cuts", None, "tile", None),
        check_vma=False,
    )
```

```python
import jax
import jax.numpy as jnp
import numpy as np
from jax import lax
from jax.experimental import pallas as pl
from jax.experimental.pallas import tpu as pltpu
from jax.sharding import PartitionSpec as P


def passed_along(value, axis, steps):
    count = lax.axis_size(axis)
    pairs = [(source, (source + steps) % count) for source in range(count)]
    return lax.ppermute(value, axis, pairs)


def crossed(value, axis, mask):
    pairs = [(source, source ^ mask) for source in range(lax.axis_size(axis))]
    return lax.ppermute(value, axis, pairs)


def fourier_matrix(width):
    index = np.arange(width)
    angle = 2.0 * np.pi * (index[:, None] * index[None, :] % width) / width
    return np.stack([np.cos(angle), -np.sin(angle)]) / np.sqrt(width)


def dot(left, right):
    return jnp.dot(left, right, preferred_element_type=jnp.float32)


def left_product(real, imag, field):
    top = jnp.concatenate([real, -imag], axis=1)
    bottom = jnp.concatenate([imag, real], axis=1)
    return dot(jnp.concatenate([top, bottom], axis=0), field)


def right_product(field, real, imag):
    width = real.shape[0]
    turned = jnp.concatenate([-field[width:], field[:width]], axis=0)
    return dot(jnp.concatenate([field, turned], axis=1), jnp.concatenate([real, imag], axis=0))


def sandwich(left_real, left_imag, field, right_real, right_imag):
    inner = left_product(left_real, left_imag, field).astype(jnp.bfloat16)
    return right_product(inner, right_real, right_imag)


def complex_mul(first, second, sign):
    width = first.shape[1]
    fr = first[:width].astype(jnp.float32)
    fi = first[width:].astype(jnp.float32) * sign
    sr = second[:width].astype(jnp.float32)
    si = second[width:].astype(jnp.float32)
    return jnp.concatenate([fr * sr - fi * si, fr * si + fi * sr], axis=0)


def band_kernel(counts_ref, taps_ref, measured_ref, band_ref, level_ref):
    width = band_ref.shape[1]
    half = taps_ref.shape[1] // 2
    core = lax.rem(lax.axis_index("cuts"), 2)
    rows = width // 2
    first = pl.multiple_of(lax.axis_index("cuts") // 2 * rows, rows)
    level_ref[:rows, :] = measured_ref[core, pl.ds(first, rows), :].astype(jnp.bfloat16)
    live = (core < counts_ref[0]).astype(jnp.float32)
    level_ref[rows:, :] = jnp.full((level_ref.shape[0] - rows, width), live, jnp.float32).astype(jnp.bfloat16)
    rows = lax.broadcasted_iota(jnp.int32, (width, width), 0)
    columns = lax.broadcasted_iota(jnp.int32, (width, width), 1)
    inside = jnp.abs(columns - rows) <= half
    for part in range(2):
        line = taps_ref[part : part + 1, :].astype(jnp.float32)
        filler = jnp.zeros((1, width - line.shape[1]), jnp.float32)
        line = jnp.concatenate([line, filler], axis=1)
        spread = jnp.broadcast_to(line, (width, width))
        turned = pltpu.roll(spread, width - half, 1, stride=1, stride_axis=0)
        band = jnp.where(inside, turned, 0.0)
        band_ref[part] = band.astype(jnp.bfloat16)
        band_ref[part + 2] = band.T.astype(jnp.bfloat16)


def cut_kernel(tile_ref, offsets_ref, whole_ref, below_ref, right_ref, own_ref):
    half = right_ref.shape[1]
    whole_ref[...] = tile_ref[...]
    below_ref[...] = tile_ref[:, :, half:]
    right_ref[...] = tile_ref[:, half:, :]
    own_ref[:, :half, :] = tile_ref[:, half:, half:]
    shape = (own_ref.shape[1] - half, half)
    line = lax.broadcasted_iota(jnp.int32, shape, 0)
    lines = jnp.zeros(shape, jnp.float32)
    for index in range(4):
        value = offsets_ref[index // 2 : index // 2 + 1, index % 2 : index % 2 + 1].astype(jnp.float32)
        lines = jnp.where(line == index, value, lines)
    for part in range(2):
        own_ref[part, half:, :] = lines.astype(jnp.bfloat16)


def window_kernel(own_ref, rows_ref, columns_ref, rows_back_ref, columns_back_ref):
    half = own_ref.shape[2]
    width = 2 * half
    core = lax.rem(lax.axis_index("cuts"), 2)
    lines = own_ref[0, half:, :].astype(jnp.float32).astype(jnp.int32) - half

    def placed(shape, axis, shift):
        i = lax.broadcasted_iota(jnp.int32, shape, axis)
        j = lax.broadcasted_iota(jnp.int32, shape, 1 - axis)
        shift = jnp.concatenate([shift] * (shape[1] // half), axis=1)
        return jnp.where(j - i == shift, 1.0, 0.0).astype(jnp.bfloat16)

    for place in range(2):
        second = core != place
        row = jnp.where(second, lines[2:3], lines[0:1])
        column = jnp.where(second, lines[3:4], lines[1:2])
        rows_ref[place * half : (place + 1) * half, :] = placed((half, width), 0, row)
        columns_ref[place] = placed((width + half, width), 1, column)
        rows_back_ref[place] = placed((width + half, width), 1, row)
        columns_back_ref[place * width : (place + 1) * width, :] = placed((width, width + half), 0, column)


def extract_kernel(rows_ref, columns_ref, tile_ref, below_ref, right_ref, own_ref, first_ref, second_ref):
    width = tile_ref.shape[1]
    half = width // 2
    wide = width + half
    blocks = []
    for part in range(2):
        upper = jnp.concatenate([own_ref[part, :half], right_ref[part]], axis=1)
        lower = jnp.concatenate([below_ref[part], tile_ref[part]], axis=1)
        blocks.append(jnp.concatenate([upper, lower], axis=0))
    block = jnp.concatenate(blocks, axis=1)
    strips = [dot(rows_ref[...], block[top : top + width]).astype(jnp.bfloat16) for top in (0, half)]
    for place, out_ref in enumerate((first_ref, second_ref)):
        mine = [strip[place * half : (place + 1) * half, part * wide : (part + 1) * wide] for part in range(2) for strip in strips]
        out_ref[...] = dot(jnp.concatenate(mine, axis=0), columns_ref[place]).astype(jnp.bfloat16)


def forward(probe_ref, band_ref, patch_ref, spread_ref, first, last):
    for level in range(first, last + 1):
        if level == 0:
            spread_ref[0] = probe_ref[...]
        else:
            wave = complex_mul(spread_ref[level - 1], patch_ref[level - 1], 1.0).astype(jnp.bfloat16)
            spread = sandwich(band_ref[0], band_ref[1], wave, band_ref[2], band_ref[3])
            spread_ref[level] = spread.astype(jnp.bfloat16)


def head_kernel(probe_ref, band_ref, p0_ref, p1_ref, spread_ref, patch_ref):
    cut = lax.axis_index("cuts")

    @pl.when(cut < 2)
    def _():
        patch_ref[cut] = p0_ref[...]
        patch_ref[1 - cut] = p1_ref[...]
        forward(probe_ref, band_ref, patch_ref, spread_ref, 0, 2)


def chain_kernel(
    probe_ref, p0_ref, p1_ref, p2_ref, p3_ref, level_ref, far_level_ref, band_ref, fourier_ref, head_ref, mine_ref, other_ref, patch_ref, spread_ref, back_ref
):
    width = probe_ref.shape[1]
    cut = lax.axis_index("cuts")
    for mask, ref in enumerate((p0_ref, p1_ref, p2_ref, p3_ref)):
        patch_ref[lax.bitwise_xor(cut, mask)] = ref[...]

    @pl.when(cut < 2)
    def _():
        spread_ref[0:3] = head_ref[...]

    @pl.when(cut >= 2)
    def _():
        forward(probe_ref, band_ref, patch_ref, spread_ref, 0, 2)

    forward(probe_ref, band_ref, patch_ref, spread_ref, 3, 3)
    fourier_r, fourier_i = fourier_ref[0], fourier_ref[1]
    wave = complex_mul(spread_ref[3], patch_ref[3], 1.0).astype(jnp.bfloat16)
    far = sandwich(fourier_r, fourier_i, wave, fourier_r, fourier_i)
    far_r, far_i = far[:width], far[width:]
    rows = width // 2
    level, far_level = level_ref[:rows, :].astype(jnp.float32), far_level_ref[:rows, :].astype(jnp.float32)
    level = jnp.concatenate([jnp.where(cut < 2, level, far_level), jnp.where(cut < 2, far_level, level)], axis=0)
    live = level_ref[rows : rows + 1, :].astype(jnp.float32)
    excess = 2.0 * live * (far_r * far_r + far_i * far_i - level)
    residual = jnp.concatenate([excess * far_r, excess * far_i], axis=0).astype(jnp.bfloat16)
    back_ref[...] = sandwich(fourier_r, -fourier_i, residual, fourier_r, -fourier_i).astype(jnp.bfloat16)

    def term(level):
        value = complex_mul(spread_ref[level], back_ref[...], -1.0).astype(jnp.bfloat16)

        @pl.when(level == cut)
        def _():
            mine_ref[...] = value

        @pl.when(level != cut)
        def _():
            other_ref[...] = value

    def carry(level):
        carried = complex_mul(patch_ref[level], back_ref[...], -1.0).astype(jnp.bfloat16)
        back = sandwich(band_ref[2], -band_ref[3], carried, band_ref[0], -band_ref[1])
        back_ref[...] = back.astype(jnp.bfloat16)

    @pl.when(cut >= 2)
    def _():
        term(3)

    carry(3)

    @pl.when(cut >= 2)
    def _():
        term(2)

    @pl.when(cut < 2)
    def _():
        carry(2)
        term(1)
        carry(1)
        term(0)


def scatter_kernel(rows_ref, columns_ref, mine_ref, other_ref, tile_ref, below_ref, right_ref, own_ref):
    width = tile_ref.shape[1]
    half = width // 2
    strips = []
    for place, ref in enumerate((mine_ref, other_ref)):
        field = jnp.concatenate([ref[:width, :], ref[width:, :]], axis=1)
        strips.append(dot(rows_ref[place], field).astype(jnp.bfloat16))
    for part in range(2):
        strip = jnp.concatenate([strip[:, part * width : (part + 1) * width] for strip in strips], axis=1)
        total = dot(strip, columns_ref[...])
        tile_ref[part] = total[half:, half:]
        below_ref[part] = total[half:, :half].astype(jnp.bfloat16)
        right_ref[part] = total[:half, half:].astype(jnp.bfloat16)
        own_ref[part] = total[:half, :half].astype(jnp.bfloat16)


def total_kernel(tile_ref, below_ref, right_ref, own_ref, out_ref):
    half = right_ref.shape[1]
    below = below_ref[...].astype(jnp.float32)
    right = right_ref[...].astype(jnp.float32)
    own = own_ref[...].astype(jnp.float32)
    out_ref[0, :, :half, :half] = tile_ref[:, :half, :half]
    out_ref[0, :, :half, half:] = tile_ref[:, :half, half:] + below[:, :half]
    out_ref[0, :, half:, :half] = tile_ref[:, half:, :half] + right[:, :, :half]
    out_ref[0, :, half:, half:] = tile_ref[:, half:, half:] + below[:, half:] + right[:, :, half:] + own


VMEM = pl.BlockSpec(memory_space=pltpu.VMEM)
SMEM = pl.BlockSpec(memory_space=pltpu.SMEM)
PARAMS = pltpu.CompilerParams(vmem_limit_bytes=48 * 1024 * 1024)


def shaped(*shape, dtype=jnp.bfloat16):
    return jax.ShapeDtypeStruct(shape, dtype)


def kernel(body, name, in_specs, out_shape, scratch=()):
    return pl.pallas_call(
        body, in_specs=in_specs, out_specs=[VMEM] * len(out_shape), out_shape=out_shape, scratch_shapes=scratch, compiler_params=PARAMS, name=name
    )


def local(object_slices, probe, fresnel_taps, offsets, counts, measured):
    width = probe.shape[1]
    half = width // 2
    wide = width + half
    full = shaped(2 * width, width)
    part = shaped(width, width)
    row_tiles = max(lax.axis_size("tile") // 16, 2)
    probe = probe.reshape(2 * width, width)
    fourier = jnp.asarray(fourier_matrix(width), jnp.bfloat16)

    far_tile = crossed(object_slices[0], "cuts", 2)
    tile, below, right, own = kernel(
        cut_kernel, "cut", [VMEM] * 2, [shaped(2, width, width), shaped(2, width, half), shaped(2, half, width), shaped(2, half + 16, half)]
    )(object_slices[0], offsets)
    below = passed_along(below, "tile", 1)
    right = passed_along(right, "tile", row_tiles)
    own = passed_along(own, "tile", row_tiles + 1)
    below, far_tile = lax.optimization_barrier((below, far_tile))
    far_below = crossed(below, "cuts", 2)
    far_right = crossed(right, "cuts", 2)
    far_own = crossed(own, "cuts", 2)
    level = shaped(half + 16, width)
    band, level = kernel(band_kernel, "band", [SMEM, VMEM, VMEM], [shaped(4, width, width), level])(counts, fresnel_taps, measured)
    level, right = lax.optimization_barrier((level, right))
    level = passed_along(level, "tile", row_tiles + 1)
    rows, columns, rows_back, columns_back = kernel(
        window_kernel,
        "window",
        [VMEM],
        [part, shaped(2, wide, width), shaped(2, wide, width), shaped(2 * width, wide)],
    )(own)
    first, second = kernel(extract_kernel, "near", [VMEM] * 6, [full, full])(rows, columns, tile, below, right, own)
    swapped = crossed(second, "cuts", 1)
    far_level = crossed(level, "cuts", 2)
    far_own, far_level = lax.optimization_barrier((far_own, far_level))
    straight, far_second = kernel(extract_kernel, "far", [VMEM] * 6, [full, full])(rows, columns, far_tile, far_below, far_right, far_own)
    diagonal = crossed(far_second, "cuts", 1)
    (head,) = kernel(head_kernel, "head", [VMEM] * 4, [shaped(3, 2 * width, width)], [pltpu.VMEM((2, 2 * width, width), jnp.bfloat16)])(
        probe, band, first, swapped
    )
    mine, other = kernel(
        chain_kernel,
        "chain",
        [VMEM] * 10,
        [full, full],
        [
            pltpu.VMEM((4, 2 * width, width), jnp.bfloat16),
            pltpu.VMEM((4, 2 * width, width), jnp.bfloat16),
            pltpu.VMEM((2 * width, width), jnp.bfloat16),
        ],
    )(probe, first, swapped, straight, diagonal, level, far_level, band, fourier, head)
    other = crossed(other, "cuts", 1)
    total, below, right, own = kernel(
        scatter_kernel,
        "scatter",
        [VMEM] * 4,
        [shaped(2, width, width, dtype=jnp.float32), shaped(2, width, half), shaped(2, half, width), shaped(2, half, half)],
    )(rows_back, columns_back, mine, other)
    below = passed_along(below, "tile", -1)
    right = passed_along(right, "tile", -row_tiles)
    own = passed_along(own, "tile", -row_tiles - 1)
    (out,) = kernel(total_kernel, "total", [VMEM] * 4, [shaped(1, 2, width, width, dtype=jnp.float32)])(total, below, right, own)
    return out


def solution(mesh):
    return jax.shard_map(
        local,
        mesh=mesh,
        in_specs=(
            P("cuts", None, "tile", None),
            P(),
            P(),
            P("tile", None),
            P("tile"),
            P("tile", None, None),
        ),
        out_specs=P("cuts", None, "tile", None),
        check_vma=False,
    )
```

```python
import jax
import jax.numpy as jnp
import numpy as np
from jax import lax
from jax.experimental import pallas as pl
from jax.experimental.pallas import tpu as pltpu
from jax.sharding import PartitionSpec as P


def passed_along(value, axis, steps):
    count = lax.axis_size(axis)
    pairs = [(source, (source + steps) % count) for source in range(count)]
    return lax.ppermute(value, axis, pairs)


def crossed(value, axis, mask):
    pairs = [(source, source ^ mask) for source in range(lax.axis_size(axis))]
    return lax.ppermute(value, axis, pairs)


def stepped(value, axis, even, odd):
    count = lax.axis_size(axis)
    pairs = [(source, (source + (odd if source % 2 else even)) % count) for source in range(count)]
    return lax.ppermute(value, axis, pairs)


def fourier_matrix(width):
    index = np.arange(width)
    angle = 2.0 * np.pi * (index[:, None] * index[None, :] % width) / width
    return np.stack([np.cos(angle), -np.sin(angle)]) / np.sqrt(width)


def dot(left, right):
    return jnp.dot(left, right, preferred_element_type=jnp.float32)


def left_product(real, imag, field):
    top = jnp.concatenate([real, -imag], axis=1)
    bottom = jnp.concatenate([imag, real], axis=1)
    return dot(jnp.concatenate([top, bottom], axis=0), field)


def right_product(field, real, imag):
    width = real.shape[0]
    turned = jnp.concatenate([-field[width:], field[:width]], axis=0)
    return dot(jnp.concatenate([field, turned], axis=1), jnp.concatenate([real, imag], axis=0))


def sandwich(left_real, left_imag, field, right_real, right_imag):
    inner = left_product(left_real, left_imag, field).astype(jnp.bfloat16)
    return right_product(inner, right_real, right_imag)


def complex_mul(first, second, sign):
    width = first.shape[1]
    fr = first[:width].astype(jnp.float32)
    fi = first[width:].astype(jnp.float32) * sign
    sr = second[:width].astype(jnp.float32)
    si = second[width:].astype(jnp.float32)
    return jnp.concatenate([fr * sr - fi * si, fr * si + fi * sr], axis=0)


def band_kernel(counts_ref, taps_ref, measured_ref, band_ref, level_ref):
    width = band_ref.shape[1]
    half = taps_ref.shape[1] // 2
    core = lax.rem(lax.axis_index("cuts"), 2)
    level_ref[:width, :] = measured_ref[core].astype(jnp.bfloat16)
    live = (core < counts_ref[0]).astype(jnp.float32)
    level_ref[width:, :] = jnp.full((level_ref.shape[0] - width, width), live, jnp.float32).astype(jnp.bfloat16)
    rows = lax.broadcasted_iota(jnp.int32, (width, width), 0)
    columns = lax.broadcasted_iota(jnp.int32, (width, width), 1)
    inside = jnp.abs(columns - rows) <= half
    for part in range(2):
        line = taps_ref[part : part + 1, :].astype(jnp.float32)
        filler = jnp.zeros((1, width - line.shape[1]), jnp.float32)
        line = jnp.concatenate([line, filler], axis=1)
        spread = jnp.broadcast_to(line, (width, width))
        turned = pltpu.roll(spread, width - half, 1, stride=1, stride_axis=0)
        band = jnp.where(inside, turned, 0.0)
        band_ref[part] = band.astype(jnp.bfloat16)
        band_ref[part + 2] = band.T.astype(jnp.bfloat16)


def cut_kernel(tile_ref, offsets_ref, whole_ref, below_ref, right_ref, own_ref):
    half = right_ref.shape[1]
    whole_ref[...] = tile_ref[...]
    below_ref[...] = tile_ref[:, :, half:]
    right_ref[...] = tile_ref[:, half:, :]
    own_ref[:, :half, :] = tile_ref[:, half:, half:]
    shape = (own_ref.shape[1] - half, half)
    line = lax.broadcasted_iota(jnp.int32, shape, 0)
    lines = jnp.zeros(shape, jnp.float32)
    for index in range(4):
        value = offsets_ref[index // 2 : index // 2 + 1, index % 2 : index % 2 + 1].astype(jnp.float32)
        lines = jnp.where(line == index, value, lines)
    for part in range(2):
        own_ref[part, half:, :] = lines.astype(jnp.bfloat16)


def window_kernel(own_ref, rows_ref, columns_ref, rows_back_ref, columns_back_ref):
    half = own_ref.shape[2]
    width = 2 * half
    core = lax.rem(lax.axis_index("cuts"), 2)
    lines = own_ref[0, half:, :].astype(jnp.float32).astype(jnp.int32) - half

    def placed(shape, axis, shift):
        i = lax.broadcasted_iota(jnp.int32, shape, axis)
        j = lax.broadcasted_iota(jnp.int32, shape, 1 - axis)
        shift = jnp.concatenate([shift] * (shape[1] // half), axis=1)
        return jnp.where(j - i == shift, 1.0, 0.0).astype(jnp.bfloat16)

    for place in range(2):
        second = core != place
        row = jnp.where(second, lines[2:3], lines[0:1])
        column = jnp.where(second, lines[3:4], lines[1:2])
        rows_ref[place * half : (place + 1) * half, :] = placed((half, width), 0, row)
        columns_ref[place] = placed((width + half, width), 1, column)
        rows_back_ref[place] = placed((width + half, width), 1, row)
        columns_back_ref[place * width : (place + 1) * width, :] = placed((width, width + half), 0, column)


def extract_kernel(rows_ref, columns_ref, tile_ref, below_ref, right_ref, own_ref, first_ref, second_ref):
    width = tile_ref.shape[1]
    half = width // 2
    wide = width + half
    blocks = []
    for part in range(2):
        upper = jnp.concatenate([own_ref[part, :half], right_ref[part]], axis=1)
        lower = jnp.concatenate([below_ref[part], tile_ref[part]], axis=1)
        blocks.append(jnp.concatenate([upper, lower], axis=0))
    block = jnp.concatenate(blocks, axis=1)
    strips = [dot(rows_ref[...], block[top : top + width]).astype(jnp.bfloat16) for top in (0, half)]
    for place, out_ref in enumerate((first_ref, second_ref)):
        mine = [strip[place * half : (place + 1) * half, part * wide : (part + 1) * wide] for part in range(2) for strip in strips]
        out_ref[...] = dot(jnp.concatenate(mine, axis=0), columns_ref[place]).astype(jnp.bfloat16)


def forward(probe_ref, band_ref, patch_ref, spread_ref, first, last):
    for level in range(first, last + 1):
        if level == 0:
            spread_ref[0] = probe_ref[...]
        else:
            wave = complex_mul(spread_ref[level - 1], patch_ref[level - 1], 1.0).astype(jnp.bfloat16)
            spread = sandwich(band_ref[0], band_ref[1], wave, band_ref[2], band_ref[3])
            spread_ref[level] = spread.astype(jnp.bfloat16)


def head_kernel(probe_ref, band_ref, p0_ref, p1_ref, spread_ref, patch_ref):
    cut = lax.axis_index("cuts")

    @pl.when(cut < 2)
    def _():
        patch_ref[cut] = p0_ref[...]
        patch_ref[1 - cut] = p1_ref[...]
        forward(probe_ref, band_ref, patch_ref, spread_ref, 0, 2)


def chain_kernel(
    probe_ref, p0_ref, p1_ref, p2_ref, p3_ref, level_ref, band_ref, fourier_ref, head_ref, mine_ref, other_ref, patch_ref, spread_ref, back_ref
):
    width = probe_ref.shape[1]
    cut = lax.axis_index("cuts")
    for mask, ref in enumerate((p0_ref, p1_ref, p2_ref, p3_ref)):
        patch_ref[lax.bitwise_xor(cut, mask)] = ref[...]

    @pl.when(cut < 2)
    def _():
        spread_ref[0:3] = head_ref[...]

    @pl.when(cut >= 2)
    def _():
        forward(probe_ref, band_ref, patch_ref, spread_ref, 0, 2)

    forward(probe_ref, band_ref, patch_ref, spread_ref, 3, 3)
    fourier_r, fourier_i = fourier_ref[0], fourier_ref[1]
    wave = complex_mul(spread_ref[3], patch_ref[3], 1.0).astype(jnp.bfloat16)
    far = sandwich(fourier_r, fourier_i, wave, fourier_r, fourier_i)
    far_r, far_i = far[:width], far[width:]
    level = level_ref[:width, :].astype(jnp.float32)
    live = level_ref[width : width + 1, :].astype(jnp.float32)
    excess = 2.0 * live * (far_r * far_r + far_i * far_i - level)
    residual = jnp.concatenate([excess * far_r, excess * far_i], axis=0).astype(jnp.bfloat16)
    back_ref[...] = sandwich(fourier_r, -fourier_i, residual, fourier_r, -fourier_i).astype(jnp.bfloat16)

    def term(level):
        value = complex_mul(spread_ref[level], back_ref[...], -1.0).astype(jnp.bfloat16)

        @pl.when(level == cut)
        def _():
            mine_ref[...] = value

        @pl.when(level != cut)
        def _():
            other_ref[...] = value

    def carry(level):
        carried = complex_mul(patch_ref[level], back_ref[...], -1.0).astype(jnp.bfloat16)
        back = sandwich(band_ref[2], -band_ref[3], carried, band_ref[0], -band_ref[1])
        back_ref[...] = back.astype(jnp.bfloat16)

    @pl.when(cut >= 2)
    def _():
        term(3)

    carry(3)

    @pl.when(cut >= 2)
    def _():
        term(2)

    @pl.when(cut < 2)
    def _():
        carry(2)
        term(1)
        carry(1)
        term(0)


def scatter_kernel(rows_ref, columns_ref, mine_ref, other_ref, tile_ref, below_ref, right_ref, own_ref):
    width = tile_ref.shape[1]
    half = width // 2
    strips = []
    for place, ref in enumerate((mine_ref, other_ref)):
        field = jnp.concatenate([ref[:width, :], ref[width:, :]], axis=1)
        strips.append(dot(rows_ref[place], field).astype(jnp.bfloat16))
    for part in range(2):
        strip = jnp.concatenate([strip[:, part * width : (part + 1) * width] for strip in strips], axis=1)
        total = dot(strip, columns_ref[...])
        tile_ref[part] = total[half:, half:]
        below_ref[part] = total[half:, :half].astype(jnp.bfloat16)
        right_ref[part] = total[:half, half:].astype(jnp.bfloat16)
        own_ref[part] = total[:half, :half].astype(jnp.bfloat16)


def total_kernel(tile_ref, below_ref, right_ref, own_ref, out_ref):
    half = right_ref.shape[1]
    below = below_ref[...].astype(jnp.float32)
    right = right_ref[...].astype(jnp.float32)
    own = own_ref[...].astype(jnp.float32)
    out_ref[0, :, :half, :half] = tile_ref[:, :half, :half]
    out_ref[0, :, :half, half:] = tile_ref[:, :half, half:] + below[:, :half]
    out_ref[0, :, half:, :half] = tile_ref[:, half:, :half] + right[:, :, :half]
    out_ref[0, :, half:, half:] = tile_ref[:, half:, half:] + below[:, half:] + right[:, :, half:] + own


VMEM = pl.BlockSpec(memory_space=pltpu.VMEM)
SMEM = pl.BlockSpec(memory_space=pltpu.SMEM)
PARAMS = pltpu.CompilerParams(vmem_limit_bytes=48 * 1024 * 1024)


def shaped(*shape, dtype=jnp.bfloat16):
    return jax.ShapeDtypeStruct(shape, dtype)


def kernel(body, name, in_specs, out_shape, scratch=()):
    return pl.pallas_call(
        body, in_specs=in_specs, out_specs=[VMEM] * len(out_shape), out_shape=out_shape, scratch_shapes=scratch, compiler_params=PARAMS, name=name
    )


def local(object_slices, probe, fresnel_taps, offsets, counts, measured):
    width = probe.shape[1]
    half = width // 2
    wide = width + half
    full = shaped(2 * width, width)
    part = shaped(width, width)
    row_tiles = max(lax.axis_size("tile") // 16, 2)
    probe = probe.reshape(2 * width, width)
    fourier = jnp.asarray(fourier_matrix(width), jnp.bfloat16)

    far_tile = crossed(object_slices[0], "cuts", 2)
    tile, below, right, own = kernel(
        cut_kernel, "cut", [VMEM] * 2, [shaped(2, width, width), shaped(2, width, half), shaped(2, half, width), shaped(2, half + 16, half)]
    )(object_slices[0], offsets)
    below = passed_along(below, "tile", 1)
    right = passed_along(right, "tile", row_tiles)
    own = passed_along(own, "tile", row_tiles + 1)
    far_right = crossed(right, "cuts", 2)
    far_own = crossed(own, "cuts", 2)
    level = shaped(width + 16, width)
    band, level = kernel(band_kernel, "band", [SMEM, VMEM, VMEM], [shaped(4, width, width), level])(counts, fresnel_taps, measured)
    level, below, far_tile = lax.optimization_barrier((level, below, far_tile))
    level = passed_along(level, "tile", row_tiles + 1)
    far_below = crossed(below, "cuts", 2)
    rows, columns, rows_back, columns_back = kernel(
        window_kernel,
        "window",
        [VMEM],
        [part, shaped(2, wide, width), shaped(2, wide, width), shaped(2 * width, wide)],
    )(own)
    first, second = kernel(extract_kernel, "near", [VMEM] * 6, [full, full])(rows, columns, tile, below, right, own)
    swapped = crossed(second, "cuts", 1)
    far_own, level = lax.optimization_barrier((far_own, level))
    straight, far_second = kernel(extract_kernel, "far", [VMEM] * 6, [full, full])(rows, columns, far_tile, far_below, far_right, far_own)
    diagonal = crossed(far_second, "cuts", 1)
    (head,) = kernel(head_kernel, "head", [VMEM] * 4, [shaped(3, 2 * width, width)], [pltpu.VMEM((2, 2 * width, width), jnp.bfloat16)])(
        probe, band, first, swapped
    )
    mine, other = kernel(
        chain_kernel,
        "chain",
        [VMEM] * 9,
        [full, full],
        [
            pltpu.VMEM((4, 2 * width, width), jnp.bfloat16),
            pltpu.VMEM((4, 2 * width, width), jnp.bfloat16),
            pltpu.VMEM((2 * width, width), jnp.bfloat16),
        ],
    )(probe, first, swapped, straight, diagonal, level, band, fourier, head)
    other = crossed(other, "cuts", 1)
    total, below, right, own = kernel(
        scatter_kernel,
        "scatter",
        [VMEM] * 4,
        [shaped(2, width, width, dtype=jnp.float32), shaped(2, width, half), shaped(2, half, width), shaped(2, half, half)],
    )(rows_back, columns_back, mine, other)
    below = passed_along(below, "tile", -1)
    right = passed_along(right, "tile", -row_tiles)
    own = stepped(stepped(own, "tile", -row_tiles - 2, -row_tiles), "tile", 1, -1)
    (out,) = kernel(total_kernel, "total", [VMEM] * 4, [shaped(1, 2, width, width, dtype=jnp.float32)])(total, below, right, own)
    return out


def solution(mesh):
    return jax.shard_map(
        local,
        mesh=mesh,
        in_specs=(
            P("cuts", None, "tile", None),
            P(),
            P(),
            P("tile", None),
            P("tile"),
            P("tile", None, None),
        ),
        out_specs=P("cuts", None, "tile", None),
        check_vma=False,
    )
```

```python
import jax
import jax.numpy as jnp
import numpy as np
from jax import lax
from jax.experimental import pallas as pl
from jax.experimental.pallas import tpu as pltpu
from jax.sharding import PartitionSpec as P


def passed_along(value, axis, steps):
    count = lax.axis_size(axis)
    pairs = [(source, (source + steps) % count) for source in range(count)]
    return lax.ppermute(value, axis, pairs)


def crossed(value, axis, mask):
    pairs = [(source, source ^ mask) for source in range(lax.axis_size(axis))]
    return lax.ppermute(value, axis, pairs)


def fourier_matrix(width):
    index = np.arange(width)
    angle = 2.0 * np.pi * (index[:, None] * index[None, :] % width) / width
    return np.stack([np.cos(angle), -np.sin(angle)]) / np.sqrt(width)


def dot(left, right):
    return jnp.dot(left, right, preferred_element_type=jnp.float32)


def left_product(real, imag, field):
    top = jnp.concatenate([real, -imag], axis=1)
    bottom = jnp.concatenate([imag, real], axis=1)
    return dot(jnp.concatenate([top, bottom], axis=0), field)


def right_product(field, real, imag):
    width = real.shape[0]
    turned = jnp.concatenate([-field[width:], field[:width]], axis=0)
    return dot(jnp.concatenate([field, turned], axis=1), jnp.concatenate([real, imag], axis=0))


def sandwich(left_real, left_imag, field, right_real, right_imag):
    inner = left_product(left_real, left_imag, field).astype(jnp.bfloat16)
    return right_product(inner, right_real, right_imag)


def complex_mul(first, second, sign):
    width = first.shape[1]
    fr = first[:width].astype(jnp.float32)
    fi = first[width:].astype(jnp.float32) * sign
    sr = second[:width].astype(jnp.float32)
    si = second[width:].astype(jnp.float32)
    return jnp.concatenate([fr * sr - fi * si, fr * si + fi * sr], axis=0)


def band_kernel(counts_ref, taps_ref, measured_ref, band_ref, level_ref):
    width = band_ref.shape[1]
    half = taps_ref.shape[1] // 2
    core = lax.rem(lax.axis_index("cuts"), 2)
    level_ref[:width, :] = measured_ref[core].astype(jnp.bfloat16)
    live = (core < counts_ref[0]).astype(jnp.float32)
    level_ref[width:, :] = jnp.full((level_ref.shape[0] - width, width), live, jnp.float32).astype(jnp.bfloat16)
    rows = lax.broadcasted_iota(jnp.int32, (width, width), 0)
    columns = lax.broadcasted_iota(jnp.int32, (width, width), 1)
    inside = jnp.abs(columns - rows) <= half
    for part in range(2):
        line = taps_ref[part : part + 1, :].astype(jnp.float32)
        filler = jnp.zeros((1, width - line.shape[1]), jnp.float32)
        line = jnp.concatenate([line, filler], axis=1)
        spread = jnp.broadcast_to(line, (width, width))
        turned = pltpu.roll(spread, width - half, 1, stride=1, stride_axis=0)
        band = jnp.where(inside, turned, 0.0)
        band_ref[part] = band.astype(jnp.bfloat16)
        band_ref[part + 2] = band.T.astype(jnp.bfloat16)


def cut_kernel(tile_ref, offsets_ref, whole_ref, below_ref, right_ref, own_ref):
    half = right_ref.shape[1]
    whole_ref[...] = tile_ref[...]
    below_ref[...] = tile_ref[:, :, half:]
    right_ref[...] = tile_ref[:, half:, :]
    own_ref[:, :half, :] = tile_ref[:, half:, half:]
    shape = (own_ref.shape[1] - half, half)
    line = lax.broadcasted_iota(jnp.int32, shape, 0)
    lines = jnp.zeros(shape, jnp.float32)
    for index in range(4):
        value = offsets_ref[index // 2 : index // 2 + 1, index % 2 : index % 2 + 1].astype(jnp.float32)
        lines = jnp.where(line == index, value, lines)
    for part in range(2):
        own_ref[part, half:, :] = lines.astype(jnp.bfloat16)


def window_kernel(own_ref, rows_ref, columns_ref, rows_back_ref, columns_back_ref):
    half = own_ref.shape[2]
    width = 2 * half
    core = lax.rem(lax.axis_index("cuts"), 2)
    lines = own_ref[0, half:, :].astype(jnp.float32).astype(jnp.int32) - half

    def placed(shape, axis, shift):
        i = lax.broadcasted_iota(jnp.int32, shape, axis)
        j = lax.broadcasted_iota(jnp.int32, shape, 1 - axis)
        shift = jnp.concatenate([shift] * (shape[1] // half), axis=1)
        return jnp.where(j - i == shift, 1.0, 0.0).astype(jnp.bfloat16)

    for place in range(2):
        second = core != place
        row = jnp.where(second, lines[2:3], lines[0:1])
        column = jnp.where(second, lines[3:4], lines[1:2])
        rows_ref[place * half : (place + 1) * half, :] = placed((half, width), 0, row)
        columns_ref[place] = placed((width + half, width), 1, column)
        rows_back_ref[place] = placed((width + half, width), 1, row)
        columns_back_ref[place * width : (place + 1) * width, :] = placed((width, width + half), 0, column)


def extract_kernel(rows_ref, columns_ref, tile_ref, below_ref, right_ref, own_ref, first_ref, second_ref):
    width = tile_ref.shape[1]
    half = width // 2
    wide = width + half
    blocks = []
    for part in range(2):
        upper = jnp.concatenate([own_ref[part, :half], right_ref[part]], axis=1)
        lower = jnp.concatenate([below_ref[part], tile_ref[part]], axis=1)
        blocks.append(jnp.concatenate([upper, lower], axis=0))
    block = jnp.concatenate(blocks, axis=1)
    strips = [dot(rows_ref[...], block[top : top + width]).astype(jnp.bfloat16) for top in (0, half)]
    for place, out_ref in enumerate((first_ref, second_ref)):
        mine = [strip[place * half : (place + 1) * half, part * wide : (part + 1) * wide] for part in range(2) for strip in strips]
        out_ref[...] = dot(jnp.concatenate(mine, axis=0), columns_ref[place]).astype(jnp.bfloat16)


def forward(probe_ref, band_ref, patch_ref, spread_ref, first, last):
    for level in range(first, last + 1):
        if level == 0:
            spread_ref[0] = probe_ref[...]
        else:
            wave = complex_mul(spread_ref[level - 1], patch_ref[level - 1], 1.0).astype(jnp.bfloat16)
            spread = sandwich(band_ref[0], band_ref[1], wave, band_ref[2], band_ref[3])
            spread_ref[level] = spread.astype(jnp.bfloat16)


def head_kernel(probe_ref, band_ref, p0_ref, p1_ref, spread_ref, patch_ref):
    cut = lax.axis_index("cuts")

    @pl.when(cut < 2)
    def _():
        patch_ref[cut] = p0_ref[...]
        patch_ref[1 - cut] = p1_ref[...]
        forward(probe_ref, band_ref, patch_ref, spread_ref, 0, 2)


def chain_kernel(
    probe_ref, p0_ref, p1_ref, p2_ref, p3_ref, level_ref, band_ref, fourier_ref, head_ref, mine_ref, other_ref, patch_ref, spread_ref, back_ref
):
    width = probe_ref.shape[1]
    cut = lax.axis_index("cuts")
    for mask, ref in enumerate((p0_ref, p1_ref, p2_ref, p3_ref)):
        patch_ref[lax.bitwise_xor(cut, mask)] = ref[...]

    @pl.when(cut < 2)
    def _():
        spread_ref[0:3] = head_ref[...]

    @pl.when(cut >= 2)
    def _():
        forward(probe_ref, band_ref, patch_ref, spread_ref, 0, 2)

    forward(probe_ref, band_ref, patch_ref, spread_ref, 3, 3)
    fourier_r, fourier_i = fourier_ref[0], fourier_ref[1]
    wave = complex_mul(spread_ref[3], patch_ref[3], 1.0).astype(jnp.bfloat16)
    far = sandwich(fourier_r, fourier_i, wave, fourier_r, fourier_i)
    far_r, far_i = far[:width], far[width:]
    level = level_ref[:width, :].astype(jnp.float32)
    live = level_ref[width : width + 1, :].astype(jnp.float32)
    excess = 2.0 * live * (far_r * far_r + far_i * far_i - level)
    residual = jnp.concatenate([excess * far_r, excess * far_i], axis=0).astype(jnp.bfloat16)
    back_ref[...] = sandwich(fourier_r, -fourier_i, residual, fourier_r, -fourier_i).astype(jnp.bfloat16)

    def term(level):
        value = complex_mul(spread_ref[level], back_ref[...], -1.0).astype(jnp.bfloat16)

        @pl.when(level == cut)
        def _():
            mine_ref[...] = value

        @pl.when(level != cut)
        def _():
            other_ref[...] = value

    def carry(level):
        carried = complex_mul(patch_ref[level], back_ref[...], -1.0).astype(jnp.bfloat16)
        back = sandwich(band_ref[2], -band_ref[3], carried, band_ref[0], -band_ref[1])
        back_ref[...] = back.astype(jnp.bfloat16)

    @pl.when(cut >= 2)
    def _():
        term(3)

    carry(3)

    @pl.when(cut >= 2)
    def _():
        term(2)

    @pl.when(cut < 2)
    def _():
        carry(2)
        term(1)
        carry(1)
        term(0)


def scatter_kernel(rows_ref, columns_ref, mine_ref, other_ref, tile_ref, below_ref, right_ref, own_ref):
    width = tile_ref.shape[1]
    half = width // 2
    strips = []
    for place, ref in enumerate((mine_ref, other_ref)):
        field = jnp.concatenate([ref[:width, :], ref[width:, :]], axis=1)
        strips.append(dot(rows_ref[place], field).astype(jnp.bfloat16))
    for part in range(2):
        strip = jnp.concatenate([strip[:, part * width : (part + 1) * width] for strip in strips], axis=1)
        total = dot(strip, columns_ref[...])
        tile_ref[part] = total[half:, half:]
        below_ref[part] = total[half:, :half].astype(jnp.bfloat16)
        right_ref[part] = total[:half, half:].astype(jnp.bfloat16)
        own_ref[part] = total[:half, :half].astype(jnp.bfloat16)


def total_kernel(tile_ref, below_ref, right_ref, own_ref, out_ref):
    half = right_ref.shape[1]
    below = below_ref[...].astype(jnp.float32)
    right = right_ref[...].astype(jnp.float32)
    own = own_ref[...].astype(jnp.float32)
    out_ref[0, :, :half, :half] = tile_ref[:, :half, :half]
    out_ref[0, :, :half, half:] = tile_ref[:, :half, half:] + below[:, :half]
    out_ref[0, :, half:, :half] = tile_ref[:, half:, :half] + right[:, :, :half]
    out_ref[0, :, half:, half:] = tile_ref[:, half:, half:] + below[:, half:] + right[:, :, half:] + own


VMEM = pl.BlockSpec(memory_space=pltpu.VMEM)
SMEM = pl.BlockSpec(memory_space=pltpu.SMEM)
PARAMS = pltpu.CompilerParams(vmem_limit_bytes=48 * 1024 * 1024)


def shaped(*shape, dtype=jnp.bfloat16):
    return jax.ShapeDtypeStruct(shape, dtype)


def kernel(body, name, in_specs, out_shape, scratch=()):
    return pl.pallas_call(
        body, in_specs=in_specs, out_specs=[VMEM] * len(out_shape), out_shape=out_shape, scratch_shapes=scratch, compiler_params=PARAMS, name=name
    )


def local(object_slices, probe, fresnel_taps, offsets, counts, measured):
    width = probe.shape[1]
    half = width // 2
    wide = width + half
    full = shaped(2 * width, width)
    part = shaped(width, width)
    row_tiles = max(lax.axis_size("tile") // 16, 2)
    probe = probe.reshape(2 * width, width)
    fourier = jnp.asarray(fourier_matrix(width), jnp.bfloat16)

    far_tile = crossed(object_slices[0], "cuts", 2)
    tile, below, right, own = kernel(
        cut_kernel, "cut", [VMEM] * 2, [shaped(2, width, width), shaped(2, width, half), shaped(2, half, width), shaped(2, half + 16, half)]
    )(object_slices[0], offsets)
    below = passed_along(below, "tile", 1)
    right = passed_along(right, "tile", row_tiles)
    own = passed_along(own, "tile", row_tiles + 1)
    far_right = crossed(right, "cuts", 2)
    far_own = crossed(own, "cuts", 2)
    level = shaped(width + 16, width)
    band, level = kernel(band_kernel, "band", [SMEM, VMEM, VMEM], [shaped(4, width, width), level])(counts, fresnel_taps, measured)
    level, below, right, far_tile = lax.optimization_barrier((level, below, right, far_tile))
    level = passed_along(level, "tile", row_tiles + 1)
    far_below = crossed(below, "cuts", 2)
    rows, columns, rows_back, columns_back = kernel(
        window_kernel,
        "window",
        [VMEM],
        [part, shaped(2, wide, width), shaped(2, wide, width), shaped(2 * width, wide)],
    )(own)
    first, second = kernel(extract_kernel, "near", [VMEM] * 6, [full, full])(rows, columns, tile, below, right, own)
    swapped = crossed(second, "cuts", 1)
    far_own, level = lax.optimization_barrier((far_own, level))
    straight, far_second = kernel(extract_kernel, "far", [VMEM] * 6, [full, full])(rows, columns, far_tile, far_below, far_right, far_own)
    diagonal = crossed(far_second, "cuts", 1)
    (head,) = kernel(head_kernel, "head", [VMEM] * 4, [shaped(3, 2 * width, width)], [pltpu.VMEM((2, 2 * width, width), jnp.bfloat16)])(
        probe, band, first, swapped
    )
    mine, other = kernel(
        chain_kernel,
        "chain",
        [VMEM] * 9,
        [full, full],
        [
            pltpu.VMEM((4, 2 * width, width), jnp.bfloat16),
            pltpu.VMEM((4, 2 * width, width), jnp.bfloat16),
            pltpu.VMEM((2 * width, width), jnp.bfloat16),
        ],
    )(probe, first, swapped, straight, diagonal, level, band, fourier, head)
    other = crossed(other, "cuts", 1)
    total, below, right, own = kernel(
        scatter_kernel,
        "scatter",
        [VMEM] * 4,
        [shaped(2, width, width, dtype=jnp.float32), shaped(2, width, half), shaped(2, half, width), shaped(2, half, half)],
    )(rows_back, columns_back, mine, other)
    below = passed_along(below, "tile", -1)
    right = passed_along(right, "tile", -row_tiles)
    own = passed_along(own, "tile", -row_tiles - 1)
    (out,) = kernel(total_kernel, "total", [VMEM] * 4, [shaped(1, 2, width, width, dtype=jnp.float32)])(total, below, right, own)
    return out


def solution(mesh):
    return jax.shard_map(
        local,
        mesh=mesh,
        in_specs=(
            P("cuts", None, "tile", None),
            P(),
            P(),
            P("tile", None),
            P("tile"),
            P("tile", None, None),
        ),
        out_specs=P("cuts", None, "tile", None),
        check_vma=False,
    )
```

```python
import jax
import jax.numpy as jnp
import numpy as np
from jax import lax
from jax.experimental import pallas as pl
from jax.experimental.pallas import tpu as pltpu
from jax.sharding import PartitionSpec as P


NOTES = 16
SPARE = 32


def stepped(value, even, odd):
    count = lax.axis_size("tile")
    steps = [odd if source % 2 else even for source in range(count)]
    pairs = [(source, (source + steps[source]) % count) for source in range(count) if steps[source] is not None]
    return lax.ppermute(value, "tile", pairs)


def crossed(value, axis, mask):
    pairs = [(source, source ^ mask) for source in range(lax.axis_size(axis))]
    return lax.ppermute(value, axis, pairs)


def fourier_matrix(width):
    index = np.arange(width)
    angle = 2.0 * np.pi * (index[:, None] * index[None, :] % width) / width
    return np.stack([np.cos(angle), -np.sin(angle)]) / np.sqrt(width)


def dot(left, right):
    return jnp.dot(left, right, preferred_element_type=jnp.float32)


def left_product(real, imag, field):
    top = jnp.concatenate([real, -imag], axis=1)
    bottom = jnp.concatenate([imag, real], axis=1)
    return dot(jnp.concatenate([top, bottom], axis=0), field)


def right_product(field, real, imag):
    width = real.shape[0]
    turned = jnp.concatenate([-field[width:], field[:width]], axis=0)
    return dot(jnp.concatenate([field, turned], axis=1), jnp.concatenate([real, imag], axis=0))


def sandwich(left_real, left_imag, field, right_real, right_imag):
    inner = left_product(left_real, left_imag, field).astype(jnp.bfloat16)
    return right_product(inner, right_real, right_imag)


def complex_mul(first, second, sign):
    width = first.shape[1]
    fr = first[:width].astype(jnp.float32)
    fi = first[width:].astype(jnp.float32) * sign
    sr = second[:width].astype(jnp.float32)
    si = second[width:].astype(jnp.float32)
    return jnp.concatenate([fr * sr - fi * si, fr * si + fi * sr], axis=0)


def is_odd():
    return lax.rem(lax.axis_index("tile"), 2) == 1


def cut_kernel(tile_ref, low_ref, high_ref, side_ref):
    half = low_ref.shape[1]
    low_ref[...] = tile_ref[:, :half, :]
    high_ref[...] = tile_ref[:, half:, :]
    side_ref[:, : 2 * half, :] = tile_ref[:, :, half:]
    side_ref[:, 2 * half :, :] = jnp.zeros((2, SPARE, half), jnp.bfloat16)


def seal_kernel(high_ref, offsets_ref, counts_ref, measured_ref, own_ref):
    half = high_ref.shape[1]
    own_ref[:, :half, :] = high_ref[:, :, half:]
    cut = lax.axis_index("cuts")
    core = lax.rem(cut, 2)
    shape = (NOTES, half)
    line = lax.broadcasted_iota(jnp.int32, shape, 0)
    lines = jnp.where(core < counts_ref[0], jnp.ones(shape, jnp.float32), 0.0)
    for index in range(4):
        value = offsets_ref[index // 2 : index // 2 + 1, index % 2 : index % 2 + 1].astype(jnp.float32)
        lines = jnp.where(line == index, value, lines)
    level = measured_ref[core, pl.ds(pl.multiple_of(cut // 2 * half, half), half), :].astype(jnp.bfloat16)
    for part in range(2):
        own_ref[part, half : half + NOTES, :] = lines.astype(jnp.bfloat16)
        own_ref[part, half + NOTES :, :] = level[:, part * half : (part + 1) * half]


def choose_kernel(low_ref, come_ref, out_ref):
    half = low_ref.shape[1]
    out_ref[:, :half, :] = jnp.where(is_odd(), low_ref[...], come_ref[:, :half, :])
    out_ref[:, half:, :] = come_ref[:, half:, :]


def band_kernel(taps_ref, band_ref):
    width = band_ref.shape[1]
    half = taps_ref.shape[1] // 2
    rows = lax.broadcasted_iota(jnp.int32, (width, width), 0)
    columns = lax.broadcasted_iota(jnp.int32, (width, width), 1)
    inside = jnp.abs(columns - rows) <= half
    for part in range(2):
        line = taps_ref[part : part + 1, :].astype(jnp.float32)
        filler = jnp.zeros((1, width - line.shape[1]), jnp.float32)
        line = jnp.concatenate([line, filler], axis=1)
        spread = jnp.broadcast_to(line, (width, width))
        turned = pltpu.roll(spread, width - half, 1, stride=1, stride_axis=0)
        band = jnp.where(inside, turned, 0.0)
        band_ref[part] = band.astype(jnp.bfloat16)
        band_ref[part + 2] = band.T.astype(jnp.bfloat16)


def window_kernel(own_ref, rows_ref, columns_ref, rows_back_ref, columns_back_ref):
    half = own_ref.shape[2]
    width = 2 * half
    core = lax.rem(lax.axis_index("cuts"), 2)
    lines = own_ref[0, half : half + NOTES, :].astype(jnp.float32).astype(jnp.int32) - half

    def placed(shape, axis, shift):
        i = lax.broadcasted_iota(jnp.int32, shape, axis)
        j = lax.broadcasted_iota(jnp.int32, shape, 1 - axis)
        shift = jnp.concatenate([shift] * (shape[1] // half), axis=1)
        return jnp.where(j - i == shift, 1.0, 0.0).astype(jnp.bfloat16)

    for place in range(2):
        second = core != place
        row = jnp.where(second, lines[2:3], lines[0:1])
        column = jnp.where(second, lines[3:4], lines[1:2])
        rows_ref[place * half : (place + 1) * half, :] = placed((half, width), 0, row)
        columns_ref[place] = placed((width + half, width), 1, column)
        rows_back_ref[place] = placed((width + half, width), 1, row)
        columns_back_ref[place * width : (place + 1) * width, :] = placed((width, width + half), 0, column)


def extract_kernel(rows_ref, columns_ref, come_ref, high_ref, side_ref, own_ref, first_ref, second_ref):
    half = high_ref.shape[1]
    width = 2 * half
    wide = width + half
    odd = is_odd()
    blocks = []
    for part in range(2):
        high, come = high_ref[part], come_ref[part, half:]
        top = jnp.concatenate([own_ref[part, :half], jnp.where(odd, come, high)], axis=1)
        corner = jnp.concatenate([come_ref[part, :half], jnp.where(odd, high, come)], axis=0)
        blocks.append(jnp.concatenate([top, jnp.concatenate([side_ref[part, :width], corner], axis=1)], axis=0))
    block = jnp.concatenate(blocks, axis=1)
    strips = [dot(rows_ref[...], block[top : top + width]).astype(jnp.bfloat16) for top in (0, half)]
    for place, out_ref in enumerate((first_ref, second_ref)):
        mine = [strip[place * half : (place + 1) * half, part * wide : (part + 1) * wide] for part in range(2) for strip in strips]
        out_ref[...] = dot(jnp.concatenate(mine, axis=0), columns_ref[place]).astype(jnp.bfloat16)


def forward(probe_ref, band_ref, patch_ref, spread_ref, first, last):
    for level in range(first, last + 1):
        if level == 0:
            spread_ref[0] = probe_ref[...]
        else:
            wave = complex_mul(spread_ref[level - 1], patch_ref[level - 1], 1.0).astype(jnp.bfloat16)
            spread = sandwich(band_ref[0], band_ref[1], wave, band_ref[2], band_ref[3])
            spread_ref[level] = spread.astype(jnp.bfloat16)


def head_kernel(probe_ref, band_ref, p0_ref, p1_ref, spread_ref, patch_ref):
    cut = lax.axis_index("cuts")

    @pl.when(cut < 2)
    def _():
        patch_ref[cut] = p0_ref[...]
        patch_ref[1 - cut] = p1_ref[...]
        forward(probe_ref, band_ref, patch_ref, spread_ref, 0, 2)


def chain_kernel(
    probe_ref, p0_ref, p1_ref, p2_ref, p3_ref, own_ref, far_own_ref, band_ref, fourier_ref, head_ref, mine_ref, other_ref, patch_ref, spread_ref, back_ref
):
    width = probe_ref.shape[1]
    cut = lax.axis_index("cuts")
    for mask, ref in enumerate((p0_ref, p1_ref, p2_ref, p3_ref)):
        patch_ref[lax.bitwise_xor(cut, mask)] = ref[...]

    @pl.when(cut < 2)
    def _():
        spread_ref[0:3] = head_ref[...]

    @pl.when(cut >= 2)
    def _():
        forward(probe_ref, band_ref, patch_ref, spread_ref, 0, 2)

    forward(probe_ref, band_ref, patch_ref, spread_ref, 3, 3)
    fourier_r, fourier_i = fourier_ref[0], fourier_ref[1]
    wave = complex_mul(spread_ref[3], patch_ref[3], 1.0).astype(jnp.bfloat16)
    far = sandwich(fourier_r, fourier_i, wave, fourier_r, fourier_i)
    far_r, far_i = far[:width], far[width:]
    half = width // 2
    levels = []
    for ref in (own_ref, far_own_ref):
        levels.append(jnp.concatenate([ref[part, half + NOTES :, :] for part in range(2)], axis=1).astype(jnp.float32))
    level = jnp.concatenate([jnp.where(cut < 2, *levels), jnp.where(cut < 2, *levels[::-1])], axis=0)
    live = jnp.concatenate([own_ref[0, half + 4 : half + 5, :]] * 2, axis=1).astype(jnp.float32)
    excess = 2.0 * live * (far_r * far_r + far_i * far_i - level)
    residual = jnp.concatenate([excess * far_r, excess * far_i], axis=0).astype(jnp.bfloat16)
    back_ref[...] = sandwich(fourier_r, -fourier_i, residual, fourier_r, -fourier_i).astype(jnp.bfloat16)

    def term(level):
        value = complex_mul(spread_ref[level], back_ref[...], -1.0).astype(jnp.bfloat16)

        @pl.when(level == cut)
        def _():
            mine_ref[...] = value

        @pl.when(level != cut)
        def _():
            other_ref[...] = value

    def carry(level):
        carried = complex_mul(patch_ref[level], back_ref[...], -1.0).astype(jnp.bfloat16)
        back = sandwich(band_ref[2], -band_ref[3], carried, band_ref[0], -band_ref[1])
        back_ref[...] = back.astype(jnp.bfloat16)

    @pl.when(cut >= 2)
    def _():
        term(3)

    carry(3)

    @pl.when(cut >= 2)
    def _():
        term(2)

    @pl.when(cut < 2)
    def _():
        carry(2)
        term(1)
        carry(1)
        term(0)


def scatter_kernel(rows_ref, columns_ref, mine_ref, other_ref, tile_ref, come_ref, side_ref, own_ref):
    width = tile_ref.shape[1]
    half = width // 2
    odd = is_odd()
    strips = []
    for place, ref in enumerate((mine_ref, other_ref)):
        field = jnp.concatenate([ref[:width, :], ref[width:, :]], axis=1)
        strips.append(dot(rows_ref[place], field).astype(jnp.bfloat16))
    for part in range(2):
        strip = jnp.concatenate([strip[:, part * width : (part + 1) * width] for strip in strips], axis=1)
        total = dot(strip, columns_ref[...])
        right, upper, lower = total[:half, half:], total[half:width, half:], total[width:, half:]
        tile_ref[part, :half, :] = jnp.where(odd, upper, 0.0)
        tile_ref[part, half:, :] = jnp.where(odd, lower, right)
        come_ref[part, :half, :] = jnp.where(odd, 0.0, upper).astype(jnp.bfloat16)
        come_ref[part, half:, :] = jnp.where(odd, right, lower).astype(jnp.bfloat16)
        side_ref[part] = total[half:, :half].astype(jnp.bfloat16)
        own_ref[part] = total[:half, :half].astype(jnp.bfloat16)


def total_kernel(tile_ref, come_ref, side_ref, own_ref, out_ref):
    half = own_ref.shape[1]
    side = side_ref[...].astype(jnp.float32)
    own = own_ref[...].astype(jnp.float32)
    sum_left = tile_ref[:, :, :half] + come_ref[:, :, :half].astype(jnp.float32)
    sum_right = tile_ref[:, :, half:] + come_ref[:, :, half:].astype(jnp.float32) + side
    out_ref[0, :, :, :half] = sum_left
    out_ref[0, :, :half, half:] = sum_right[:, :half]
    out_ref[0, :, half:, half:] = sum_right[:, half:] + own


VMEM = pl.BlockSpec(memory_space=pltpu.VMEM)
SMEM = pl.BlockSpec(memory_space=pltpu.SMEM)
PARAMS = pltpu.CompilerParams(vmem_limit_bytes=48 * 1024 * 1024)


def shaped(*shape, dtype=jnp.bfloat16):
    return jax.ShapeDtypeStruct(shape, dtype)


def kernel(body, name, in_specs, out_shape, scratch=()):
    return pl.pallas_call(
        body, in_specs=in_specs, out_specs=[VMEM] * len(out_shape), out_shape=out_shape, scratch_shapes=scratch, compiler_params=PARAMS, name=name
    )


def local(object_slices, probe, fresnel_taps, offsets, counts, measured):
    width = probe.shape[1]
    half = width // 2
    wide = width + half
    full = shaped(2 * width, width)
    part = shaped(width, width)
    row_tiles = max(lax.axis_size("tile") // 16, 2)
    probe = probe.reshape(2 * width, width)
    fourier = jnp.asarray(fourier_matrix(width), jnp.bfloat16)

    strip = shaped(2, half, width)
    come = stepped(object_slices[0], -row_tiles, row_tiles)
    low, high, side = kernel(cut_kernel, "cut", [VMEM], [strip, strip, shaped(2, width + SPARE, half)])(object_slices[0])
    (own,) = kernel(seal_kernel, "seal", [VMEM, VMEM, SMEM, VMEM], [shaped(2, width + NOTES, half)])(high, offsets, counts, measured)
    far_high = crossed(high, "cuts", 2)
    side = stepped(side, 1, 1 - row_tiles)
    own = stepped(own, row_tiles + 1, 1)
    (come,) = kernel(choose_kernel, "choose", [VMEM] * 2, [shaped(2, width, width)])(low, come)
    side, far_high = lax.optimization_barrier((side, far_high))
    far_side = crossed(side, "cuts", 2)
    far_come = crossed(come, "cuts", 2)
    far_own = crossed(own, "cuts", 2)
    (band,) = kernel(band_kernel, "band", [VMEM], [shaped(4, width, width)])(fresnel_taps)
    rows, columns, rows_back, columns_back = kernel(
        window_kernel,
        "window",
        [VMEM],
        [part, shaped(2, wide, width), shaped(2, wide, width), shaped(2 * width, wide)],
    )(own)
    first, second = kernel(extract_kernel, "near", [VMEM] * 6, [full, full])(rows, columns, come, high, side, own)
    swapped = crossed(second, "cuts", 1)
    straight, far_second = kernel(extract_kernel, "far", [VMEM] * 6, [full, full])(rows, columns, far_come, far_high, far_side, far_own)
    diagonal = crossed(far_second, "cuts", 1)
    (head,) = kernel(head_kernel, "head", [VMEM] * 4, [shaped(3, 2 * width, width)], [pltpu.VMEM((2, 2 * width, width), jnp.bfloat16)])(
        probe, band, first, swapped
    )
    mine, other = kernel(
        chain_kernel,
        "chain",
        [VMEM] * 10,
        [full, full],
        [
            pltpu.VMEM((4, 2 * width, width), jnp.bfloat16),
            pltpu.VMEM((4, 2 * width, width), jnp.bfloat16),
            pltpu.VMEM((2 * width, width), jnp.bfloat16),
        ],
    )(probe, first, swapped, straight, diagonal, own, far_own, band, fourier, head)
    other = crossed(other, "cuts", 1)
    total, come, side, own = kernel(
        scatter_kernel,
        "scatter",
        [VMEM] * 4,
        [shaped(2, width, width, dtype=jnp.float32), shaped(2, width, width), shaped(2, width, half), shaped(2, half, half)],
    )(rows_back, columns_back, mine, other)
    come = stepped(come, row_tiles, -row_tiles)
    side = stepped(side, row_tiles - 1, -1)
    own = stepped(own, -1, -row_tiles - 1)
    (out,) = kernel(total_kernel, "total", [VMEM] * 4, [shaped(1, 2, width, width, dtype=jnp.float32)])(total, come, side, own)
    return out


def solution(mesh):
    return jax.shard_map(
        local,
        mesh=mesh,
        in_specs=(
            P("cuts", None, "tile", None),
            P(),
            P(),
            P("tile", None),
            P("tile"),
            P("tile", None, None),
        ),
        out_specs=P("cuts", None, "tile", None),
        check_vma=False,
    )
```

```python
import jax
import jax.numpy as jnp
import numpy as np
from jax import lax
from jax.experimental import pallas as pl
from jax.experimental.pallas import tpu as pltpu
from jax.sharding import PartitionSpec as P


def passed_along(value, axis, steps):
    count = lax.axis_size(axis)
    pairs = [(source, (source + steps) % count) for source in range(count)]
    return lax.ppermute(value, axis, pairs)


def crossed(value, axis, mask):
    pairs = [(source, source ^ mask) for source in range(lax.axis_size(axis))]
    return lax.ppermute(value, axis, pairs)


def fourier_matrix(width):
    index = np.arange(width)
    angle = 2.0 * np.pi * (index[:, None] * index[None, :] % width) / width
    return np.stack([np.cos(angle), -np.sin(angle)]) / np.sqrt(width)


def dot(left, right):
    return jnp.dot(left, right, preferred_element_type=jnp.float32)


def left_product(real, imag, field):
    top = jnp.concatenate([real, -imag], axis=1)
    bottom = jnp.concatenate([imag, real], axis=1)
    return dot(jnp.concatenate([top, bottom], axis=0), field)


def right_product(field, real, imag):
    width = real.shape[0]
    turned = jnp.concatenate([-field[width:], field[:width]], axis=0)
    return dot(jnp.concatenate([field, turned], axis=1), jnp.concatenate([real, imag], axis=0))


def sandwich(left_real, left_imag, field, right_real, right_imag):
    inner = left_product(left_real, left_imag, field).astype(jnp.bfloat16)
    return right_product(inner, right_real, right_imag)


def complex_mul(first, second, sign):
    width = first.shape[1]
    fr = first[:width].astype(jnp.float32)
    fi = first[width:].astype(jnp.float32) * sign
    sr = second[:width].astype(jnp.float32)
    si = second[width:].astype(jnp.float32)
    return jnp.concatenate([fr * sr - fi * si, fr * si + fi * sr], axis=0)


def band_kernel(counts_ref, taps_ref, measured_ref, band_ref, level_ref):
    width = band_ref.shape[1]
    half = taps_ref.shape[1] // 2
    core = lax.rem(lax.axis_index("cuts"), 2)
    rows = width // 2
    first = pl.multiple_of(lax.axis_index("cuts") // 2 * rows, rows)
    level_ref[:rows, :] = measured_ref[core, pl.ds(first, rows), :].astype(jnp.bfloat16)
    live = (core < counts_ref[0]).astype(jnp.float32)
    level_ref[rows:, :] = jnp.full((level_ref.shape[0] - rows, width), live, jnp.float32).astype(jnp.bfloat16)
    rows = lax.broadcasted_iota(jnp.int32, (width, width), 0)
    columns = lax.broadcasted_iota(jnp.int32, (width, width), 1)
    inside = jnp.abs(columns - rows) <= half
    for part in range(2):
        line = taps_ref[part : part + 1, :].astype(jnp.float32)
        filler = jnp.zeros((1, width - line.shape[1]), jnp.float32)
        line = jnp.concatenate([line, filler], axis=1)
        spread = jnp.broadcast_to(line, (width, width))
        turned = pltpu.roll(spread, width - half, 1, stride=1, stride_axis=0)
        band = jnp.where(inside, turned, 0.0)
        band_ref[part] = band.astype(jnp.bfloat16)
        band_ref[part + 2] = band.T.astype(jnp.bfloat16)


def cut_kernel(tile_ref, whole_ref, below_ref, right_ref):
    half = right_ref.shape[1]
    whole_ref[...] = tile_ref[...]
    below_ref[...] = tile_ref[:, :, half:]
    right_ref[...] = tile_ref[:, half:, :]


def seal_kernel(tile_ref, offsets_ref, own_ref):
    half = tile_ref.shape[1] // 2
    own_ref[:, :half, :] = tile_ref[:, half:, half:]
    shape = (own_ref.shape[1] - half, half)
    line = lax.broadcasted_iota(jnp.int32, shape, 0)
    lines = jnp.zeros(shape, jnp.float32)
    for index in range(4):
        value = offsets_ref[index // 2 : index // 2 + 1, index % 2 : index % 2 + 1].astype(jnp.float32)
        lines = jnp.where(line == index, value, lines)
    for part in range(2):
        own_ref[part, half:, :] = lines.astype(jnp.bfloat16)


def window_kernel(own_ref, rows_ref, columns_ref, rows_back_ref, columns_back_ref):
    half = own_ref.shape[2]
    width = 2 * half
    core = lax.rem(lax.axis_index("cuts"), 2)
    lines = own_ref[0, half:, :].astype(jnp.float32).astype(jnp.int32) - half

    def placed(shape, axis, shift):
        i = lax.broadcasted_iota(jnp.int32, shape, axis)
        j = lax.broadcasted_iota(jnp.int32, shape, 1 - axis)
        shift = jnp.concatenate([shift] * (shape[1] // half), axis=1)
        return jnp.where(j - i == shift, 1.0, 0.0).astype(jnp.bfloat16)

    for place in range(2):
        second = core != place
        row = jnp.where(second, lines[2:3], lines[0:1])
        column = jnp.where(second, lines[3:4], lines[1:2])
        rows_ref[place * half : (place + 1) * half, :] = placed((half, width), 0, row)
        columns_ref[place] = placed((width + half, width), 1, column)
        rows_back_ref[place] = placed((width + half, width), 1, row)
        columns_back_ref[place * width : (place + 1) * width, :] = placed((width, width + half), 0, column)


def extract_kernel(rows_ref, columns_ref, tile_ref, below_ref, right_ref, own_ref, first_ref, second_ref):
    width = tile_ref.shape[1]
    half = width // 2
    wide = width + half
    blocks = []
    for part in range(2):
        upper = jnp.concatenate([own_ref[part, :half], right_ref[part]], axis=1)
        lower = jnp.concatenate([below_ref[part], tile_ref[part]], axis=1)
        blocks.append(jnp.concatenate([upper, lower], axis=0))
    block = jnp.concatenate(blocks, axis=1)
    strips = [dot(rows_ref[...], block[top : top + width]).astype(jnp.bfloat16) for top in (0, half)]
    for place, out_ref in enumerate((first_ref, second_ref)):
        mine = [strip[place * half : (place + 1) * half, part * wide : (part + 1) * wide] for part in range(2) for strip in strips]
        out_ref[...] = dot(jnp.concatenate(mine, axis=0), columns_ref[place]).astype(jnp.bfloat16)


def forward(probe_ref, band_ref, patch_ref, spread_ref, first, last):
    for level in range(first, last + 1):
        if level == 0:
            spread_ref[0] = probe_ref[...]
        else:
            wave = complex_mul(spread_ref[level - 1], patch_ref[level - 1], 1.0).astype(jnp.bfloat16)
            spread = sandwich(band_ref[0], band_ref[1], wave, band_ref[2], band_ref[3])
            spread_ref[level] = spread.astype(jnp.bfloat16)


def head_kernel(probe_ref, band_ref, p0_ref, p1_ref, spread_ref, patch_ref):
    cut = lax.axis_index("cuts")

    @pl.when(cut < 2)
    def _():
        patch_ref[cut] = p0_ref[...]
        patch_ref[1 - cut] = p1_ref[...]
        forward(probe_ref, band_ref, patch_ref, spread_ref, 0, 2)


def chain_kernel(
    probe_ref, p0_ref, p1_ref, p2_ref, p3_ref, level_ref, far_level_ref, band_ref, fourier_ref, head_ref, mine_ref, other_ref, patch_ref, spread_ref, back_ref
):
    width = probe_ref.shape[1]
    cut = lax.axis_index("cuts")
    for mask, ref in enumerate((p0_ref, p1_ref, p2_ref, p3_ref)):
        patch_ref[lax.bitwise_xor(cut, mask)] = ref[...]

    @pl.when(cut < 2)
    def _():
        spread_ref[0:3] = head_ref[...]

    @pl.when(cut >= 2)
    def _():
        forward(probe_ref, band_ref, patch_ref, spread_ref, 0, 2)

    forward(probe_ref, band_ref, patch_ref, spread_ref, 3, 3)
    fourier_r, fourier_i = fourier_ref[0], fourier_ref[1]
    wave = complex_mul(spread_ref[3], patch_ref[3], 1.0).astype(jnp.bfloat16)
    far = sandwich(fourier_r, fourier_i, wave, fourier_r, fourier_i)
    far_r, far_i = far[:width], far[width:]
    rows = width // 2
    level, far_level = level_ref[:rows, :].astype(jnp.float32), far_level_ref[:rows, :].astype(jnp.float32)
    level = jnp.concatenate([jnp.where(cut < 2, level, far_level), jnp.where(cut < 2, far_level, level)], axis=0)
    live = level_ref[rows : rows + 1, :].astype(jnp.float32)
    excess = 2.0 * live * (far_r * far_r + far_i * far_i - level)
    residual = jnp.concatenate([excess * far_r, excess * far_i], axis=0).astype(jnp.bfloat16)
    back_ref[...] = sandwich(fourier_r, -fourier_i, residual, fourier_r, -fourier_i).astype(jnp.bfloat16)

    def term(level):
        value = complex_mul(spread_ref[level], back_ref[...], -1.0).astype(jnp.bfloat16)

        @pl.when(level == cut)
        def _():
            mine_ref[...] = value

        @pl.when(level != cut)
        def _():
            other_ref[...] = value

    def carry(level):
        carried = complex_mul(patch_ref[level], back_ref[...], -1.0).astype(jnp.bfloat16)
        back = sandwich(band_ref[2], -band_ref[3], carried, band_ref[0], -band_ref[1])
        back_ref[...] = back.astype(jnp.bfloat16)

    @pl.when(cut >= 2)
    def _():
        term(3)

    carry(3)

    @pl.when(cut >= 2)
    def _():
        term(2)

    @pl.when(cut < 2)
    def _():
        carry(2)
        term(1)
        carry(1)
        term(0)


def scatter_kernel(rows_ref, columns_ref, mine_ref, other_ref, tile_ref, below_ref, right_ref, own_ref):
    width = tile_ref.shape[1]
    half = width // 2
    strips = []
    for place, ref in enumerate((mine_ref, other_ref)):
        field = jnp.concatenate([ref[:width, :], ref[width:, :]], axis=1)
        strips.append(dot(rows_ref[place], field).astype(jnp.bfloat16))
    for part in range(2):
        strip = jnp.concatenate([strip[:, part * width : (part + 1) * width] for strip in strips], axis=1)
        total = dot(strip, columns_ref[...])
        tile_ref[part] = total[half:, half:]
        below_ref[part] = total[half:, :half].astype(jnp.bfloat16)
        right_ref[part] = total[:half, half:].astype(jnp.bfloat16)
        own_ref[part] = total[:half, :half].astype(jnp.bfloat16)


def total_kernel(tile_ref, below_ref, right_ref, own_ref, out_ref):
    half = right_ref.shape[1]
    below = below_ref[...].astype(jnp.float32)
    right = right_ref[...].astype(jnp.float32)
    own = own_ref[...].astype(jnp.float32)
    out_ref[0, :, :half, :half] = tile_ref[:, :half, :half]
    out_ref[0, :, :half, half:] = tile_ref[:, :half, half:] + below[:, :half]
    out_ref[0, :, half:, :half] = tile_ref[:, half:, :half] + right[:, :, :half]
    out_ref[0, :, half:, half:] = tile_ref[:, half:, half:] + below[:, half:] + right[:, :, half:] + own


VMEM = pl.BlockSpec(memory_space=pltpu.VMEM)
SMEM = pl.BlockSpec(memory_space=pltpu.SMEM)
PARAMS = pltpu.CompilerParams(vmem_limit_bytes=48 * 1024 * 1024)


def shaped(*shape, dtype=jnp.bfloat16):
    return jax.ShapeDtypeStruct(shape, dtype)


def kernel(body, name, in_specs, out_shape, scratch=()):
    return pl.pallas_call(
        body, in_specs=in_specs, out_specs=[VMEM] * len(out_shape), out_shape=out_shape, scratch_shapes=scratch, compiler_params=PARAMS, name=name
    )


def local(object_slices, probe, fresnel_taps, offsets, counts, measured):
    width = probe.shape[1]
    half = width // 2
    wide = width + half
    full = shaped(2 * width, width)
    part = shaped(width, width)
    row_tiles = max(lax.axis_size("tile") // 16, 2)
    probe = probe.reshape(2 * width, width)
    fourier = jnp.asarray(fourier_matrix(width), jnp.bfloat16)

    far_tile = crossed(object_slices[0], "cuts", 2)
    tile, below, right = kernel(cut_kernel, "cut", [VMEM], [shaped(2, width, width), shaped(2, width, half), shaped(2, half, width)])(
        object_slices[0]
    )
    (own,) = kernel(seal_kernel, "seal", [VMEM, VMEM], [shaped(2, half + 16, half)])(tile, offsets)
    below = passed_along(below, "tile", 1)
    right = passed_along(right, "tile", row_tiles)
    own = passed_along(own, "tile", row_tiles + 1)
    below, far_tile = lax.optimization_barrier((below, far_tile))
    far_below = crossed(below, "cuts", 2)
    far_right = crossed(right, "cuts", 2)
    far_own = crossed(own, "cuts", 2)
    level = shaped(half + 16, width)
    band, level = kernel(band_kernel, "band", [SMEM, VMEM, VMEM], [shaped(4, width, width), level])(counts, fresnel_taps, measured)
    level, right = lax.optimization_barrier((level, right))
    level = passed_along(level, "tile", row_tiles + 1)
    rows, columns, rows_back, columns_back = kernel(
        window_kernel,
        "window",
        [VMEM],
        [part, shaped(2, wide, width), shaped(2, wide, width), shaped(2 * width, wide)],
    )(own)
    first, second = kernel(extract_kernel, "near", [VMEM] * 6, [full, full])(rows, columns, tile, below, right, own)
    swapped = crossed(second, "cuts", 1)
    far_level = crossed(level, "cuts", 2)
    straight, far_second = kernel(extract_kernel, "far", [VMEM] * 6, [full, full])(rows, columns, far_tile, far_below, far_right, far_own)
    far_second, far_level = lax.optimization_barrier((far_second, far_level))
    diagonal = crossed(far_second, "cuts", 1)
    (head,) = kernel(head_kernel, "head", [VMEM] * 4, [shaped(3, 2 * width, width)], [pltpu.VMEM((2, 2 * width, width), jnp.bfloat16)])(
        probe, band, first, swapped
    )
    mine, other = kernel(
        chain_kernel,
        "chain",
        [VMEM] * 10,
        [full, full],
        [
            pltpu.VMEM((4, 2 * width, width), jnp.bfloat16),
            pltpu.VMEM((4, 2 * width, width), jnp.bfloat16),
            pltpu.VMEM((2 * width, width), jnp.bfloat16),
        ],
    )(probe, first, swapped, straight, diagonal, level, far_level, band, fourier, head)
    other = crossed(other, "cuts", 1)
    total, below, right, own = kernel(
        scatter_kernel,
        "scatter",
        [VMEM] * 4,
        [shaped(2, width, width, dtype=jnp.float32), shaped(2, width, half), shaped(2, half, width), shaped(2, half, half)],
    )(rows_back, columns_back, mine, other)
    below = passed_along(below, "tile", -1)
    right = passed_along(right, "tile", -row_tiles)
    own = passed_along(own, "tile", -row_tiles - 1)
    (out,) = kernel(total_kernel, "total", [VMEM] * 4, [shaped(1, 2, width, width, dtype=jnp.float32)])(total, below, right, own)
    return out


def solution(mesh):
    return jax.shard_map(
        local,
        mesh=mesh,
        in_specs=(
            P("cuts", None, "tile", None),
            P(),
            P(),
            P("tile", None),
            P("tile"),
            P("tile", None, None),
        ),
        out_specs=P("cuts", None, "tile", None),
        check_vma=False,
    )
```

```python
import jax
import jax.numpy as jnp
import numpy as np
from jax import lax
from jax.experimental import pallas as pl
from jax.experimental.pallas import tpu as pltpu
from jax.sharding import PartitionSpec as P


def passed_along(value, axis, steps):
    count = lax.axis_size(axis)
    pairs = [(source, (source + steps) % count) for source in range(count)]
    return lax.ppermute(value, axis, pairs)


def crossed(value, axis, mask):
    pairs = [(source, source ^ mask) for source in range(lax.axis_size(axis))]
    return lax.ppermute(value, axis, pairs)


def fourier_matrix(width):
    index = np.arange(width)
    angle = 2.0 * np.pi * (index[:, None] * index[None, :] % width) / width
    return np.stack([np.cos(angle), -np.sin(angle)]) / np.sqrt(width)


def dot(left, right):
    return jnp.dot(left, right, preferred_element_type=jnp.float32)


def left_product(real, imag, field):
    top = jnp.concatenate([real, -imag], axis=1)
    bottom = jnp.concatenate([imag, real], axis=1)
    return dot(jnp.concatenate([top, bottom], axis=0), field)


def right_product(field, real, imag):
    width = real.shape[0]
    turned = jnp.concatenate([-field[width:], field[:width]], axis=0)
    return dot(jnp.concatenate([field, turned], axis=1), jnp.concatenate([real, imag], axis=0))


def sandwich(left_real, left_imag, field, right_real, right_imag):
    inner = left_product(left_real, left_imag, field).astype(jnp.bfloat16)
    return right_product(inner, right_real, right_imag)


def complex_mul(first, second, sign):
    width = first.shape[1]
    fr = first[:width].astype(jnp.float32)
    fi = first[width:].astype(jnp.float32) * sign
    sr = second[:width].astype(jnp.float32)
    si = second[width:].astype(jnp.float32)
    return jnp.concatenate([fr * sr - fi * si, fr * si + fi * sr], axis=0)


def band_kernel(counts_ref, taps_ref, measured_ref, band_ref, level_ref):
    width = band_ref.shape[1]
    half = taps_ref.shape[1] // 2
    core = lax.rem(lax.axis_index("cuts"), 2)
    rows = width // 2
    first = pl.multiple_of(lax.axis_index("cuts") // 2 * rows, rows)
    level_ref[:rows, :] = measured_ref[core, pl.ds(first, rows), :].astype(jnp.bfloat16)
    live = (core < counts_ref[0]).astype(jnp.float32)
    level_ref[rows:, :] = jnp.full((level_ref.shape[0] - rows, width), live, jnp.float32).astype(jnp.bfloat16)
    rows = lax.broadcasted_iota(jnp.int32, (width, width), 0)
    columns = lax.broadcasted_iota(jnp.int32, (width, width), 1)
    inside = jnp.abs(columns - rows) <= half
    for part in range(2):
        line = taps_ref[part : part + 1, :].astype(jnp.float32)
        filler = jnp.zeros((1, width - line.shape[1]), jnp.float32)
        line = jnp.concatenate([line, filler], axis=1)
        spread = jnp.broadcast_to(line, (width, width))
        turned = pltpu.roll(spread, width - half, 1, stride=1, stride_axis=0)
        band = jnp.where(inside, turned, 0.0)
        band_ref[part] = band.astype(jnp.bfloat16)
        band_ref[part + 2] = band.T.astype(jnp.bfloat16)


def cut_kernel(tile_ref, whole_ref, below_ref, right_ref):
    half = right_ref.shape[1]
    whole_ref[...] = tile_ref[...]
    below_ref[...] = tile_ref[:, :, half:]
    right_ref[...] = tile_ref[:, half:, :]


def seal_kernel(tile_ref, offsets_ref, own_ref):
    half = tile_ref.shape[1] // 2
    own_ref[:, :half, :] = tile_ref[:, half:, half:]
    shape = (own_ref.shape[1] - half, half)
    line = lax.broadcasted_iota(jnp.int32, shape, 0)
    lines = jnp.zeros(shape, jnp.float32)
    for index in range(4):
        value = offsets_ref[index // 2 : index // 2 + 1, index % 2 : index % 2 + 1].astype(jnp.float32)
        lines = jnp.where(line == index, value, lines)
    for part in range(2):
        own_ref[part, half:, :] = lines.astype(jnp.bfloat16)


def window_kernel(own_ref, rows_ref, columns_ref, rows_back_ref, columns_back_ref):
    half = own_ref.shape[2]
    width = 2 * half
    core = lax.rem(lax.axis_index("cuts"), 2)
    lines = own_ref[0, half:, :].astype(jnp.float32).astype(jnp.int32) - half

    def placed(shape, axis, shift):
        i = lax.broadcasted_iota(jnp.int32, shape, axis)
        j = lax.broadcasted_iota(jnp.int32, shape, 1 - axis)
        shift = jnp.concatenate([shift] * (shape[1] // half), axis=1)
        return jnp.where(j - i == shift, 1.0, 0.0).astype(jnp.bfloat16)

    for place in range(2):
        second = core != place
        row = jnp.where(second, lines[2:3], lines[0:1])
        column = jnp.where(second, lines[3:4], lines[1:2])
        rows_ref[place * half : (place + 1) * half, :] = placed((half, width), 0, row)
        columns_ref[place] = placed((width + half, width), 1, column)
        rows_back_ref[place] = placed((width + half, width), 1, row)
        columns_back_ref[place * width : (place + 1) * width, :] = placed((width, width + half), 0, column)


def extract_kernel(rows_ref, columns_ref, tile_ref, below_ref, right_ref, own_ref, first_ref, second_ref):
    width = tile_ref.shape[1]
    half = width // 2
    wide = width + half
    blocks = []
    for part in range(2):
        upper = jnp.concatenate([own_ref[part, :half], right_ref[part]], axis=1)
        lower = jnp.concatenate([below_ref[part], tile_ref[part]], axis=1)
        blocks.append(jnp.concatenate([upper, lower], axis=0))
    block = jnp.concatenate(blocks, axis=1)
    strips = [dot(rows_ref[...], block[top : top + width]).astype(jnp.bfloat16) for top in (0, half)]
    for place, out_ref in enumerate((first_ref, second_ref)):
        mine = [strip[place * half : (place + 1) * half, part * wide : (part + 1) * wide] for part in range(2) for strip in strips]
        out_ref[...] = dot(jnp.concatenate(mine, axis=0), columns_ref[place]).astype(jnp.bfloat16)


def ordered(first_ref, second_ref):
    odd = lax.rem(lax.axis_index("cuts"), 2) == 1
    first, second = first_ref[...], second_ref[...]
    return jnp.where(odd, second, first), jnp.where(odd, first, second)


def near_chip():
    return lax.axis_index("cuts") < 2


def spread_on(spread, patch, band_ref):
    wave = complex_mul(spread, patch, 1.0).astype(jnp.bfloat16)
    return sandwich(band_ref[0], band_ref[1], wave, band_ref[2], band_ref[3]).astype(jnp.bfloat16)


def back_on(back, patch, band_ref):
    carried = complex_mul(patch, back, -1.0).astype(jnp.bfloat16)
    return sandwich(band_ref[2], -band_ref[3], carried, band_ref[0], -band_ref[1]).astype(jnp.bfloat16)


def head_kernel(probe_ref, band_ref, p0_ref, p1_ref, one_ref, two_ref):
    @pl.when(near_chip())
    def _():
        patch_0, patch_1 = ordered(p0_ref, p1_ref)
        one_ref[...] = spread_on(probe_ref[...], patch_0, band_ref)
        two_ref[...] = spread_on(one_ref[...], patch_1, band_ref)


def forward_kernel(
    probe_ref, p0_ref, p1_ref, p2_ref, p3_ref, band_ref, fourier_ref, one_ref, two_ref, far_ref, keep_two_ref, keep_three_ref, wave_ref
):
    @pl.when(near_chip())
    def _():
        patch_2, patch_3 = ordered(p2_ref, p3_ref)
        spread = spread_on(two_ref[...], patch_2, band_ref)
        wave_ref[...] = complex_mul(spread, patch_3, 1.0).astype(jnp.bfloat16)

    @pl.when(jnp.logical_not(near_chip()))
    def _():
        patch_0, patch_1 = ordered(p2_ref, p3_ref)
        patch_2, patch_3 = ordered(p0_ref, p1_ref)
        spread = spread_on(probe_ref[...], patch_0, band_ref)
        keep_two_ref[...] = spread_on(spread, patch_1, band_ref)
        keep_three_ref[...] = spread_on(keep_two_ref[...], patch_2, band_ref)
        wave_ref[...] = complex_mul(keep_three_ref[...], patch_3, 1.0).astype(jnp.bfloat16)

    far_ref[...] = sandwich(fourier_ref[0], fourier_ref[1], wave_ref[...], fourier_ref[0], fourier_ref[1])


def backward_kernel(
    probe_ref, p0_ref, p1_ref, p2_ref, p3_ref, band_ref, fourier_ref, one_ref, far_ref, keep_two_ref, keep_three_ref, level_ref, far_level_ref,
    mine_ref, other_ref, back_ref
):
    width = probe_ref.shape[1]
    far_r, far_i = far_ref[:width, :], far_ref[width:, :]
    rows = width // 2
    level, far_level = level_ref[:rows, :].astype(jnp.float32), far_level_ref[:rows, :].astype(jnp.float32)
    level = jnp.concatenate([jnp.where(near_chip(), level, far_level), jnp.where(near_chip(), far_level, level)], axis=0)
    live = level_ref[rows : rows + 1, :].astype(jnp.float32)
    excess = 2.0 * live * (far_r * far_r + far_i * far_i - level)
    residual = jnp.concatenate([excess * far_r, excess * far_i], axis=0).astype(jnp.bfloat16)
    fourier_r, fourier_i = fourier_ref[0], fourier_ref[1]
    back_ref[...] = sandwich(fourier_r, -fourier_i, residual, fourier_r, -fourier_i).astype(jnp.bfloat16)
    odd = lax.rem(lax.axis_index("cuts"), 2) == 1

    def out(low, high):
        mine_ref[...] = jnp.where(odd, high, low)
        other_ref[...] = jnp.where(odd, low, high)

    @pl.when(near_chip())
    def _():
        _, patch_1 = ordered(p0_ref, p1_ref)
        patch_2, patch_3 = ordered(p2_ref, p3_ref)
        back = back_on(back_ref[...], patch_3, band_ref)
        back = back_on(back, patch_2, band_ref)
        high = complex_mul(one_ref[...], back, -1.0).astype(jnp.bfloat16)
        back = back_on(back, patch_1, band_ref)
        out(complex_mul(probe_ref[...], back, -1.0).astype(jnp.bfloat16), high)

    @pl.when(jnp.logical_not(near_chip()))
    def _():
        _, patch_3 = ordered(p0_ref, p1_ref)
        back = back_ref[...]
        high = complex_mul(keep_three_ref[...], back, -1.0).astype(jnp.bfloat16)
        back = back_on(back, patch_3, band_ref)
        out(complex_mul(keep_two_ref[...], back, -1.0).astype(jnp.bfloat16), high)


def scatter_kernel(rows_ref, columns_ref, mine_ref, other_ref, tile_ref, below_ref, right_ref, own_ref):
    width = tile_ref.shape[1]
    half = width // 2
    strips = []
    for place, ref in enumerate((mine_ref, other_ref)):
        field = jnp.concatenate([ref[:width, :], ref[width:, :]], axis=1)
        strips.append(dot(rows_ref[place], field).astype(jnp.bfloat16))
    for part in range(2):
        strip = jnp.concatenate([strip[:, part * width : (part + 1) * width] for strip in strips], axis=1)
        total = dot(strip, columns_ref[...])
        tile_ref[part] = total[half:, half:]
        below_ref[part] = total[half:, :half].astype(jnp.bfloat16)
        right_ref[part] = total[:half, half:].astype(jnp.bfloat16)
        own_ref[part] = total[:half, :half].astype(jnp.bfloat16)


def total_kernel(tile_ref, below_ref, right_ref, own_ref, out_ref):
    half = right_ref.shape[1]
    below = below_ref[...].astype(jnp.float32)
    right = right_ref[...].astype(jnp.float32)
    own = own_ref[...].astype(jnp.float32)
    out_ref[0, :, :half, :half] = tile_ref[:, :half, :half]
    out_ref[0, :, :half, half:] = tile_ref[:, :half, half:] + below[:, :half]
    out_ref[0, :, half:, :half] = tile_ref[:, half:, :half] + right[:, :, :half]
    out_ref[0, :, half:, half:] = tile_ref[:, half:, half:] + below[:, half:] + right[:, :, half:] + own


VMEM = pl.BlockSpec(memory_space=pltpu.VMEM)
SMEM = pl.BlockSpec(memory_space=pltpu.SMEM)
PARAMS = pltpu.CompilerParams(vmem_limit_bytes=48 * 1024 * 1024)


def shaped(*shape, dtype=jnp.bfloat16):
    return jax.ShapeDtypeStruct(shape, dtype)


def kernel(body, name, in_specs, out_shape, scratch=()):
    return pl.pallas_call(
        body, in_specs=in_specs, out_specs=[VMEM] * len(out_shape), out_shape=out_shape, scratch_shapes=scratch, compiler_params=PARAMS, name=name
    )


def local(object_slices, probe, fresnel_taps, offsets, counts, measured):
    width = probe.shape[1]
    half = width // 2
    wide = width + half
    full = shaped(2 * width, width)
    part = shaped(width, width)
    row_tiles = max(lax.axis_size("tile") // 16, 2)
    probe = probe.reshape(2 * width, width)
    fourier = jnp.asarray(fourier_matrix(width), jnp.bfloat16)

    far_tile = crossed(object_slices[0], "cuts", 2)
    tile, below, right = kernel(cut_kernel, "cut", [VMEM], [shaped(2, width, width), shaped(2, width, half), shaped(2, half, width)])(
        object_slices[0]
    )
    (own,) = kernel(seal_kernel, "seal", [VMEM, VMEM], [shaped(2, half + 16, half)])(tile, offsets)
    below = passed_along(below, "tile", 1)
    right = passed_along(right, "tile", row_tiles)
    own = passed_along(own, "tile", row_tiles + 1)
    below, far_tile = lax.optimization_barrier((below, far_tile))
    far_below = crossed(below, "cuts", 2)
    far_right = crossed(right, "cuts", 2)
    far_own = crossed(own, "cuts", 2)
    level = shaped(half + 16, width)
    band, level = kernel(band_kernel, "band", [SMEM, VMEM, VMEM], [shaped(4, width, width), level])(counts, fresnel_taps, measured)
    level, own = lax.optimization_barrier((level, own))
    level = passed_along(level, "tile", row_tiles + 1)
    rows, columns, rows_back, columns_back = kernel(
        window_kernel,
        "window",
        [VMEM],
        [part, shaped(2, wide, width), shaped(2, wide, width), shaped(2 * width, wide)],
    )(own)
    first, second = kernel(extract_kernel, "near", [VMEM] * 6, [full, full])(rows, columns, tile, below, right, own)
    swapped = crossed(second, "cuts", 1)
    far_own, level = lax.optimization_barrier((far_own, level))
    straight, far_second = kernel(extract_kernel, "far", [VMEM] * 6, [full, full])(rows, columns, far_tile, far_below, far_right, far_own)
    diagonal = crossed(far_second, "cuts", 1)
    far_level = crossed(level, "cuts", 2)
    one, two = kernel(head_kernel, "head", [VMEM] * 4, [full, full])(probe, band, first, swapped)
    patches = first, swapped, straight, diagonal
    wave = shaped(2 * width, width, dtype=jnp.float32)
    farfield, keep_two, keep_three = kernel(
        forward_kernel, "forward", [VMEM] * 9, [wave, full, full], [pltpu.VMEM((2 * width, width), jnp.bfloat16)]
    )(probe, *patches, band, fourier, one, two)
    mine, other = kernel(backward_kernel, "backward", [VMEM] * 13, [full, full], [pltpu.VMEM((2 * width, width), jnp.bfloat16)])(
        probe, *patches, band, fourier, one, farfield, keep_two, keep_three, level, far_level
    )
    other = crossed(other, "cuts", 1)
    total, below, right, own = kernel(
        scatter_kernel,
        "scatter",
        [VMEM] * 4,
        [shaped(2, width, width, dtype=jnp.float32), shaped(2, width, half), shaped(2, half, width), shaped(2, half, half)],
    )(rows_back, columns_back, mine, other)
    below = passed_along(below, "tile", -1)
    right = passed_along(right, "tile", -row_tiles)
    own = passed_along(own, "tile", -row_tiles - 1)
    (out,) = kernel(total_kernel, "total", [VMEM] * 4, [shaped(1, 2, width, width, dtype=jnp.float32)])(total, below, right, own)
    return out


def solution(mesh):
    return jax.shard_map(
        local,
        mesh=mesh,
        in_specs=(
            P("cuts", None, "tile", None),
            P(),
            P(),
            P("tile", None),
            P("tile"),
            P("tile", None, None),
        ),
        out_specs=P("cuts", None, "tile", None),
        check_vma=False,
    )
```

```python
import jax
import jax.numpy as jnp
import numpy as np
from jax import lax
from jax.experimental import pallas as pl
from jax.experimental.pallas import tpu as pltpu
from jax.sharding import PartitionSpec as P


NOTES = 16


def passed_along(value, axis, steps):
    count = lax.axis_size(axis)
    pairs = [(source, (source + steps) % count) for source in range(count)]
    return lax.ppermute(value, axis, pairs)


def crossed(value, axis, mask):
    pairs = [(source, source ^ mask) for source in range(lax.axis_size(axis))]
    return lax.ppermute(value, axis, pairs)


def fourier_matrix(width):
    index = np.arange(width)
    angle = 2.0 * np.pi * (index[:, None] * index[None, :] % width) / width
    return np.stack([np.cos(angle), -np.sin(angle)]) / np.sqrt(width)


def dot(left, right):
    return jnp.dot(left, right, preferred_element_type=jnp.float32)


def left_product(real, imag, field):
    top = jnp.concatenate([real, -imag], axis=1)
    bottom = jnp.concatenate([imag, real], axis=1)
    return dot(jnp.concatenate([top, bottom], axis=0), field)


def right_product(field, real, imag):
    width = real.shape[0]
    turned = jnp.concatenate([-field[width:], field[:width]], axis=0)
    return dot(jnp.concatenate([field, turned], axis=1), jnp.concatenate([real, imag], axis=0))


def sandwich(left_real, left_imag, field, right_real, right_imag):
    inner = left_product(left_real, left_imag, field).astype(jnp.bfloat16)
    return right_product(inner, right_real, right_imag)


def complex_mul(first, second, sign):
    width = first.shape[1]
    fr = first[:width].astype(jnp.float32)
    fi = first[width:].astype(jnp.float32) * sign
    sr = second[:width].astype(jnp.float32)
    si = second[width:].astype(jnp.float32)
    return jnp.concatenate([fr * sr - fi * si, fr * si + fi * sr], axis=0)


def band_kernel(taps_ref, band_ref):
    width = band_ref.shape[1]
    half = taps_ref.shape[1] // 2
    rows = lax.broadcasted_iota(jnp.int32, (width, width), 0)
    columns = lax.broadcasted_iota(jnp.int32, (width, width), 1)
    inside = jnp.abs(columns - rows) <= half
    for part in range(2):
        line = taps_ref[part : part + 1, :].astype(jnp.float32)
        filler = jnp.zeros((1, width - line.shape[1]), jnp.float32)
        line = jnp.concatenate([line, filler], axis=1)
        spread = jnp.broadcast_to(line, (width, width))
        turned = pltpu.roll(spread, width - half, 1, stride=1, stride_axis=0)
        band = jnp.where(inside, turned, 0.0)
        band_ref[part] = band.astype(jnp.bfloat16)
        band_ref[part + 2] = band.T.astype(jnp.bfloat16)


def cut_kernel(tile_ref, whole_ref, below_ref, right_ref):
    half = right_ref.shape[1]
    whole_ref[...] = tile_ref[...]
    below_ref[...] = tile_ref[:, :, half:]
    right_ref[...] = tile_ref[:, half:, :]


def seal_kernel(tile_ref, offsets_ref, counts_ref, measured_ref, own_ref):
    half = tile_ref.shape[1] // 2
    own_ref[:, :half, :] = tile_ref[:, half:, half:]
    cut = lax.axis_index("cuts")
    core = lax.rem(cut, 2)
    shape = (NOTES, half)
    line = lax.broadcasted_iota(jnp.int32, shape, 0)
    lines = jnp.where(core < counts_ref[0], jnp.ones(shape, jnp.float32), 0.0)
    for index in range(4):
        value = offsets_ref[index // 2 : index // 2 + 1, index % 2 : index % 2 + 1].astype(jnp.float32)
        lines = jnp.where(line == index, value, lines)
    level = measured_ref[core, pl.ds(pl.multiple_of(cut // 2 * half, half), half), :].astype(jnp.bfloat16)
    for part in range(2):
        own_ref[part, half : half + NOTES, :] = lines.astype(jnp.bfloat16)
        own_ref[part, half + NOTES :, :] = level[:, part * half : (part + 1) * half]


def window_kernel(own_ref, quarter_ref, level_ref, rows_ref, columns_ref, rows_back_ref, columns_back_ref):
    half = own_ref.shape[2]
    width = 2 * half
    core = lax.rem(lax.axis_index("cuts"), 2)
    quarter_ref[...] = own_ref[:, : half + NOTES, :]
    for part in range(2):
        level_ref[:, part * half : (part + 1) * half] = own_ref[part, half + NOTES :, :]
    lines = own_ref[0, half : half + NOTES, :].astype(jnp.float32).astype(jnp.int32) - half

    def placed(shape, axis, shift):
        i = lax.broadcasted_iota(jnp.int32, shape, axis)
        j = lax.broadcasted_iota(jnp.int32, shape, 1 - axis)
        shift = jnp.concatenate([shift] * (shape[1] // half), axis=1)
        return jnp.where(j - i == shift, 1.0, 0.0).astype(jnp.bfloat16)

    for place in range(2):
        second = core != place
        row = jnp.where(second, lines[2:3], lines[0:1])
        column = jnp.where(second, lines[3:4], lines[1:2])
        rows_ref[place * half : (place + 1) * half, :] = placed((half, width), 0, row)
        columns_ref[place] = placed((width + half, width), 1, column)
        rows_back_ref[place] = placed((width + half, width), 1, row)
        columns_back_ref[place * width : (place + 1) * width, :] = placed((width, width + half), 0, column)


def extract_kernel(rows_ref, columns_ref, tile_ref, below_ref, right_ref, own_ref, first_ref, second_ref):
    width = tile_ref.shape[1]
    half = width // 2
    wide = width + half
    blocks = []
    for part in range(2):
        upper = jnp.concatenate([own_ref[part, :half], right_ref[part]], axis=1)
        lower = jnp.concatenate([below_ref[part], tile_ref[part]], axis=1)
        blocks.append(jnp.concatenate([upper, lower], axis=0))
    block = jnp.concatenate(blocks, axis=1)
    strips = [dot(rows_ref[...], block[top : top + width]).astype(jnp.bfloat16) for top in (0, half)]
    for place, out_ref in enumerate((first_ref, second_ref)):
        mine = [strip[place * half : (place + 1) * half, part * wide : (part + 1) * wide] for part in range(2) for strip in strips]
        out_ref[...] = dot(jnp.concatenate(mine, axis=0), columns_ref[place]).astype(jnp.bfloat16)


def forward(probe_ref, band_ref, patch_ref, spread_ref, first, last):
    for level in range(first, last + 1):
        if level == 0:
            spread_ref[0] = probe_ref[...]
        else:
            wave = complex_mul(spread_ref[level - 1], patch_ref[level - 1], 1.0).astype(jnp.bfloat16)
            spread = sandwich(band_ref[0], band_ref[1], wave, band_ref[2], band_ref[3])
            spread_ref[level] = spread.astype(jnp.bfloat16)


def head_kernel(probe_ref, band_ref, p0_ref, p1_ref, spread_ref, patch_ref):
    cut = lax.axis_index("cuts")

    @pl.when(cut < 2)
    def _():
        patch_ref[cut] = p0_ref[...]
        patch_ref[1 - cut] = p1_ref[...]
        forward(probe_ref, band_ref, patch_ref, spread_ref, 0, 2)


def chain_kernel(
    probe_ref, p0_ref, p1_ref, p2_ref, p3_ref, own_ref, level_ref, far_level_ref, band_ref, fourier_ref, head_ref, mine_ref, other_ref, patch_ref, spread_ref, back_ref
):
    width = probe_ref.shape[1]
    cut = lax.axis_index("cuts")
    for mask, ref in enumerate((p0_ref, p1_ref, p2_ref, p3_ref)):
        patch_ref[lax.bitwise_xor(cut, mask)] = ref[...]

    @pl.when(cut < 2)
    def _():
        spread_ref[0:3] = head_ref[...]

    @pl.when(cut >= 2)
    def _():
        forward(probe_ref, band_ref, patch_ref, spread_ref, 0, 2)

    forward(probe_ref, band_ref, patch_ref, spread_ref, 3, 3)
    fourier_r, fourier_i = fourier_ref[0], fourier_ref[1]
    wave = complex_mul(spread_ref[3], patch_ref[3], 1.0).astype(jnp.bfloat16)
    far = sandwich(fourier_r, fourier_i, wave, fourier_r, fourier_i)
    far_r, far_i = far[:width], far[width:]
    level, far_level = level_ref[...].astype(jnp.float32), far_level_ref[...].astype(jnp.float32)
    level = jnp.concatenate([jnp.where(cut < 2, level, far_level), jnp.where(cut < 2, far_level, level)], axis=0)
    half = width // 2
    live = jnp.concatenate([own_ref[0, half + 4 : half + 5, :]] * 2, axis=1).astype(jnp.float32)
    excess = 2.0 * live * (far_r * far_r + far_i * far_i - level)
    residual = jnp.concatenate([excess * far_r, excess * far_i], axis=0).astype(jnp.bfloat16)
    back_ref[...] = sandwich(fourier_r, -fourier_i, residual, fourier_r, -fourier_i).astype(jnp.bfloat16)

    def term(level):
        value = complex_mul(spread_ref[level], back_ref[...], -1.0).astype(jnp.bfloat16)

        @pl.when(level == cut)
        def _():
            mine_ref[...] = value

        @pl.when(level != cut)
        def _():
            other_ref[...] = value

    def carry(level):
        carried = complex_mul(patch_ref[level], back_ref[...], -1.0).astype(jnp.bfloat16)
        back = sandwich(band_ref[2], -band_ref[3], carried, band_ref[0], -band_ref[1])
        back_ref[...] = back.astype(jnp.bfloat16)

    @pl.when(cut >= 2)
    def _():
        term(3)

    carry(3)

    @pl.when(cut >= 2)
    def _():
        term(2)

    @pl.when(cut < 2)
    def _():
        carry(2)
        term(1)
        carry(1)
        term(0)


def scatter_kernel(rows_ref, columns_ref, mine_ref, other_ref, tile_ref, below_ref, right_ref, own_ref):
    width = tile_ref.shape[1]
    half = width // 2
    strips = []
    for place, ref in enumerate((mine_ref, other_ref)):
        field = jnp.concatenate([ref[:width, :], ref[width:, :]], axis=1)
        strips.append(dot(rows_ref[place], field).astype(jnp.bfloat16))
    for part in range(2):
        strip = jnp.concatenate([strip[:, part * width : (part + 1) * width] for strip in strips], axis=1)
        total = dot(strip, columns_ref[...])
        tile_ref[part] = total[half:, half:]
        below_ref[part] = total[half:, :half].astype(jnp.bfloat16)
        right_ref[part] = total[:half, half:].astype(jnp.bfloat16)
        own_ref[part] = total[:half, :half].astype(jnp.bfloat16)


def total_kernel(tile_ref, below_ref, right_ref, own_ref, out_ref):
    half = right_ref.shape[1]
    below = below_ref[...].astype(jnp.float32)
    right = right_ref[...].astype(jnp.float32)
    own = own_ref[...].astype(jnp.float32)
    out_ref[0, :, :half, :half] = tile_ref[:, :half, :half]
    out_ref[0, :, :half, half:] = tile_ref[:, :half, half:] + below[:, :half]
    out_ref[0, :, half:, :half] = tile_ref[:, half:, :half] + right[:, :, :half]
    out_ref[0, :, half:, half:] = tile_ref[:, half:, half:] + below[:, half:] + right[:, :, half:] + own


VMEM = pl.BlockSpec(memory_space=pltpu.VMEM)
SMEM = pl.BlockSpec(memory_space=pltpu.SMEM)
PARAMS = pltpu.CompilerParams(vmem_limit_bytes=48 * 1024 * 1024)


def shaped(*shape, dtype=jnp.bfloat16):
    return jax.ShapeDtypeStruct(shape, dtype)


def kernel(body, name, in_specs, out_shape, scratch=()):
    return pl.pallas_call(
        body, in_specs=in_specs, out_specs=[VMEM] * len(out_shape), out_shape=out_shape, scratch_shapes=scratch, compiler_params=PARAMS, name=name
    )


def local(object_slices, probe, fresnel_taps, offsets, counts, measured):
    width = probe.shape[1]
    half = width // 2
    wide = width + half
    full = shaped(2 * width, width)
    part = shaped(width, width)
    row_tiles = max(lax.axis_size("tile") // 16, 2)
    probe = probe.reshape(2 * width, width)
    fourier = jnp.asarray(fourier_matrix(width), jnp.bfloat16)

    far_tile = crossed(object_slices[0], "cuts", 2)
    tile, below, right = kernel(cut_kernel, "cut", [VMEM], [shaped(2, width, width), shaped(2, width, half), shaped(2, half, width)])(
        object_slices[0]
    )
    (own,) = kernel(seal_kernel, "seal", [VMEM, VMEM, SMEM, VMEM], [shaped(2, width + NOTES, half)])(tile, offsets, counts, measured)
    below = passed_along(below, "tile", 1)
    right = passed_along(right, "tile", row_tiles)
    own = passed_along(own, "tile", row_tiles + 1)
    below, far_tile = lax.optimization_barrier((below, far_tile))
    far_below = crossed(below, "cuts", 2)
    far_right = crossed(right, "cuts", 2)
    (band,) = kernel(band_kernel, "band", [VMEM], [shaped(4, width, width)])(fresnel_taps)
    own, level, rows, columns, rows_back, columns_back = kernel(
        window_kernel,
        "window",
        [VMEM],
        [
            shaped(2, half + NOTES, half),
            shaped(half, width),
            part,
            shaped(2, wide, width),
            shaped(2, wide, width),
            shaped(2 * width, wide),
        ],
    )(own)
    far_own = crossed(own, "cuts", 2)
    first, second = kernel(extract_kernel, "near", [VMEM] * 6, [full, full])(rows, columns, tile, below, right, own)
    swapped = crossed(second, "cuts", 1)
    far_level = crossed(level, "cuts", 2)
    straight, far_second = kernel(extract_kernel, "far", [VMEM] * 6, [full, full])(rows, columns, far_tile, far_below, far_right, far_own)
    far_second, far_level = lax.optimization_barrier((far_second, far_level))
    diagonal = crossed(far_second, "cuts", 1)
    (head,) = kernel(head_kernel, "head", [VMEM] * 4, [shaped(3, 2 * width, width)], [pltpu.VMEM((2, 2 * width, width), jnp.bfloat16)])(
        probe, band, first, swapped
    )
    mine, other = kernel(
        chain_kernel,
        "chain",
        [VMEM] * 11,
        [full, full],
        [
            pltpu.VMEM((4, 2 * width, width), jnp.bfloat16),
            pltpu.VMEM((4, 2 * width, width), jnp.bfloat16),
            pltpu.VMEM((2 * width, width), jnp.bfloat16),
        ],
    )(probe, first, swapped, straight, diagonal, own, level, far_level, band, fourier, head)
    other = crossed(other, "cuts", 1)
    total, below, right, own = kernel(
        scatter_kernel,
        "scatter",
        [VMEM] * 4,
        [shaped(2, width, width, dtype=jnp.float32), shaped(2, width, half), shaped(2, half, width), shaped(2, half, half)],
    )(rows_back, columns_back, mine, other)
    below = passed_along(below, "tile", -1)
    right = passed_along(right, "tile", -row_tiles)
    own = passed_along(own, "tile", -row_tiles - 1)
    (out,) = kernel(total_kernel, "total", [VMEM] * 4, [shaped(1, 2, width, width, dtype=jnp.float32)])(total, below, right, own)
    return out


def solution(mesh):
    return jax.shard_map(
        local,
        mesh=mesh,
        in_specs=(
            P("cuts", None, "tile", None),
            P(),
            P(),
            P("tile", None),
            P("tile"),
            P("tile", None, None),
        ),
        out_specs=P("cuts", None, "tile", None),
        check_vma=False,
    )
```

```python
import jax
import jax.numpy as jnp
import numpy as np
from jax import lax
from jax.experimental import pallas as pl
from jax.experimental.pallas import tpu as pltpu
from jax.sharding import PartitionSpec as P


def passed_along(value, axis, steps):
    count = lax.axis_size(axis)
    pairs = [(source, (source + steps) % count) for source in range(count)]
    return lax.ppermute(value, axis, pairs)


def crossed(value, axis, mask):
    pairs = [(source, source ^ mask) for source in range(lax.axis_size(axis))]
    return lax.ppermute(value, axis, pairs)


def fourier_matrix(width):
    index = np.arange(width)
    angle = 2.0 * np.pi * (index[:, None] * index[None, :] % width) / width
    return np.stack([np.cos(angle), -np.sin(angle)]) / np.sqrt(width)


def dot(left, right):
    return jnp.dot(left, right, preferred_element_type=jnp.float32)


def left_product(real, imag, field):
    top = jnp.concatenate([real, -imag], axis=1)
    bottom = jnp.concatenate([imag, real], axis=1)
    return dot(jnp.concatenate([top, bottom], axis=0), field)


def right_product(field, real, imag):
    width = real.shape[0]
    turned = jnp.concatenate([-field[width:], field[:width]], axis=0)
    return dot(jnp.concatenate([field, turned], axis=1), jnp.concatenate([real, imag], axis=0))


def sandwich(left_real, left_imag, field, right_real, right_imag):
    inner = left_product(left_real, left_imag, field).astype(jnp.bfloat16)
    return right_product(inner, right_real, right_imag)


def complex_mul(first, second, sign):
    width = first.shape[1]
    fr = first[:width].astype(jnp.float32)
    fi = first[width:].astype(jnp.float32) * sign
    sr = second[:width].astype(jnp.float32)
    si = second[width:].astype(jnp.float32)
    return jnp.concatenate([fr * sr - fi * si, fr * si + fi * sr], axis=0)


def band_kernel(counts_ref, taps_ref, measured_ref, band_ref, level_ref):
    width = band_ref.shape[1]
    half = taps_ref.shape[1] // 2
    core = lax.rem(lax.axis_index("cuts"), 2)
    rows = width // 2
    first = pl.multiple_of(lax.axis_index("cuts") // 2 * rows, rows)
    level_ref[:rows, :] = measured_ref[core, pl.ds(first, rows), :].astype(jnp.bfloat16)
    live = (core < counts_ref[0]).astype(jnp.float32)
    level_ref[rows:, :] = jnp.full((level_ref.shape[0] - rows, width), live, jnp.float32).astype(jnp.bfloat16)
    rows = lax.broadcasted_iota(jnp.int32, (width, width), 0)
    columns = lax.broadcasted_iota(jnp.int32, (width, width), 1)
    inside = jnp.abs(columns - rows) <= half
    for part in range(2):
        line = taps_ref[part : part + 1, :].astype(jnp.float32)
        filler = jnp.zeros((1, width - line.shape[1]), jnp.float32)
        line = jnp.concatenate([line, filler], axis=1)
        spread = jnp.broadcast_to(line, (width, width))
        turned = pltpu.roll(spread, width - half, 1, stride=1, stride_axis=0)
        band = jnp.where(inside, turned, 0.0)
        band_ref[part] = band.astype(jnp.bfloat16)
        band_ref[part + 2] = band.T.astype(jnp.bfloat16)


def cut_kernel(tile_ref, whole_ref, below_ref, right_ref):
    half = right_ref.shape[1]
    whole_ref[...] = tile_ref[...]
    below_ref[...] = tile_ref[:, :, half:]
    right_ref[...] = tile_ref[:, half:, :]


def seal_kernel(tile_ref, offsets_ref, own_ref):
    half = tile_ref.shape[1] // 2
    own_ref[:, :half, :] = tile_ref[:, half:, half:]
    shape = (own_ref.shape[1] - half, half)
    line = lax.broadcasted_iota(jnp.int32, shape, 0)
    lines = jnp.zeros(shape, jnp.float32)
    for index in range(4):
        value = offsets_ref[index // 2 : index // 2 + 1, index % 2 : index % 2 + 1].astype(jnp.float32)
        lines = jnp.where(line == index, value, lines)
    for part in range(2):
        own_ref[part, half:, :] = lines.astype(jnp.bfloat16)


def window_kernel(own_ref, rows_ref, columns_ref, rows_back_ref, columns_back_ref):
    half = own_ref.shape[2]
    width = 2 * half
    core = lax.rem(lax.axis_index("cuts"), 2)
    lines = own_ref[0, half:, :].astype(jnp.float32).astype(jnp.int32) - half

    def placed(shape, axis, shift):
        i = lax.broadcasted_iota(jnp.int32, shape, axis)
        j = lax.broadcasted_iota(jnp.int32, shape, 1 - axis)
        shift = jnp.concatenate([shift] * (shape[1] // half), axis=1)
        return jnp.where(j - i == shift, 1.0, 0.0).astype(jnp.bfloat16)

    for place in range(2):
        second = core != place
        row = jnp.where(second, lines[2:3], lines[0:1])
        column = jnp.where(second, lines[3:4], lines[1:2])
        rows_ref[place * half : (place + 1) * half, :] = placed((half, width), 0, row)
        columns_ref[place] = placed((width + half, width), 1, column)
        rows_back_ref[place] = placed((width + half, width), 1, row)
        columns_back_ref[place * width : (place + 1) * width, :] = placed((width, width + half), 0, column)


def extract_kernel(rows_ref, columns_ref, tile_ref, below_ref, right_ref, own_ref, first_ref, second_ref):
    width = tile_ref.shape[1]
    half = width // 2
    wide = width + half
    blocks = []
    for part in range(2):
        upper = jnp.concatenate([own_ref[part, :half], right_ref[part]], axis=1)
        lower = jnp.concatenate([below_ref[part], tile_ref[part]], axis=1)
        blocks.append(jnp.concatenate([upper, lower], axis=0))
    block = jnp.concatenate(blocks, axis=1)
    strips = [dot(rows_ref[...], block[top : top + width]).astype(jnp.bfloat16) for top in (0, half)]
    for place, out_ref in enumerate((first_ref, second_ref)):
        mine = [strip[place * half : (place + 1) * half, part * wide : (part + 1) * wide] for part in range(2) for strip in strips]
        out_ref[...] = dot(jnp.concatenate(mine, axis=0), columns_ref[place]).astype(jnp.bfloat16)


def forward(probe_ref, band_ref, patch_ref, spread_ref, first, last):
    for level in range(first, last + 1):
        if level == 0:
            spread_ref[0] = probe_ref[...]
        else:
            wave = complex_mul(spread_ref[level - 1], patch_ref[level - 1], 1.0).astype(jnp.bfloat16)
            spread = sandwich(band_ref[0], band_ref[1], wave, band_ref[2], band_ref[3])
            spread_ref[level] = spread.astype(jnp.bfloat16)


def head_kernel(probe_ref, band_ref, p0_ref, p1_ref, spread_ref, patch_ref):
    cut = lax.axis_index("cuts")

    @pl.when(cut < 2)
    def _():
        patch_ref[cut] = p0_ref[...]
        patch_ref[1 - cut] = p1_ref[...]
        forward(probe_ref, band_ref, patch_ref, spread_ref, 0, 2)


def chain_kernel(
    probe_ref, p0_ref, p1_ref, p2_ref, p3_ref, level_ref, far_level_ref, band_ref, fourier_ref, head_ref, mine_ref, other_ref, patch_ref, spread_ref, back_ref
):
    width = probe_ref.shape[1]
    cut = lax.axis_index("cuts")
    for mask, ref in enumerate((p0_ref, p1_ref, p2_ref, p3_ref)):
        patch_ref[lax.bitwise_xor(cut, mask)] = ref[...]

    @pl.when(cut < 2)
    def _():
        spread_ref[0:3] = head_ref[...]

    @pl.when(cut >= 2)
    def _():
        forward(probe_ref, band_ref, patch_ref, spread_ref, 0, 2)

    forward(probe_ref, band_ref, patch_ref, spread_ref, 3, 3)
    fourier_r, fourier_i = fourier_ref[0], fourier_ref[1]
    wave = complex_mul(spread_ref[3], patch_ref[3], 1.0).astype(jnp.bfloat16)
    far = sandwich(fourier_r, fourier_i, wave, fourier_r, fourier_i)
    far_r, far_i = far[:width], far[width:]
    rows = width // 2
    level, far_level = level_ref[:rows, :].astype(jnp.float32), far_level_ref[:rows, :].astype(jnp.float32)
    level = jnp.concatenate([jnp.where(cut < 2, level, far_level), jnp.where(cut < 2, far_level, level)], axis=0)
    live = level_ref[rows : rows + 1, :].astype(jnp.float32)
    excess = 2.0 * live * (far_r * far_r + far_i * far_i - level)
    residual = jnp.concatenate([excess * far_r, excess * far_i], axis=0).astype(jnp.bfloat16)
    back_ref[...] = sandwich(fourier_r, -fourier_i, residual, fourier_r, -fourier_i).astype(jnp.bfloat16)

    def term(level):
        value = complex_mul(spread_ref[level], back_ref[...], -1.0).astype(jnp.bfloat16)

        @pl.when(level == cut)
        def _():
            mine_ref[...] = value

        @pl.when(level != cut)
        def _():
            other_ref[...] = value

    def carry(level):
        carried = complex_mul(patch_ref[level], back_ref[...], -1.0).astype(jnp.bfloat16)
        back = sandwich(band_ref[2], -band_ref[3], carried, band_ref[0], -band_ref[1])
        back_ref[...] = back.astype(jnp.bfloat16)

    @pl.when(cut >= 2)
    def _():
        term(3)

    carry(3)

    @pl.when(cut >= 2)
    def _():
        term(2)

    @pl.when(cut < 2)
    def _():
        carry(2)
        term(1)
        carry(1)
        term(0)


def scatter_kernel(rows_ref, columns_ref, mine_ref, other_ref, tile_ref, below_ref, right_ref, own_ref):
    width = tile_ref.shape[1]
    half = width // 2
    strips = []
    for place, ref in enumerate((mine_ref, other_ref)):
        field = jnp.concatenate([ref[:width, :], ref[width:, :]], axis=1)
        strips.append(dot(rows_ref[place], field).astype(jnp.bfloat16))
    for part in range(2):
        strip = jnp.concatenate([strip[:, part * width : (part + 1) * width] for strip in strips], axis=1)
        total = dot(strip, columns_ref[...])
        tile_ref[part] = total[half:, half:]
        below_ref[part] = total[half:, :half].astype(jnp.bfloat16)
        right_ref[part] = total[:half, half:].astype(jnp.bfloat16)
        own_ref[part] = total[:half, :half].astype(jnp.bfloat16)


def total_kernel(tile_ref, below_ref, right_ref, own_ref, out_ref):
    half = right_ref.shape[1]
    below = below_ref[...].astype(jnp.float32)
    right = right_ref[...].astype(jnp.float32)
    own = own_ref[...].astype(jnp.float32)
    out_ref[0, :, :half, :half] = tile_ref[:, :half, :half]
    out_ref[0, :, :half, half:] = tile_ref[:, :half, half:] + below[:, :half]
    out_ref[0, :, half:, :half] = tile_ref[:, half:, :half] + right[:, :, :half]
    out_ref[0, :, half:, half:] = tile_ref[:, half:, half:] + below[:, half:] + right[:, :, half:] + own


VMEM = pl.BlockSpec(memory_space=pltpu.VMEM)
SMEM = pl.BlockSpec(memory_space=pltpu.SMEM)
PARAMS = pltpu.CompilerParams(vmem_limit_bytes=48 * 1024 * 1024)


def shaped(*shape, dtype=jnp.bfloat16):
    return jax.ShapeDtypeStruct(shape, dtype)


def kernel(body, name, in_specs, out_shape, scratch=()):
    return pl.pallas_call(
        body, in_specs=in_specs, out_specs=[VMEM] * len(out_shape), out_shape=out_shape, scratch_shapes=scratch, compiler_params=PARAMS, name=name
    )


def local(object_slices, probe, fresnel_taps, offsets, counts, measured):
    width = probe.shape[1]
    half = width // 2
    wide = width + half
    full = shaped(2 * width, width)
    part = shaped(width, width)
    row_tiles = max(lax.axis_size("tile") // 16, 2)
    probe = probe.reshape(2 * width, width)
    fourier = jnp.asarray(fourier_matrix(width), jnp.bfloat16)

    far_tile = crossed(object_slices[0], "cuts", 2)
    tile, below, right = kernel(cut_kernel, "cut", [VMEM], [shaped(2, width, width), shaped(2, width, half), shaped(2, half, width)])(
        object_slices[0]
    )
    (own,) = kernel(seal_kernel, "seal", [VMEM, VMEM], [shaped(2, half + 16, half)])(tile, offsets)
    below = passed_along(below, "tile", 1)
    right = passed_along(right, "tile", row_tiles)
    own = passed_along(own, "tile", row_tiles + 1)
    below, far_tile = lax.optimization_barrier((below, far_tile))
    far_below = crossed(below, "cuts", 2)
    far_right = crossed(right, "cuts", 2)
    far_own = crossed(own, "cuts", 2)
    level = shaped(half + 16, width)
    band, level = kernel(band_kernel, "band", [SMEM, VMEM, VMEM], [shaped(4, width, width), level])(counts, fresnel_taps, measured)
    level = passed_along(level, "tile", row_tiles + 1)
    far_level = crossed(level, "cuts", 2)
    own, far_level = lax.optimization_barrier((own, far_level))
    rows, columns, rows_back, columns_back = kernel(
        window_kernel,
        "window",
        [VMEM],
        [part, shaped(2, wide, width), shaped(2, wide, width), shaped(2 * width, wide)],
    )(own)
    first, second = kernel(extract_kernel, "near", [VMEM] * 6, [full, full])(rows, columns, tile, below, right, own)
    swapped = crossed(second, "cuts", 1)
    straight, far_second = kernel(extract_kernel, "far", [VMEM] * 6, [full, full])(rows, columns, far_tile, far_below, far_right, far_own)
    diagonal = crossed(far_second, "cuts", 1)
    (head,) = kernel(head_kernel, "head", [VMEM] * 4, [shaped(3, 2 * width, width)], [pltpu.VMEM((2, 2 * width, width), jnp.bfloat16)])(
        probe, band, first, swapped
    )
    mine, other = kernel(
        chain_kernel,
        "chain",
        [VMEM] * 10,
        [full, full],
        [
            pltpu.VMEM((4, 2 * width, width), jnp.bfloat16),
            pltpu.VMEM((4, 2 * width, width), jnp.bfloat16),
            pltpu.VMEM((2 * width, width), jnp.bfloat16),
        ],
    )(probe, first, swapped, straight, diagonal, level, far_level, band, fourier, head)
    other = crossed(other, "cuts", 1)
    total, below, right, own = kernel(
        scatter_kernel,
        "scatter",
        [VMEM] * 4,
        [shaped(2, width, width, dtype=jnp.float32), shaped(2, width, half), shaped(2, half, width), shaped(2, half, half)],
    )(rows_back, columns_back, mine, other)
    below = passed_along(below, "tile", -1)
    right = passed_along(right, "tile", -row_tiles)
    own = passed_along(own, "tile", -row_tiles - 1)
    (out,) = kernel(total_kernel, "total", [VMEM] * 4, [shaped(1, 2, width, width, dtype=jnp.float32)])(total, below, right, own)
    return out


def solution(mesh):
    return jax.shard_map(
        local,
        mesh=mesh,
        in_specs=(
            P("cuts", None, "tile", None),
            P(),
            P(),
            P("tile", None),
            P("tile"),
            P("tile", None, None),
        ),
        out_specs=P("cuts", None, "tile", None),
        check_vma=False,
    )
```

```python
import jax
import jax.numpy as jnp
import numpy as np
from jax import lax
from jax.experimental import pallas as pl
from jax.experimental.pallas import tpu as pltpu
from jax.sharding import PartitionSpec as P


def passed_along(value, axis, steps):
    count = lax.axis_size(axis)
    pairs = [(source, (source + steps) % count) for source in range(count)]
    return lax.ppermute(value, axis, pairs)


def crossed(value, axis, mask):
    pairs = [(source, source ^ mask) for source in range(lax.axis_size(axis))]
    return lax.ppermute(value, axis, pairs)


def fourier_matrix(width):
    index = np.arange(width)
    angle = 2.0 * np.pi * (index[:, None] * index[None, :] % width) / width
    return np.stack([np.cos(angle), -np.sin(angle)]) / np.sqrt(width)


def dot(left, right):
    return jnp.dot(left, right, preferred_element_type=jnp.float32)


def left_product(real, imag, field):
    top = dot(jnp.concatenate([real, -imag], axis=1), field)
    bottom = dot(jnp.concatenate([imag, real], axis=1), field)
    return jnp.concatenate([top, bottom], axis=0)


def right_product(field, real, imag):
    width = real.shape[0]
    field_real, field_imag = field[:width], field[width:]
    right = jnp.concatenate([real, imag], axis=0)
    top = dot(jnp.concatenate([field_real, -field_imag], axis=1), right)
    bottom = dot(jnp.concatenate([field_imag, field_real], axis=1), right)
    return jnp.concatenate([top, bottom], axis=0)


def sandwich(left_real, left_imag, field, right_real, right_imag):
    inner = left_product(left_real, left_imag, field).astype(jnp.bfloat16)
    return right_product(inner, right_real, right_imag)


def complex_mul(first, second, sign):
    width = first.shape[1]
    fr = first[:width].astype(jnp.float32)
    fi = first[width:].astype(jnp.float32) * sign
    sr = second[:width].astype(jnp.float32)
    si = second[width:].astype(jnp.float32)
    return jnp.concatenate([fr * sr - fi * si, fr * si + fi * sr], axis=0)


def band_kernel(counts_ref, taps_ref, measured_ref, band_ref, level_ref):
    width = band_ref.shape[1]
    half = taps_ref.shape[1] // 2
    core = lax.rem(lax.axis_index("cuts"), 2)
    rows = width // 2
    first = pl.multiple_of(lax.axis_index("cuts") // 2 * rows, rows)
    level_ref[:rows, :] = measured_ref[core, pl.ds(first, rows), :].astype(jnp.bfloat16)
    live = (core < counts_ref[0]).astype(jnp.float32)
    level_ref[rows:, :] = jnp.full((level_ref.shape[0] - rows, width), live, jnp.float32).astype(jnp.bfloat16)
    rows = lax.broadcasted_iota(jnp.int32, (width, width), 0)
    columns = lax.broadcasted_iota(jnp.int32, (width, width), 1)
    inside = jnp.abs(columns - rows) <= half
    for part in range(2):
        line = taps_ref[part : part + 1, :].astype(jnp.float32)
        filler = jnp.zeros((1, width - line.shape[1]), jnp.float32)
        line = jnp.concatenate([line, filler], axis=1)
        spread = jnp.broadcast_to(line, (width, width))
        turned = pltpu.roll(spread, width - half, 1, stride=1, stride_axis=0)
        band = jnp.where(inside, turned, 0.0)
        band_ref[part] = band.astype(jnp.bfloat16)
        band_ref[part + 2] = band.T.astype(jnp.bfloat16)


def cut_kernel(tile_ref, whole_ref, below_ref, right_ref):
    half = right_ref.shape[1]
    whole_ref[...] = tile_ref[...]
    below_ref[...] = tile_ref[:, :, half:]
    right_ref[...] = tile_ref[:, half:, :]


def seal_kernel(tile_ref, offsets_ref, own_ref):
    half = tile_ref.shape[1] // 2
    own_ref[:, :half, :] = tile_ref[:, half:, half:]
    shape = (own_ref.shape[1] - half, half)
    line = lax.broadcasted_iota(jnp.int32, shape, 0)
    lines = jnp.zeros(shape, jnp.float32)
    for index in range(4):
        value = offsets_ref[index // 2 : index // 2 + 1, index % 2 : index % 2 + 1].astype(jnp.float32)
        lines = jnp.where(line == index, value, lines)
    for part in range(2):
        own_ref[part, half:, :] = lines.astype(jnp.bfloat16)


def window_kernel(own_ref, rows_ref, columns_ref, rows_back_ref, columns_back_ref):
    half = own_ref.shape[2]
    width = 2 * half
    core = lax.rem(lax.axis_index("cuts"), 2)
    lines = own_ref[0, half:, :].astype(jnp.float32).astype(jnp.int32) - half

    def placed(shape, axis, shift):
        i = lax.broadcasted_iota(jnp.int32, shape, axis)
        j = lax.broadcasted_iota(jnp.int32, shape, 1 - axis)
        shift = jnp.concatenate([shift] * (shape[1] // half), axis=1)
        return jnp.where(j - i == shift, 1.0, 0.0).astype(jnp.bfloat16)

    for place in range(2):
        second = core != place
        row = jnp.where(second, lines[2:3], lines[0:1])
        column = jnp.where(second, lines[3:4], lines[1:2])
        rows_ref[place * half : (place + 1) * half, :] = placed((half, width), 0, row)
        columns_ref[place] = placed((width + half, width), 1, column)
        rows_back_ref[place] = placed((width + half, width), 1, row)
        columns_back_ref[place * width : (place + 1) * width, :] = placed((width, width + half), 0, column)


def extract_kernel(rows_ref, columns_ref, tile_ref, below_ref, right_ref, own_ref, first_ref, second_ref):
    width = tile_ref.shape[1]
    half = width // 2
    wide = width + half
    blocks = []
    for part in range(2):
        upper = jnp.concatenate([own_ref[part, :half], right_ref[part]], axis=1)
        lower = jnp.concatenate([below_ref[part], tile_ref[part]], axis=1)
        blocks.append(jnp.concatenate([upper, lower], axis=0))
    block = jnp.concatenate(blocks, axis=1)
    strips = [dot(rows_ref[...], block[top : top + width]).astype(jnp.bfloat16) for top in (0, half)]
    for place, out_ref in enumerate((first_ref, second_ref)):
        mine = [strip[place * half : (place + 1) * half, part * wide : (part + 1) * wide] for part in range(2) for strip in strips]
        out_ref[...] = dot(jnp.concatenate(mine, axis=0), columns_ref[place]).astype(jnp.bfloat16)


def forward(probe_ref, band_ref, patch_ref, spread_ref, first, last):
    for level in range(first, last + 1):
        if level == 0:
            spread_ref[0] = probe_ref[...]
        else:
            wave = complex_mul(spread_ref[level - 1], patch_ref[level - 1], 1.0).astype(jnp.bfloat16)
            spread = sandwich(band_ref[0], band_ref[1], wave, band_ref[2], band_ref[3])
            spread_ref[level] = spread.astype(jnp.bfloat16)


def head_kernel(probe_ref, band_ref, p0_ref, p1_ref, spread_ref, patch_ref):
    cut = lax.axis_index("cuts")

    @pl.when(cut < 2)
    def _():
        patch_ref[cut] = p0_ref[...]
        patch_ref[1 - cut] = p1_ref[...]
        forward(probe_ref, band_ref, patch_ref, spread_ref, 0, 2)


def chain_kernel(
    probe_ref, p0_ref, p1_ref, p2_ref, p3_ref, level_ref, far_level_ref, band_ref, fourier_ref, head_ref, mine_ref, other_ref, patch_ref, spread_ref, back_ref
):
    width = probe_ref.shape[1]
    cut = lax.axis_index("cuts")
    for mask, ref in enumerate((p0_ref, p1_ref, p2_ref, p3_ref)):
        patch_ref[lax.bitwise_xor(cut, mask)] = ref[...]

    @pl.when(cut < 2)
    def _():
        spread_ref[0:3] = head_ref[...]

    @pl.when(cut >= 2)
    def _():
        forward(probe_ref, band_ref, patch_ref, spread_ref, 0, 2)

    forward(probe_ref, band_ref, patch_ref, spread_ref, 3, 3)
    fourier_r, fourier_i = fourier_ref[0], fourier_ref[1]
    wave = complex_mul(spread_ref[3], patch_ref[3], 1.0).astype(jnp.bfloat16)
    far = sandwich(fourier_r, fourier_i, wave, fourier_r, fourier_i)
    far_r, far_i = far[:width], far[width:]
    rows = width // 2
    level, far_level = level_ref[:rows, :].astype(jnp.float32), far_level_ref[:rows, :].astype(jnp.float32)
    level = jnp.concatenate([jnp.where(cut < 2, level, far_level), jnp.where(cut < 2, far_level, level)], axis=0)
    live = level_ref[rows : rows + 1, :].astype(jnp.float32)
    excess = 2.0 * live * (far_r * far_r + far_i * far_i - level)
    residual = jnp.concatenate([excess * far_r, excess * far_i], axis=0).astype(jnp.bfloat16)
    back_ref[...] = sandwich(fourier_r, -fourier_i, residual, fourier_r, -fourier_i).astype(jnp.bfloat16)

    def term(level):
        value = complex_mul(spread_ref[level], back_ref[...], -1.0).astype(jnp.bfloat16)

        @pl.when(level == cut)
        def _():
            mine_ref[...] = value

        @pl.when(level != cut)
        def _():
            other_ref[...] = value

    def carry(level):
        carried = complex_mul(patch_ref[level], back_ref[...], -1.0).astype(jnp.bfloat16)
        back = sandwich(band_ref[2], -band_ref[3], carried, band_ref[0], -band_ref[1])
        back_ref[...] = back.astype(jnp.bfloat16)

    @pl.when(cut >= 2)
    def _():
        term(3)

    carry(3)

    @pl.when(cut >= 2)
    def _():
        term(2)

    @pl.when(cut < 2)
    def _():
        carry(2)
        term(1)
        carry(1)
        term(0)


def scatter_kernel(rows_ref, columns_ref, mine_ref, other_ref, tile_ref, below_ref, right_ref, own_ref):
    width = tile_ref.shape[1]
    half = width // 2
    strips = []
    for place, ref in enumerate((mine_ref, other_ref)):
        field = jnp.concatenate([ref[:width, :], ref[width:, :]], axis=1)
        strips.append(dot(rows_ref[place], field).astype(jnp.bfloat16))
    for part in range(2):
        strip = jnp.concatenate([strip[:, part * width : (part + 1) * width] for strip in strips], axis=1)
        total = dot(strip, columns_ref[...])
        tile_ref[part] = total[half:, half:]
        below_ref[part] = total[half:, :half].astype(jnp.bfloat16)
        right_ref[part] = total[:half, half:].astype(jnp.bfloat16)
        own_ref[part] = total[:half, :half].astype(jnp.bfloat16)


def total_kernel(tile_ref, below_ref, right_ref, own_ref, out_ref):
    half = right_ref.shape[1]
    below = below_ref[...].astype(jnp.float32)
    right = right_ref[...].astype(jnp.float32)
    own = own_ref[...].astype(jnp.float32)
    out_ref[0, :, :half, :half] = tile_ref[:, :half, :half]
    out_ref[0, :, :half, half:] = tile_ref[:, :half, half:] + below[:, :half]
    out_ref[0, :, half:, :half] = tile_ref[:, half:, :half] + right[:, :, :half]
    out_ref[0, :, half:, half:] = tile_ref[:, half:, half:] + below[:, half:] + right[:, :, half:] + own


VMEM = pl.BlockSpec(memory_space=pltpu.VMEM)
SMEM = pl.BlockSpec(memory_space=pltpu.SMEM)
PARAMS = pltpu.CompilerParams(vmem_limit_bytes=48 * 1024 * 1024)


def shaped(*shape, dtype=jnp.bfloat16):
    return jax.ShapeDtypeStruct(shape, dtype)


def kernel(body, name, in_specs, out_shape, scratch=()):
    return pl.pallas_call(
        body, in_specs=in_specs, out_specs=[VMEM] * len(out_shape), out_shape=out_shape, scratch_shapes=scratch, compiler_params=PARAMS, name=name
    )


def local(object_slices, probe, fresnel_taps, offsets, counts, measured):
    width = probe.shape[1]
    half = width // 2
    wide = width + half
    full = shaped(2 * width, width)
    part = shaped(width, width)
    row_tiles = max(lax.axis_size("tile") // 16, 2)
    probe = probe.reshape(2 * width, width)
    fourier = jnp.asarray(fourier_matrix(width), jnp.bfloat16)

    far_tile = crossed(object_slices[0], "cuts", 2)
    tile, below, right = kernel(cut_kernel, "cut", [VMEM], [shaped(2, width, width), shaped(2, width, half), shaped(2, half, width)])(
        object_slices[0]
    )
    (own,) = kernel(seal_kernel, "seal", [VMEM, VMEM], [shaped(2, half + 16, half)])(tile, offsets)
    below = passed_along(below, "tile", 1)
    right = passed_along(right, "tile", row_tiles)
    own = passed_along(own, "tile", row_tiles + 1)
    below, far_tile = lax.optimization_barrier((below, far_tile))
    far_below = crossed(below, "cuts", 2)
    far_right = crossed(right, "cuts", 2)
    far_own = crossed(own, "cuts", 2)
    level = shaped(half + 16, width)
    band, level = kernel(band_kernel, "band", [SMEM, VMEM, VMEM], [shaped(4, width, width), level])(counts, fresnel_taps, measured)
    level, right = lax.optimization_barrier((level, right))
    level = passed_along(level, "tile", row_tiles + 1)
    rows, columns, rows_back, columns_back = kernel(
        window_kernel,
        "window",
        [VMEM],
        [part, shaped(2, wide, width), shaped(2, wide, width), shaped(2 * width, wide)],
    )(own)
    first, second = kernel(extract_kernel, "near", [VMEM] * 6, [full, full])(rows, columns, tile, below, right, own)
    swapped = crossed(second, "cuts", 1)
    far_level = crossed(level, "cuts", 2)
    straight, far_second = kernel(extract_kernel, "far", [VMEM] * 6, [full, full])(rows, columns, far_tile, far_below, far_right, far_own)
    far_second, far_level = lax.optimization_barrier((far_second, far_level))
    diagonal = crossed(far_second, "cuts", 1)
    (head,) = kernel(head_kernel, "head", [VMEM] * 4, [shaped(3, 2 * width, width)], [pltpu.VMEM((2, 2 * width, width), jnp.bfloat16)])(
        probe, band, first, swapped
    )
    mine, other = kernel(
        chain_kernel,
        "chain",
        [VMEM] * 10,
        [full, full],
        [
            pltpu.VMEM((4, 2 * width, width), jnp.bfloat16),
            pltpu.VMEM((4, 2 * width, width), jnp.bfloat16),
            pltpu.VMEM((2 * width, width), jnp.bfloat16),
        ],
    )(probe, first, swapped, straight, diagonal, level, far_level, band, fourier, head)
    other = crossed(other, "cuts", 1)
    total, below, right, own = kernel(
        scatter_kernel,
        "scatter",
        [VMEM] * 4,
        [shaped(2, width, width, dtype=jnp.float32), shaped(2, width, half), shaped(2, half, width), shaped(2, half, half)],
    )(rows_back, columns_back, mine, other)
    below = passed_along(below, "tile", -1)
    right = passed_along(right, "tile", -row_tiles)
    own = passed_along(own, "tile", -row_tiles - 1)
    (out,) = kernel(total_kernel, "total", [VMEM] * 4, [shaped(1, 2, width, width, dtype=jnp.float32)])(total, below, right, own)
    return out


def solution(mesh):
    return jax.shard_map(
        local,
        mesh=mesh,
        in_specs=(
            P("cuts", None, "tile", None),
            P(),
            P(),
            P("tile", None),
            P("tile"),
            P("tile", None, None),
        ),
        out_specs=P("cuts", None, "tile", None),
        check_vma=False,
    )
```

```python
import jax
import jax.numpy as jnp
import numpy as np
from jax import lax
from jax.experimental import pallas as pl
from jax.experimental.pallas import tpu as pltpu
from jax.sharding import PartitionSpec as P


BLOCKS = 2


def passed_along(value, axis, steps):
    count = lax.axis_size(axis)
    pairs = [(source, (source + steps) % count) for source in range(count)]
    return lax.ppermute(value, axis, pairs)


def crossed(value, axis, mask):
    pairs = [(source, source ^ mask) for source in range(lax.axis_size(axis))]
    return lax.ppermute(value, axis, pairs)


def fourier_matrix(width):
    index = np.arange(width)
    angle = 2.0 * np.pi * (index[:, None] * index[None, :] % width) / width
    return np.stack([np.cos(angle), -np.sin(angle)]) / np.sqrt(width)


def dot(left, right):
    return jnp.dot(left, right, preferred_element_type=jnp.float32)


def sandwich(left_real, left_imag, field, right_real, right_imag):
    width = left_real.shape[0]
    right = jnp.concatenate([right_real, right_imag], axis=0)
    tops, bottoms = [], []
    for first in range(0, width, width // BLOCKS):
        real, imag = left_real[first : first + width // BLOCKS], left_imag[first : first + width // BLOCKS]
        top = dot(jnp.concatenate([real, -imag], axis=1), field).astype(jnp.bfloat16)
        bottom = dot(jnp.concatenate([imag, real], axis=1), field).astype(jnp.bfloat16)
        tops.append(dot(jnp.concatenate([top, -bottom], axis=1), right))
        bottoms.append(dot(jnp.concatenate([bottom, top], axis=1), right))
    return jnp.concatenate(tops + bottoms, axis=0)


def complex_mul(first, second, sign):
    width = first.shape[1]
    fr = first[:width].astype(jnp.float32)
    fi = first[width:].astype(jnp.float32) * sign
    sr = second[:width].astype(jnp.float32)
    si = second[width:].astype(jnp.float32)
    return jnp.concatenate([fr * sr - fi * si, fr * si + fi * sr], axis=0)


def band_kernel(counts_ref, taps_ref, measured_ref, band_ref, level_ref):
    width = band_ref.shape[1]
    half = taps_ref.shape[1] // 2
    core = lax.rem(lax.axis_index("cuts"), 2)
    rows = width // 2
    first = pl.multiple_of(lax.axis_index("cuts") // 2 * rows, rows)
    level_ref[:rows, :] = measured_ref[core, pl.ds(first, rows), :].astype(jnp.bfloat16)
    live = (core < counts_ref[0]).astype(jnp.float32)
    level_ref[rows:, :] = jnp.full((level_ref.shape[0] - rows, width), live, jnp.float32).astype(jnp.bfloat16)
    rows = lax.broadcasted_iota(jnp.int32, (width, width), 0)
    columns = lax.broadcasted_iota(jnp.int32, (width, width), 1)
    inside = jnp.abs(columns - rows) <= half
    for part in range(2):
        line = taps_ref[part : part + 1, :].astype(jnp.float32)
        filler = jnp.zeros((1, width - line.shape[1]), jnp.float32)
        line = jnp.concatenate([line, filler], axis=1)
        spread = jnp.broadcast_to(line, (width, width))
        turned = pltpu.roll(spread, width - half, 1, stride=1, stride_axis=0)
        band = jnp.where(inside, turned, 0.0)
        band_ref[part] = band.astype(jnp.bfloat16)
        band_ref[part + 2] = band.T.astype(jnp.bfloat16)


def cut_kernel(tile_ref, whole_ref, below_ref, right_ref):
    half = right_ref.shape[1]
    whole_ref[...] = tile_ref[...]
    below_ref[...] = tile_ref[:, :, half:]
    right_ref[...] = tile_ref[:, half:, :]


def seal_kernel(tile_ref, offsets_ref, own_ref):
    half = tile_ref.shape[1] // 2
    own_ref[:, :half, :] = tile_ref[:, half:, half:]
    shape = (own_ref.shape[1] - half, half)
    line = lax.broadcasted_iota(jnp.int32, shape, 0)
    lines = jnp.zeros(shape, jnp.float32)
    for index in range(4):
        value = offsets_ref[index // 2 : index // 2 + 1, index % 2 : index % 2 + 1].astype(jnp.float32)
        lines = jnp.where(line == index, value, lines)
    for part in range(2):
        own_ref[part, half:, :] = lines.astype(jnp.bfloat16)


def window_kernel(own_ref, rows_ref, columns_ref, rows_back_ref, columns_back_ref):
    half = own_ref.shape[2]
    width = 2 * half
    core = lax.rem(lax.axis_index("cuts"), 2)
    lines = own_ref[0, half:, :].astype(jnp.float32).astype(jnp.int32) - half

    def placed(shape, axis, shift):
        i = lax.broadcasted_iota(jnp.int32, shape, axis)
        j = lax.broadcasted_iota(jnp.int32, shape, 1 - axis)
        shift = jnp.concatenate([shift] * (shape[1] // half), axis=1)
        return jnp.where(j - i == shift, 1.0, 0.0).astype(jnp.bfloat16)

    for place in range(2):
        second = core != place
        row = jnp.where(second, lines[2:3], lines[0:1])
        column = jnp.where(second, lines[3:4], lines[1:2])
        rows_ref[place * half : (place + 1) * half, :] = placed((half, width), 0, row)
        columns_ref[place] = placed((width + half, width), 1, column)
        rows_back_ref[place] = placed((width + half, width), 1, row)
        columns_back_ref[place * width : (place + 1) * width, :] = placed((width, width + half), 0, column)


def extract_kernel(rows_ref, columns_ref, tile_ref, below_ref, right_ref, own_ref, first_ref, second_ref):
    width = tile_ref.shape[1]
    half = width // 2
    wide = width + half
    blocks = []
    for part in range(2):
        upper = jnp.concatenate([own_ref[part, :half], right_ref[part]], axis=1)
        lower = jnp.concatenate([below_ref[part], tile_ref[part]], axis=1)
        blocks.append(jnp.concatenate([upper, lower], axis=0))
    block = jnp.concatenate(blocks, axis=1)
    strips = [dot(rows_ref[...], block[top : top + width]).astype(jnp.bfloat16) for top in (0, half)]
    for place, out_ref in enumerate((first_ref, second_ref)):
        for part in range(2):
            mine = [strip[place * half : (place + 1) * half, part * wide : (part + 1) * wide] for strip in strips]
            patch = dot(jnp.concatenate(mine, axis=0), columns_ref[place])
            out_ref[part * width : (part + 1) * width, :] = patch.astype(jnp.bfloat16)


def forward(probe_ref, band_ref, patch_ref, spread_ref, first, last):
    for level in range(first, last + 1):
        if level == 0:
            spread_ref[0] = probe_ref[...]
        else:
            wave = complex_mul(spread_ref[level - 1], patch_ref[level - 1], 1.0).astype(jnp.bfloat16)
            spread = sandwich(band_ref[0], band_ref[1], wave, band_ref[2], band_ref[3])
            spread_ref[level] = spread.astype(jnp.bfloat16)


def head_kernel(probe_ref, band_ref, p0_ref, p1_ref, spread_ref, patch_ref):
    cut = lax.axis_index("cuts")

    @pl.when(cut < 2)
    def _():
        patch_ref[cut] = p0_ref[...]
        patch_ref[1 - cut] = p1_ref[...]
        forward(probe_ref, band_ref, patch_ref, spread_ref, 0, 2)


def chain_kernel(
    probe_ref, p0_ref, p1_ref, p2_ref, p3_ref, level_ref, far_level_ref, band_ref, fourier_ref, head_ref, mine_ref, other_ref, patch_ref, spread_ref, back_ref
):
    width = probe_ref.shape[1]
    cut = lax.axis_index("cuts")
    for mask, ref in enumerate((p0_ref, p1_ref, p2_ref, p3_ref)):
        patch_ref[lax.bitwise_xor(cut, mask)] = ref[...]

    @pl.when(cut < 2)
    def _():
        spread_ref[0:3] = head_ref[...]

    @pl.when(cut >= 2)
    def _():
        forward(probe_ref, band_ref, patch_ref, spread_ref, 0, 2)

    forward(probe_ref, band_ref, patch_ref, spread_ref, 3, 3)
    fourier_r, fourier_i = fourier_ref[0], fourier_ref[1]
    wave = complex_mul(spread_ref[3], patch_ref[3], 1.0).astype(jnp.bfloat16)
    far = sandwich(fourier_r, fourier_i, wave, fourier_r, fourier_i)
    far_r, far_i = far[:width], far[width:]
    rows = width // 2
    level, far_level = level_ref[:rows, :].astype(jnp.float32), far_level_ref[:rows, :].astype(jnp.float32)
    level = jnp.concatenate([jnp.where(cut < 2, level, far_level), jnp.where(cut < 2, far_level, level)], axis=0)
    live = level_ref[rows : rows + 1, :].astype(jnp.float32)
    excess = 2.0 * live * (far_r * far_r + far_i * far_i - level)
    residual = jnp.concatenate([excess * far_r, excess * far_i], axis=0).astype(jnp.bfloat16)
    back_ref[...] = sandwich(fourier_r, -fourier_i, residual, fourier_r, -fourier_i).astype(jnp.bfloat16)

    def term(level):
        value = complex_mul(spread_ref[level], back_ref[...], -1.0).astype(jnp.bfloat16)

        @pl.when(level == cut)
        def _():
            mine_ref[...] = value

        @pl.when(level != cut)
        def _():
            other_ref[...] = value

    def carry(level):
        carried = complex_mul(patch_ref[level], back_ref[...], -1.0).astype(jnp.bfloat16)
        back = sandwich(band_ref[2], -band_ref[3], carried, band_ref[0], -band_ref[1])
        back_ref[...] = back.astype(jnp.bfloat16)

    @pl.when(cut >= 2)
    def _():
        term(3)

    carry(3)

    @pl.when(cut >= 2)
    def _():
        term(2)

    @pl.when(cut < 2)
    def _():
        carry(2)
        term(1)
        carry(1)
        term(0)


def scatter_kernel(rows_ref, columns_ref, mine_ref, other_ref, tile_ref, below_ref, right_ref, own_ref):
    width = tile_ref.shape[1]
    half = width // 2
    strips = []
    for place, ref in enumerate((mine_ref, other_ref)):
        field = jnp.concatenate([ref[:width, :], ref[width:, :]], axis=1)
        strips.append(dot(rows_ref[place], field).astype(jnp.bfloat16))
    for part in range(2):
        strip = jnp.concatenate([strip[:, part * width : (part + 1) * width] for strip in strips], axis=1)
        total = dot(strip, columns_ref[...])
        tile_ref[part] = total[half:, half:]
        below_ref[part] = total[half:, :half].astype(jnp.bfloat16)
        right_ref[part] = total[:half, half:].astype(jnp.bfloat16)
        own_ref[part] = total[:half, :half].astype(jnp.bfloat16)


def total_kernel(tile_ref, below_ref, right_ref, own_ref, out_ref):
    half = right_ref.shape[1]
    below = below_ref[...].astype(jnp.float32)
    right = right_ref[...].astype(jnp.float32)
    own = own_ref[...].astype(jnp.float32)
    out_ref[0, :, :half, :half] = tile_ref[:, :half, :half]
    out_ref[0, :, :half, half:] = tile_ref[:, :half, half:] + below[:, :half]
    out_ref[0, :, half:, :half] = tile_ref[:, half:, :half] + right[:, :, :half]
    out_ref[0, :, half:, half:] = tile_ref[:, half:, half:] + below[:, half:] + right[:, :, half:] + own


VMEM = pl.BlockSpec(memory_space=pltpu.VMEM)
SMEM = pl.BlockSpec(memory_space=pltpu.SMEM)
PARAMS = pltpu.CompilerParams(vmem_limit_bytes=48 * 1024 * 1024)


def shaped(*shape, dtype=jnp.bfloat16):
    return jax.ShapeDtypeStruct(shape, dtype)


def kernel(body, name, in_specs, out_shape, scratch=()):
    return pl.pallas_call(
        body, in_specs=in_specs, out_specs=[VMEM] * len(out_shape), out_shape=out_shape, scratch_shapes=scratch, compiler_params=PARAMS, name=name
    )


def local(object_slices, probe, fresnel_taps, offsets, counts, measured):
    width = probe.shape[1]
    half = width // 2
    wide = width + half
    full = shaped(2 * width, width)
    part = shaped(width, width)
    row_tiles = max(lax.axis_size("tile") // 16, 2)
    probe = probe.reshape(2 * width, width)
    fourier = jnp.asarray(fourier_matrix(width), jnp.bfloat16)

    far_tile = crossed(object_slices[0], "cuts", 2)
    tile, below, right = kernel(cut_kernel, "cut", [VMEM], [shaped(2, width, width), shaped(2, width, half), shaped(2, half, width)])(
        object_slices[0]
    )
    (own,) = kernel(seal_kernel, "seal", [VMEM, VMEM], [shaped(2, half + 16, half)])(tile, offsets)
    below = passed_along(below, "tile", 1)
    right = passed_along(right, "tile", row_tiles)
    own = passed_along(own, "tile", row_tiles + 1)
    below, far_tile = lax.optimization_barrier((below, far_tile))
    far_below = crossed(below, "cuts", 2)
    far_right = crossed(right, "cuts", 2)
    far_own = crossed(own, "cuts", 2)
    level = shaped(half + 16, width)
    band, level = kernel(band_kernel, "band", [SMEM, VMEM, VMEM], [shaped(4, width, width), level])(counts, fresnel_taps, measured)
    level, right = lax.optimization_barrier((level, right))
    level = passed_along(level, "tile", row_tiles + 1)
    rows, columns, rows_back, columns_back = kernel(
        window_kernel,
        "window",
        [VMEM],
        [part, shaped(2, wide, width), shaped(2, wide, width), shaped(2 * width, wide)],
    )(own)
    first, second = kernel(extract_kernel, "near", [VMEM] * 6, [full, full])(rows, columns, tile, below, right, own)
    swapped = crossed(second, "cuts", 1)
    far_level = crossed(level, "cuts", 2)
    straight, far_second = kernel(extract_kernel, "far", [VMEM] * 6, [full, full])(rows, columns, far_tile, far_below, far_right, far_own)
    far_second, far_level = lax.optimization_barrier((far_second, far_level))
    diagonal = crossed(far_second, "cuts", 1)
    (head,) = kernel(head_kernel, "head", [VMEM] * 4, [shaped(3, 2 * width, width)], [pltpu.VMEM((2, 2 * width, width), jnp.bfloat16)])(
        probe, band, first, swapped
    )
    mine, other = kernel(
        chain_kernel,
        "chain",
        [VMEM] * 10,
        [full, full],
        [
            pltpu.VMEM((4, 2 * width, width), jnp.bfloat16),
            pltpu.VMEM((4, 2 * width, width), jnp.bfloat16),
            pltpu.VMEM((2 * width, width), jnp.bfloat16),
        ],
    )(probe, first, swapped, straight, diagonal, level, far_level, band, fourier, head)
    other = crossed(other, "cuts", 1)
    total, below, right, own = kernel(
        scatter_kernel,
        "scatter",
        [VMEM] * 4,
        [shaped(2, width, width, dtype=jnp.float32), shaped(2, width, half), shaped(2, half, width), shaped(2, half, half)],
    )(rows_back, columns_back, mine, other)
    below = passed_along(below, "tile", -1)
    right = passed_along(right, "tile", -row_tiles)
    own = passed_along(own, "tile", -row_tiles - 1)
    (out,) = kernel(total_kernel, "total", [VMEM] * 4, [shaped(1, 2, width, width, dtype=jnp.float32)])(total, below, right, own)
    return out


def solution(mesh):
    return jax.shard_map(
        local,
        mesh=mesh,
        in_specs=(
            P("cuts", None, "tile", None),
            P(),
            P(),
            P("tile", None),
            P("tile"),
            P("tile", None, None),
        ),
        out_specs=P("cuts", None, "tile", None),
        check_vma=False,
    )
```

```python
import jax
import jax.numpy as jnp
import numpy as np
from jax import lax
from jax.experimental import pallas as pl
from jax.experimental.pallas import tpu as pltpu
from jax.sharding import PartitionSpec as P


def passed_along(value, axis, steps):
    count = lax.axis_size(axis)
    pairs = [(source, (source + steps) % count) for source in range(count)]
    return lax.ppermute(value, axis, pairs)


def crossed(value, axis, mask):
    pairs = [(source, source ^ mask) for source in range(lax.axis_size(axis))]
    return lax.ppermute(value, axis, pairs)


def fourier_matrix(width):
    index = np.arange(width)
    angle = 2.0 * np.pi * (index[:, None] * index[None, :] % width) / width
    return np.stack([np.cos(angle), -np.sin(angle)]) / np.sqrt(width)


def dot(left, right):
    return jnp.dot(left, right, preferred_element_type=jnp.float32)


def left_product(real, imag, field):
    width = real.shape[0]
    by_real = dot(jnp.concatenate([real, imag], axis=0), field[:width])
    by_imag = dot(jnp.concatenate([-imag, real], axis=0), field[width:])
    return by_real + by_imag


def right_product(field, real, imag):
    width = real.shape[0]
    turned = jnp.concatenate([-field[width:], field[:width]], axis=0)
    return dot(field, real) + dot(turned, imag)


def sandwich(left_real, left_imag, field, right_real, right_imag):
    inner = left_product(left_real, left_imag, field).astype(jnp.bfloat16)
    return right_product(inner, right_real, right_imag)


def complex_mul(first, second, sign):
    width = first.shape[1]
    fr = first[:width].astype(jnp.float32)
    fi = first[width:].astype(jnp.float32) * sign
    sr = second[:width].astype(jnp.float32)
    si = second[width:].astype(jnp.float32)
    return jnp.concatenate([fr * sr - fi * si, fr * si + fi * sr], axis=0)


def band_kernel(counts_ref, taps_ref, measured_ref, band_ref, level_ref):
    width = band_ref.shape[1]
    half = taps_ref.shape[1] // 2
    core = lax.rem(lax.axis_index("cuts"), 2)
    rows = width // 2
    first = pl.multiple_of(lax.axis_index("cuts") // 2 * rows, rows)
    level_ref[:rows, :] = measured_ref[core, pl.ds(first, rows), :].astype(jnp.bfloat16)
    live = (core < counts_ref[0]).astype(jnp.float32)
    level_ref[rows:, :] = jnp.full((level_ref.shape[0] - rows, width), live, jnp.float32).astype(jnp.bfloat16)
    rows = lax.broadcasted_iota(jnp.int32, (width, width), 0)
    columns = lax.broadcasted_iota(jnp.int32, (width, width), 1)
    inside = jnp.abs(columns - rows) <= half
    for part in range(2):
        line = taps_ref[part : part + 1, :].astype(jnp.float32)
        filler = jnp.zeros((1, width - line.shape[1]), jnp.float32)
        line = jnp.concatenate([line, filler], axis=1)
        spread = jnp.broadcast_to(line, (width, width))
        turned = pltpu.roll(spread, width - half, 1, stride=1, stride_axis=0)
        band = jnp.where(inside, turned, 0.0)
        band_ref[part] = band.astype(jnp.bfloat16)
        band_ref[part + 2] = band.T.astype(jnp.bfloat16)


def cut_kernel(tile_ref, whole_ref, below_ref, right_ref):
    half = right_ref.shape[1]
    whole_ref[...] = tile_ref[...]
    below_ref[...] = tile_ref[:, :, half:]
    right_ref[...] = tile_ref[:, half:, :]


def seal_kernel(tile_ref, offsets_ref, own_ref):
    half = tile_ref.shape[1] // 2
    own_ref[:, :half, :] = tile_ref[:, half:, half:]
    shape = (own_ref.shape[1] - half, half)
    line = lax.broadcasted_iota(jnp.int32, shape, 0)
    lines = jnp.zeros(shape, jnp.float32)
    for index in range(4):
        value = offsets_ref[index // 2 : index // 2 + 1, index % 2 : index % 2 + 1].astype(jnp.float32)
        lines = jnp.where(line == index, value, lines)
    for part in range(2):
        own_ref[part, half:, :] = lines.astype(jnp.bfloat16)


def window_kernel(own_ref, rows_ref, columns_ref, rows_back_ref, columns_back_ref):
    half = own_ref.shape[2]
    width = 2 * half
    core = lax.rem(lax.axis_index("cuts"), 2)
    lines = own_ref[0, half:, :].astype(jnp.float32).astype(jnp.int32) - half

    def placed(shape, axis, shift):
        i = lax.broadcasted_iota(jnp.int32, shape, axis)
        j = lax.broadcasted_iota(jnp.int32, shape, 1 - axis)
        shift = jnp.concatenate([shift] * (shape[1] // half), axis=1)
        return jnp.where(j - i == shift, 1.0, 0.0).astype(jnp.bfloat16)

    for place in range(2):
        second = core != place
        row = jnp.where(second, lines[2:3], lines[0:1])
        column = jnp.where(second, lines[3:4], lines[1:2])
        rows_ref[place * half : (place + 1) * half, :] = placed((half, width), 0, row)
        columns_ref[place] = placed((width + half, width), 1, column)
        rows_back_ref[place] = placed((width + half, width), 1, row)
        columns_back_ref[place * width : (place + 1) * width, :] = placed((width, width + half), 0, column)


def extract_kernel(rows_ref, columns_ref, tile_ref, below_ref, right_ref, own_ref, first_ref, second_ref):
    width = tile_ref.shape[1]
    half = width // 2
    wide = width + half
    blocks = []
    for part in range(2):
        upper = jnp.concatenate([own_ref[part, :half], right_ref[part]], axis=1)
        lower = jnp.concatenate([below_ref[part], tile_ref[part]], axis=1)
        blocks.append(jnp.concatenate([upper, lower], axis=0))
    block = jnp.concatenate(blocks, axis=1)
    strips = [dot(rows_ref[...], block[top : top + width]).astype(jnp.bfloat16) for top in (0, half)]
    for place, out_ref in enumerate((first_ref, second_ref)):
        mine = [strip[place * half : (place + 1) * half, part * wide : (part + 1) * wide] for part in range(2) for strip in strips]
        out_ref[...] = dot(jnp.concatenate(mine, axis=0), columns_ref[place]).astype(jnp.bfloat16)


def forward(probe_ref, band_ref, patch_ref, spread_ref, first, last):
    for level in range(first, last + 1):
        if level == 0:
            spread_ref[0] = probe_ref[...]
        else:
            wave = complex_mul(spread_ref[level - 1], patch_ref[level - 1], 1.0).astype(jnp.bfloat16)
            spread = sandwich(band_ref[0], band_ref[1], wave, band_ref[2], band_ref[3])
            spread_ref[level] = spread.astype(jnp.bfloat16)


def head_kernel(probe_ref, band_ref, p0_ref, p1_ref, spread_ref, patch_ref):
    cut = lax.axis_index("cuts")

    @pl.when(cut < 2)
    def _():
        patch_ref[cut] = p0_ref[...]
        patch_ref[1 - cut] = p1_ref[...]
        forward(probe_ref, band_ref, patch_ref, spread_ref, 0, 2)


def chain_kernel(
    probe_ref, p0_ref, p1_ref, p2_ref, p3_ref, level_ref, far_level_ref, band_ref, fourier_ref, head_ref, mine_ref, other_ref, patch_ref, spread_ref, back_ref
):
    width = probe_ref.shape[1]
    cut = lax.axis_index("cuts")
    for mask, ref in enumerate((p0_ref, p1_ref, p2_ref, p3_ref)):
        patch_ref[lax.bitwise_xor(cut, mask)] = ref[...]

    @pl.when(cut < 2)
    def _():
        spread_ref[0:3] = head_ref[...]

    @pl.when(cut >= 2)
    def _():
        forward(probe_ref, band_ref, patch_ref, spread_ref, 0, 2)

    forward(probe_ref, band_ref, patch_ref, spread_ref, 3, 3)
    fourier_r, fourier_i = fourier_ref[0], fourier_ref[1]
    wave = complex_mul(spread_ref[3], patch_ref[3], 1.0).astype(jnp.bfloat16)
    far = sandwich(fourier_r, fourier_i, wave, fourier_r, fourier_i)
    far_r, far_i = far[:width], far[width:]
    rows = width // 2
    level, far_level = level_ref[:rows, :].astype(jnp.float32), far_level_ref[:rows, :].astype(jnp.float32)
    level = jnp.concatenate([jnp.where(cut < 2, level, far_level), jnp.where(cut < 2, far_level, level)], axis=0)
    live = level_ref[rows : rows + 1, :].astype(jnp.float32)
    excess = 2.0 * live * (far_r * far_r + far_i * far_i - level)
    residual = jnp.concatenate([excess * far_r, excess * far_i], axis=0).astype(jnp.bfloat16)
    back_ref[...] = sandwich(fourier_r, -fourier_i, residual, fourier_r, -fourier_i).astype(jnp.bfloat16)

    def term(level):
        value = complex_mul(spread_ref[level], back_ref[...], -1.0).astype(jnp.bfloat16)

        @pl.when(level == cut)
        def _():
            mine_ref[...] = value

        @pl.when(level != cut)
        def _():
            other_ref[...] = value

    def carry(level):
        carried = complex_mul(patch_ref[level], back_ref[...], -1.0).astype(jnp.bfloat16)
        back = sandwich(band_ref[2], -band_ref[3], carried, band_ref[0], -band_ref[1])
        back_ref[...] = back.astype(jnp.bfloat16)

    @pl.when(cut >= 2)
    def _():
        term(3)

    carry(3)

    @pl.when(cut >= 2)
    def _():
        term(2)

    @pl.when(cut < 2)
    def _():
        carry(2)
        term(1)
        carry(1)
        term(0)


def scatter_kernel(rows_ref, columns_ref, mine_ref, other_ref, tile_ref, below_ref, right_ref, own_ref):
    width = tile_ref.shape[1]
    half = width // 2
    strips = []
    for place, ref in enumerate((mine_ref, other_ref)):
        field = jnp.concatenate([ref[:width, :], ref[width:, :]], axis=1)
        strips.append(dot(rows_ref[place], field).astype(jnp.bfloat16))
    for part in range(2):
        strip = jnp.concatenate([strip[:, part * width : (part + 1) * width] for strip in strips], axis=1)
        total = dot(strip, columns_ref[...])
        tile_ref[part] = total[half:, half:]
        below_ref[part] = total[half:, :half].astype(jnp.bfloat16)
        right_ref[part] = total[:half, half:].astype(jnp.bfloat16)
        own_ref[part] = total[:half, :half].astype(jnp.bfloat16)


def total_kernel(tile_ref, below_ref, right_ref, own_ref, out_ref):
    half = right_ref.shape[1]
    below = below_ref[...].astype(jnp.float32)
    right = right_ref[...].astype(jnp.float32)
    own = own_ref[...].astype(jnp.float32)
    out_ref[0, :, :half, :half] = tile_ref[:, :half, :half]
    out_ref[0, :, :half, half:] = tile_ref[:, :half, half:] + below[:, :half]
    out_ref[0, :, half:, :half] = tile_ref[:, half:, :half] + right[:, :, :half]
    out_ref[0, :, half:, half:] = tile_ref[:, half:, half:] + below[:, half:] + right[:, :, half:] + own


VMEM = pl.BlockSpec(memory_space=pltpu.VMEM)
SMEM = pl.BlockSpec(memory_space=pltpu.SMEM)
PARAMS = pltpu.CompilerParams(vmem_limit_bytes=48 * 1024 * 1024)


def shaped(*shape, dtype=jnp.bfloat16):
    return jax.ShapeDtypeStruct(shape, dtype)


def kernel(body, name, in_specs, out_shape, scratch=()):
    return pl.pallas_call(
        body, in_specs=in_specs, out_specs=[VMEM] * len(out_shape), out_shape=out_shape, scratch_shapes=scratch, compiler_params=PARAMS, name=name
    )


def local(object_slices, probe, fresnel_taps, offsets, counts, measured):
    width = probe.shape[1]
    half = width // 2
    wide = width + half
    full = shaped(2 * width, width)
    part = shaped(width, width)
    row_tiles = max(lax.axis_size("tile") // 16, 2)
    probe = probe.reshape(2 * width, width)
    fourier = jnp.asarray(fourier_matrix(width), jnp.bfloat16)

    far_tile = crossed(object_slices[0], "cuts", 2)
    tile, below, right = kernel(cut_kernel, "cut", [VMEM], [shaped(2, width, width), shaped(2, width, half), shaped(2, half, width)])(
        object_slices[0]
    )
    (own,) = kernel(seal_kernel, "seal", [VMEM, VMEM], [shaped(2, half + 16, half)])(tile, offsets)
    below = passed_along(below, "tile", 1)
    right = passed_along(right, "tile", row_tiles)
    own = passed_along(own, "tile", row_tiles + 1)
    below, far_tile = lax.optimization_barrier((below, far_tile))
    far_below = crossed(below, "cuts", 2)
    far_right = crossed(right, "cuts", 2)
    far_own = crossed(own, "cuts", 2)
    level = shaped(half + 16, width)
    band, level = kernel(band_kernel, "band", [SMEM, VMEM, VMEM], [shaped(4, width, width), level])(counts, fresnel_taps, measured)
    level, right = lax.optimization_barrier((level, right))
    level = passed_along(level, "tile", row_tiles + 1)
    rows, columns, rows_back, columns_back = kernel(
        window_kernel,
        "window",
        [VMEM],
        [part, shaped(2, wide, width), shaped(2, wide, width), shaped(2 * width, wide)],
    )(own)
    first, second = kernel(extract_kernel, "near", [VMEM] * 6, [full, full])(rows, columns, tile, below, right, own)
    swapped = crossed(second, "cuts", 1)
    far_level = crossed(level, "cuts", 2)
    straight, far_second = kernel(extract_kernel, "far", [VMEM] * 6, [full, full])(rows, columns, far_tile, far_below, far_right, far_own)
    far_second, far_level = lax.optimization_barrier((far_second, far_level))
    diagonal = crossed(far_second, "cuts", 1)
    (head,) = kernel(head_kernel, "head", [VMEM] * 4, [shaped(3, 2 * width, width)], [pltpu.VMEM((2, 2 * width, width), jnp.bfloat16)])(
        probe, band, first, swapped
    )
    mine, other = kernel(
        chain_kernel,
        "chain",
        [VMEM] * 10,
        [full, full],
        [
            pltpu.VMEM((4, 2 * width, width), jnp.bfloat16),
            pltpu.VMEM((4, 2 * width, width), jnp.bfloat16),
            pltpu.VMEM((2 * width, width), jnp.bfloat16),
        ],
    )(probe, first, swapped, straight, diagonal, level, far_level, band, fourier, head)
    other = crossed(other, "cuts", 1)
    total, below, right, own = kernel(
        scatter_kernel,
        "scatter",
        [VMEM] * 4,
        [shaped(2, width, width, dtype=jnp.float32), shaped(2, width, half), shaped(2, half, width), shaped(2, half, half)],
    )(rows_back, columns_back, mine, other)
    below = passed_along(below, "tile", -1)
    right = passed_along(right, "tile", -row_tiles)
    own = passed_along(own, "tile", -row_tiles - 1)
    (out,) = kernel(total_kernel, "total", [VMEM] * 4, [shaped(1, 2, width, width, dtype=jnp.float32)])(total, below, right, own)
    return out


def solution(mesh):
    return jax.shard_map(
        local,
        mesh=mesh,
        in_specs=(
            P("cuts", None, "tile", None),
            P(),
            P(),
            P("tile", None),
            P("tile"),
            P("tile", None, None),
        ),
        out_specs=P("cuts", None, "tile", None),
        check_vma=False,
    )
```

```python
import jax
import jax.numpy as jnp
import numpy as np
from jax import lax
from jax.experimental import pallas as pl
from jax.experimental.pallas import tpu as pltpu
from jax.sharding import PartitionSpec as P


def passed_along(value, axis, steps):
    count = lax.axis_size(axis)
    pairs = [(source, (source + steps) % count) for source in range(count)]
    return lax.ppermute(value, axis, pairs)


def crossed(value, axis, mask):
    pairs = [(source, source ^ mask) for source in range(lax.axis_size(axis))]
    return lax.ppermute(value, axis, pairs)


def fourier_matrix(width):
    index = np.arange(width)
    angle = 2.0 * np.pi * (index[:, None] * index[None, :] % width) / width
    return np.stack([np.cos(angle), -np.sin(angle)]) / np.sqrt(width)


def dot(left, right):
    return jnp.dot(left, right, preferred_element_type=jnp.float32)


def left_product(real, imag, field):
    top = dot(jnp.concatenate([real, -imag], axis=1), field)
    bottom = dot(jnp.concatenate([imag, real], axis=1), field)
    return jnp.concatenate([top, bottom], axis=0)


def right_product(field, real, imag):
    width = real.shape[0]
    field_real, field_imag = field[:width], field[width:]
    right = jnp.concatenate([real, imag], axis=0)
    top = dot(jnp.concatenate([field_real, -field_imag], axis=1), right)
    bottom = dot(jnp.concatenate([field_imag, field_real], axis=1), right)
    return jnp.concatenate([top, bottom], axis=0)


def sandwich(left_real, left_imag, field, right_real, right_imag):
    inner = left_product(left_real, left_imag, field).astype(jnp.bfloat16)
    return right_product(inner, right_real, right_imag)


def complex_mul(first, second, sign):
    width = first.shape[1]
    fr = first[:width].astype(jnp.float32)
    fi = first[width:].astype(jnp.float32) * sign
    sr = second[:width].astype(jnp.float32)
    si = second[width:].astype(jnp.float32)
    return jnp.concatenate([fr * sr - fi * si, fr * si + fi * sr], axis=0)


def band_kernel(counts_ref, taps_ref, measured_ref, band_ref, level_ref):
    width = band_ref.shape[1]
    half = taps_ref.shape[1] // 2
    core = lax.rem(lax.axis_index("cuts"), 2)
    rows = width // 2
    first = pl.multiple_of(lax.axis_index("cuts") // 2 * rows, rows)
    level_ref[:rows, :] = measured_ref[core, pl.ds(first, rows), :].astype(jnp.bfloat16)
    live = (core < counts_ref[0]).astype(jnp.float32)
    level_ref[rows:, :] = jnp.full((level_ref.shape[0] - rows, width), live, jnp.float32).astype(jnp.bfloat16)
    rows = lax.broadcasted_iota(jnp.int32, (width, width), 0)
    columns = lax.broadcasted_iota(jnp.int32, (width, width), 1)
    inside = jnp.abs(columns - rows) <= half
    for part in range(2):
        line = taps_ref[part : part + 1, :].astype(jnp.float32)
        filler = jnp.zeros((1, width - line.shape[1]), jnp.float32)
        line = jnp.concatenate([line, filler], axis=1)
        spread = jnp.broadcast_to(line, (width, width))
        turned = pltpu.roll(spread, width - half, 1, stride=1, stride_axis=0)
        band = jnp.where(inside, turned, 0.0)
        band_ref[part] = band.astype(jnp.bfloat16)
        band_ref[part + 2] = band.T.astype(jnp.bfloat16)


def cut_kernel(tile_ref, whole_ref, below_ref, right_ref):
    half = right_ref.shape[1]
    whole_ref[...] = tile_ref[...]
    below_ref[...] = tile_ref[:, :, half:]
    right_ref[...] = tile_ref[:, half:, :]


def seal_kernel(tile_ref, offsets_ref, own_ref):
    half = tile_ref.shape[1] // 2
    own_ref[:, :half, :] = tile_ref[:, half:, half:]
    shape = (own_ref.shape[1] - half, half)
    line = lax.broadcasted_iota(jnp.int32, shape, 0)
    lines = jnp.zeros(shape, jnp.float32)
    for index in range(4):
        value = offsets_ref[index // 2 : index // 2 + 1, index % 2 : index % 2 + 1].astype(jnp.float32)
        lines = jnp.where(line == index, value, lines)
    for part in range(2):
        own_ref[part, half:, :] = lines.astype(jnp.bfloat16)


def window_kernel(own_ref, rows_ref, columns_ref, rows_back_ref, columns_back_ref):
    half = own_ref.shape[2]
    width = 2 * half
    core = lax.rem(lax.axis_index("cuts"), 2)
    lines = own_ref[0, half:, :].astype(jnp.float32).astype(jnp.int32) - half

    def placed(shape, axis, shift):
        i = lax.broadcasted_iota(jnp.int32, shape, axis)
        j = lax.broadcasted_iota(jnp.int32, shape, 1 - axis)
        shift = jnp.concatenate([shift] * (shape[1] // half), axis=1)
        return jnp.where(j - i == shift, 1.0, 0.0).astype(jnp.bfloat16)

    for place in range(2):
        second = core != place
        row = jnp.where(second, lines[2:3], lines[0:1])
        column = jnp.where(second, lines[3:4], lines[1:2])
        rows_ref[place * half : (place + 1) * half, :] = placed((half, width), 0, row)
        columns_ref[place] = placed((width + half, width), 1, column)
        rows_back_ref[place] = placed((width + half, width), 1, row)
        columns_back_ref[place * width : (place + 1) * width, :] = placed((width, width + half), 0, column)


def extract_kernel(rows_ref, columns_ref, tile_ref, below_ref, right_ref, own_ref, first_ref, second_ref):
    width = tile_ref.shape[1]
    half = width // 2
    wide = width + half
    blocks = []
    for part in range(2):
        upper = jnp.concatenate([own_ref[part, :half], right_ref[part]], axis=1)
        lower = jnp.concatenate([below_ref[part], tile_ref[part]], axis=1)
        blocks.append(jnp.concatenate([upper, lower], axis=0))
    block = jnp.concatenate(blocks, axis=1)
    strips = [dot(rows_ref[...], block[top : top + width]).astype(jnp.bfloat16) for top in (0, half)]
    for place, out_ref in enumerate((first_ref, second_ref)):
        mine = [strip[place * half : (place + 1) * half, part * wide : (part + 1) * wide] for part in range(2) for strip in strips]
        out_ref[...] = dot(jnp.concatenate(mine, axis=0), columns_ref[place]).astype(jnp.bfloat16)


def forward(probe_ref, band_ref, patch_ref, spread_ref, first, last):
    for level in range(first, last + 1):
        if level == 0:
            spread_ref[0] = probe_ref[...]
        else:
            wave = complex_mul(spread_ref[level - 1], patch_ref[level - 1], 1.0).astype(jnp.bfloat16)
            spread = sandwich(band_ref[0], band_ref[1], wave, band_ref[2], band_ref[3])
            spread_ref[level] = spread.astype(jnp.bfloat16)


def head_kernel(probe_ref, band_ref, p0_ref, p1_ref, spread_ref, patch_ref):
    cut = lax.axis_index("cuts")

    @pl.when(cut < 2)
    def _():
        patch_ref[cut] = p0_ref[...]
        patch_ref[1 - cut] = p1_ref[...]
        forward(probe_ref, band_ref, patch_ref, spread_ref, 0, 2)


def chain_kernel(
    probe_ref, p0_ref, p1_ref, p2_ref, p3_ref, level_ref, far_level_ref, band_ref, fourier_ref, head_ref, mine_ref, other_ref, patch_ref, spread_ref, back_ref
):
    width = probe_ref.shape[1]
    cut = lax.axis_index("cuts")
    for mask, ref in enumerate((p0_ref, p1_ref, p2_ref, p3_ref)):
        patch_ref[lax.bitwise_xor(cut, mask)] = ref[...]

    @pl.when(cut < 2)
    def _():
        spread_ref[0:3] = head_ref[...]

    @pl.when(cut >= 2)
    def _():
        forward(probe_ref, band_ref, patch_ref, spread_ref, 0, 2)

    forward(probe_ref, band_ref, patch_ref, spread_ref, 3, 3)
    fourier_r, fourier_i = fourier_ref[0], fourier_ref[1]
    wave = complex_mul(spread_ref[3], patch_ref[3], 1.0).astype(jnp.bfloat16)
    far = sandwich(fourier_r, fourier_i, wave, fourier_r, fourier_i)
    far_r, far_i = far[:width], far[width:]
    rows = width // 2
    level, far_level = level_ref[:rows, :].astype(jnp.float32), far_level_ref[:rows, :].astype(jnp.float32)
    level = jnp.concatenate([jnp.where(cut < 2, level, far_level), jnp.where(cut < 2, far_level, level)], axis=0)
    live = level_ref[rows : rows + 1, :].astype(jnp.float32)
    excess = 2.0 * live * (far_r * far_r + far_i * far_i - level)
    residual = jnp.concatenate([excess * far_r, excess * far_i], axis=0).astype(jnp.bfloat16)
    back_ref[...] = sandwich(fourier_r, -fourier_i, residual, fourier_r, -fourier_i).astype(jnp.bfloat16)

    def term(level):
        value = complex_mul(spread_ref[level], back_ref[...], -1.0).astype(jnp.bfloat16)

        @pl.when(level == cut)
        def _():
            mine_ref[...] = value

        @pl.when(level != cut)
        def _():
            other_ref[...] = value

    def carry(level):
        carried = complex_mul(patch_ref[level], back_ref[...], -1.0).astype(jnp.bfloat16)
        back = sandwich(band_ref[2], -band_ref[3], carried, band_ref[0], -band_ref[1])
        back_ref[...] = back.astype(jnp.bfloat16)

    @pl.when(cut >= 2)
    def _():
        term(3)

    carry(3)

    @pl.when(cut >= 2)
    def _():
        term(2)

    @pl.when(cut < 2)
    def _():
        carry(2)
        term(1)
        carry(1)
        term(0)


def scatter_kernel(rows_ref, columns_ref, mine_ref, other_ref, tile_ref, below_ref, right_ref, own_ref):
    width = tile_ref.shape[1]
    half = width // 2
    strips = []
    for place, ref in enumerate((mine_ref, other_ref)):
        field = jnp.concatenate([ref[:width, :], ref[width:, :]], axis=1)
        strips.append(dot(rows_ref[place], field).astype(jnp.bfloat16))
    for part in range(2):
        strip = jnp.concatenate([strip[:, part * width : (part + 1) * width] for strip in strips], axis=1)
        total = dot(strip, columns_ref[...])
        tile_ref[part] = total[half:, half:]
        below_ref[part] = total[half:, :half].astype(jnp.bfloat16)
        right_ref[part] = total[:half, half:].astype(jnp.bfloat16)
        own_ref[part] = total[:half, :half].astype(jnp.bfloat16)


def lower_kernel(tile_ref, right_ref, out_ref):
    half = right_ref.shape[1]
    out_ref[...] = tile_ref[:, half:, :] + right_ref[...].astype(jnp.float32)


def total_kernel(tile_ref, below_ref, lower_ref, own_ref, out_ref):
    half = lower_ref.shape[1]
    below = below_ref[...].astype(jnp.float32)
    own = own_ref[...].astype(jnp.float32)
    out_ref[0, :, :half, :half] = tile_ref[:, :half, :half]
    out_ref[0, :, :half, half:] = tile_ref[:, :half, half:] + below[:, :half]
    out_ref[0, :, half:, :half] = lower_ref[:, :, :half]
    out_ref[0, :, half:, half:] = lower_ref[:, :, half:] + below[:, half:] + own


VMEM = pl.BlockSpec(memory_space=pltpu.VMEM)
SMEM = pl.BlockSpec(memory_space=pltpu.SMEM)
PARAMS = pltpu.CompilerParams(vmem_limit_bytes=48 * 1024 * 1024)


def shaped(*shape, dtype=jnp.bfloat16):
    return jax.ShapeDtypeStruct(shape, dtype)


def kernel(body, name, in_specs, out_shape, scratch=()):
    return pl.pallas_call(
        body, in_specs=in_specs, out_specs=[VMEM] * len(out_shape), out_shape=out_shape, scratch_shapes=scratch, compiler_params=PARAMS, name=name
    )


def local(object_slices, probe, fresnel_taps, offsets, counts, measured):
    width = probe.shape[1]
    half = width // 2
    wide = width + half
    full = shaped(2 * width, width)
    part = shaped(width, width)
    row_tiles = max(lax.axis_size("tile") // 16, 2)
    probe = probe.reshape(2 * width, width)
    fourier = jnp.asarray(fourier_matrix(width), jnp.bfloat16)

    far_tile = crossed(object_slices[0], "cuts", 2)
    tile, below, right = kernel(cut_kernel, "cut", [VMEM], [shaped(2, width, width), shaped(2, width, half), shaped(2, half, width)])(
        object_slices[0]
    )
    (own,) = kernel(seal_kernel, "seal", [VMEM, VMEM], [shaped(2, half + 16, half)])(tile, offsets)
    below = passed_along(below, "tile", 1)
    right = passed_along(right, "tile", row_tiles)
    own = passed_along(own, "tile", row_tiles + 1)
    below, far_tile = lax.optimization_barrier((below, far_tile))
    far_below = crossed(below, "cuts", 2)
    far_right = crossed(right, "cuts", 2)
    far_own = crossed(own, "cuts", 2)
    level = shaped(half + 16, width)
    band, level = kernel(band_kernel, "band", [SMEM, VMEM, VMEM], [shaped(4, width, width), level])(counts, fresnel_taps, measured)
    level, right = lax.optimization_barrier((level, right))
    level = passed_along(level, "tile", row_tiles + 1)
    rows, columns, rows_back, columns_back = kernel(
        window_kernel,
        "window",
        [VMEM],
        [part, shaped(2, wide, width), shaped(2, wide, width), shaped(2 * width, wide)],
    )(own)
    first, second = kernel(extract_kernel, "near", [VMEM] * 6, [full, full])(rows, columns, tile, below, right, own)
    swapped = crossed(second, "cuts", 1)
    far_level = crossed(level, "cuts", 2)
    straight, far_second = kernel(extract_kernel, "far", [VMEM] * 6, [full, full])(rows, columns, far_tile, far_below, far_right, far_own)
    far_second, far_level = lax.optimization_barrier((far_second, far_level))
    diagonal = crossed(far_second, "cuts", 1)
    (head,) = kernel(head_kernel, "head", [VMEM] * 4, [shaped(3, 2 * width, width)], [pltpu.VMEM((2, 2 * width, width), jnp.bfloat16)])(
        probe, band, first, swapped
    )
    mine, other = kernel(
        chain_kernel,
        "chain",
        [VMEM] * 10,
        [full, full],
        [
            pltpu.VMEM((4, 2 * width, width), jnp.bfloat16),
            pltpu.VMEM((4, 2 * width, width), jnp.bfloat16),
            pltpu.VMEM((2 * width, width), jnp.bfloat16),
        ],
    )(probe, first, swapped, straight, diagonal, level, far_level, band, fourier, head)
    other = crossed(other, "cuts", 1)
    total, below, right, own = kernel(
        scatter_kernel,
        "scatter",
        [VMEM] * 4,
        [shaped(2, width, width, dtype=jnp.float32), shaped(2, width, half), shaped(2, half, width), shaped(2, half, half)],
    )(rows_back, columns_back, mine, other)
    below = passed_along(below, "tile", -1)
    right = passed_along(right, "tile", -row_tiles)
    own = passed_along(own, "tile", -row_tiles - 1)
    (lower,) = kernel(lower_kernel, "lower", [VMEM] * 2, [shaped(2, half, width, dtype=jnp.float32)])(total, right)
    (out,) = kernel(total_kernel, "total", [VMEM] * 4, [shaped(1, 2, width, width, dtype=jnp.float32)])(total, below, lower, own)
    return out


def solution(mesh):
    return jax.shard_map(
        local,
        mesh=mesh,
        in_specs=(
            P("cuts", None, "tile", None),
            P(),
            P(),
            P("tile", None),
            P("tile"),
            P("tile", None, None),
        ),
        out_specs=P("cuts", None, "tile", None),
        check_vma=False,
    )
```

```python
import jax
import jax.numpy as jnp
import numpy as np
from jax import lax
from jax.experimental import pallas as pl
from jax.experimental.pallas import tpu as pltpu
from jax.sharding import PartitionSpec as P


def passed_along(value, axis, steps):
    count = lax.axis_size(axis)
    pairs = [(source, (source + steps) % count) for source in range(count)]
    return lax.ppermute(value, axis, pairs)


def crossed(value, axis, mask):
    pairs = [(source, source ^ mask) for source in range(lax.axis_size(axis))]
    return lax.ppermute(value, axis, pairs)


def fourier_matrix(width):
    index = np.arange(width)
    angle = 2.0 * np.pi * (index[:, None] * index[None, :] % width) / width
    return np.stack([np.cos(angle), -np.sin(angle)]) / np.sqrt(width)


def dot(left, right):
    return jnp.dot(left, right, preferred_element_type=jnp.float32)


def sandwich(left_real, left_imag, field, right_real, right_imag):
    right = jnp.concatenate([right_real, right_imag], axis=0)
    top = dot(jnp.concatenate([left_real, -left_imag], axis=1), field).astype(jnp.bfloat16)
    bottom = dot(jnp.concatenate([left_imag, left_real], axis=1), field).astype(jnp.bfloat16)
    real = dot(jnp.concatenate([top, -bottom], axis=1), right)
    imag = dot(jnp.concatenate([bottom, top], axis=1), right)
    return jnp.concatenate([real, imag], axis=0)


def complex_mul(first, second, sign):
    width = first.shape[1]
    fr = first[:width].astype(jnp.float32)
    fi = first[width:].astype(jnp.float32) * sign
    sr = second[:width].astype(jnp.float32)
    si = second[width:].astype(jnp.float32)
    return jnp.concatenate([fr * sr - fi * si, fr * si + fi * sr], axis=0)


def band_kernel(counts_ref, taps_ref, measured_ref, band_ref, level_ref):
    width = band_ref.shape[1]
    half = taps_ref.shape[1] // 2
    core = lax.rem(lax.axis_index("cuts"), 2)
    rows = width // 2
    first = pl.multiple_of(lax.axis_index("cuts") // 2 * rows, rows)
    level_ref[:rows, :] = measured_ref[core, pl.ds(first, rows), :].astype(jnp.bfloat16)
    live = (core < counts_ref[0]).astype(jnp.float32)
    level_ref[rows:, :] = jnp.full((level_ref.shape[0] - rows, width), live, jnp.float32).astype(jnp.bfloat16)
    rows = lax.broadcasted_iota(jnp.int32, (width, width), 0)
    columns = lax.broadcasted_iota(jnp.int32, (width, width), 1)
    inside = jnp.abs(columns - rows) <= half
    for part in range(2):
        line = taps_ref[part : part + 1, :].astype(jnp.float32)
        filler = jnp.zeros((1, width - line.shape[1]), jnp.float32)
        line = jnp.concatenate([line, filler], axis=1)
        spread = jnp.broadcast_to(line, (width, width))
        turned = pltpu.roll(spread, width - half, 1, stride=1, stride_axis=0)
        band = jnp.where(inside, turned, 0.0)
        band_ref[part] = band.astype(jnp.bfloat16)
        band_ref[part + 2] = band.T.astype(jnp.bfloat16)


def cut_kernel(tile_ref, whole_ref, below_ref, right_ref):
    half = right_ref.shape[1]
    whole_ref[...] = tile_ref[...]
    below_ref[...] = tile_ref[:, :, half:]
    right_ref[...] = tile_ref[:, half:, :]


def seal_kernel(tile_ref, offsets_ref, own_ref):
    half = tile_ref.shape[1] // 2
    own_ref[:, :half, :] = tile_ref[:, half:, half:]
    shape = (own_ref.shape[1] - half, half)
    line = lax.broadcasted_iota(jnp.int32, shape, 0)
    lines = jnp.zeros(shape, jnp.float32)
    for index in range(4):
        value = offsets_ref[index // 2 : index // 2 + 1, index % 2 : index % 2 + 1].astype(jnp.float32)
        lines = jnp.where(line == index, value, lines)
    for part in range(2):
        own_ref[part, half:, :] = lines.astype(jnp.bfloat16)


def window_kernel(own_ref, rows_ref, columns_ref, rows_back_ref, columns_back_ref):
    half = own_ref.shape[2]
    width = 2 * half
    core = lax.rem(lax.axis_index("cuts"), 2)
    lines = own_ref[0, half:, :].astype(jnp.float32).astype(jnp.int32) - half

    def placed(shape, axis, shift):
        i = lax.broadcasted_iota(jnp.int32, shape, axis)
        j = lax.broadcasted_iota(jnp.int32, shape, 1 - axis)
        shift = jnp.concatenate([shift] * (shape[1] // half), axis=1)
        return jnp.where(j - i == shift, 1.0, 0.0).astype(jnp.bfloat16)

    for place in range(2):
        second = core != place
        row = jnp.where(second, lines[2:3], lines[0:1])
        column = jnp.where(second, lines[3:4], lines[1:2])
        rows_ref[place * half : (place + 1) * half, :] = placed((half, width), 0, row)
        columns_ref[place] = placed((width + half, width), 1, column)
        rows_back_ref[place] = placed((width + half, width), 1, row)
        columns_back_ref[place * width : (place + 1) * width, :] = placed((width, width + half), 0, column)


def extract_kernel(rows_ref, columns_ref, tile_ref, below_ref, right_ref, own_ref, first_ref, second_ref):
    width = tile_ref.shape[1]
    half = width // 2
    wide = width + half
    blocks = []
    for part in range(2):
        upper = jnp.concatenate([own_ref[part, :half], right_ref[part]], axis=1)
        lower = jnp.concatenate([below_ref[part], tile_ref[part]], axis=1)
        blocks.append(jnp.concatenate([upper, lower], axis=0))
    block = jnp.concatenate(blocks, axis=1)
    strips = [dot(rows_ref[...], block[top : top + width]).astype(jnp.bfloat16) for top in (0, half)]
    for place, out_ref in enumerate((first_ref, second_ref)):
        mine = [strip[place * half : (place + 1) * half, part * wide : (part + 1) * wide] for part in range(2) for strip in strips]
        out_ref[...] = dot(jnp.concatenate(mine, axis=0), columns_ref[place]).astype(jnp.bfloat16)


def forward(probe_ref, band_ref, patch_ref, spread_ref, first, last):
    for level in range(first, last + 1):
        if level == 0:
            spread_ref[0] = probe_ref[...]
        else:
            wave = complex_mul(spread_ref[level - 1], patch_ref[level - 1], 1.0).astype(jnp.bfloat16)
            spread = sandwich(band_ref[0], band_ref[1], wave, band_ref[2], band_ref[3])
            spread_ref[level] = spread.astype(jnp.bfloat16)


def head_kernel(probe_ref, band_ref, p0_ref, p1_ref, spread_ref, patch_ref):
    cut = lax.axis_index("cuts")

    @pl.when(cut < 2)
    def _():
        patch_ref[cut] = p0_ref[...]
        patch_ref[1 - cut] = p1_ref[...]
        forward(probe_ref, band_ref, patch_ref, spread_ref, 0, 2)


def chain_kernel(
    probe_ref, p0_ref, p1_ref, p2_ref, p3_ref, level_ref, far_level_ref, band_ref, fourier_ref, head_ref, mine_ref, other_ref, patch_ref, spread_ref, back_ref
):
    width = probe_ref.shape[1]
    cut = lax.axis_index("cuts")
    for mask, ref in enumerate((p0_ref, p1_ref, p2_ref, p3_ref)):
        patch_ref[lax.bitwise_xor(cut, mask)] = ref[...]

    @pl.when(cut < 2)
    def _():
        spread_ref[0:3] = head_ref[...]

    @pl.when(cut >= 2)
    def _():
        forward(probe_ref, band_ref, patch_ref, spread_ref, 0, 2)

    forward(probe_ref, band_ref, patch_ref, spread_ref, 3, 3)
    fourier_r, fourier_i = fourier_ref[0], fourier_ref[1]
    wave = complex_mul(spread_ref[3], patch_ref[3], 1.0).astype(jnp.bfloat16)
    far = sandwich(fourier_r, fourier_i, wave, fourier_r, fourier_i)
    far_r, far_i = far[:width], far[width:]
    rows = width // 2
    level, far_level = level_ref[:rows, :].astype(jnp.float32), far_level_ref[:rows, :].astype(jnp.float32)
    level = jnp.concatenate([jnp.where(cut < 2, level, far_level), jnp.where(cut < 2, far_level, level)], axis=0)
    live = level_ref[rows : rows + 1, :].astype(jnp.float32)
    excess = 2.0 * live * (far_r * far_r + far_i * far_i - level)
    residual = jnp.concatenate([excess * far_r, excess * far_i], axis=0).astype(jnp.bfloat16)
    back_ref[...] = sandwich(fourier_r, -fourier_i, residual, fourier_r, -fourier_i).astype(jnp.bfloat16)

    def term(level):
        value = complex_mul(spread_ref[level], back_ref[...], -1.0).astype(jnp.bfloat16)

        @pl.when(level == cut)
        def _():
            mine_ref[...] = value

        @pl.when(level != cut)
        def _():
            other_ref[...] = value

    def carry(level):
        carried = complex_mul(patch_ref[level], back_ref[...], -1.0).astype(jnp.bfloat16)
        back = sandwich(band_ref[2], -band_ref[3], carried, band_ref[0], -band_ref[1])
        back_ref[...] = back.astype(jnp.bfloat16)

    @pl.when(cut >= 2)
    def _():
        term(3)

    carry(3)

    @pl.when(cut >= 2)
    def _():
        term(2)

    @pl.when(cut < 2)
    def _():
        carry(2)
        term(1)
        carry(1)
        term(0)


def scatter_kernel(rows_ref, columns_ref, mine_ref, other_ref, tile_ref, below_ref, right_ref, own_ref):
    width = tile_ref.shape[1]
    half = width // 2
    strips = []
    for place, ref in enumerate((mine_ref, other_ref)):
        field = jnp.concatenate([ref[:width, :], ref[width:, :]], axis=1)
        strips.append(dot(rows_ref[place], field).astype(jnp.bfloat16))
    for part in range(2):
        strip = jnp.concatenate([strip[:, part * width : (part + 1) * width] for strip in strips], axis=1)
        total = dot(strip, columns_ref[...])
        tile_ref[part] = total[half:, half:]
        below_ref[part] = total[half:, :half].astype(jnp.bfloat16)
        right_ref[part] = total[:half, half:].astype(jnp.bfloat16)
        own_ref[part] = total[:half, :half].astype(jnp.bfloat16)


def total_kernel(tile_ref, below_ref, right_ref, out_ref, quarter_ref):
    half = right_ref.shape[1]
    below = below_ref[...].astype(jnp.float32)
    right = right_ref[...].astype(jnp.float32)
    quarter = tile_ref[:, half:, half:] + below[:, half:] + right[:, :, half:]
    out_ref[0, :, :half, :half] = tile_ref[:, :half, :half]
    out_ref[0, :, :half, half:] = tile_ref[:, :half, half:] + below[:, :half]
    out_ref[0, :, half:, :half] = tile_ref[:, half:, :half] + right[:, :, :half]
    out_ref[0, :, half:, half:] = quarter
    quarter_ref[...] = quarter


def quarter_kernel(out_ref, quarter_ref, own_ref, same_ref, sum_ref, sem):
    half = quarter_ref.shape[1]
    sum_ref[...] = quarter_ref[...] + own_ref[...].astype(jnp.float32)
    copy = pltpu.make_async_copy(sum_ref, same_ref.at[0, :, pl.ds(half, half), pl.ds(half, half)], sem)
    copy.start()
    copy.wait()


VMEM = pl.BlockSpec(memory_space=pltpu.VMEM)
ANY = pl.BlockSpec(memory_space=pl.ANY)
SMEM = pl.BlockSpec(memory_space=pltpu.SMEM)
PARAMS = pltpu.CompilerParams(vmem_limit_bytes=48 * 1024 * 1024)


def shaped(*shape, dtype=jnp.bfloat16):
    return jax.ShapeDtypeStruct(shape, dtype)


def kernel(body, name, in_specs, out_shape, scratch=()):
    return pl.pallas_call(
        body, in_specs=in_specs, out_specs=[VMEM] * len(out_shape), out_shape=out_shape, scratch_shapes=scratch, compiler_params=PARAMS, name=name
    )


def local(object_slices, probe, fresnel_taps, offsets, counts, measured):
    width = probe.shape[1]
    half = width // 2
    wide = width + half
    full = shaped(2 * width, width)
    part = shaped(width, width)
    row_tiles = max(lax.axis_size("tile") // 16, 2)
    probe = probe.reshape(2 * width, width)
    fourier = jnp.asarray(fourier_matrix(width), jnp.bfloat16)

    far_tile = crossed(object_slices[0], "cuts", 2)
    tile, below, right = kernel(cut_kernel, "cut", [VMEM], [shaped(2, width, width), shaped(2, width, half), shaped(2, half, width)])(
        object_slices[0]
    )
    (own,) = kernel(seal_kernel, "seal", [VMEM, VMEM], [shaped(2, half + 16, half)])(tile, offsets)
    below = passed_along(below, "tile", 1)
    right = passed_along(right, "tile", row_tiles)
    own = passed_along(own, "tile", row_tiles + 1)
    below, far_tile = lax.optimization_barrier((below, far_tile))
    far_below = crossed(below, "cuts", 2)
    far_right = crossed(right, "cuts", 2)
    far_own = crossed(own, "cuts", 2)
    level = shaped(half + 16, width)
    band, level = kernel(band_kernel, "band", [SMEM, VMEM, VMEM], [shaped(4, width, width), level])(counts, fresnel_taps, measured)
    level, right = lax.optimization_barrier((level, right))
    level = passed_along(level, "tile", row_tiles + 1)
    rows, columns, rows_back, columns_back = kernel(
        window_kernel,
        "window",
        [VMEM],
        [part, shaped(2, wide, width), shaped(2, wide, width), shaped(2 * width, wide)],
    )(own)
    first, second = kernel(extract_kernel, "near", [VMEM] * 6, [full, full])(rows, columns, tile, below, right, own)
    swapped = crossed(second, "cuts", 1)
    far_level = crossed(level, "cuts", 2)
    straight, far_second = kernel(extract_kernel, "far", [VMEM] * 6, [full, full])(rows, columns, far_tile, far_below, far_right, far_own)
    far_second, far_level = lax.optimization_barrier((far_second, far_level))
    diagonal = crossed(far_second, "cuts", 1)
    (head,) = kernel(head_kernel, "head", [VMEM] * 4, [shaped(3, 2 * width, width)], [pltpu.VMEM((2, 2 * width, width), jnp.bfloat16)])(
        probe, band, first, swapped
    )
    mine, other = kernel(
        chain_kernel,
        "chain",
        [VMEM] * 10,
        [full, full],
        [
            pltpu.VMEM((4, 2 * width, width), jnp.bfloat16),
            pltpu.VMEM((4, 2 * width, width), jnp.bfloat16),
            pltpu.VMEM((2 * width, width), jnp.bfloat16),
        ],
    )(probe, first, swapped, straight, diagonal, level, far_level, band, fourier, head)
    other = crossed(other, "cuts", 1)
    total, below, right, own = kernel(
        scatter_kernel,
        "scatter",
        [VMEM] * 4,
        [shaped(2, width, width, dtype=jnp.float32), shaped(2, width, half), shaped(2, half, width), shaped(2, half, half)],
    )(rows_back, columns_back, mine, other)
    below = passed_along(below, "tile", -1)
    right = passed_along(right, "tile", -row_tiles)
    own = passed_along(own, "tile", -row_tiles - 1)
    whole = shaped(1, 2, width, width, dtype=jnp.float32)
    quarter = shaped(2, half, half, dtype=jnp.float32)
    out, quarter = kernel(total_kernel, "total", [VMEM] * 3, [whole, quarter])(total, below, right)
    out = pl.pallas_call(
        quarter_kernel,
        in_specs=[ANY, VMEM, VMEM],
        out_specs=ANY,
        out_shape=whole,
        input_output_aliases={0: 0},
        scratch_shapes=[pltpu.VMEM((2, half, half), jnp.float32), pltpu.SemaphoreType.DMA],
        compiler_params=PARAMS,
        name="quarter",
    )(out, quarter, own)
    return out


def solution(mesh):
    return jax.shard_map(
        local,
        mesh=mesh,
        in_specs=(
            P("cuts", None, "tile", None),
            P(),
            P(),
            P("tile", None),
            P("tile"),
            P("tile", None, None),
        ),
        out_specs=P("cuts", None, "tile", None),
        check_vma=False,
    )
```

```python
import jax
import jax.numpy as jnp
import numpy as np
from jax import lax
from jax.experimental import pallas as pl
from jax.experimental.pallas import tpu as pltpu
from jax.sharding import PartitionSpec as P


def passed_along(value, axis, steps):
    count = lax.axis_size(axis)
    pairs = [(source, (source + steps) % count) for source in range(count)]
    return lax.ppermute(value, axis, pairs)


def detoured(value, mask):
    cuts = lax.axis_size("cuts")
    return lax.ppermute(value, ("tile", "cuts"), [(cuts + cut, cut ^ mask) for cut in range(cuts)])


def crossed(value, axis, mask):
    pairs = [(source, source ^ mask) for source in range(lax.axis_size(axis))]
    return lax.ppermute(value, axis, pairs)


def fourier_matrix(width):
    index = np.arange(width)
    angle = 2.0 * np.pi * (index[:, None] * index[None, :] % width) / width
    return np.stack([np.cos(angle), -np.sin(angle)]) / np.sqrt(width)


def dot(left, right):
    return jnp.dot(left, right, preferred_element_type=jnp.float32)


def sandwich(left_real, left_imag, field, right_real, right_imag):
    right = jnp.concatenate([right_real, right_imag], axis=0)
    top = dot(jnp.concatenate([left_real, -left_imag], axis=1), field).astype(jnp.bfloat16)
    bottom = dot(jnp.concatenate([left_imag, left_real], axis=1), field).astype(jnp.bfloat16)
    real = dot(jnp.concatenate([top, -bottom], axis=1), right)
    imag = dot(jnp.concatenate([bottom, top], axis=1), right)
    return jnp.concatenate([real, imag], axis=0)


def complex_mul(first, second, sign):
    width = first.shape[1]
    fr = first[:width].astype(jnp.float32)
    fi = first[width:].astype(jnp.float32) * sign
    sr = second[:width].astype(jnp.float32)
    si = second[width:].astype(jnp.float32)
    return jnp.concatenate([fr * sr - fi * si, fr * si + fi * sr], axis=0)


def band_kernel(counts_ref, taps_ref, measured_ref, band_ref, level_ref):
    width = band_ref.shape[1]
    half = taps_ref.shape[1] // 2
    core = lax.rem(lax.axis_index("cuts"), 2)
    rows = width // 2
    first = pl.multiple_of(lax.axis_index("cuts") // 2 * rows, rows)
    level_ref[:rows, :] = measured_ref[core, pl.ds(first, rows), :].astype(jnp.bfloat16)
    live = (core < counts_ref[0]).astype(jnp.float32)
    level_ref[rows:, :] = jnp.full((level_ref.shape[0] - rows, width), live, jnp.float32).astype(jnp.bfloat16)
    rows = lax.broadcasted_iota(jnp.int32, (width, width), 0)
    columns = lax.broadcasted_iota(jnp.int32, (width, width), 1)
    inside = jnp.abs(columns - rows) <= half
    for part in range(2):
        line = taps_ref[part : part + 1, :].astype(jnp.float32)
        filler = jnp.zeros((1, width - line.shape[1]), jnp.float32)
        line = jnp.concatenate([line, filler], axis=1)
        spread = jnp.broadcast_to(line, (width, width))
        turned = pltpu.roll(spread, width - half, 1, stride=1, stride_axis=0)
        band = jnp.where(inside, turned, 0.0)
        band_ref[part] = band.astype(jnp.bfloat16)
        band_ref[part + 2] = band.T.astype(jnp.bfloat16)


def cut_kernel(tile_ref, whole_ref, below_ref, right_ref):
    half = right_ref.shape[1]
    whole_ref[...] = tile_ref[...]
    below_ref[...] = tile_ref[:, :, half:]
    right_ref[...] = tile_ref[:, half:, :]


def seal_kernel(tile_ref, offsets_ref, own_ref):
    half = tile_ref.shape[1] // 2
    own_ref[:, :half, :] = tile_ref[:, half:, half:]
    shape = (own_ref.shape[1] - half, half)
    line = lax.broadcasted_iota(jnp.int32, shape, 0)
    lines = jnp.zeros(shape, jnp.float32)
    for index in range(4):
        value = offsets_ref[index // 2 : index // 2 + 1, index % 2 : index % 2 + 1].astype(jnp.float32)
        lines = jnp.where(line == index, value, lines)
    for part in range(2):
        own_ref[part, half:, :] = lines.astype(jnp.bfloat16)


def quarter_of(own_ref, detour_ref):
    return jnp.where(lax.axis_index("tile") == 0, detour_ref[...], own_ref[...])


def window_kernel(own_ref, detour_ref, rows_ref, columns_ref, rows_back_ref, columns_back_ref):
    half = own_ref.shape[2]
    width = 2 * half
    core = lax.rem(lax.axis_index("cuts"), 2)
    lines = quarter_of(own_ref, detour_ref)[0, half:, :].astype(jnp.float32).astype(jnp.int32) - half

    def placed(shape, axis, shift):
        i = lax.broadcasted_iota(jnp.int32, shape, axis)
        j = lax.broadcasted_iota(jnp.int32, shape, 1 - axis)
        shift = jnp.concatenate([shift] * (shape[1] // half), axis=1)
        return jnp.where(j - i == shift, 1.0, 0.0).astype(jnp.bfloat16)

    for place in range(2):
        second = core != place
        row = jnp.where(second, lines[2:3], lines[0:1])
        column = jnp.where(second, lines[3:4], lines[1:2])
        rows_ref[place * half : (place + 1) * half, :] = placed((half, width), 0, row)
        columns_ref[place] = placed((width + half, width), 1, column)
        rows_back_ref[place] = placed((width + half, width), 1, row)
        columns_back_ref[place * width : (place + 1) * width, :] = placed((width, width + half), 0, column)


def extract_kernel(rows_ref, columns_ref, tile_ref, below_ref, right_ref, own_ref, detour_ref, first_ref, second_ref):
    width = tile_ref.shape[1]
    half = width // 2
    wide = width + half
    blocks = []
    quarter = quarter_of(own_ref, detour_ref)
    for part in range(2):
        upper = jnp.concatenate([quarter[part, :half], right_ref[part]], axis=1)
        lower = jnp.concatenate([below_ref[part], tile_ref[part]], axis=1)
        blocks.append(jnp.concatenate([upper, lower], axis=0))
    block = jnp.concatenate(blocks, axis=1)
    strips = [dot(rows_ref[...], block[top : top + width]).astype(jnp.bfloat16) for top in (0, half)]
    for place, out_ref in enumerate((first_ref, second_ref)):
        mine = [strip[place * half : (place + 1) * half, part * wide : (part + 1) * wide] for part in range(2) for strip in strips]
        out_ref[...] = dot(jnp.concatenate(mine, axis=0), columns_ref[place]).astype(jnp.bfloat16)


def forward(probe_ref, band_ref, patch_ref, spread_ref, first, last):
    for level in range(first, last + 1):
        if level == 0:
            spread_ref[0] = probe_ref[...]
        else:
            wave = complex_mul(spread_ref[level - 1], patch_ref[level - 1], 1.0).astype(jnp.bfloat16)
            spread = sandwich(band_ref[0], band_ref[1], wave, band_ref[2], band_ref[3])
            spread_ref[level] = spread.astype(jnp.bfloat16)


def head_kernel(probe_ref, band_ref, p0_ref, p1_ref, spread_ref, patch_ref):
    cut = lax.axis_index("cuts")

    @pl.when(cut < 2)
    def _():
        patch_ref[cut] = p0_ref[...]
        patch_ref[1 - cut] = p1_ref[...]
        forward(probe_ref, band_ref, patch_ref, spread_ref, 0, 2)


def chain_kernel(
    probe_ref, p0_ref, p1_ref, p2_ref, p3_ref, level_ref, far_level_ref, band_ref, fourier_ref, head_ref, mine_ref, other_ref, patch_ref, spread_ref, back_ref
):
    width = probe_ref.shape[1]
    cut = lax.axis_index("cuts")
    for mask, ref in enumerate((p0_ref, p1_ref, p2_ref, p3_ref)):
        patch_ref[lax.bitwise_xor(cut, mask)] = ref[...]

    @pl.when(cut < 2)
    def _():
        spread_ref[0:3] = head_ref[...]

    @pl.when(cut >= 2)
    def _():
        forward(probe_ref, band_ref, patch_ref, spread_ref, 0, 2)

    forward(probe_ref, band_ref, patch_ref, spread_ref, 3, 3)
    fourier_r, fourier_i = fourier_ref[0], fourier_ref[1]
    wave = complex_mul(spread_ref[3], patch_ref[3], 1.0).astype(jnp.bfloat16)
    far = sandwich(fourier_r, fourier_i, wave, fourier_r, fourier_i)
    far_r, far_i = far[:width], far[width:]
    rows = width // 2
    level, far_level = level_ref[:rows, :].astype(jnp.float32), far_level_ref[:rows, :].astype(jnp.float32)
    level = jnp.concatenate([jnp.where(cut < 2, level, far_level), jnp.where(cut < 2, far_level, level)], axis=0)
    live = level_ref[rows : rows + 1, :].astype(jnp.float32)
    excess = 2.0 * live * (far_r * far_r + far_i * far_i - level)
    residual = jnp.concatenate([excess * far_r, excess * far_i], axis=0).astype(jnp.bfloat16)
    back_ref[...] = sandwich(fourier_r, -fourier_i, residual, fourier_r, -fourier_i).astype(jnp.bfloat16)

    def term(level):
        value = complex_mul(spread_ref[level], back_ref[...], -1.0).astype(jnp.bfloat16)

        @pl.when(level == cut)
        def _():
            mine_ref[...] = value

        @pl.when(level != cut)
        def _():
            other_ref[...] = value

    def carry(level):
        carried = complex_mul(patch_ref[level], back_ref[...], -1.0).astype(jnp.bfloat16)
        back = sandwich(band_ref[2], -band_ref[3], carried, band_ref[0], -band_ref[1])
        back_ref[...] = back.astype(jnp.bfloat16)

    @pl.when(cut >= 2)
    def _():
        term(3)

    carry(3)

    @pl.when(cut >= 2)
    def _():
        term(2)

    @pl.when(cut < 2)
    def _():
        carry(2)
        term(1)
        carry(1)
        term(0)


def scatter_kernel(rows_ref, columns_ref, mine_ref, other_ref, tile_ref, below_ref, right_ref, own_ref):
    width = tile_ref.shape[1]
    half = width // 2
    strips = []
    for place, ref in enumerate((mine_ref, other_ref)):
        field = jnp.concatenate([ref[:width, :], ref[width:, :]], axis=1)
        strips.append(dot(rows_ref[place], field).astype(jnp.bfloat16))
    for part in range(2):
        strip = jnp.concatenate([strip[:, part * width : (part + 1) * width] for strip in strips], axis=1)
        total = dot(strip, columns_ref[...])
        tile_ref[part] = total[half:, half:]
        below_ref[part] = total[half:, :half].astype(jnp.bfloat16)
        right_ref[part] = total[:half, half:].astype(jnp.bfloat16)
        own_ref[part] = total[:half, :half].astype(jnp.bfloat16)


def total_kernel(tile_ref, below_ref, right_ref, out_ref, quarter_ref):
    half = right_ref.shape[1]
    below = below_ref[...].astype(jnp.float32)
    right = right_ref[...].astype(jnp.float32)
    quarter = tile_ref[:, half:, half:] + below[:, half:] + right[:, :, half:]
    out_ref[0, :, :half, :half] = tile_ref[:, :half, :half]
    out_ref[0, :, :half, half:] = tile_ref[:, :half, half:] + below[:, :half]
    out_ref[0, :, half:, :half] = tile_ref[:, half:, :half] + right[:, :, :half]
    out_ref[0, :, half:, half:] = quarter
    quarter_ref[...] = quarter


def quarter_kernel(out_ref, quarter_ref, own_ref, same_ref, sum_ref, sem):
    half = quarter_ref.shape[1]
    sum_ref[...] = quarter_ref[...] + own_ref[...].astype(jnp.float32)
    copy = pltpu.make_async_copy(sum_ref, same_ref.at[0, :, pl.ds(half, half), pl.ds(half, half)], sem)
    copy.start()
    copy.wait()


VMEM = pl.BlockSpec(memory_space=pltpu.VMEM)
ANY = pl.BlockSpec(memory_space=pl.ANY)
SMEM = pl.BlockSpec(memory_space=pltpu.SMEM)
PARAMS = pltpu.CompilerParams(vmem_limit_bytes=48 * 1024 * 1024)


def shaped(*shape, dtype=jnp.bfloat16):
    return jax.ShapeDtypeStruct(shape, dtype)


def kernel(body, name, in_specs, out_shape, scratch=()):
    return pl.pallas_call(
        body, in_specs=in_specs, out_specs=[VMEM] * len(out_shape), out_shape=out_shape, scratch_shapes=scratch, compiler_params=PARAMS, name=name
    )


def local(object_slices, probe, fresnel_taps, offsets, counts, measured):
    width = probe.shape[1]
    half = width // 2
    wide = width + half
    full = shaped(2 * width, width)
    part = shaped(width, width)
    row_tiles = max(lax.axis_size("tile") // 16, 2)
    probe = probe.reshape(2 * width, width)
    fourier = jnp.asarray(fourier_matrix(width), jnp.bfloat16)

    far_tile = crossed(object_slices[0], "cuts", 2)
    tile, below, right = kernel(cut_kernel, "cut", [VMEM], [shaped(2, width, width), shaped(2, width, half), shaped(2, half, width)])(
        object_slices[0]
    )
    (own,) = kernel(seal_kernel, "seal", [VMEM, VMEM], [shaped(2, half + 16, half)])(tile, offsets)
    below = passed_along(below, "tile", 1)
    right = passed_along(right, "tile", row_tiles)
    count = lax.axis_size("tile")
    last = count - row_tiles - 1
    detour = lax.ppermute(own, "tile", [(last, 1)])
    own = lax.ppermute(own, "tile", [(source, (source + row_tiles + 1) % count) for source in range(count) if source != last])
    far_detour = detoured(detour, 2)
    detour = detoured(detour, 0)
    below, far_tile = lax.optimization_barrier((below, far_tile))
    far_below = crossed(below, "cuts", 2)
    far_right = crossed(right, "cuts", 2)
    far_own = crossed(own, "cuts", 2)
    level = shaped(half + 16, width)
    band, level = kernel(band_kernel, "band", [SMEM, VMEM, VMEM], [shaped(4, width, width), level])(counts, fresnel_taps, measured)
    level, right = lax.optimization_barrier((level, right))
    level = passed_along(level, "tile", row_tiles + 1)
    rows, columns, rows_back, columns_back = kernel(
        window_kernel,
        "window",
        [VMEM] * 2,
        [part, shaped(2, wide, width), shaped(2, wide, width), shaped(2 * width, wide)],
    )(own, detour)
    first, second = kernel(extract_kernel, "near", [VMEM] * 7, [full, full])(rows, columns, tile, below, right, own, detour)
    swapped = crossed(second, "cuts", 1)
    far_level = crossed(level, "cuts", 2)
    straight, far_second = kernel(extract_kernel, "far", [VMEM] * 7, [full, full])(
        rows, columns, far_tile, far_below, far_right, far_own, far_detour
    )
    far_second, far_level = lax.optimization_barrier((far_second, far_level))
    diagonal = crossed(far_second, "cuts", 1)
    (head,) = kernel(head_kernel, "head", [VMEM] * 4, [shaped(3, 2 * width, width)], [pltpu.VMEM((2, 2 * width, width), jnp.bfloat16)])(
        probe, band, first, swapped
    )
    mine, other = kernel(
        chain_kernel,
        "chain",
        [VMEM] * 10,
        [full, full],
        [
            pltpu.VMEM((4, 2 * width, width), jnp.bfloat16),
            pltpu.VMEM((4, 2 * width, width), jnp.bfloat16),
            pltpu.VMEM((2 * width, width), jnp.bfloat16),
        ],
    )(probe, first, swapped, straight, diagonal, level, far_level, band, fourier, head)
    other = crossed(other, "cuts", 1)
    total, below, right, own = kernel(
        scatter_kernel,
        "scatter",
        [VMEM] * 4,
        [shaped(2, width, width, dtype=jnp.float32), shaped(2, width, half), shaped(2, half, width), shaped(2, half, half)],
    )(rows_back, columns_back, mine, other)
    below = passed_along(below, "tile", -1)
    right = passed_along(right, "tile", -row_tiles)
    own = passed_along(own, "tile", -row_tiles - 1)
    whole = shaped(1, 2, width, width, dtype=jnp.float32)
    quarter = shaped(2, half, half, dtype=jnp.float32)
    out, quarter = kernel(total_kernel, "total", [VMEM] * 3, [whole, quarter])(total, below, right)
    out = pl.pallas_call(
        quarter_kernel,
        in_specs=[ANY, VMEM, VMEM],
        out_specs=ANY,
        out_shape=whole,
        input_output_aliases={0: 0},
        scratch_shapes=[pltpu.VMEM((2, half, half), jnp.float32), pltpu.SemaphoreType.DMA],
        compiler_params=PARAMS,
        name="quarter",
    )(out, quarter, own)
    return out


def solution(mesh):
    return jax.shard_map(
        local,
        mesh=mesh,
        in_specs=(
            P("cuts", None, "tile", None),
            P(),
            P(),
            P("tile", None),
            P("tile"),
            P("tile", None, None),
        ),
        out_specs=P("cuts", None, "tile", None),
        check_vma=False,
    )
```

```python
import jax
import jax.numpy as jnp
import numpy as np
from jax import lax
from jax.experimental import pallas as pl
from jax.experimental.pallas import tpu as pltpu
from jax.sharding import PartitionSpec as P


def passed_along(value, axis, steps):
    count = lax.axis_size(axis)
    pairs = [(source, (source + steps) % count) for source in range(count)]
    return lax.ppermute(value, axis, pairs)


def crossed(value, axis, mask):
    pairs = [(source, source ^ mask) for source in range(lax.axis_size(axis))]
    return lax.ppermute(value, axis, pairs)


def fourier_matrix(width):
    index = np.arange(width)
    angle = 2.0 * np.pi * (index[:, None] * index[None, :] % width) / width
    return np.stack([np.cos(angle), -np.sin(angle)]) / np.sqrt(width)


def dot(left, right):
    return jnp.dot(left, right, preferred_element_type=jnp.float32)


def sandwich(left_real, left_imag, field, right_real, right_imag):
    right = jnp.concatenate([right_real, right_imag], axis=0)
    top = dot(jnp.concatenate([left_real, -left_imag], axis=1), field).astype(jnp.bfloat16)
    bottom = dot(jnp.concatenate([left_imag, left_real], axis=1), field).astype(jnp.bfloat16)
    real = dot(jnp.concatenate([top, -bottom], axis=1), right)
    imag = dot(jnp.concatenate([bottom, top], axis=1), right)
    return jnp.concatenate([real, imag], axis=0)


def complex_mul(first, second, sign):
    width = first.shape[1]
    fr = first[:width].astype(jnp.float32)
    fi = first[width:].astype(jnp.float32) * sign
    sr = second[:width].astype(jnp.float32)
    si = second[width:].astype(jnp.float32)
    return jnp.concatenate([fr * sr - fi * si, fr * si + fi * sr], axis=0)


def band_kernel(counts_ref, taps_ref, measured_ref, band_ref, level_ref):
    width = band_ref.shape[1]
    half = taps_ref.shape[1] // 2
    core = lax.rem(lax.axis_index("cuts"), 2)
    rows = width // 2
    first = pl.multiple_of(lax.axis_index("cuts") // 2 * rows, rows)
    level_ref[:rows, :] = measured_ref[core, pl.ds(first, rows), :].astype(jnp.bfloat16)
    live = (core < counts_ref[0]).astype(jnp.float32)
    level_ref[rows:, :] = jnp.full((level_ref.shape[0] - rows, width), live, jnp.float32).astype(jnp.bfloat16)
    rows = lax.broadcasted_iota(jnp.int32, (width, width), 0)
    columns = lax.broadcasted_iota(jnp.int32, (width, width), 1)
    inside = jnp.abs(columns - rows) <= half
    for part in range(2):
        line = taps_ref[part : part + 1, :].astype(jnp.float32)
        filler = jnp.zeros((1, width - line.shape[1]), jnp.float32)
        line = jnp.concatenate([line, filler], axis=1)
        spread = jnp.broadcast_to(line, (width, width))
        turned = pltpu.roll(spread, width - half, 1, stride=1, stride_axis=0)
        band = jnp.where(inside, turned, 0.0)
        band_ref[part] = band.astype(jnp.bfloat16)
        band_ref[part + 2] = band.T.astype(jnp.bfloat16)


def cut_kernel(tile_ref, whole_ref, below_ref, right_ref):
    half = right_ref.shape[1]
    whole_ref[...] = tile_ref[...]
    below_ref[...] = tile_ref[:, :, half:]
    right_ref[...] = tile_ref[:, half:, :]


def seal_kernel(tile_ref, offsets_ref, own_ref):
    half = tile_ref.shape[1] // 2
    own_ref[:, :half, :] = tile_ref[:, half:, half:]
    shape = (own_ref.shape[1] - half, half)
    line = lax.broadcasted_iota(jnp.int32, shape, 0)
    lines = jnp.zeros(shape, jnp.float32)
    for index in range(4):
        value = offsets_ref[index // 2 : index // 2 + 1, index % 2 : index % 2 + 1].astype(jnp.float32)
        lines = jnp.where(line == index, value, lines)
    for part in range(2):
        own_ref[part, half:, :] = lines.astype(jnp.bfloat16)


def window_kernel(own_ref, rows_ref, columns_ref, rows_back_ref, columns_back_ref):
    half = own_ref.shape[2]
    width = 2 * half
    core = lax.rem(lax.axis_index("cuts"), 2)
    lines = own_ref[0, half:, :].astype(jnp.float32).astype(jnp.int32) - half

    def placed(shape, axis, shift):
        i = lax.broadcasted_iota(jnp.int32, shape, axis)
        j = lax.broadcasted_iota(jnp.int32, shape, 1 - axis)
        shift = jnp.concatenate([shift] * (shape[1] // half), axis=1)
        return jnp.where(j - i == shift, 1.0, 0.0).astype(jnp.bfloat16)

    for place in range(2):
        second = core != place
        row = jnp.where(second, lines[2:3], lines[0:1])
        column = jnp.where(second, lines[3:4], lines[1:2])
        rows_ref[place * half : (place + 1) * half, :] = placed((half, width), 0, row)
        columns_ref[place] = placed((width + half, width), 1, column)
        rows_back_ref[place] = placed((width + half, width), 1, row)
        columns_back_ref[place * width : (place + 1) * width, :] = placed((width, width + half), 0, column)


def extract_kernel(rows_ref, columns_ref, tile_ref, below_ref, right_ref, own_ref, first_ref, second_ref):
    width = tile_ref.shape[1]
    half = width // 2
    wide = width + half
    blocks = []
    for part in range(2):
        upper = jnp.concatenate([own_ref[part, :half], right_ref[part]], axis=1)
        lower = jnp.concatenate([below_ref[part], tile_ref[part]], axis=1)
        blocks.append(jnp.concatenate([upper, lower], axis=0))
    block = jnp.concatenate(blocks, axis=1)
    strips = [dot(rows_ref[...], block[top : top + width]).astype(jnp.bfloat16) for top in (0, half)]
    for place, out_ref in enumerate((first_ref, second_ref)):
        mine = [strip[place * half : (place + 1) * half, part * wide : (part + 1) * wide] for part in range(2) for strip in strips]
        out_ref[...] = dot(jnp.concatenate(mine, axis=0), columns_ref[place]).astype(jnp.bfloat16)


def forward(probe_ref, band_ref, patch_ref, spread_ref, first, last):
    for level in range(first, last + 1):
        if level == 0:
            spread_ref[0] = probe_ref[...]
        else:
            wave = complex_mul(spread_ref[level - 1], patch_ref[level - 1], 1.0).astype(jnp.bfloat16)
            spread = sandwich(band_ref[0], band_ref[1], wave, band_ref[2], band_ref[3])
            spread_ref[level] = spread.astype(jnp.bfloat16)


def head_kernel(probe_ref, band_ref, p0_ref, p1_ref, spread_ref, patch_ref):
    cut = lax.axis_index("cuts")

    @pl.when(cut < 2)
    def _():
        patch_ref[cut] = p0_ref[...]
        patch_ref[1 - cut] = p1_ref[...]
        forward(probe_ref, band_ref, patch_ref, spread_ref, 0, 2)


def chain_kernel(
    probe_ref, p0_ref, p1_ref, p2_ref, p3_ref, level_ref, far_level_ref, band_ref, fourier_ref, head_ref, mine_ref, other_ref, patch_ref, spread_ref, back_ref
):
    width = probe_ref.shape[1]
    cut = lax.axis_index("cuts")
    for mask, ref in enumerate((p0_ref, p1_ref, p2_ref, p3_ref)):
        patch_ref[lax.bitwise_xor(cut, mask)] = ref[...]

    @pl.when(cut < 2)
    def _():
        spread_ref[0:3] = head_ref[...]

    @pl.when(cut >= 2)
    def _():
        forward(probe_ref, band_ref, patch_ref, spread_ref, 0, 2)

    forward(probe_ref, band_ref, patch_ref, spread_ref, 3, 3)
    fourier_r, fourier_i = fourier_ref[0], fourier_ref[1]
    wave = complex_mul(spread_ref[3], patch_ref[3], 1.0).astype(jnp.bfloat16)
    far = sandwich(fourier_r, fourier_i, wave, fourier_r, fourier_i)
    far_r, far_i = far[:width], far[width:]
    rows = width // 2
    level, far_level = level_ref[:rows, :].astype(jnp.float32), far_level_ref[:rows, :].astype(jnp.float32)
    level = jnp.concatenate([jnp.where(cut < 2, level, far_level), jnp.where(cut < 2, far_level, level)], axis=0)
    live = level_ref[rows : rows + 1, :].astype(jnp.float32)
    excess = 2.0 * live * (far_r * far_r + far_i * far_i - level)
    residual = jnp.concatenate([excess * far_r, excess * far_i], axis=0).astype(jnp.bfloat16)
    back_ref[...] = sandwich(fourier_r, -fourier_i, residual, fourier_r, -fourier_i).astype(jnp.bfloat16)

    def term(level):
        value = complex_mul(spread_ref[level], back_ref[...], -1.0).astype(jnp.bfloat16)

        @pl.when(level == cut)
        def _():
            mine_ref[...] = value

        @pl.when(level != cut)
        def _():
            other_ref[...] = value

    def carry(level):
        carried = complex_mul(patch_ref[level], back_ref[...], -1.0).astype(jnp.bfloat16)
        back = sandwich(band_ref[2], -band_ref[3], carried, band_ref[0], -band_ref[1])
        back_ref[...] = back.astype(jnp.bfloat16)

    @pl.when(cut >= 2)
    def _():
        term(3)

    carry(3)

    @pl.when(cut >= 2)
    def _():
        term(2)

    @pl.when(cut < 2)
    def _():
        carry(2)
        term(1)
        carry(1)
        term(0)


def scatter_kernel(rows_ref, columns_ref, mine_ref, other_ref, tile_ref, below_ref, right_ref, own_ref):
    width = tile_ref.shape[1]
    half = width // 2
    strips = []
    for place, ref in enumerate((mine_ref, other_ref)):
        field = jnp.concatenate([ref[:width, :], ref[width:, :]], axis=1)
        strips.append(dot(rows_ref[place], field).astype(jnp.bfloat16))
    for part in range(2):
        strip = jnp.concatenate([strip[:, part * width : (part + 1) * width] for strip in strips], axis=1)
        total = dot(strip, columns_ref[...])
        tile_ref[part] = total[half:, half:]
        below_ref[part] = total[half:, :half].astype(jnp.bfloat16)
        right_ref[part] = total[:half, half:].astype(jnp.bfloat16)
        own_ref[part] = total[:half, :half].astype(jnp.bfloat16)


def total_kernel(tile_ref, below_ref, right_ref, out_ref, quarter_ref):
    half = right_ref.shape[1]
    below = below_ref[...].astype(jnp.float32)
    right = right_ref[...].astype(jnp.float32)
    quarter = tile_ref[:, half:, half:] + below[:, half:] + right[:, :, half:]
    out_ref[0, :, :half, :half] = tile_ref[:, :half, :half]
    out_ref[0, :, :half, half:] = tile_ref[:, :half, half:] + below[:, :half]
    out_ref[0, :, half:, :half] = tile_ref[:, half:, :half] + right[:, :, :half]
    out_ref[0, :, half:, half:] = quarter
    quarter_ref[...] = quarter


def quarter_kernel(out_ref, quarter_ref, own_ref, same_ref, sum_ref, sem):
    half = quarter_ref.shape[1]
    sum_ref[...] = quarter_ref[...] + own_ref[...].astype(jnp.float32)
    copy = pltpu.make_async_copy(sum_ref, same_ref.at[0, :, pl.ds(half, half), pl.ds(half, half)], sem)
    copy.start()
    copy.wait()


VMEM = pl.BlockSpec(memory_space=pltpu.VMEM)
ANY = pl.BlockSpec(memory_space=pl.ANY)
SMEM = pl.BlockSpec(memory_space=pltpu.SMEM)
PARAMS = pltpu.CompilerParams(vmem_limit_bytes=48 * 1024 * 1024)


def shaped(*shape, dtype=jnp.bfloat16):
    return jax.ShapeDtypeStruct(shape, dtype)


def kernel(body, name, in_specs, out_shape, scratch=()):
    return pl.pallas_call(
        body, in_specs=in_specs, out_specs=[VMEM] * len(out_shape), out_shape=out_shape, scratch_shapes=scratch, compiler_params=PARAMS, name=name
    )


def local(object_slices, probe, fresnel_taps, offsets, counts, measured):
    width = probe.shape[1]
    half = width // 2
    wide = width + half
    full = shaped(2 * width, width)
    part = shaped(width, width)
    row_tiles = max(lax.axis_size("tile") // 16, 2)
    probe = probe.reshape(2 * width, width)
    fourier = jnp.asarray(fourier_matrix(width), jnp.bfloat16)

    far_tile = crossed(object_slices[0], "cuts", 2)
    tile, below, right = kernel(cut_kernel, "cut", [VMEM], [shaped(2, width, width), shaped(2, width, half), shaped(2, half, width)])(
        object_slices[0]
    )
    (own,) = kernel(seal_kernel, "seal", [VMEM, VMEM], [shaped(2, half + 16, half)])(tile, offsets)
    below = passed_along(below, "tile", 1)
    right = passed_along(right, "tile", row_tiles)
    own = passed_along(own, "tile", row_tiles + 1)
    far_below = crossed(below, "cuts", 2)
    far_right = crossed(right, "cuts", 2)
    far_own = crossed(own, "cuts", 2)
    level = shaped(half + 16, width)
    band, level = kernel(band_kernel, "band", [SMEM, VMEM, VMEM], [shaped(4, width, width), level])(counts, fresnel_taps, measured)
    level, right = lax.optimization_barrier((level, right))
    level = passed_along(level, "tile", row_tiles + 1)
    rows, columns, rows_back, columns_back = kernel(
        window_kernel,
        "window",
        [VMEM],
        [part, shaped(2, wide, width), shaped(2, wide, width), shaped(2 * width, wide)],
    )(own)
    first, second = kernel(extract_kernel, "near", [VMEM] * 6, [full, full])(rows, columns, tile, below, right, own)
    swapped = crossed(second, "cuts", 1)
    far_level = crossed(level, "cuts", 2)
    straight, far_second = kernel(extract_kernel, "far", [VMEM] * 6, [full, full])(rows, columns, far_tile, far_below, far_right, far_own)
    far_second, far_level = lax.optimization_barrier((far_second, far_level))
    diagonal = crossed(far_second, "cuts", 1)
    (head,) = kernel(head_kernel, "head", [VMEM] * 4, [shaped(3, 2 * width, width)], [pltpu.VMEM((2, 2 * width, width), jnp.bfloat16)])(
        probe, band, first, swapped
    )
    mine, other = kernel(
        chain_kernel,
        "chain",
        [VMEM] * 10,
        [full, full],
        [
            pltpu.VMEM((4, 2 * width, width), jnp.bfloat16),
            pltpu.VMEM((4, 2 * width, width), jnp.bfloat16),
            pltpu.VMEM((2 * width, width), jnp.bfloat16),
        ],
    )(probe, first, swapped, straight, diagonal, level, far_level, band, fourier, head)
    other = crossed(other, "cuts", 1)
    total, below, right, own = kernel(
        scatter_kernel,
        "scatter",
        [VMEM] * 4,
        [shaped(2, width, width, dtype=jnp.float32), shaped(2, width, half), shaped(2, half, width), shaped(2, half, half)],
    )(rows_back, columns_back, mine, other)
    below = passed_along(below, "tile", -1)
    right = passed_along(right, "tile", -row_tiles)
    own = passed_along(own, "tile", -row_tiles - 1)
    whole = shaped(1, 2, width, width, dtype=jnp.float32)
    quarter = shaped(2, half, half, dtype=jnp.float32)
    out, quarter = kernel(total_kernel, "total", [VMEM] * 3, [whole, quarter])(total, below, right)
    out = pl.pallas_call(
        quarter_kernel,
        in_specs=[ANY, VMEM, VMEM],
        out_specs=ANY,
        out_shape=whole,
        input_output_aliases={0: 0},
        scratch_shapes=[pltpu.VMEM((2, half, half), jnp.float32), pltpu.SemaphoreType.DMA],
        compiler_params=PARAMS,
        name="quarter",
    )(out, quarter, own)
    return out


def solution(mesh):
    return jax.shard_map(
        local,
        mesh=mesh,
        in_specs=(
            P("cuts", None, "tile", None),
            P(),
            P(),
            P("tile", None),
            P("tile"),
            P("tile", None, None),
        ),
        out_specs=P("cuts", None, "tile", None),
        check_vma=False,
    )
```

```python
import jax
import jax.numpy as jnp
import numpy as np
from jax import lax
from jax.experimental import pallas as pl
from jax.experimental.pallas import tpu as pltpu
from jax.sharding import PartitionSpec as P


def passed_along(value, axis, steps):
    count = lax.axis_size(axis)
    pairs = [(source, (source + steps) % count) for source in range(count)]
    return lax.ppermute(value, axis, pairs)


def crossed(value, axis, mask):
    pairs = [(source, source ^ mask) for source in range(lax.axis_size(axis))]
    return lax.ppermute(value, axis, pairs)


def fourier_matrix(width):
    index = np.arange(width)
    angle = 2.0 * np.pi * (index[:, None] * index[None, :] % width) / width
    return np.stack([np.cos(angle), -np.sin(angle)]) / np.sqrt(width)


def dot(left, right):
    return jnp.dot(left, right, preferred_element_type=jnp.float32)


def sandwich(left_real, left_imag, field, right_real, right_imag):
    right = jnp.concatenate([right_real, right_imag], axis=0)
    top = dot(jnp.concatenate([left_real, -left_imag], axis=1), field).astype(jnp.bfloat16)
    bottom = dot(jnp.concatenate([left_imag, left_real], axis=1), field).astype(jnp.bfloat16)
    real = dot(jnp.concatenate([top, -bottom], axis=1), right)
    imag = dot(jnp.concatenate([bottom, top], axis=1), right)
    return jnp.concatenate([real, imag], axis=0)


def complex_mul(first, second, sign):
    width = first.shape[1]
    fr = first[:width].astype(jnp.float32)
    fi = first[width:].astype(jnp.float32) * sign
    sr = second[:width].astype(jnp.float32)
    si = second[width:].astype(jnp.float32)
    return jnp.concatenate([fr * sr - fi * si, fr * si + fi * sr], axis=0)


def band_kernel(counts_ref, taps_ref, measured_ref, band_ref, level_ref):
    width = band_ref.shape[1]
    half = taps_ref.shape[1] // 2
    core = lax.rem(lax.axis_index("cuts"), 2)
    rows = width // 2
    first = pl.multiple_of(lax.axis_index("cuts") // 2 * rows, rows)
    level_ref[:rows, :] = measured_ref[core, pl.ds(first, rows), :].astype(jnp.bfloat16)
    live = (core < counts_ref[0]).astype(jnp.float32)
    level_ref[rows:, :] = jnp.full((level_ref.shape[0] - rows, width), live, jnp.float32).astype(jnp.bfloat16)
    rows = lax.broadcasted_iota(jnp.int32, (width, width), 0)
    columns = lax.broadcasted_iota(jnp.int32, (width, width), 1)
    inside = jnp.abs(columns - rows) <= half
    for part in range(2):
        line = taps_ref[part : part + 1, :].astype(jnp.float32)
        filler = jnp.zeros((1, width - line.shape[1]), jnp.float32)
        line = jnp.concatenate([line, filler], axis=1)
        spread = jnp.broadcast_to(line, (width, width))
        turned = pltpu.roll(spread, width - half, 1, stride=1, stride_axis=0)
        band = jnp.where(inside, turned, 0.0)
        band_ref[part] = band.astype(jnp.bfloat16)
        band_ref[part + 2] = band.T.astype(jnp.bfloat16)


def cut_kernel(tile_ref, whole_ref, below_ref, right_ref):
    half = right_ref.shape[1]
    whole_ref[...] = tile_ref[...]
    below_ref[...] = tile_ref[:, :, half:]
    right_ref[...] = tile_ref[:, half:, :]


def seal_kernel(tile_ref, offsets_ref, own_ref):
    half = tile_ref.shape[1] // 2
    own_ref[:, :half, :] = tile_ref[:, half:, half:]
    shape = (own_ref.shape[1] - half, half)
    line = lax.broadcasted_iota(jnp.int32, shape, 0)
    lines = jnp.zeros(shape, jnp.float32)
    for index in range(4):
        value = offsets_ref[index // 2 : index // 2 + 1, index % 2 : index % 2 + 1].astype(jnp.float32)
        lines = jnp.where(line == index, value, lines)
    for part in range(2):
        own_ref[part, half:, :] = lines.astype(jnp.bfloat16)


def window_kernel(own_ref, rows_ref, columns_ref, rows_back_ref, columns_back_ref):
    half = own_ref.shape[2]
    width = 2 * half
    core = lax.rem(lax.axis_index("cuts"), 2)
    lines = own_ref[0, half:, :].astype(jnp.float32).astype(jnp.int32) - half

    def placed(shape, axis, shift):
        i = lax.broadcasted_iota(jnp.int32, shape, axis)
        j = lax.broadcasted_iota(jnp.int32, shape, 1 - axis)
        shift = jnp.concatenate([shift] * (shape[1] // half), axis=1)
        return jnp.where(j - i == shift, 1.0, 0.0).astype(jnp.bfloat16)

    for place in range(2):
        second = core != place
        row = jnp.where(second, lines[2:3], lines[0:1])
        column = jnp.where(second, lines[3:4], lines[1:2])
        rows_ref[place * half : (place + 1) * half, :] = placed((half, width), 0, row)
        columns_ref[place] = placed((width + half, width), 1, column)
        rows_back_ref[place] = placed((width + half, width), 1, row)
        columns_back_ref[place * width : (place + 1) * width, :] = placed((width, width + half), 0, column)


def extract_kernel(rows_ref, columns_ref, tile_ref, below_ref, right_ref, own_ref, first_ref, second_ref):
    width = tile_ref.shape[1]
    half = width // 2
    wide = width + half
    blocks = []
    for part in range(2):
        upper = jnp.concatenate([own_ref[part, :half], right_ref[part]], axis=1)
        lower = jnp.concatenate([below_ref[part], tile_ref[part]], axis=1)
        blocks.append(jnp.concatenate([upper, lower], axis=0))
    block = jnp.concatenate(blocks, axis=1)
    strips = [dot(rows_ref[...], block[top : top + width]).astype(jnp.bfloat16) for top in (0, half)]
    for place, out_ref in enumerate((first_ref, second_ref)):
        mine = [strip[place * half : (place + 1) * half, part * wide : (part + 1) * wide] for part in range(2) for strip in strips]
        out_ref[...] = dot(jnp.concatenate(mine, axis=0), columns_ref[place]).astype(jnp.bfloat16)


def ordered(first_ref, second_ref):
    odd = lax.rem(lax.axis_index("cuts"), 2) == 1
    first, second = first_ref[...], second_ref[...]
    return jnp.where(odd, second, first), jnp.where(odd, first, second)


def near_chip():
    return lax.axis_index("cuts") < 2


def spread_on(spread, patch, band_ref):
    wave = complex_mul(spread, patch, 1.0).astype(jnp.bfloat16)
    return sandwich(band_ref[0], band_ref[1], wave, band_ref[2], band_ref[3]).astype(jnp.bfloat16)


def back_on(back, patch, band_ref):
    carried = complex_mul(patch, back, -1.0).astype(jnp.bfloat16)
    return sandwich(band_ref[2], -band_ref[3], carried, band_ref[0], -band_ref[1]).astype(jnp.bfloat16)


def head_kernel(probe_ref, band_ref, p0_ref, p1_ref, one_ref, two_ref):
    @pl.when(near_chip())
    def _():
        patch_0, patch_1 = ordered(p0_ref, p1_ref)
        one_ref[...] = spread_on(probe_ref[...], patch_0, band_ref)
        two_ref[...] = spread_on(one_ref[...], patch_1, band_ref)


def chain_kernel(
    probe_ref, p0_ref, p1_ref, p2_ref, p3_ref, level_ref, far_level_ref, band_ref, fourier_ref, one_ref, two_ref, mine_ref, other_ref,
    keep_two_ref, keep_three_ref, wave_ref
):
    width = probe_ref.shape[1]

    @pl.when(near_chip())
    def _():
        patch_2, patch_3 = ordered(p2_ref, p3_ref)
        spread = spread_on(two_ref[...], patch_2, band_ref)
        wave_ref[...] = complex_mul(spread, patch_3, 1.0).astype(jnp.bfloat16)

    @pl.when(jnp.logical_not(near_chip()))
    def _():
        patch_0, patch_1 = ordered(p2_ref, p3_ref)
        patch_2, patch_3 = ordered(p0_ref, p1_ref)
        spread = spread_on(probe_ref[...], patch_0, band_ref)
        keep_two_ref[...] = spread_on(spread, patch_1, band_ref)
        keep_three_ref[...] = spread_on(keep_two_ref[...], patch_2, band_ref)
        wave_ref[...] = complex_mul(keep_three_ref[...], patch_3, 1.0).astype(jnp.bfloat16)

    fourier_r, fourier_i = fourier_ref[0], fourier_ref[1]
    far = sandwich(fourier_r, fourier_i, wave_ref[...], fourier_r, fourier_i)
    far_r, far_i = far[:width], far[width:]
    rows = width // 2
    level, far_level = level_ref[:rows, :].astype(jnp.float32), far_level_ref[:rows, :].astype(jnp.float32)
    level = jnp.concatenate([jnp.where(near_chip(), level, far_level), jnp.where(near_chip(), far_level, level)], axis=0)
    live = level_ref[rows : rows + 1, :].astype(jnp.float32)
    excess = 2.0 * live * (far_r * far_r + far_i * far_i - level)
    residual = jnp.concatenate([excess * far_r, excess * far_i], axis=0).astype(jnp.bfloat16)
    wave_ref[...] = sandwich(fourier_r, -fourier_i, residual, fourier_r, -fourier_i).astype(jnp.bfloat16)
    odd = lax.rem(lax.axis_index("cuts"), 2) == 1

    def out(low, high):
        mine_ref[...] = jnp.where(odd, high, low)
        other_ref[...] = jnp.where(odd, low, high)

    @pl.when(near_chip())
    def _():
        _, patch_1 = ordered(p0_ref, p1_ref)
        patch_2, patch_3 = ordered(p2_ref, p3_ref)
        back = back_on(wave_ref[...], patch_3, band_ref)
        back = back_on(back, patch_2, band_ref)
        high = complex_mul(one_ref[...], back, -1.0).astype(jnp.bfloat16)
        back = back_on(back, patch_1, band_ref)
        out(complex_mul(probe_ref[...], back, -1.0).astype(jnp.bfloat16), high)

    @pl.when(jnp.logical_not(near_chip()))
    def _():
        _, patch_3 = ordered(p0_ref, p1_ref)
        back = wave_ref[...]
        high = complex_mul(keep_three_ref[...], back, -1.0).astype(jnp.bfloat16)
        back = back_on(back, patch_3, band_ref)
        out(complex_mul(keep_two_ref[...], back, -1.0).astype(jnp.bfloat16), high)


def scatter_kernel(rows_ref, columns_ref, mine_ref, other_ref, tile_ref, below_ref, right_ref, own_ref):
    width = tile_ref.shape[1]
    half = width // 2
    strips = []
    for place, ref in enumerate((mine_ref, other_ref)):
        field = jnp.concatenate([ref[:width, :], ref[width:, :]], axis=1)
        strips.append(dot(rows_ref[place], field).astype(jnp.bfloat16))
    for part in range(2):
        strip = jnp.concatenate([strip[:, part * width : (part + 1) * width] for strip in strips], axis=1)
        total = dot(strip, columns_ref[...])
        tile_ref[part] = total[half:, half:]
        below_ref[part] = total[half:, :half].astype(jnp.bfloat16)
        right_ref[part] = total[:half, half:].astype(jnp.bfloat16)
        own_ref[part] = total[:half, :half].astype(jnp.bfloat16)


def total_kernel(tile_ref, below_ref, right_ref, out_ref, quarter_ref):
    half = right_ref.shape[1]
    below = below_ref[...].astype(jnp.float32)
    right = right_ref[...].astype(jnp.float32)
    quarter = tile_ref[:, half:, half:] + below[:, half:] + right[:, :, half:]
    out_ref[0, :, :half, :half] = tile_ref[:, :half, :half]
    out_ref[0, :, :half, half:] = tile_ref[:, :half, half:] + below[:, :half]
    out_ref[0, :, half:, :half] = tile_ref[:, half:, :half] + right[:, :, :half]
    out_ref[0, :, half:, half:] = quarter
    quarter_ref[...] = quarter


def quarter_kernel(out_ref, quarter_ref, own_ref, same_ref, sum_ref, sem):
    half = quarter_ref.shape[1]
    sum_ref[...] = quarter_ref[...] + own_ref[...].astype(jnp.float32)
    copy = pltpu.make_async_copy(sum_ref, same_ref.at[0, :, pl.ds(half, half), pl.ds(half, half)], sem)
    copy.start()
    copy.wait()


VMEM = pl.BlockSpec(memory_space=pltpu.VMEM)
ANY = pl.BlockSpec(memory_space=pl.ANY)
SMEM = pl.BlockSpec(memory_space=pltpu.SMEM)
PARAMS = pltpu.CompilerParams(vmem_limit_bytes=48 * 1024 * 1024)


def shaped(*shape, dtype=jnp.bfloat16):
    return jax.ShapeDtypeStruct(shape, dtype)


def kernel(body, name, in_specs, out_shape, scratch=()):
    return pl.pallas_call(
        body, in_specs=in_specs, out_specs=[VMEM] * len(out_shape), out_shape=out_shape, scratch_shapes=scratch, compiler_params=PARAMS, name=name
    )


def local(object_slices, probe, fresnel_taps, offsets, counts, measured):
    width = probe.shape[1]
    half = width // 2
    wide = width + half
    full = shaped(2 * width, width)
    part = shaped(width, width)
    row_tiles = max(lax.axis_size("tile") // 16, 2)
    probe = probe.reshape(2 * width, width)
    fourier = jnp.asarray(fourier_matrix(width), jnp.bfloat16)

    far_tile = crossed(object_slices[0], "cuts", 2)
    tile, below, right = kernel(cut_kernel, "cut", [VMEM], [shaped(2, width, width), shaped(2, width, half), shaped(2, half, width)])(
        object_slices[0]
    )
    (own,) = kernel(seal_kernel, "seal", [VMEM, VMEM], [shaped(2, half + 16, half)])(tile, offsets)
    below = passed_along(below, "tile", 1)
    right = passed_along(right, "tile", row_tiles)
    own = passed_along(own, "tile", row_tiles + 1)
    below, far_tile = lax.optimization_barrier((below, far_tile))
    far_below = crossed(below, "cuts", 2)
    far_right = crossed(right, "cuts", 2)
    far_own = crossed(own, "cuts", 2)
    level = shaped(half + 16, width)
    band, level = kernel(band_kernel, "band", [SMEM, VMEM, VMEM], [shaped(4, width, width), level])(counts, fresnel_taps, measured)
    level, right = lax.optimization_barrier((level, right))
    level = passed_along(level, "tile", row_tiles + 1)
    rows, columns, rows_back, columns_back = kernel(
        window_kernel,
        "window",
        [VMEM],
        [part, shaped(2, wide, width), shaped(2, wide, width), shaped(2 * width, wide)],
    )(own)
    first, second = kernel(extract_kernel, "near", [VMEM] * 6, [full, full])(rows, columns, tile, below, right, own)
    swapped = crossed(second, "cuts", 1)
    far_level = crossed(level, "cuts", 2)
    straight, far_second = kernel(extract_kernel, "far", [VMEM] * 6, [full, full])(rows, columns, far_tile, far_below, far_right, far_own)
    far_second, far_level = lax.optimization_barrier((far_second, far_level))
    diagonal = crossed(far_second, "cuts", 1)
    one, two = kernel(head_kernel, "head", [VMEM] * 4, [full, full])(probe, band, first, swapped)
    mine, other = kernel(chain_kernel, "chain", [VMEM] * 11, [full, full], [pltpu.VMEM((2 * width, width), jnp.bfloat16)] * 3)(
        probe, first, swapped, straight, diagonal, level, far_level, band, fourier, one, two
    )
    other = crossed(other, "cuts", 1)
    total, below, right, own = kernel(
        scatter_kernel,
        "scatter",
        [VMEM] * 4,
        [shaped(2, width, width, dtype=jnp.float32), shaped(2, width, half), shaped(2, half, width), shaped(2, half, half)],
    )(rows_back, columns_back, mine, other)
    below = passed_along(below, "tile", -1)
    right = passed_along(right, "tile", -row_tiles)
    own = passed_along(own, "tile", -row_tiles - 1)
    whole = shaped(1, 2, width, width, dtype=jnp.float32)
    quarter = shaped(2, half, half, dtype=jnp.float32)
    out, quarter = kernel(total_kernel, "total", [VMEM] * 3, [whole, quarter])(total, below, right)
    out = pl.pallas_call(
        quarter_kernel,
        in_specs=[ANY, VMEM, VMEM],
        out_specs=ANY,
        out_shape=whole,
        input_output_aliases={0: 0},
        scratch_shapes=[pltpu.VMEM((2, half, half), jnp.float32), pltpu.SemaphoreType.DMA],
        compiler_params=PARAMS,
        name="quarter",
    )(out, quarter, own)
    return out


def solution(mesh):
    return jax.shard_map(
        local,
        mesh=mesh,
        in_specs=(
            P("cuts", None, "tile", None),
            P(),
            P(),
            P("tile", None),
            P("tile"),
            P("tile", None, None),
        ),
        out_specs=P("cuts", None, "tile", None),
        check_vma=False,
    )
```

```python
import jax
import jax.numpy as jnp
import numpy as np
from jax import lax
from jax.experimental import pallas as pl
from jax.experimental.pallas import tpu as pltpu
from jax.sharding import PartitionSpec as P


def passed_along(value, axis, steps):
    count = lax.axis_size(axis)
    pairs = [(source, (source + steps) % count) for source in range(count)]
    return lax.ppermute(value, axis, pairs)


def turned(value, even, odd):
    count = lax.axis_size("tile")
    value = lax.ppermute(value, "tile", [(source, source ^ 1) for source in range(count)])
    return lax.ppermute(value, "tile", [(source, (source + (odd if source % 2 else even)) % count) for source in range(count)])


def crossed(value, axis, mask):
    pairs = [(source, source ^ mask) for source in range(lax.axis_size(axis))]
    return lax.ppermute(value, axis, pairs)


def fourier_matrix(width):
    index = np.arange(width)
    angle = 2.0 * np.pi * (index[:, None] * index[None, :] % width) / width
    return np.stack([np.cos(angle), -np.sin(angle)]) / np.sqrt(width)


def dot(left, right):
    return jnp.dot(left, right, preferred_element_type=jnp.float32)


def sandwich(left_real, left_imag, field, right_real, right_imag):
    right = jnp.concatenate([right_real, right_imag], axis=0)
    top = dot(jnp.concatenate([left_real, -left_imag], axis=1), field).astype(jnp.bfloat16)
    bottom = dot(jnp.concatenate([left_imag, left_real], axis=1), field).astype(jnp.bfloat16)
    real = dot(jnp.concatenate([top, -bottom], axis=1), right)
    imag = dot(jnp.concatenate([bottom, top], axis=1), right)
    return jnp.concatenate([real, imag], axis=0)


def complex_mul(first, second, sign):
    width = first.shape[1]
    fr = first[:width].astype(jnp.float32)
    fi = first[width:].astype(jnp.float32) * sign
    sr = second[:width].astype(jnp.float32)
    si = second[width:].astype(jnp.float32)
    return jnp.concatenate([fr * sr - fi * si, fr * si + fi * sr], axis=0)


def band_kernel(counts_ref, taps_ref, measured_ref, band_ref, level_ref):
    width = band_ref.shape[1]
    half = taps_ref.shape[1] // 2
    core = lax.rem(lax.axis_index("cuts"), 2)
    rows = width // 2
    first = pl.multiple_of(lax.axis_index("cuts") // 2 * rows, rows)
    level_ref[:rows, :] = measured_ref[core, pl.ds(first, rows), :].astype(jnp.bfloat16)
    live = (core < counts_ref[0]).astype(jnp.float32)
    level_ref[rows:, :] = jnp.full((level_ref.shape[0] - rows, width), live, jnp.float32).astype(jnp.bfloat16)
    rows = lax.broadcasted_iota(jnp.int32, (width, width), 0)
    columns = lax.broadcasted_iota(jnp.int32, (width, width), 1)
    inside = jnp.abs(columns - rows) <= half
    for part in range(2):
        line = taps_ref[part : part + 1, :].astype(jnp.float32)
        filler = jnp.zeros((1, width - line.shape[1]), jnp.float32)
        line = jnp.concatenate([line, filler], axis=1)
        spread = jnp.broadcast_to(line, (width, width))
        turned = pltpu.roll(spread, width - half, 1, stride=1, stride_axis=0)
        band = jnp.where(inside, turned, 0.0)
        band_ref[part] = band.astype(jnp.bfloat16)
        band_ref[part + 2] = band.T.astype(jnp.bfloat16)


def cut_kernel(tile_ref, whole_ref, below_ref, right_ref):
    half = right_ref.shape[1]
    whole_ref[...] = tile_ref[...]
    below_ref[...] = tile_ref[:, :, half:]
    right_ref[...] = tile_ref[:, half:, :]


def seal_kernel(tile_ref, offsets_ref, own_ref):
    half = tile_ref.shape[1] // 2
    own_ref[:, :half, :] = tile_ref[:, half:, half:]
    shape = (own_ref.shape[1] - half, half)
    line = lax.broadcasted_iota(jnp.int32, shape, 0)
    lines = jnp.zeros(shape, jnp.float32)
    for index in range(4):
        value = offsets_ref[index // 2 : index // 2 + 1, index % 2 : index % 2 + 1].astype(jnp.float32)
        lines = jnp.where(line == index, value, lines)
    for part in range(2):
        own_ref[part, half:, :] = lines.astype(jnp.bfloat16)


def window_kernel(own_ref, rows_ref, columns_ref, rows_back_ref, columns_back_ref):
    half = own_ref.shape[2]
    width = 2 * half
    core = lax.rem(lax.axis_index("cuts"), 2)
    lines = own_ref[0, half:, :].astype(jnp.float32).astype(jnp.int32) - half

    def placed(shape, axis, shift):
        i = lax.broadcasted_iota(jnp.int32, shape, axis)
        j = lax.broadcasted_iota(jnp.int32, shape, 1 - axis)
        shift = jnp.concatenate([shift] * (shape[1] // half), axis=1)
        return jnp.where(j - i == shift, 1.0, 0.0).astype(jnp.bfloat16)

    for place in range(2):
        second = core != place
        row = jnp.where(second, lines[2:3], lines[0:1])
        column = jnp.where(second, lines[3:4], lines[1:2])
        rows_ref[place * half : (place + 1) * half, :] = placed((half, width), 0, row)
        columns_ref[place] = placed((width + half, width), 1, column)
        rows_back_ref[place] = placed((width + half, width), 1, row)
        columns_back_ref[place * width : (place + 1) * width, :] = placed((width, width + half), 0, column)


def extract_kernel(rows_ref, columns_ref, tile_ref, below_ref, right_ref, own_ref, first_ref, second_ref):
    width = tile_ref.shape[1]
    half = width // 2
    wide = width + half
    blocks = []
    for part in range(2):
        upper = jnp.concatenate([own_ref[part, :half], right_ref[part]], axis=1)
        lower = jnp.concatenate([below_ref[part], tile_ref[part]], axis=1)
        blocks.append(jnp.concatenate([upper, lower], axis=0))
    block = jnp.concatenate(blocks, axis=1)
    strips = [dot(rows_ref[...], block[top : top + width]).astype(jnp.bfloat16) for top in (0, half)]
    for place, out_ref in enumerate((first_ref, second_ref)):
        mine = [strip[place * half : (place + 1) * half, part * wide : (part + 1) * wide] for part in range(2) for strip in strips]
        out_ref[...] = dot(jnp.concatenate(mine, axis=0), columns_ref[place]).astype(jnp.bfloat16)


def ordered(first_ref, second_ref):
    odd = lax.rem(lax.axis_index("cuts"), 2) == 1
    first, second = first_ref[...], second_ref[...]
    return jnp.where(odd, second, first), jnp.where(odd, first, second)


def near_chip():
    return lax.axis_index("cuts") < 2


def spread_on(spread, patch, band_ref):
    wave = complex_mul(spread, patch, 1.0).astype(jnp.bfloat16)
    return sandwich(band_ref[0], band_ref[1], wave, band_ref[2], band_ref[3]).astype(jnp.bfloat16)


def back_on(back, patch, band_ref):
    carried = complex_mul(patch, back, -1.0).astype(jnp.bfloat16)
    return sandwich(band_ref[2], -band_ref[3], carried, band_ref[0], -band_ref[1]).astype(jnp.bfloat16)


def head_kernel(probe_ref, band_ref, p0_ref, p1_ref, one_ref, two_ref):
    @pl.when(near_chip())
    def _():
        patch_0, patch_1 = ordered(p0_ref, p1_ref)
        one_ref[...] = spread_on(probe_ref[...], patch_0, band_ref)
        two_ref[...] = spread_on(one_ref[...], patch_1, band_ref)


def chain_kernel(
    probe_ref, p0_ref, p1_ref, p2_ref, p3_ref, level_ref, far_level_ref, band_ref, fourier_ref, one_ref, two_ref, mine_ref, other_ref,
    keep_two_ref, keep_three_ref, wave_ref
):
    width = probe_ref.shape[1]

    @pl.when(near_chip())
    def _():
        patch_2, patch_3 = ordered(p2_ref, p3_ref)
        spread = spread_on(two_ref[...], patch_2, band_ref)
        wave_ref[...] = complex_mul(spread, patch_3, 1.0).astype(jnp.bfloat16)

    @pl.when(jnp.logical_not(near_chip()))
    def _():
        patch_0, patch_1 = ordered(p2_ref, p3_ref)
        patch_2, patch_3 = ordered(p0_ref, p1_ref)
        spread = spread_on(probe_ref[...], patch_0, band_ref)
        keep_two_ref[...] = spread_on(spread, patch_1, band_ref)
        keep_three_ref[...] = spread_on(keep_two_ref[...], patch_2, band_ref)
        wave_ref[...] = complex_mul(keep_three_ref[...], patch_3, 1.0).astype(jnp.bfloat16)

    fourier_r, fourier_i = fourier_ref[0], fourier_ref[1]
    far = sandwich(fourier_r, fourier_i, wave_ref[...], fourier_r, fourier_i)
    far_r, far_i = far[:width], far[width:]
    rows = width // 2
    level, far_level = level_ref[:rows, :].astype(jnp.float32), far_level_ref[:rows, :].astype(jnp.float32)
    level = jnp.concatenate([jnp.where(near_chip(), level, far_level), jnp.where(near_chip(), far_level, level)], axis=0)
    live = level_ref[rows : rows + 1, :].astype(jnp.float32)
    excess = 2.0 * live * (far_r * far_r + far_i * far_i - level)
    residual = jnp.concatenate([excess * far_r, excess * far_i], axis=0).astype(jnp.bfloat16)
    wave_ref[...] = sandwich(fourier_r, -fourier_i, residual, fourier_r, -fourier_i).astype(jnp.bfloat16)
    odd = lax.rem(lax.axis_index("cuts"), 2) == 1

    def out(low, high):
        mine_ref[...] = jnp.where(odd, high, low)
        other_ref[...] = jnp.where(odd, low, high)

    @pl.when(near_chip())
    def _():
        _, patch_1 = ordered(p0_ref, p1_ref)
        patch_2, patch_3 = ordered(p2_ref, p3_ref)
        back = back_on(wave_ref[...], patch_3, band_ref)
        back = back_on(back, patch_2, band_ref)
        high = complex_mul(one_ref[...], back, -1.0).astype(jnp.bfloat16)
        back = back_on(back, patch_1, band_ref)
        out(complex_mul(probe_ref[...], back, -1.0).astype(jnp.bfloat16), high)

    @pl.when(jnp.logical_not(near_chip()))
    def _():
        _, patch_3 = ordered(p0_ref, p1_ref)
        back = wave_ref[...]
        high = complex_mul(keep_three_ref[...], back, -1.0).astype(jnp.bfloat16)
        back = back_on(back, patch_3, band_ref)
        out(complex_mul(keep_two_ref[...], back, -1.0).astype(jnp.bfloat16), high)


def scatter_kernel(rows_ref, columns_ref, mine_ref, other_ref, tile_ref, below_ref, right_ref, own_ref):
    width = tile_ref.shape[1]
    half = width // 2
    strips = []
    for place, ref in enumerate((mine_ref, other_ref)):
        field = jnp.concatenate([ref[:width, :], ref[width:, :]], axis=1)
        strips.append(dot(rows_ref[place], field).astype(jnp.bfloat16))
    for part in range(2):
        strip = jnp.concatenate([strip[:, part * width : (part + 1) * width] for strip in strips], axis=1)
        total = dot(strip, columns_ref[...])
        tile_ref[part] = total[half:, half:]
        below_ref[part] = total[half:, :half].astype(jnp.bfloat16)
        right_ref[part] = total[:half, half:].astype(jnp.bfloat16)
        own_ref[part] = total[:half, :half].astype(jnp.bfloat16)


def total_kernel(tile_ref, below_ref, right_ref, out_ref, quarter_ref):
    half = right_ref.shape[1]
    below = below_ref[...].astype(jnp.float32)
    right = right_ref[...].astype(jnp.float32)
    quarter = tile_ref[:, half:, half:] + below[:, half:] + right[:, :, half:]
    out_ref[0, :, :half, :half] = tile_ref[:, :half, :half]
    out_ref[0, :, :half, half:] = tile_ref[:, :half, half:] + below[:, :half]
    out_ref[0, :, half:, :half] = tile_ref[:, half:, :half] + right[:, :, :half]
    out_ref[0, :, half:, half:] = quarter
    quarter_ref[...] = quarter


def quarter_kernel(out_ref, quarter_ref, own_ref, same_ref, sum_ref, sem):
    half = quarter_ref.shape[1]
    sum_ref[...] = quarter_ref[...] + own_ref[...].astype(jnp.float32)
    copy = pltpu.make_async_copy(sum_ref, same_ref.at[0, :, pl.ds(half, half), pl.ds(half, half)], sem)
    copy.start()
    copy.wait()


VMEM = pl.BlockSpec(memory_space=pltpu.VMEM)
ANY = pl.BlockSpec(memory_space=pl.ANY)
SMEM = pl.BlockSpec(memory_space=pltpu.SMEM)
PARAMS = pltpu.CompilerParams(vmem_limit_bytes=48 * 1024 * 1024)


def shaped(*shape, dtype=jnp.bfloat16):
    return jax.ShapeDtypeStruct(shape, dtype)


def kernel(body, name, in_specs, out_shape, scratch=()):
    return pl.pallas_call(
        body, in_specs=in_specs, out_specs=[VMEM] * len(out_shape), out_shape=out_shape, scratch_shapes=scratch, compiler_params=PARAMS, name=name
    )


def local(object_slices, probe, fresnel_taps, offsets, counts, measured):
    width = probe.shape[1]
    half = width // 2
    wide = width + half
    full = shaped(2 * width, width)
    part = shaped(width, width)
    row_tiles = max(lax.axis_size("tile") // 16, 2)
    probe = probe.reshape(2 * width, width)
    fourier = jnp.asarray(fourier_matrix(width), jnp.bfloat16)

    far_tile = crossed(object_slices[0], "cuts", 2)
    tile, below, right = kernel(cut_kernel, "cut", [VMEM], [shaped(2, width, width), shaped(2, width, half), shaped(2, half, width)])(
        object_slices[0]
    )
    (own,) = kernel(seal_kernel, "seal", [VMEM, VMEM], [shaped(2, half + 16, half)])(tile, offsets)
    below = passed_along(below, "tile", 1)
    right = passed_along(right, "tile", row_tiles)
    own = turned(own, row_tiles + 2, row_tiles)
    below, far_tile = lax.optimization_barrier((below, far_tile))
    far_below = crossed(below, "cuts", 2)
    far_right = crossed(right, "cuts", 2)
    far_own = crossed(own, "cuts", 2)
    level = shaped(half + 16, width)
    band, level = kernel(band_kernel, "band", [SMEM, VMEM, VMEM], [shaped(4, width, width), level])(counts, fresnel_taps, measured)
    level, right = lax.optimization_barrier((level, right))
    level = passed_along(level, "tile", row_tiles + 1)
    rows, columns, rows_back, columns_back = kernel(
        window_kernel,
        "window",
        [VMEM],
        [part, shaped(2, wide, width), shaped(2, wide, width), shaped(2 * width, wide)],
    )(own)
    first, second = kernel(extract_kernel, "near", [VMEM] * 6, [full, full])(rows, columns, tile, below, right, own)
    swapped = crossed(second, "cuts", 1)
    far_level = crossed(level, "cuts", 2)
    straight, far_second = kernel(extract_kernel, "far", [VMEM] * 6, [full, full])(rows, columns, far_tile, far_below, far_right, far_own)
    far_second, far_level = lax.optimization_barrier((far_second, far_level))
    diagonal = crossed(far_second, "cuts", 1)
    one, two = kernel(head_kernel, "head", [VMEM] * 4, [full, full])(probe, band, first, swapped)
    mine, other = kernel(chain_kernel, "chain", [VMEM] * 11, [full, full], [pltpu.VMEM((2 * width, width), jnp.bfloat16)] * 3)(
        probe, first, swapped, straight, diagonal, level, far_level, band, fourier, one, two
    )
    other = crossed(other, "cuts", 1)
    total, below, right, own = kernel(
        scatter_kernel,
        "scatter",
        [VMEM] * 4,
        [shaped(2, width, width, dtype=jnp.float32), shaped(2, width, half), shaped(2, half, width), shaped(2, half, half)],
    )(rows_back, columns_back, mine, other)
    below = passed_along(below, "tile", -1)
    right = passed_along(right, "tile", -row_tiles)
    own = passed_along(own, "tile", -row_tiles - 1)
    whole = shaped(1, 2, width, width, dtype=jnp.float32)
    quarter = shaped(2, half, half, dtype=jnp.float32)
    out, quarter = kernel(total_kernel, "total", [VMEM] * 3, [whole, quarter])(total, below, right)
    out = pl.pallas_call(
        quarter_kernel,
        in_specs=[ANY, VMEM, VMEM],
        out_specs=ANY,
        out_shape=whole,
        input_output_aliases={0: 0},
        scratch_shapes=[pltpu.VMEM((2, half, half), jnp.float32), pltpu.SemaphoreType.DMA],
        compiler_params=PARAMS,
        name="quarter",
    )(out, quarter, own)
    return out


def solution(mesh):
    return jax.shard_map(
        local,
        mesh=mesh,
        in_specs=(
            P("cuts", None, "tile", None),
            P(),
            P(),
            P("tile", None),
            P("tile"),
            P("tile", None, None),
        ),
        out_specs=P("cuts", None, "tile", None),
        check_vma=False,
    )
```

```python
import jax
import jax.numpy as jnp
import numpy as np
from jax import lax
from jax.experimental import pallas as pl
from jax.experimental.pallas import tpu as pltpu
from jax.sharding import PartitionSpec as P


def passed_along(value, axis, steps):
    count = lax.axis_size(axis)
    pairs = [(source, (source + steps) % count) for source in range(count)]
    return lax.ppermute(value, axis, pairs)


def crossed(value, axis, mask):
    pairs = [(source, source ^ mask) for source in range(lax.axis_size(axis))]
    return lax.ppermute(value, axis, pairs)


def fourier_matrix(width):
    index = np.arange(width)
    angle = 2.0 * np.pi * (index[:, None] * index[None, :] % width) / width
    return np.stack([np.cos(angle), -np.sin(angle)]) / np.sqrt(width)


def dot(left, right):
    return jnp.dot(left, right, preferred_element_type=jnp.float32)


def sandwich(left_real, left_imag, field, right_real, right_imag):
    right = jnp.concatenate([right_real, right_imag], axis=0)
    top = dot(jnp.concatenate([left_real, -left_imag], axis=1), field).astype(jnp.bfloat16)
    bottom = dot(jnp.concatenate([left_imag, left_real], axis=1), field).astype(jnp.bfloat16)
    real = dot(jnp.concatenate([top, -bottom], axis=1), right)
    imag = dot(jnp.concatenate([bottom, top], axis=1), right)
    return jnp.concatenate([real, imag], axis=0)


def complex_mul(first, second, sign):
    width = first.shape[1]
    fr = first[:width].astype(jnp.float32)
    fi = first[width:].astype(jnp.float32) * sign
    sr = second[:width].astype(jnp.float32)
    si = second[width:].astype(jnp.float32)
    return jnp.concatenate([fr * sr - fi * si, fr * si + fi * sr], axis=0)


def band_kernel(counts_ref, taps_ref, measured_ref, band_ref, level_ref):
    width = band_ref.shape[1]
    half = taps_ref.shape[1] // 2
    core = lax.rem(lax.axis_index("cuts"), 2)
    rows = width // 2
    first = pl.multiple_of(lax.axis_index("cuts") // 2 * rows, rows)
    level_ref[:rows, :] = measured_ref[core, pl.ds(first, rows), :].astype(jnp.bfloat16)
    live = (core < counts_ref[0]).astype(jnp.float32)
    level_ref[rows:, :] = jnp.full((level_ref.shape[0] - rows, width), live, jnp.float32).astype(jnp.bfloat16)
    rows = lax.broadcasted_iota(jnp.int32, (width, width), 0)
    columns = lax.broadcasted_iota(jnp.int32, (width, width), 1)
    inside = jnp.abs(columns - rows) <= half
    for part in range(2):
        line = taps_ref[part : part + 1, :].astype(jnp.float32)
        filler = jnp.zeros((1, width - line.shape[1]), jnp.float32)
        line = jnp.concatenate([line, filler], axis=1)
        spread = jnp.broadcast_to(line, (width, width))
        turned = pltpu.roll(spread, width - half, 1, stride=1, stride_axis=0)
        band = jnp.where(inside, turned, 0.0)
        band_ref[part] = band.astype(jnp.bfloat16)
        band_ref[part + 2] = band.T.astype(jnp.bfloat16)


def cut_kernel(tile_ref, whole_ref, below_ref, right_ref):
    half = right_ref.shape[1]
    whole_ref[...] = tile_ref[...]
    below_ref[...] = tile_ref[:, :, half:]
    right_ref[...] = tile_ref[:, half:, :]


def seal_kernel(tile_ref, offsets_ref, own_ref):
    half = tile_ref.shape[1] // 2
    own_ref[:, :half, :] = tile_ref[:, half:, half:]
    shape = (own_ref.shape[1] - half, half)
    line = lax.broadcasted_iota(jnp.int32, shape, 0)
    lines = jnp.zeros(shape, jnp.float32)
    for index in range(4):
        value = offsets_ref[index // 2 : index // 2 + 1, index % 2 : index % 2 + 1].astype(jnp.float32)
        lines = jnp.where(line == index, value, lines)
    for part in range(2):
        own_ref[part, half:, :] = lines.astype(jnp.bfloat16)


def window_kernel(own_ref, rows_ref, columns_ref, rows_back_ref, columns_back_ref):
    half = own_ref.shape[2]
    width = 2 * half
    core = lax.rem(lax.axis_index("cuts"), 2)
    lines = own_ref[0, half:, :].astype(jnp.float32).astype(jnp.int32) - half

    def placed(shape, axis, shift):
        i = lax.broadcasted_iota(jnp.int32, shape, axis)
        j = lax.broadcasted_iota(jnp.int32, shape, 1 - axis)
        shift = jnp.concatenate([shift] * (shape[1] // half), axis=1)
        return jnp.where(j - i == shift, 1.0, 0.0).astype(jnp.bfloat16)

    for place in range(2):
        second = core != place
        row = jnp.where(second, lines[2:3], lines[0:1])
        column = jnp.where(second, lines[3:4], lines[1:2])
        rows_ref[place * half : (place + 1) * half, :] = placed((half, width), 0, row)
        columns_ref[place] = placed((width + half, width), 1, column)
        rows_back_ref[place] = placed((width + half, width), 1, row)
        columns_back_ref[place * width : (place + 1) * width, :] = placed((width, width + half), 0, column)


def extract_kernel(rows_ref, columns_ref, tile_ref, below_ref, right_ref, own_ref, first_ref, second_ref):
    width = tile_ref.shape[1]
    half = width // 2
    wide = width + half
    blocks = []
    for part in range(2):
        upper = jnp.concatenate([own_ref[part, :half], right_ref[part]], axis=1)
        lower = jnp.concatenate([below_ref[part], tile_ref[part]], axis=1)
        blocks.append(jnp.concatenate([upper, lower], axis=0))
    block = jnp.concatenate(blocks, axis=1)
    strips = [dot(rows_ref[...], block[top : top + width]).astype(jnp.bfloat16) for top in (0, half)]
    for place, out_ref in enumerate((first_ref, second_ref)):
        mine = [strip[place * half : (place + 1) * half, part * wide : (part + 1) * wide] for part in range(2) for strip in strips]
        out_ref[...] = dot(jnp.concatenate(mine, axis=0), columns_ref[place]).astype(jnp.bfloat16)


def ordered(first_ref, second_ref):
    odd = lax.rem(lax.axis_index("cuts"), 2) == 1
    first, second = first_ref[...], second_ref[...]
    return jnp.where(odd, second, first), jnp.where(odd, first, second)


def near_chip():
    return lax.axis_index("cuts") < 2


def spread_on(spread, patch, band_ref):
    wave = complex_mul(spread, patch, 1.0).astype(jnp.bfloat16)
    return sandwich(band_ref[0], band_ref[1], wave, band_ref[2], band_ref[3]).astype(jnp.bfloat16)


def back_on(back, patch, band_ref):
    carried = complex_mul(patch, back, -1.0).astype(jnp.bfloat16)
    return sandwich(band_ref[2], -band_ref[3], carried, band_ref[0], -band_ref[1]).astype(jnp.bfloat16)


def head_kernel(probe_ref, band_ref, p0_ref, p1_ref, one_ref, two_ref):
    @pl.when(near_chip())
    def _():
        patch_0, patch_1 = ordered(p0_ref, p1_ref)
        one_ref[...] = spread_on(probe_ref[...], patch_0, band_ref)
        two_ref[...] = spread_on(one_ref[...], patch_1, band_ref)


def chain_kernel(
    probe_ref, p0_ref, p1_ref, p2_ref, p3_ref, level_ref, far_level_ref, band_ref, fourier_ref, one_ref, two_ref, mine_ref, other_ref,
    keep_two_ref, keep_three_ref, wave_ref
):
    width = probe_ref.shape[1]

    @pl.when(near_chip())
    def _():
        patch_2, patch_3 = ordered(p2_ref, p3_ref)
        spread = spread_on(two_ref[...], patch_2, band_ref)
        wave_ref[...] = complex_mul(spread, patch_3, 1.0).astype(jnp.bfloat16)

    @pl.when(jnp.logical_not(near_chip()))
    def _():
        patch_0, patch_1 = ordered(p2_ref, p3_ref)
        patch_2, patch_3 = ordered(p0_ref, p1_ref)
        spread = spread_on(probe_ref[...], patch_0, band_ref)
        keep_two_ref[...] = spread_on(spread, patch_1, band_ref)
        keep_three_ref[...] = spread_on(keep_two_ref[...], patch_2, band_ref)
        wave_ref[...] = complex_mul(keep_three_ref[...], patch_3, 1.0).astype(jnp.bfloat16)

    fourier_r, fourier_i = fourier_ref[0], fourier_ref[1]
    far = sandwich(fourier_r, fourier_i, wave_ref[...], fourier_r, fourier_i)
    far_r, far_i = far[:width], far[width:]
    rows = width // 2
    level, far_level = level_ref[:rows, :].astype(jnp.float32), far_level_ref[:rows, :].astype(jnp.float32)
    level = jnp.concatenate([jnp.where(near_chip(), level, far_level), jnp.where(near_chip(), far_level, level)], axis=0)
    live = level_ref[rows : rows + 1, :].astype(jnp.float32)
    excess = 2.0 * live * (far_r * far_r + far_i * far_i - level)
    residual = jnp.concatenate([excess * far_r, excess * far_i], axis=0).astype(jnp.bfloat16)
    wave_ref[...] = sandwich(fourier_r, -fourier_i, residual, fourier_r, -fourier_i).astype(jnp.bfloat16)
    odd = lax.rem(lax.axis_index("cuts"), 2) == 1

    def out(low, high):
        mine_ref[...] = jnp.where(odd, high, low)
        other_ref[...] = jnp.where(odd, low, high)

    @pl.when(near_chip())
    def _():
        _, patch_1 = ordered(p0_ref, p1_ref)
        patch_2, patch_3 = ordered(p2_ref, p3_ref)
        back = back_on(wave_ref[...], patch_3, band_ref)
        back = back_on(back, patch_2, band_ref)
        high = complex_mul(one_ref[...], back, -1.0).astype(jnp.bfloat16)
        back = back_on(back, patch_1, band_ref)
        out(complex_mul(probe_ref[...], back, -1.0).astype(jnp.bfloat16), high)

    @pl.when(jnp.logical_not(near_chip()))
    def _():
        _, patch_3 = ordered(p0_ref, p1_ref)
        back = wave_ref[...]
        high = complex_mul(keep_three_ref[...], back, -1.0).astype(jnp.bfloat16)
        back = back_on(back, patch_3, band_ref)
        out(complex_mul(keep_two_ref[...], back, -1.0).astype(jnp.bfloat16), high)


def placed_rows(rows, ref):
    width = ref.shape[1]
    return dot(rows, jnp.concatenate([ref[:width, :], ref[width:, :]], axis=1)).astype(jnp.bfloat16)


def rows_kernel(rows_ref, mine_ref, strip_ref):
    strip_ref[...] = placed_rows(rows_ref[0], mine_ref)


def scatter_kernel(rows_ref, columns_ref, strip_ref, other_ref, tile_ref, below_ref, right_ref, own_ref):
    width = tile_ref.shape[1]
    half = width // 2
    strips = [strip_ref[...], placed_rows(rows_ref[1], other_ref)]
    for part in range(2):
        strip = jnp.concatenate([strip[:, part * width : (part + 1) * width] for strip in strips], axis=1)
        total = dot(strip, columns_ref[...])
        tile_ref[part] = total[half:, half:]
        below_ref[part] = total[half:, :half].astype(jnp.bfloat16)
        right_ref[part] = total[:half, half:].astype(jnp.bfloat16)
        own_ref[part] = total[:half, :half].astype(jnp.bfloat16)


def total_kernel(tile_ref, below_ref, right_ref, out_ref, quarter_ref):
    half = right_ref.shape[1]
    below = below_ref[...].astype(jnp.float32)
    right = right_ref[...].astype(jnp.float32)
    quarter = tile_ref[:, half:, half:] + below[:, half:] + right[:, :, half:]
    out_ref[0, :, :half, :half] = tile_ref[:, :half, :half]
    out_ref[0, :, :half, half:] = tile_ref[:, :half, half:] + below[:, :half]
    out_ref[0, :, half:, :half] = tile_ref[:, half:, :half] + right[:, :, :half]
    out_ref[0, :, half:, half:] = quarter
    quarter_ref[...] = quarter


def quarter_kernel(out_ref, quarter_ref, own_ref, same_ref, sum_ref, sem):
    half = quarter_ref.shape[1]
    sum_ref[...] = quarter_ref[...] + own_ref[...].astype(jnp.float32)
    copy = pltpu.make_async_copy(sum_ref, same_ref.at[0, :, pl.ds(half, half), pl.ds(half, half)], sem)
    copy.start()
    copy.wait()


VMEM = pl.BlockSpec(memory_space=pltpu.VMEM)
ANY = pl.BlockSpec(memory_space=pl.ANY)
SMEM = pl.BlockSpec(memory_space=pltpu.SMEM)
PARAMS = pltpu.CompilerParams(vmem_limit_bytes=48 * 1024 * 1024)


def shaped(*shape, dtype=jnp.bfloat16):
    return jax.ShapeDtypeStruct(shape, dtype)


def kernel(body, name, in_specs, out_shape, scratch=()):
    return pl.pallas_call(
        body, in_specs=in_specs, out_specs=[VMEM] * len(out_shape), out_shape=out_shape, scratch_shapes=scratch, compiler_params=PARAMS, name=name
    )


def local(object_slices, probe, fresnel_taps, offsets, counts, measured):
    width = probe.shape[1]
    half = width // 2
    wide = width + half
    full = shaped(2 * width, width)
    part = shaped(width, width)
    row_tiles = max(lax.axis_size("tile") // 16, 2)
    probe = probe.reshape(2 * width, width)
    fourier = jnp.asarray(fourier_matrix(width), jnp.bfloat16)

    far_tile = crossed(object_slices[0], "cuts", 2)
    tile, below, right = kernel(cut_kernel, "cut", [VMEM], [shaped(2, width, width), shaped(2, width, half), shaped(2, half, width)])(
        object_slices[0]
    )
    (own,) = kernel(seal_kernel, "seal", [VMEM, VMEM], [shaped(2, half + 16, half)])(tile, offsets)
    below = passed_along(below, "tile", 1)
    right = passed_along(right, "tile", row_tiles)
    own = passed_along(own, "tile", row_tiles + 1)
    below, far_tile = lax.optimization_barrier((below, far_tile))
    far_below = crossed(below, "cuts", 2)
    far_right = crossed(right, "cuts", 2)
    far_own = crossed(own, "cuts", 2)
    level = shaped(half + 16, width)
    band, level = kernel(band_kernel, "band", [SMEM, VMEM, VMEM], [shaped(4, width, width), level])(counts, fresnel_taps, measured)
    level, right = lax.optimization_barrier((level, right))
    level = passed_along(level, "tile", row_tiles + 1)
    rows, columns, rows_back, columns_back = kernel(
        window_kernel,
        "window",
        [VMEM],
        [part, shaped(2, wide, width), shaped(2, wide, width), shaped(2 * width, wide)],
    )(own)
    first, second = kernel(extract_kernel, "near", [VMEM] * 6, [full, full])(rows, columns, tile, below, right, own)
    swapped = crossed(second, "cuts", 1)
    far_level = crossed(level, "cuts", 2)
    straight, far_second = kernel(extract_kernel, "far", [VMEM] * 6, [full, full])(rows, columns, far_tile, far_below, far_right, far_own)
    far_second, far_level = lax.optimization_barrier((far_second, far_level))
    diagonal = crossed(far_second, "cuts", 1)
    one, two = kernel(head_kernel, "head", [VMEM] * 4, [full, full])(probe, band, first, swapped)
    mine, other = kernel(chain_kernel, "chain", [VMEM] * 11, [full, full], [pltpu.VMEM((2 * width, width), jnp.bfloat16)] * 3)(
        probe, first, swapped, straight, diagonal, level, far_level, band, fourier, one, two
    )
    other = crossed(other, "cuts", 1)
    (strip,) = kernel(rows_kernel, "rows", [VMEM] * 2, [shaped(wide, 2 * width)])(rows_back, mine)
    total, below, right, own = kernel(
        scatter_kernel,
        "scatter",
        [VMEM] * 4,
        [shaped(2, width, width, dtype=jnp.float32), shaped(2, width, half), shaped(2, half, width), shaped(2, half, half)],
    )(rows_back, columns_back, strip, other)
    below = passed_along(below, "tile", -1)
    right = passed_along(right, "tile", -row_tiles)
    own = passed_along(own, "tile", -row_tiles - 1)
    whole = shaped(1, 2, width, width, dtype=jnp.float32)
    quarter = shaped(2, half, half, dtype=jnp.float32)
    out, quarter = kernel(total_kernel, "total", [VMEM] * 3, [whole, quarter])(total, below, right)
    out = pl.pallas_call(
        quarter_kernel,
        in_specs=[ANY, VMEM, VMEM],
        out_specs=ANY,
        out_shape=whole,
        input_output_aliases={0: 0},
        scratch_shapes=[pltpu.VMEM((2, half, half), jnp.float32), pltpu.SemaphoreType.DMA],
        compiler_params=PARAMS,
        name="quarter",
    )(out, quarter, own)
    return out


def solution(mesh):
    return jax.shard_map(
        local,
        mesh=mesh,
        in_specs=(
            P("cuts", None, "tile", None),
            P(),
            P(),
            P("tile", None),
            P("tile"),
            P("tile", None, None),
        ),
        out_specs=P("cuts", None, "tile", None),
        check_vma=False,
    )
```

```python
import jax
import jax.numpy as jnp
import numpy as np
from jax import lax
from jax.experimental import pallas as pl
from jax.experimental.pallas import tpu as pltpu
from jax.sharding import PartitionSpec as P


def passed_along(value, axis, steps):
    count = lax.axis_size(axis)
    pairs = [(source, (source + steps) % count) for source in range(count)]
    return lax.ppermute(value, axis, pairs)


def crossed(value, axis, mask):
    pairs = [(source, source ^ mask) for source in range(lax.axis_size(axis))]
    return lax.ppermute(value, axis, pairs)


def fourier_matrix(width):
    index = np.arange(width)
    angle = 2.0 * np.pi * (index[:, None] * index[None, :] % width) / width
    return np.stack([np.cos(angle), -np.sin(angle)]) / np.sqrt(width)


def dot(left, right):
    return jnp.dot(left, right, preferred_element_type=jnp.float32)


def sandwich(left_real, left_imag, field, right_real, right_imag):
    right = jnp.concatenate([right_real, right_imag], axis=0)
    top = dot(jnp.concatenate([left_real, -left_imag], axis=1), field).astype(jnp.bfloat16)
    bottom = dot(jnp.concatenate([left_imag, left_real], axis=1), field).astype(jnp.bfloat16)
    real = dot(jnp.concatenate([top, -bottom], axis=1), right)
    imag = dot(jnp.concatenate([bottom, top], axis=1), right)
    return jnp.concatenate([real, imag], axis=0)


def complex_mul(first, second, sign):
    width = first.shape[1]
    fr = first[:width].astype(jnp.float32)
    fi = first[width:].astype(jnp.float32) * sign
    sr = second[:width].astype(jnp.float32)
    si = second[width:].astype(jnp.float32)
    return jnp.concatenate([fr * sr - fi * si, fr * si + fi * sr], axis=0)


def band_kernel(counts_ref, taps_ref, measured_ref, band_ref, level_ref):
    width = band_ref.shape[1]
    half = taps_ref.shape[1] // 2
    core = lax.rem(lax.axis_index("cuts"), 2)
    rows = width // 2
    first = pl.multiple_of(lax.axis_index("cuts") // 2 * rows, rows)
    level_ref[:rows, :] = measured_ref[core, pl.ds(first, rows), :].astype(jnp.bfloat16)
    live = (core < counts_ref[0]).astype(jnp.float32)
    level_ref[rows:, :] = jnp.full((level_ref.shape[0] - rows, width), live, jnp.float32).astype(jnp.bfloat16)
    rows = lax.broadcasted_iota(jnp.int32, (width, width), 0)
    columns = lax.broadcasted_iota(jnp.int32, (width, width), 1)
    inside = jnp.abs(columns - rows) <= half
    for part in range(2):
        line = taps_ref[part : part + 1, :].astype(jnp.float32)
        filler = jnp.zeros((1, width - line.shape[1]), jnp.float32)
        line = jnp.concatenate([line, filler], axis=1)
        spread = jnp.broadcast_to(line, (width, width))
        turned = pltpu.roll(spread, width - half, 1, stride=1, stride_axis=0)
        band = jnp.where(inside, turned, 0.0)
        band_ref[part] = band.astype(jnp.bfloat16)
        band_ref[part + 2] = band.T.astype(jnp.bfloat16)


def cut_kernel(tile_ref, whole_ref, below_ref, right_ref):
    half = right_ref.shape[1]
    whole_ref[...] = tile_ref[...]
    below_ref[...] = tile_ref[:, :, half:]
    right_ref[...] = tile_ref[:, half:, :]


def seal_kernel(tile_ref, offsets_ref, own_ref):
    half = tile_ref.shape[1] // 2
    own_ref[:, :half, :] = tile_ref[:, half:, half:]
    shape = (own_ref.shape[1] - half, half)
    line = lax.broadcasted_iota(jnp.int32, shape, 0)
    lines = jnp.zeros(shape, jnp.float32)
    for index in range(4):
        value = offsets_ref[index // 2 : index // 2 + 1, index % 2 : index % 2 + 1].astype(jnp.float32)
        lines = jnp.where(line == index, value, lines)
    for part in range(2):
        own_ref[part, half:, :] = lines.astype(jnp.bfloat16)


def window_kernel(own_ref, rows_ref, columns_ref, rows_back_ref, columns_back_ref):
    half = own_ref.shape[2]
    width = 2 * half
    core = lax.rem(lax.axis_index("cuts"), 2)
    lines = own_ref[0, half:, :].astype(jnp.float32).astype(jnp.int32) - half

    def placed(shape, axis, shift):
        i = lax.broadcasted_iota(jnp.int32, shape, axis)
        j = lax.broadcasted_iota(jnp.int32, shape, 1 - axis)
        shift = jnp.concatenate([shift] * (shape[1] // half), axis=1)
        return jnp.where(j - i == shift, 1.0, 0.0).astype(jnp.bfloat16)

    for place in range(2):
        second = core != place
        row = jnp.where(second, lines[2:3], lines[0:1])
        column = jnp.where(second, lines[3:4], lines[1:2])
        rows_ref[place * half : (place + 1) * half, :] = placed((half, width), 0, row)
        columns_ref[place] = placed((width + half, width), 1, column)
        rows_back_ref[place] = placed((width + half, width), 1, row)
        columns_back_ref[place * width : (place + 1) * width, :] = placed((width, width + half), 0, column)


def extract_kernel(rows_ref, columns_ref, tile_ref, below_ref, right_ref, own_ref, first_ref, second_ref):
    width = tile_ref.shape[1]
    half = width // 2
    wide = width + half
    blocks = []
    for part in range(2):
        upper = jnp.concatenate([own_ref[part, :half], right_ref[part]], axis=1)
        lower = jnp.concatenate([below_ref[part], tile_ref[part]], axis=1)
        blocks.append(jnp.concatenate([upper, lower], axis=0))
    block = jnp.concatenate(blocks, axis=1)
    strips = [dot(rows_ref[...], block[top : top + width]).astype(jnp.bfloat16) for top in (0, half)]
    for place, out_ref in enumerate((first_ref, second_ref)):
        mine = [strip[place * half : (place + 1) * half, part * wide : (part + 1) * wide] for part in range(2) for strip in strips]
        out_ref[...] = dot(jnp.concatenate(mine, axis=0), columns_ref[place]).astype(jnp.bfloat16)


def ordered(first_ref, second_ref):
    odd = lax.rem(lax.axis_index("cuts"), 2) == 1
    first, second = first_ref[...], second_ref[...]
    return jnp.where(odd, second, first), jnp.where(odd, first, second)


def near_chip():
    return lax.axis_index("cuts") < 2


def spread_on(spread, patch, band_ref):
    wave = complex_mul(spread, patch, 1.0).astype(jnp.bfloat16)
    return sandwich(band_ref[0], band_ref[1], wave, band_ref[2], band_ref[3]).astype(jnp.bfloat16)


def back_on(back, patch, band_ref):
    carried = complex_mul(patch, back, -1.0).astype(jnp.bfloat16)
    return sandwich(band_ref[2], -band_ref[3], carried, band_ref[0], -band_ref[1]).astype(jnp.bfloat16)


def head_kernel(probe_ref, band_ref, p0_ref, p1_ref, one_ref, two_ref):
    @pl.when(near_chip())
    def _():
        patch_0, patch_1 = ordered(p0_ref, p1_ref)
        one_ref[...] = spread_on(probe_ref[...], patch_0, band_ref)
        two_ref[...] = spread_on(one_ref[...], patch_1, band_ref)


def chain_kernel(
    probe_ref, p0_ref, p1_ref, p2_ref, p3_ref, level_ref, far_level_ref, band_ref, fourier_ref, one_ref, two_ref, mine_ref, other_ref,
    keep_two_ref, keep_three_ref, wave_ref
):
    width = probe_ref.shape[1]

    @pl.when(near_chip())
    def _():
        patch_2, patch_3 = ordered(p2_ref, p3_ref)
        spread = spread_on(two_ref[...], patch_2, band_ref)
        wave_ref[...] = complex_mul(spread, patch_3, 1.0).astype(jnp.bfloat16)

    @pl.when(jnp.logical_not(near_chip()))
    def _():
        patch_0, patch_1 = ordered(p2_ref, p3_ref)
        patch_2, patch_3 = ordered(p0_ref, p1_ref)
        spread = spread_on(probe_ref[...], patch_0, band_ref)
        keep_two_ref[...] = spread_on(spread, patch_1, band_ref)
        keep_three_ref[...] = spread_on(keep_two_ref[...], patch_2, band_ref)
        wave_ref[...] = complex_mul(keep_three_ref[...], patch_3, 1.0).astype(jnp.bfloat16)

    fourier_r, fourier_i = fourier_ref[0], fourier_ref[1]
    far = sandwich(fourier_r, fourier_i, wave_ref[...], fourier_r, fourier_i)
    far_r, far_i = far[:width], far[width:]
    rows = width // 2
    level, far_level = level_ref[:rows, :].astype(jnp.float32), far_level_ref[:rows, :].astype(jnp.float32)
    level = jnp.concatenate([jnp.where(near_chip(), level, far_level), jnp.where(near_chip(), far_level, level)], axis=0)
    live = level_ref[rows : rows + 1, :].astype(jnp.float32)
    excess = 2.0 * live * (far_r * far_r + far_i * far_i - level)
    residual = jnp.concatenate([excess * far_r, excess * far_i], axis=0).astype(jnp.bfloat16)
    wave_ref[...] = sandwich(fourier_r, -fourier_i, residual, fourier_r, -fourier_i).astype(jnp.bfloat16)
    odd = lax.rem(lax.axis_index("cuts"), 2) == 1

    def out(low, high):
        mine_ref[...] = jnp.where(odd, high, low)
        other_ref[...] = jnp.where(odd, low, high)

    @pl.when(near_chip())
    def _():
        _, patch_1 = ordered(p0_ref, p1_ref)
        patch_2, patch_3 = ordered(p2_ref, p3_ref)
        back = back_on(wave_ref[...], patch_3, band_ref)
        back = back_on(back, patch_2, band_ref)
        high = complex_mul(one_ref[...], back, -1.0).astype(jnp.bfloat16)
        back = back_on(back, patch_1, band_ref)
        out(complex_mul(probe_ref[...], back, -1.0).astype(jnp.bfloat16), high)

    @pl.when(jnp.logical_not(near_chip()))
    def _():
        _, patch_3 = ordered(p0_ref, p1_ref)
        back = wave_ref[...]
        high = complex_mul(keep_three_ref[...], back, -1.0).astype(jnp.bfloat16)
        back = back_on(back, patch_3, band_ref)
        out(complex_mul(keep_two_ref[...], back, -1.0).astype(jnp.bfloat16), high)


def placed_rows(rows, ref):
    width = ref.shape[1]
    return dot(rows, jnp.concatenate([ref[:width, :], ref[width:, :]], axis=1)).astype(jnp.bfloat16)


def rows_kernel(rows_ref, mine_ref, strip_ref):
    strip_ref[...] = placed_rows(rows_ref[0], mine_ref)


def scatter_kernel(rows_ref, columns_ref, strip_ref, other_ref, tile_ref, below_ref, right_ref, own_ref):
    width = tile_ref.shape[1]
    half = width // 2
    strips = [strip_ref[...], placed_rows(rows_ref[1], other_ref)]
    for part in range(2):
        strip = jnp.concatenate([strip[:, part * width : (part + 1) * width] for strip in strips], axis=1)
        total = dot(strip, columns_ref[...])
        tile_ref[part] = total[half:, half:]
        below_ref[part] = total[half:, :half].astype(jnp.bfloat16)
        right_ref[part] = total[:half, half:].astype(jnp.bfloat16)
        own_ref[part] = total[:half, :half].astype(jnp.bfloat16)


def total_kernel(tile_ref, below_ref, right_ref, out_ref, quarter_ref):
    half = right_ref.shape[1]
    below = below_ref[...].astype(jnp.float32)
    right = right_ref[...].astype(jnp.float32)
    quarter = tile_ref[:, half:, half:] + below[:, half:] + right[:, :, half:]
    out_ref[0, :, :half, :half] = tile_ref[:, :half, :half]
    out_ref[0, :, :half, half:] = tile_ref[:, :half, half:] + below[:, :half]
    out_ref[0, :, half:, :half] = tile_ref[:, half:, :half] + right[:, :, :half]
    out_ref[0, :, half:, half:] = quarter
    quarter_ref[...] = quarter


def quarter_kernel(out_ref, quarter_ref, own_ref, same_ref, sum_ref, sem):
    half = quarter_ref.shape[1]
    sum_ref[...] = quarter_ref[...] + own_ref[...].astype(jnp.float32)
    copy = pltpu.make_async_copy(sum_ref, same_ref.at[0, :, pl.ds(half, half), pl.ds(half, half)], sem)
    copy.start()
    copy.wait()


VMEM = pl.BlockSpec(memory_space=pltpu.VMEM)
ANY = pl.BlockSpec(memory_space=pl.ANY)
SMEM = pl.BlockSpec(memory_space=pltpu.SMEM)
PARAMS = pltpu.CompilerParams(vmem_limit_bytes=48 * 1024 * 1024)


def shaped(*shape, dtype=jnp.bfloat16):
    return jax.ShapeDtypeStruct(shape, dtype)


def kernel(body, name, in_specs, out_shape, scratch=()):
    return pl.pallas_call(
        body, in_specs=in_specs, out_specs=[VMEM] * len(out_shape), out_shape=out_shape, scratch_shapes=scratch, compiler_params=PARAMS, name=name
    )


def local(object_slices, probe, fresnel_taps, offsets, counts, measured):
    width = probe.shape[1]
    half = width // 2
    wide = width + half
    full = shaped(2 * width, width)
    part = shaped(width, width)
    row_tiles = max(lax.axis_size("tile") // 16, 2)
    probe = probe.reshape(2 * width, width)
    fourier = jnp.asarray(fourier_matrix(width), jnp.bfloat16)

    far_tile = crossed(object_slices[0], "cuts", 2)
    tile, below, right = kernel(cut_kernel, "cut", [VMEM], [shaped(2, width, width), shaped(2, width, half), shaped(2, half, width)])(
        object_slices[0]
    )
    (own,) = kernel(seal_kernel, "seal", [VMEM, VMEM], [shaped(2, half + 16, half)])(tile, offsets)
    below = passed_along(below, "tile", 1)
    right = passed_along(right, "tile", row_tiles)
    own = passed_along(own, "tile", row_tiles + 1)
    far_right = crossed(right, "cuts", 2)
    far_own = crossed(own, "cuts", 2)
    level = shaped(half + 16, width)
    band, level = kernel(band_kernel, "band", [SMEM, VMEM, VMEM], [shaped(4, width, width), level])(counts, fresnel_taps, measured)
    level, far_tile = lax.optimization_barrier((level, far_tile))
    below, far_tile = lax.optimization_barrier((below, far_tile))
    far_below = crossed(below, "cuts", 2)
    level = passed_along(level, "tile", row_tiles + 1)
    rows, columns, rows_back, columns_back = kernel(
        window_kernel,
        "window",
        [VMEM],
        [part, shaped(2, wide, width), shaped(2, wide, width), shaped(2 * width, wide)],
    )(own)
    first, second = kernel(extract_kernel, "near", [VMEM] * 6, [full, full])(rows, columns, tile, below, right, own)
    swapped = crossed(second, "cuts", 1)
    far_level = crossed(level, "cuts", 2)
    straight, far_second = kernel(extract_kernel, "far", [VMEM] * 6, [full, full])(rows, columns, far_tile, far_below, far_right, far_own)
    far_second, far_level = lax.optimization_barrier((far_second, far_level))
    diagonal = crossed(far_second, "cuts", 1)
    one, two = kernel(head_kernel, "head", [VMEM] * 4, [full, full])(probe, band, first, swapped)
    mine, other = kernel(chain_kernel, "chain", [VMEM] * 11, [full, full], [pltpu.VMEM((2 * width, width), jnp.bfloat16)] * 3)(
        probe, first, swapped, straight, diagonal, level, far_level, band, fourier, one, two
    )
    other = crossed(other, "cuts", 1)
    (strip,) = kernel(rows_kernel, "rows", [VMEM] * 2, [shaped(wide, 2 * width)])(rows_back, mine)
    total, below, right, own = kernel(
        scatter_kernel,
        "scatter",
        [VMEM] * 4,
        [shaped(2, width, width, dtype=jnp.float32), shaped(2, width, half), shaped(2, half, width), shaped(2, half, half)],
    )(rows_back, columns_back, strip, other)
    below = passed_along(below, "tile", -1)
    right = passed_along(right, "tile", -row_tiles)
    own = passed_along(own, "tile", -row_tiles - 1)
    whole = shaped(1, 2, width, width, dtype=jnp.float32)
    quarter = shaped(2, half, half, dtype=jnp.float32)
    out, quarter = kernel(total_kernel, "total", [VMEM] * 3, [whole, quarter])(total, below, right)
    out = pl.pallas_call(
        quarter_kernel,
        in_specs=[ANY, VMEM, VMEM],
        out_specs=ANY,
        out_shape=whole,
        input_output_aliases={0: 0},
        scratch_shapes=[pltpu.VMEM((2, half, half), jnp.float32), pltpu.SemaphoreType.DMA],
        compiler_params=PARAMS,
        name="quarter",
    )(out, quarter, own)
    return out


def solution(mesh):
    return jax.shard_map(
        local,
        mesh=mesh,
        in_specs=(
            P("cuts", None, "tile", None),
            P(),
            P(),
            P("tile", None),
            P("tile"),
            P("tile", None, None),
        ),
        out_specs=P("cuts", None, "tile", None),
        check_vma=False,
    )
```

```python
import jax
import jax.numpy as jnp
import numpy as np
from jax import lax
from jax.experimental import pallas as pl
from jax.experimental.pallas import tpu as pltpu
from jax.sharding import PartitionSpec as P


def passed_along(value, axis, steps):
    count = lax.axis_size(axis)
    pairs = [(source, (source + steps) % count) for source in range(count)]
    return lax.ppermute(value, axis, pairs)


def turned(value, even, odd):
    count = lax.axis_size("tile")
    value = lax.ppermute(value, "tile", [(source, source ^ 1) for source in range(count)])
    return lax.ppermute(value, "tile", [(source, (source + (odd if source % 2 else even)) % count) for source in range(count)])


def crossed(value, axis, mask):
    pairs = [(source, source ^ mask) for source in range(lax.axis_size(axis))]
    return lax.ppermute(value, axis, pairs)


def fourier_matrix(width):
    index = np.arange(width)
    angle = 2.0 * np.pi * (index[:, None] * index[None, :] % width) / width
    return np.stack([np.cos(angle), -np.sin(angle)]) / np.sqrt(width)


def dot(left, right):
    return jnp.dot(left, right, preferred_element_type=jnp.float32)


def sandwich(left_real, left_imag, field, right_real, right_imag):
    right = jnp.concatenate([right_real, right_imag], axis=0)
    top = dot(jnp.concatenate([left_real, -left_imag], axis=1), field).astype(jnp.bfloat16)
    bottom = dot(jnp.concatenate([left_imag, left_real], axis=1), field).astype(jnp.bfloat16)
    real = dot(jnp.concatenate([top, -bottom], axis=1), right)
    imag = dot(jnp.concatenate([bottom, top], axis=1), right)
    return jnp.concatenate([real, imag], axis=0)


def complex_mul(first, second, sign):
    width = first.shape[1]
    fr = first[:width].astype(jnp.float32)
    fi = first[width:].astype(jnp.float32) * sign
    sr = second[:width].astype(jnp.float32)
    si = second[width:].astype(jnp.float32)
    return jnp.concatenate([fr * sr - fi * si, fr * si + fi * sr], axis=0)


def band_kernel(counts_ref, taps_ref, measured_ref, band_ref, level_ref):
    width = band_ref.shape[1]
    half = taps_ref.shape[1] // 2
    core = lax.rem(lax.axis_index("cuts"), 2)
    rows = width // 2
    first = pl.multiple_of(lax.axis_index("cuts") // 2 * rows, rows)
    level_ref[:rows, :] = measured_ref[core, pl.ds(first, rows), :].astype(jnp.bfloat16)
    live = (core < counts_ref[0]).astype(jnp.float32)
    level_ref[rows:, :] = jnp.full((level_ref.shape[0] - rows, width), live, jnp.float32).astype(jnp.bfloat16)
    rows = lax.broadcasted_iota(jnp.int32, (width, width), 0)
    columns = lax.broadcasted_iota(jnp.int32, (width, width), 1)
    inside = jnp.abs(columns - rows) <= half
    for part in range(2):
        line = taps_ref[part : part + 1, :].astype(jnp.float32)
        filler = jnp.zeros((1, width - line.shape[1]), jnp.float32)
        line = jnp.concatenate([line, filler], axis=1)
        spread = jnp.broadcast_to(line, (width, width))
        turned = pltpu.roll(spread, width - half, 1, stride=1, stride_axis=0)
        band = jnp.where(inside, turned, 0.0)
        band_ref[part] = band.astype(jnp.bfloat16)
        band_ref[part + 2] = band.T.astype(jnp.bfloat16)


def cut_kernel(tile_ref, whole_ref, below_ref, right_ref):
    half = right_ref.shape[1]
    whole_ref[...] = tile_ref[...]
    below_ref[...] = tile_ref[:, :, half:]
    right_ref[...] = tile_ref[:, half:, :]


def seal_kernel(tile_ref, offsets_ref, own_ref):
    half = tile_ref.shape[1] // 2
    own_ref[:, :half, :] = tile_ref[:, half:, half:]
    shape = (own_ref.shape[1] - half, half)
    line = lax.broadcasted_iota(jnp.int32, shape, 0)
    lines = jnp.zeros(shape, jnp.float32)
    for index in range(4):
        value = offsets_ref[index // 2 : index // 2 + 1, index % 2 : index % 2 + 1].astype(jnp.float32)
        lines = jnp.where(line == index, value, lines)
    for part in range(2):
        own_ref[part, half:, :] = lines.astype(jnp.bfloat16)


def window_kernel(own_ref, rows_ref, columns_ref, rows_back_ref, columns_back_ref):
    half = own_ref.shape[2]
    width = 2 * half
    core = lax.rem(lax.axis_index("cuts"), 2)
    lines = own_ref[0, half:, :].astype(jnp.float32).astype(jnp.int32) - half

    def placed(shape, axis, shift):
        i = lax.broadcasted_iota(jnp.int32, shape, axis)
        j = lax.broadcasted_iota(jnp.int32, shape, 1 - axis)
        shift = jnp.concatenate([shift] * (shape[1] // half), axis=1)
        return jnp.where(j - i == shift, 1.0, 0.0).astype(jnp.bfloat16)

    for place in range(2):
        second = core != place
        row = jnp.where(second, lines[2:3], lines[0:1])
        column = jnp.where(second, lines[3:4], lines[1:2])
        rows_ref[place * half : (place + 1) * half, :] = placed((half, width), 0, row)
        columns_ref[place] = placed((width + half, width), 1, column)
        rows_back_ref[place] = placed((width + half, width), 1, row)
        columns_back_ref[place * width : (place + 1) * width, :] = placed((width, width + half), 0, column)


def extract_kernel(rows_ref, columns_ref, tile_ref, below_ref, right_ref, own_ref, first_ref, second_ref):
    width = tile_ref.shape[1]
    half = width // 2
    wide = width + half
    blocks = []
    for part in range(2):
        upper = jnp.concatenate([own_ref[part, :half], right_ref[part]], axis=1)
        lower = jnp.concatenate([below_ref[part], tile_ref[part]], axis=1)
        blocks.append(jnp.concatenate([upper, lower], axis=0))
    block = jnp.concatenate(blocks, axis=1)
    strips = [dot(rows_ref[...], block[top : top + width]).astype(jnp.bfloat16) for top in (0, half)]
    for place, out_ref in enumerate((first_ref, second_ref)):
        mine = [strip[place * half : (place + 1) * half, part * wide : (part + 1) * wide] for part in range(2) for strip in strips]
        out_ref[...] = dot(jnp.concatenate(mine, axis=0), columns_ref[place]).astype(jnp.bfloat16)


def ordered(first_ref, second_ref):
    odd = lax.rem(lax.axis_index("cuts"), 2) == 1
    first, second = first_ref[...], second_ref[...]
    return jnp.where(odd, second, first), jnp.where(odd, first, second)


def near_chip():
    return lax.axis_index("cuts") < 2


def spread_on(spread, patch, band_ref):
    wave = complex_mul(spread, patch, 1.0).astype(jnp.bfloat16)
    return sandwich(band_ref[0], band_ref[1], wave, band_ref[2], band_ref[3]).astype(jnp.bfloat16)


def back_on(back, patch, band_ref):
    carried = complex_mul(patch, back, -1.0).astype(jnp.bfloat16)
    return sandwich(band_ref[2], -band_ref[3], carried, band_ref[0], -band_ref[1]).astype(jnp.bfloat16)


def head_kernel(probe_ref, band_ref, p0_ref, p1_ref, one_ref, two_ref):
    @pl.when(near_chip())
    def _():
        patch_0, patch_1 = ordered(p0_ref, p1_ref)
        one_ref[...] = spread_on(probe_ref[...], patch_0, band_ref)
        two_ref[...] = spread_on(one_ref[...], patch_1, band_ref)


def chain_kernel(
    probe_ref, p0_ref, p1_ref, p2_ref, p3_ref, level_ref, far_level_ref, band_ref, fourier_ref, one_ref, two_ref, mine_ref, other_ref,
    keep_two_ref, keep_three_ref, wave_ref
):
    width = probe_ref.shape[1]

    @pl.when(near_chip())
    def _():
        patch_2, patch_3 = ordered(p2_ref, p3_ref)
        spread = spread_on(two_ref[...], patch_2, band_ref)
        wave_ref[...] = complex_mul(spread, patch_3, 1.0).astype(jnp.bfloat16)

    @pl.when(jnp.logical_not(near_chip()))
    def _():
        patch_0, patch_1 = ordered(p2_ref, p3_ref)
        patch_2, patch_3 = ordered(p0_ref, p1_ref)
        spread = spread_on(probe_ref[...], patch_0, band_ref)
        keep_two_ref[...] = spread_on(spread, patch_1, band_ref)
        keep_three_ref[...] = spread_on(keep_two_ref[...], patch_2, band_ref)
        wave_ref[...] = complex_mul(keep_three_ref[...], patch_3, 1.0).astype(jnp.bfloat16)

    fourier_r, fourier_i = fourier_ref[0], fourier_ref[1]
    far = sandwich(fourier_r, fourier_i, wave_ref[...], fourier_r, fourier_i)
    far_r, far_i = far[:width], far[width:]
    rows = width // 2
    level, far_level = level_ref[:rows, :].astype(jnp.float32), far_level_ref[:rows, :].astype(jnp.float32)
    level = jnp.concatenate([jnp.where(near_chip(), level, far_level), jnp.where(near_chip(), far_level, level)], axis=0)
    live = level_ref[rows : rows + 1, :].astype(jnp.float32)
    excess = 2.0 * live * (far_r * far_r + far_i * far_i - level)
    residual = jnp.concatenate([excess * far_r, excess * far_i], axis=0).astype(jnp.bfloat16)
    wave_ref[...] = sandwich(fourier_r, -fourier_i, residual, fourier_r, -fourier_i).astype(jnp.bfloat16)
    odd = lax.rem(lax.axis_index("cuts"), 2) == 1

    def out(low, high):
        mine_ref[...] = jnp.where(odd, high, low)
        other_ref[...] = jnp.where(odd, low, high)

    @pl.when(near_chip())
    def _():
        _, patch_1 = ordered(p0_ref, p1_ref)
        patch_2, patch_3 = ordered(p2_ref, p3_ref)
        back = back_on(wave_ref[...], patch_3, band_ref)
        back = back_on(back, patch_2, band_ref)
        high = complex_mul(one_ref[...], back, -1.0).astype(jnp.bfloat16)
        back = back_on(back, patch_1, band_ref)
        out(complex_mul(probe_ref[...], back, -1.0).astype(jnp.bfloat16), high)

    @pl.when(jnp.logical_not(near_chip()))
    def _():
        _, patch_3 = ordered(p0_ref, p1_ref)
        back = wave_ref[...]
        high = complex_mul(keep_three_ref[...], back, -1.0).astype(jnp.bfloat16)
        back = back_on(back, patch_3, band_ref)
        out(complex_mul(keep_two_ref[...], back, -1.0).astype(jnp.bfloat16), high)


def placed_rows(rows, ref):
    width = ref.shape[1]
    return dot(rows, jnp.concatenate([ref[:width, :], ref[width:, :]], axis=1)).astype(jnp.bfloat16)


def rows_kernel(rows_ref, mine_ref, strip_ref):
    strip_ref[...] = placed_rows(rows_ref[0], mine_ref)


def scatter_kernel(rows_ref, columns_ref, strip_ref, other_ref, tile_ref, below_ref, right_ref, own_ref):
    width = tile_ref.shape[1]
    half = width // 2
    strips = [strip_ref[...], placed_rows(rows_ref[1], other_ref)]
    for part in range(2):
        strip = jnp.concatenate([strip[:, part * width : (part + 1) * width] for strip in strips], axis=1)
        total = dot(strip, columns_ref[...])
        tile_ref[part] = total[half:, half:]
        below_ref[part] = total[half:, :half].astype(jnp.bfloat16)
        right_ref[part] = total[:half, half:].astype(jnp.bfloat16)
        own_ref[part] = total[:half, :half].astype(jnp.bfloat16)


def total_kernel(tile_ref, below_ref, right_ref, out_ref, quarter_ref):
    half = right_ref.shape[1]
    below = below_ref[...].astype(jnp.float32)
    right = right_ref[...].astype(jnp.float32)
    quarter = tile_ref[:, half:, half:] + below[:, half:] + right[:, :, half:]
    out_ref[0, :, :half, :half] = tile_ref[:, :half, :half]
    out_ref[0, :, :half, half:] = tile_ref[:, :half, half:] + below[:, :half]
    out_ref[0, :, half:, :half] = tile_ref[:, half:, :half] + right[:, :, :half]
    out_ref[0, :, half:, half:] = quarter
    quarter_ref[...] = quarter


def quarter_kernel(out_ref, quarter_ref, own_ref, same_ref, sum_ref, sem):
    half = quarter_ref.shape[1]
    sum_ref[...] = quarter_ref[...] + own_ref[...].astype(jnp.float32)
    copy = pltpu.make_async_copy(sum_ref, same_ref.at[0, :, pl.ds(half, half), pl.ds(half, half)], sem)
    copy.start()
    copy.wait()


VMEM = pl.BlockSpec(memory_space=pltpu.VMEM)
ANY = pl.BlockSpec(memory_space=pl.ANY)
SMEM = pl.BlockSpec(memory_space=pltpu.SMEM)
PARAMS = pltpu.CompilerParams(vmem_limit_bytes=48 * 1024 * 1024)


def shaped(*shape, dtype=jnp.bfloat16):
    return jax.ShapeDtypeStruct(shape, dtype)


def kernel(body, name, in_specs, out_shape, scratch=()):
    return pl.pallas_call(
        body, in_specs=in_specs, out_specs=[VMEM] * len(out_shape), out_shape=out_shape, scratch_shapes=scratch, compiler_params=PARAMS, name=name
    )


def local(object_slices, probe, fresnel_taps, offsets, counts, measured):
    width = probe.shape[1]
    half = width // 2
    wide = width + half
    full = shaped(2 * width, width)
    part = shaped(width, width)
    row_tiles = max(lax.axis_size("tile") // 16, 2)
    probe = probe.reshape(2 * width, width)
    fourier = jnp.asarray(fourier_matrix(width), jnp.bfloat16)

    far_tile = crossed(object_slices[0], "cuts", 2)
    tile, below, right = kernel(cut_kernel, "cut", [VMEM], [shaped(2, width, width), shaped(2, width, half), shaped(2, half, width)])(
        object_slices[0]
    )
    (own,) = kernel(seal_kernel, "seal", [VMEM, VMEM], [shaped(2, half + 16, half)])(tile, offsets)
    below = passed_along(below, "tile", 1)
    right = passed_along(right, "tile", row_tiles)
    own = passed_along(own, "tile", row_tiles + 1)
    far_right = crossed(right, "cuts", 2)
    far_own = crossed(own, "cuts", 2)
    level = shaped(half + 16, width)
    band, level = kernel(band_kernel, "band", [SMEM, VMEM, VMEM], [shaped(4, width, width), level])(counts, fresnel_taps, measured)
    level, far_tile = lax.optimization_barrier((level, far_tile))
    below, far_tile = lax.optimization_barrier((below, far_tile))
    far_below = crossed(below, "cuts", 2)
    level = passed_along(level, "tile", row_tiles + 1)
    rows, columns, rows_back, columns_back = kernel(
        window_kernel,
        "window",
        [VMEM],
        [part, shaped(2, wide, width), shaped(2, wide, width), shaped(2 * width, wide)],
    )(own)
    first, second = kernel(extract_kernel, "near", [VMEM] * 6, [full, full])(rows, columns, tile, below, right, own)
    swapped = crossed(second, "cuts", 1)
    far_level = crossed(level, "cuts", 2)
    straight, far_second = kernel(extract_kernel, "far", [VMEM] * 6, [full, full])(rows, columns, far_tile, far_below, far_right, far_own)
    far_second, far_level = lax.optimization_barrier((far_second, far_level))
    diagonal = crossed(far_second, "cuts", 1)
    one, two = kernel(head_kernel, "head", [VMEM] * 4, [full, full])(probe, band, first, swapped)
    mine, other = kernel(chain_kernel, "chain", [VMEM] * 11, [full, full], [pltpu.VMEM((2 * width, width), jnp.bfloat16)] * 3)(
        probe, first, swapped, straight, diagonal, level, far_level, band, fourier, one, two
    )
    other = crossed(other, "cuts", 1)
    (strip,) = kernel(rows_kernel, "rows", [VMEM] * 2, [shaped(wide, 2 * width)])(rows_back, mine)
    total, below, right, own = kernel(
        scatter_kernel,
        "scatter",
        [VMEM] * 4,
        [shaped(2, width, width, dtype=jnp.float32), shaped(2, width, half), shaped(2, half, width), shaped(2, half, half)],
    )(rows_back, columns_back, strip, other)
    below = passed_along(below, "tile", -1)
    right = passed_along(right, "tile", -row_tiles)
    own = turned(own, -row_tiles, -row_tiles - 2)
    whole = shaped(1, 2, width, width, dtype=jnp.float32)
    quarter = shaped(2, half, half, dtype=jnp.float32)
    out, quarter = kernel(total_kernel, "total", [VMEM] * 3, [whole, quarter])(total, below, right)
    out = pl.pallas_call(
        quarter_kernel,
        in_specs=[ANY, VMEM, VMEM],
        out_specs=ANY,
        out_shape=whole,
        input_output_aliases={0: 0},
        scratch_shapes=[pltpu.VMEM((2, half, half), jnp.float32), pltpu.SemaphoreType.DMA],
        compiler_params=PARAMS,
        name="quarter",
    )(out, quarter, own)
    return out


def solution(mesh):
    return jax.shard_map(
        local,
        mesh=mesh,
        in_specs=(
            P("cuts", None, "tile", None),
            P(),
            P(),
            P("tile", None),
            P("tile"),
            P("tile", None, None),
        ),
        out_specs=P("cuts", None, "tile", None),
        check_vma=False,
    )
```

```python
import jax
import jax.numpy as jnp
import numpy as np
from jax import lax
from jax.experimental import pallas as pl
from jax.experimental.pallas import tpu as pltpu
from jax.sharding import PartitionSpec as P


SPARE = 16


def passed_along(value, axis, steps):
    count = lax.axis_size(axis)
    pairs = [(source, (source + steps) % count) for source in range(count)]
    return lax.ppermute(value, axis, pairs)


def crossed(value, axis, mask):
    pairs = [(source, source ^ mask) for source in range(lax.axis_size(axis))]
    return lax.ppermute(value, axis, pairs)


def fourier_matrix(width):
    index = np.arange(width)
    angle = 2.0 * np.pi * (index[:, None] * index[None, :] % width) / width
    return np.stack([np.cos(angle), -np.sin(angle)]) / np.sqrt(width)


def dot(left, right):
    return jnp.dot(left, right, preferred_element_type=jnp.float32)


def sandwich(left_real, left_imag, field, right_real, right_imag):
    right = jnp.concatenate([right_real, right_imag], axis=0)
    top = dot(jnp.concatenate([left_real, -left_imag], axis=1), field).astype(jnp.bfloat16)
    bottom = dot(jnp.concatenate([left_imag, left_real], axis=1), field).astype(jnp.bfloat16)
    real = dot(jnp.concatenate([top, -bottom], axis=1), right)
    imag = dot(jnp.concatenate([bottom, top], axis=1), right)
    return jnp.concatenate([real, imag], axis=0)


def complex_mul(first, second, sign):
    width = first.shape[1]
    fr = first[:width].astype(jnp.float32)
    fi = first[width:].astype(jnp.float32) * sign
    sr = second[:width].astype(jnp.float32)
    si = second[width:].astype(jnp.float32)
    return jnp.concatenate([fr * sr - fi * si, fr * si + fi * sr], axis=0)


def band_kernel(counts_ref, taps_ref, measured_ref, band_ref, level_ref):
    width = band_ref.shape[1]
    half = taps_ref.shape[1] // 2
    core = lax.rem(lax.axis_index("cuts"), 2)
    rows = width // 2
    first = pl.multiple_of(lax.axis_index("cuts") // 2 * rows, rows)
    level_ref[:rows, :] = measured_ref[core, pl.ds(first, rows), :].astype(jnp.bfloat16)
    live = (core < counts_ref[0]).astype(jnp.float32)
    level_ref[rows:, :] = jnp.full((level_ref.shape[0] - rows, width), live, jnp.float32).astype(jnp.bfloat16)
    rows = lax.broadcasted_iota(jnp.int32, (width, width), 0)
    columns = lax.broadcasted_iota(jnp.int32, (width, width), 1)
    inside = jnp.abs(columns - rows) <= half
    for part in range(2):
        line = taps_ref[part : part + 1, :].astype(jnp.float32)
        filler = jnp.zeros((1, width - line.shape[1]), jnp.float32)
        line = jnp.concatenate([line, filler], axis=1)
        spread = jnp.broadcast_to(line, (width, width))
        turned = pltpu.roll(spread, width - half, 1, stride=1, stride_axis=0)
        band = jnp.where(inside, turned, 0.0)
        band_ref[part] = band.astype(jnp.bfloat16)
        band_ref[part + 2] = band.T.astype(jnp.bfloat16)


def cut_kernel(tile_ref, whole_ref, below_ref, right_ref):
    half = right_ref.shape[1]
    whole_ref[...] = tile_ref[...]
    below_ref[:, : 2 * half, :] = tile_ref[:, :, half:]
    below_ref[:, 2 * half :, :] = jnp.zeros((2, SPARE, half), jnp.bfloat16)
    right_ref[...] = tile_ref[:, half:, :]


def seal_kernel(tile_ref, offsets_ref, own_ref):
    half = tile_ref.shape[1] // 2
    own_ref[:, :half, :] = tile_ref[:, half:, half:]
    shape = (own_ref.shape[1] - half, half)
    line = lax.broadcasted_iota(jnp.int32, shape, 0)
    lines = jnp.zeros(shape, jnp.float32)
    for index in range(4):
        value = offsets_ref[index // 2 : index // 2 + 1, index % 2 : index % 2 + 1].astype(jnp.float32)
        lines = jnp.where(line == index, value, lines)
    for part in range(2):
        own_ref[part, half:, :] = lines.astype(jnp.bfloat16)


def window_kernel(own_ref, rows_ref, columns_ref, rows_back_ref, columns_back_ref):
    half = own_ref.shape[2]
    width = 2 * half
    core = lax.rem(lax.axis_index("cuts"), 2)
    lines = own_ref[0, half:, :].astype(jnp.float32).astype(jnp.int32) - half

    def placed(shape, axis, shift):
        i = lax.broadcasted_iota(jnp.int32, shape, axis)
        j = lax.broadcasted_iota(jnp.int32, shape, 1 - axis)
        shift = jnp.concatenate([shift] * (shape[1] // half), axis=1)
        return jnp.where(j - i == shift, 1.0, 0.0).astype(jnp.bfloat16)

    for place in range(2):
        second = core != place
        row = jnp.where(second, lines[2:3], lines[0:1])
        column = jnp.where(second, lines[3:4], lines[1:2])
        rows_ref[place * half : (place + 1) * half, :] = placed((half, width), 0, row)
        columns_ref[place] = placed((width + half, width), 1, column)
        rows_back_ref[place] = placed((width + half, width), 1, row)
        columns_back_ref[place * width : (place + 1) * width, :] = placed((width, width + half), 0, column)


def extract_kernel(rows_ref, columns_ref, tile_ref, below_ref, right_ref, own_ref, first_ref, second_ref):
    width = tile_ref.shape[1]
    half = width // 2
    wide = width + half
    blocks = []
    for part in range(2):
        upper = jnp.concatenate([own_ref[part, :half], right_ref[part]], axis=1)
        lower = jnp.concatenate([below_ref[part, :width], tile_ref[part]], axis=1)
        blocks.append(jnp.concatenate([upper, lower], axis=0))
    block = jnp.concatenate(blocks, axis=1)
    strips = [dot(rows_ref[...], block[top : top + width]).astype(jnp.bfloat16) for top in (0, half)]
    for place, out_ref in enumerate((first_ref, second_ref)):
        mine = [strip[place * half : (place + 1) * half, part * wide : (part + 1) * wide] for part in range(2) for strip in strips]
        out_ref[...] = dot(jnp.concatenate(mine, axis=0), columns_ref[place]).astype(jnp.bfloat16)


def ordered(first_ref, second_ref):
    odd = lax.rem(lax.axis_index("cuts"), 2) == 1
    first, second = first_ref[...], second_ref[...]
    return jnp.where(odd, second, first), jnp.where(odd, first, second)


def near_chip():
    return lax.axis_index("cuts") < 2


def spread_on(spread, patch, band_ref):
    wave = complex_mul(spread, patch, 1.0).astype(jnp.bfloat16)
    return sandwich(band_ref[0], band_ref[1], wave, band_ref[2], band_ref[3]).astype(jnp.bfloat16)


def back_on(back, patch, band_ref):
    carried = complex_mul(patch, back, -1.0).astype(jnp.bfloat16)
    return sandwich(band_ref[2], -band_ref[3], carried, band_ref[0], -band_ref[1]).astype(jnp.bfloat16)


def head_kernel(probe_ref, band_ref, p0_ref, p1_ref, one_ref, two_ref):
    @pl.when(near_chip())
    def _():
        patch_0, patch_1 = ordered(p0_ref, p1_ref)
        one_ref[...] = spread_on(probe_ref[...], patch_0, band_ref)
        two_ref[...] = spread_on(one_ref[...], patch_1, band_ref)


def chain_kernel(
    probe_ref, p0_ref, p1_ref, p2_ref, p3_ref, level_ref, far_level_ref, band_ref, fourier_ref, one_ref, two_ref, mine_ref, other_ref,
    keep_two_ref, keep_three_ref, wave_ref
):
    width = probe_ref.shape[1]

    @pl.when(near_chip())
    def _():
        patch_2, patch_3 = ordered(p2_ref, p3_ref)
        spread = spread_on(two_ref[...], patch_2, band_ref)
        wave_ref[...] = complex_mul(spread, patch_3, 1.0).astype(jnp.bfloat16)

    @pl.when(jnp.logical_not(near_chip()))
    def _():
        patch_0, patch_1 = ordered(p2_ref, p3_ref)
        patch_2, patch_3 = ordered(p0_ref, p1_ref)
        spread = spread_on(probe_ref[...], patch_0, band_ref)
        keep_two_ref[...] = spread_on(spread, patch_1, band_ref)
        keep_three_ref[...] = spread_on(keep_two_ref[...], patch_2, band_ref)
        wave_ref[...] = complex_mul(keep_three_ref[...], patch_3, 1.0).astype(jnp.bfloat16)

    fourier_r, fourier_i = fourier_ref[0], fourier_ref[1]
    far = sandwich(fourier_r, fourier_i, wave_ref[...], fourier_r, fourier_i)
    far_r, far_i = far[:width], far[width:]
    rows = width // 2
    level, far_level = level_ref[:rows, :].astype(jnp.float32), far_level_ref[:rows, :].astype(jnp.float32)
    level = jnp.concatenate([jnp.where(near_chip(), level, far_level), jnp.where(near_chip(), far_level, level)], axis=0)
    live = level_ref[rows : rows + 1, :].astype(jnp.float32)
    excess = 2.0 * live * (far_r * far_r + far_i * far_i - level)
    residual = jnp.concatenate([excess * far_r, excess * far_i], axis=0).astype(jnp.bfloat16)
    wave_ref[...] = sandwich(fourier_r, -fourier_i, residual, fourier_r, -fourier_i).astype(jnp.bfloat16)
    odd = lax.rem(lax.axis_index("cuts"), 2) == 1

    def out(low, high):
        mine_ref[...] = jnp.where(odd, high, low)
        other_ref[...] = jnp.where(odd, low, high)

    @pl.when(near_chip())
    def _():
        _, patch_1 = ordered(p0_ref, p1_ref)
        patch_2, patch_3 = ordered(p2_ref, p3_ref)
        back = back_on(wave_ref[...], patch_3, band_ref)
        back = back_on(back, patch_2, band_ref)
        high = complex_mul(one_ref[...], back, -1.0).astype(jnp.bfloat16)
        back = back_on(back, patch_1, band_ref)
        out(complex_mul(probe_ref[...], back, -1.0).astype(jnp.bfloat16), high)

    @pl.when(jnp.logical_not(near_chip()))
    def _():
        _, patch_3 = ordered(p0_ref, p1_ref)
        back = wave_ref[...]
        high = complex_mul(keep_three_ref[...], back, -1.0).astype(jnp.bfloat16)
        back = back_on(back, patch_3, band_ref)
        out(complex_mul(keep_two_ref[...], back, -1.0).astype(jnp.bfloat16), high)


def placed_rows(rows, ref):
    width = ref.shape[1]
    return dot(rows, jnp.concatenate([ref[:width, :], ref[width:, :]], axis=1)).astype(jnp.bfloat16)


def rows_kernel(rows_ref, mine_ref, strip_ref):
    strip_ref[...] = placed_rows(rows_ref[0], mine_ref)


def scatter_kernel(rows_ref, columns_ref, strip_ref, other_ref, tile_ref, below_ref, right_ref, own_ref):
    width = tile_ref.shape[1]
    half = width // 2
    strips = [strip_ref[...], placed_rows(rows_ref[1], other_ref)]
    for part in range(2):
        strip = jnp.concatenate([strip[:, part * width : (part + 1) * width] for strip in strips], axis=1)
        total = dot(strip, columns_ref[...])
        tile_ref[part] = total[half:, half:]
        below_ref[part] = total[half:, :half].astype(jnp.bfloat16)
        right_ref[part] = total[:half, half:].astype(jnp.bfloat16)
        own_ref[part] = total[:half, :half].astype(jnp.bfloat16)


def total_kernel(tile_ref, below_ref, right_ref, out_ref, quarter_ref):
    half = right_ref.shape[1]
    below = below_ref[...].astype(jnp.float32)
    right = right_ref[...].astype(jnp.float32)
    quarter = tile_ref[:, half:, half:] + below[:, half:] + right[:, :, half:]
    out_ref[0, :, :half, :half] = tile_ref[:, :half, :half]
    out_ref[0, :, :half, half:] = tile_ref[:, :half, half:] + below[:, :half]
    out_ref[0, :, half:, :half] = tile_ref[:, half:, :half] + right[:, :, :half]
    out_ref[0, :, half:, half:] = quarter
    quarter_ref[...] = quarter


def quarter_kernel(out_ref, quarter_ref, own_ref, same_ref, sum_ref, sem):
    half = quarter_ref.shape[1]
    sum_ref[...] = quarter_ref[...] + own_ref[...].astype(jnp.float32)
    copy = pltpu.make_async_copy(sum_ref, same_ref.at[0, :, pl.ds(half, half), pl.ds(half, half)], sem)
    copy.start()
    copy.wait()


VMEM = pl.BlockSpec(memory_space=pltpu.VMEM)
ANY = pl.BlockSpec(memory_space=pl.ANY)
SMEM = pl.BlockSpec(memory_space=pltpu.SMEM)
PARAMS = pltpu.CompilerParams(vmem_limit_bytes=48 * 1024 * 1024)


def shaped(*shape, dtype=jnp.bfloat16):
    return jax.ShapeDtypeStruct(shape, dtype)


def kernel(body, name, in_specs, out_shape, scratch=()):
    return pl.pallas_call(
        body, in_specs=in_specs, out_specs=[VMEM] * len(out_shape), out_shape=out_shape, scratch_shapes=scratch, compiler_params=PARAMS, name=name
    )


def local(object_slices, probe, fresnel_taps, offsets, counts, measured):
    width = probe.shape[1]
    half = width // 2
    wide = width + half
    full = shaped(2 * width, width)
    part = shaped(width, width)
    row_tiles = max(lax.axis_size("tile") // 16, 2)
    probe = probe.reshape(2 * width, width)
    fourier = jnp.asarray(fourier_matrix(width), jnp.bfloat16)

    far_tile = crossed(object_slices[0], "cuts", 2)
    tile, below, right = kernel(cut_kernel, "cut", [VMEM], [shaped(2, width, width), shaped(2, width + SPARE, half), shaped(2, half, width)])(
        object_slices[0]
    )
    (own,) = kernel(seal_kernel, "seal", [VMEM, VMEM], [shaped(2, half + 16, half)])(tile, offsets)
    below = passed_along(below, "tile", 1)
    right = passed_along(right, "tile", row_tiles)
    own = passed_along(own, "tile", row_tiles + 1)
    far_right = crossed(right, "cuts", 2)
    far_own = crossed(own, "cuts", 2)
    level = shaped(half + 16, width)
    band, level = kernel(band_kernel, "band", [SMEM, VMEM, VMEM], [shaped(4, width, width), level])(counts, fresnel_taps, measured)
    level, far_tile = lax.optimization_barrier((level, far_tile))
    below, far_tile = lax.optimization_barrier((below, far_tile))
    far_below = crossed(below, "cuts", 2)
    level = passed_along(level, "tile", row_tiles + 1)
    rows, columns, rows_back, columns_back = kernel(
        window_kernel,
        "window",
        [VMEM],
        [part, shaped(2, wide, width), shaped(2, wide, width), shaped(2 * width, wide)],
    )(own)
    first, second = kernel(extract_kernel, "near", [VMEM] * 6, [full, full])(rows, columns, tile, below, right, own)
    swapped = crossed(second, "cuts", 1)
    far_level = crossed(level, "cuts", 2)
    straight, far_second = kernel(extract_kernel, "far", [VMEM] * 6, [full, full])(rows, columns, far_tile, far_below, far_right, far_own)
    far_second, far_level = lax.optimization_barrier((far_second, far_level))
    diagonal = crossed(far_second, "cuts", 1)
    one, two = kernel(head_kernel, "head", [VMEM] * 4, [full, full])(probe, band, first, swapped)
    mine, other = kernel(chain_kernel, "chain", [VMEM] * 11, [full, full], [pltpu.VMEM((2 * width, width), jnp.bfloat16)] * 3)(
        probe, first, swapped, straight, diagonal, level, far_level, band, fourier, one, two
    )
    other = crossed(other, "cuts", 1)
    (strip,) = kernel(rows_kernel, "rows", [VMEM] * 2, [shaped(wide, 2 * width)])(rows_back, mine)
    total, below, right, own = kernel(
        scatter_kernel,
        "scatter",
        [VMEM] * 4,
        [shaped(2, width, width, dtype=jnp.float32), shaped(2, width, half), shaped(2, half, width), shaped(2, half, half)],
    )(rows_back, columns_back, strip, other)
    below = passed_along(below, "tile", -1)
    right = passed_along(right, "tile", -row_tiles)
    own = passed_along(own, "tile", -row_tiles - 1)
    whole = shaped(1, 2, width, width, dtype=jnp.float32)
    quarter = shaped(2, half, half, dtype=jnp.float32)
    out, quarter = kernel(total_kernel, "total", [VMEM] * 3, [whole, quarter])(total, below, right)
    out = pl.pallas_call(
        quarter_kernel,
        in_specs=[ANY, VMEM, VMEM],
        out_specs=ANY,
        out_shape=whole,
        input_output_aliases={0: 0},
        scratch_shapes=[pltpu.VMEM((2, half, half), jnp.float32), pltpu.SemaphoreType.DMA],
        compiler_params=PARAMS,
        name="quarter",
    )(out, quarter, own)
    return out


def solution(mesh):
    return jax.shard_map(
        local,
        mesh=mesh,
        in_specs=(
            P("cuts", None, "tile", None),
            P(),
            P(),
            P("tile", None),
            P("tile"),
            P("tile", None, None),
        ),
        out_specs=P("cuts", None, "tile", None),
        check_vma=False,
    )
```

```python
import jax
import jax.numpy as jnp
import numpy as np
from jax import lax
from jax.experimental import pallas as pl
from jax.experimental.pallas import tpu as pltpu
from jax.sharding import PartitionSpec as P


SPARE = 16


def passed_along(value, axis, steps):
    count = lax.axis_size(axis)
    pairs = [(source, (source + steps) % count) for source in range(count)]
    return lax.ppermute(value, axis, pairs)


def crossed(value, axis, mask):
    pairs = [(source, source ^ mask) for source in range(lax.axis_size(axis))]
    return lax.ppermute(value, axis, pairs)


def fourier_matrix(width):
    index = np.arange(width)
    angle = 2.0 * np.pi * (index[:, None] * index[None, :] % width) / width
    return np.stack([np.cos(angle), -np.sin(angle)]) / np.sqrt(width)


def dot(left, right):
    return jnp.dot(left, right, preferred_element_type=jnp.float32)


def sandwich(left_real, left_imag, field, right_real, right_imag):
    right = jnp.concatenate([right_real, right_imag], axis=0)
    top = dot(jnp.concatenate([left_real, -left_imag], axis=1), field).astype(jnp.bfloat16)
    bottom = dot(jnp.concatenate([left_imag, left_real], axis=1), field).astype(jnp.bfloat16)
    real = dot(jnp.concatenate([top, -bottom], axis=1), right)
    imag = dot(jnp.concatenate([bottom, top], axis=1), right)
    return jnp.concatenate([real, imag], axis=0)


def complex_mul(first, second, sign):
    width = first.shape[1]
    fr = first[:width].astype(jnp.float32)
    fi = first[width:].astype(jnp.float32) * sign
    sr = second[:width].astype(jnp.float32)
    si = second[width:].astype(jnp.float32)
    return jnp.concatenate([fr * sr - fi * si, fr * si + fi * sr], axis=0)


def band_kernel(counts_ref, taps_ref, measured_ref, band_ref, level_ref):
    width = band_ref.shape[1]
    half = taps_ref.shape[1] // 2
    core = lax.rem(lax.axis_index("cuts"), 2)
    rows = width // 2
    first = pl.multiple_of(lax.axis_index("cuts") // 2 * rows, rows)
    level_ref[:rows, :] = measured_ref[core, pl.ds(first, rows), :].astype(jnp.bfloat16)
    live = (core < counts_ref[0]).astype(jnp.float32)
    level_ref[rows:, :] = jnp.full((level_ref.shape[0] - rows, width), live, jnp.float32).astype(jnp.bfloat16)
    rows = lax.broadcasted_iota(jnp.int32, (width, width), 0)
    columns = lax.broadcasted_iota(jnp.int32, (width, width), 1)
    inside = jnp.abs(columns - rows) <= half
    for part in range(2):
        line = taps_ref[part : part + 1, :].astype(jnp.float32)
        filler = jnp.zeros((1, width - line.shape[1]), jnp.float32)
        line = jnp.concatenate([line, filler], axis=1)
        spread = jnp.broadcast_to(line, (width, width))
        turned = pltpu.roll(spread, width - half, 1, stride=1, stride_axis=0)
        band = jnp.where(inside, turned, 0.0)
        band_ref[part] = band.astype(jnp.bfloat16)
        band_ref[part + 2] = band.T.astype(jnp.bfloat16)


def cut_kernel(tile_ref, whole_ref, below_ref, right_ref):
    half = right_ref.shape[1]
    whole_ref[...] = tile_ref[...]
    below_ref[:, : 2 * half, :] = tile_ref[:, :, half:]
    below_ref[:, 2 * half :, :] = jnp.zeros((2, SPARE, half), jnp.bfloat16)
    right_ref[...] = tile_ref[:, half:, :]


def seal_kernel(tile_ref, offsets_ref, own_ref):
    half = tile_ref.shape[1] // 2
    own_ref[:, :half, :] = tile_ref[:, half:, half:]
    shape = (own_ref.shape[1] - half, half)
    line = lax.broadcasted_iota(jnp.int32, shape, 0)
    lines = jnp.zeros(shape, jnp.float32)
    for index in range(4):
        value = offsets_ref[index // 2 : index // 2 + 1, index % 2 : index % 2 + 1].astype(jnp.float32)
        lines = jnp.where(line == index, value, lines)
    for part in range(2):
        own_ref[part, half:, :] = lines.astype(jnp.bfloat16)


def window_kernel(own_ref, rows_ref, columns_ref, rows_back_ref, columns_back_ref):
    half = own_ref.shape[2]
    width = 2 * half
    core = lax.rem(lax.axis_index("cuts"), 2)
    lines = own_ref[0, half:, :].astype(jnp.float32).astype(jnp.int32) - half

    def placed(shape, axis, shift):
        i = lax.broadcasted_iota(jnp.int32, shape, axis)
        j = lax.broadcasted_iota(jnp.int32, shape, 1 - axis)
        shift = jnp.concatenate([shift] * (shape[1] // half), axis=1)
        return jnp.where(j - i == shift, 1.0, 0.0).astype(jnp.bfloat16)

    for place in range(2):
        second = core != place
        row = jnp.where(second, lines[2:3], lines[0:1])
        column = jnp.where(second, lines[3:4], lines[1:2])
        rows_ref[place * half : (place + 1) * half, :] = placed((half, width), 0, row)
        columns_ref[place] = placed((width + half, width), 1, column)
        rows_back_ref[place] = placed((width + half, width), 1, row)
        columns_back_ref[place * width : (place + 1) * width, :] = placed((width, width + half), 0, column)


def extract_kernel(rows_ref, columns_ref, tile_ref, below_ref, right_ref, own_ref, first_ref, second_ref):
    width = tile_ref.shape[1]
    half = width // 2
    wide = width + half
    blocks = []
    for part in range(2):
        upper = jnp.concatenate([own_ref[part, :half], right_ref[part]], axis=1)
        lower = jnp.concatenate([below_ref[part, :width], tile_ref[part]], axis=1)
        blocks.append(jnp.concatenate([upper, lower], axis=0))
    block = jnp.concatenate(blocks, axis=1)
    strips = [dot(rows_ref[...], block[top : top + width]).astype(jnp.bfloat16) for top in (0, half)]
    for place, out_ref in enumerate((first_ref, second_ref)):
        mine = [strip[place * half : (place + 1) * half, part * wide : (part + 1) * wide] for part in range(2) for strip in strips]
        out_ref[...] = dot(jnp.concatenate(mine, axis=0), columns_ref[place]).astype(jnp.bfloat16)


def ordered(first_ref, second_ref):
    odd = lax.rem(lax.axis_index("cuts"), 2) == 1
    first, second = first_ref[...], second_ref[...]
    return jnp.where(odd, second, first), jnp.where(odd, first, second)


def near_chip():
    return lax.axis_index("cuts") < 2


def spread_on(spread, patch, band_ref):
    wave = complex_mul(spread, patch, 1.0).astype(jnp.bfloat16)
    return sandwich(band_ref[0], band_ref[1], wave, band_ref[2], band_ref[3]).astype(jnp.bfloat16)


def back_on(back, patch, band_ref):
    carried = complex_mul(patch, back, -1.0).astype(jnp.bfloat16)
    return sandwich(band_ref[2], -band_ref[3], carried, band_ref[0], -band_ref[1]).astype(jnp.bfloat16)


def head_kernel(probe_ref, band_ref, p0_ref, p1_ref, one_ref, two_ref):
    @pl.when(near_chip())
    def _():
        patch_0, patch_1 = ordered(p0_ref, p1_ref)
        one_ref[...] = spread_on(probe_ref[...], patch_0, band_ref)
        two_ref[...] = spread_on(one_ref[...], patch_1, band_ref)


def chain_kernel(
    probe_ref, p0_ref, p1_ref, p2_ref, p3_ref, level_ref, far_level_ref, band_ref, fourier_ref, one_ref, two_ref, mine_ref, other_ref,
    keep_two_ref, keep_three_ref, wave_ref
):
    width = probe_ref.shape[1]

    @pl.when(near_chip())
    def _():
        patch_2, patch_3 = ordered(p2_ref, p3_ref)
        spread = spread_on(two_ref[...], patch_2, band_ref)
        wave_ref[...] = complex_mul(spread, patch_3, 1.0).astype(jnp.bfloat16)

    @pl.when(jnp.logical_not(near_chip()))
    def _():
        patch_0, patch_1 = ordered(p2_ref, p3_ref)
        patch_2, patch_3 = ordered(p0_ref, p1_ref)
        spread = spread_on(probe_ref[...], patch_0, band_ref)
        keep_two_ref[...] = spread_on(spread, patch_1, band_ref)
        keep_three_ref[...] = spread_on(keep_two_ref[...], patch_2, band_ref)
        wave_ref[...] = complex_mul(keep_three_ref[...], patch_3, 1.0).astype(jnp.bfloat16)

    fourier_r, fourier_i = fourier_ref[0], fourier_ref[1]
    far = sandwich(fourier_r, fourier_i, wave_ref[...], fourier_r, fourier_i)
    far_r, far_i = far[:width], far[width:]
    rows = width // 2
    level, far_level = level_ref[:rows, :].astype(jnp.float32), far_level_ref[:rows, :].astype(jnp.float32)
    level = jnp.concatenate([jnp.where(near_chip(), level, far_level), jnp.where(near_chip(), far_level, level)], axis=0)
    live = level_ref[rows : rows + 1, :].astype(jnp.float32)
    excess = 2.0 * live * (far_r * far_r + far_i * far_i - level)
    residual = jnp.concatenate([excess * far_r, excess * far_i], axis=0).astype(jnp.bfloat16)
    wave_ref[...] = sandwich(fourier_r, -fourier_i, residual, fourier_r, -fourier_i).astype(jnp.bfloat16)
    odd = lax.rem(lax.axis_index("cuts"), 2) == 1

    def out(low, high):
        mine_ref[...] = jnp.where(odd, high, low)
        other_ref[...] = jnp.where(odd, low, high)

    @pl.when(near_chip())
    def _():
        _, patch_1 = ordered(p0_ref, p1_ref)
        patch_2, patch_3 = ordered(p2_ref, p3_ref)
        back = back_on(wave_ref[...], patch_3, band_ref)
        back = back_on(back, patch_2, band_ref)
        high = complex_mul(one_ref[...], back, -1.0).astype(jnp.bfloat16)
        back = back_on(back, patch_1, band_ref)
        out(complex_mul(probe_ref[...], back, -1.0).astype(jnp.bfloat16), high)

    @pl.when(jnp.logical_not(near_chip()))
    def _():
        _, patch_3 = ordered(p0_ref, p1_ref)
        back = wave_ref[...]
        high = complex_mul(keep_three_ref[...], back, -1.0).astype(jnp.bfloat16)
        back = back_on(back, patch_3, band_ref)
        out(complex_mul(keep_two_ref[...], back, -1.0).astype(jnp.bfloat16), high)


def placed_rows(rows, ref):
    width = ref.shape[1]
    return dot(rows, jnp.concatenate([ref[:width, :], ref[width:, :]], axis=1)).astype(jnp.bfloat16)


def rows_kernel(rows_ref, mine_ref, strip_ref):
    strip_ref[...] = placed_rows(rows_ref[0], mine_ref)


def scatter_kernel(rows_ref, columns_ref, strip_ref, other_ref, tile_ref, below_ref, right_ref, own_ref):
    width = tile_ref.shape[1]
    half = width // 2
    strips = [strip_ref[...], placed_rows(rows_ref[1], other_ref)]
    for part in range(2):
        strip = jnp.concatenate([strip[:, part * width : (part + 1) * width] for strip in strips], axis=1)
        total = dot(strip, columns_ref[...])
        tile_ref[part] = total[half:, half:]
        below_ref[part] = total[half:, :half].astype(jnp.bfloat16)
        right_ref[part] = total[:half, half:].astype(jnp.bfloat16)
        own_ref[part] = total[:half, :half].astype(jnp.bfloat16)


def total_kernel(tile_ref, below_ref, right_ref, out_ref, quarter_ref):
    half = right_ref.shape[1]
    below = below_ref[...].astype(jnp.float32)
    right = right_ref[...].astype(jnp.float32)
    quarter = tile_ref[:, half:, half:] + below[:, half:] + right[:, :, half:]
    out_ref[0, :, :half, :half] = tile_ref[:, :half, :half]
    out_ref[0, :, :half, half:] = tile_ref[:, :half, half:] + below[:, :half]
    out_ref[0, :, half:, :half] = tile_ref[:, half:, :half] + right[:, :, :half]
    out_ref[0, :, half:, half:] = quarter
    quarter_ref[...] = quarter


def quarter_kernel(out_ref, quarter_ref, own_ref, same_ref, sum_ref, sem):
    half = quarter_ref.shape[1]
    sum_ref[...] = quarter_ref[...] + own_ref[...].astype(jnp.float32)
    copy = pltpu.make_async_copy(sum_ref, same_ref.at[0, :, pl.ds(half, half), pl.ds(half, half)], sem)
    copy.start()
    copy.wait()


VMEM = pl.BlockSpec(memory_space=pltpu.VMEM)
ANY = pl.BlockSpec(memory_space=pl.ANY)
SMEM = pl.BlockSpec(memory_space=pltpu.SMEM)
PARAMS = pltpu.CompilerParams(vmem_limit_bytes=48 * 1024 * 1024)


def shaped(*shape, dtype=jnp.bfloat16):
    return jax.ShapeDtypeStruct(shape, dtype)


def kernel(body, name, in_specs, out_shape, scratch=()):
    return pl.pallas_call(
        body, in_specs=in_specs, out_specs=[VMEM] * len(out_shape), out_shape=out_shape, scratch_shapes=scratch, compiler_params=PARAMS, name=name
    )


def local(object_slices, probe, fresnel_taps, offsets, counts, measured):
    width = probe.shape[1]
    half = width // 2
    wide = width + half
    full = shaped(2 * width, width)
    part = shaped(width, width)
    row_tiles = max(lax.axis_size("tile") // 16, 2)
    probe = probe.reshape(2 * width, width)
    fourier = jnp.asarray(fourier_matrix(width), jnp.bfloat16)

    far_tile = crossed(object_slices[0], "cuts", 2)
    tile, below, right = kernel(cut_kernel, "cut", [VMEM], [shaped(2, width, width), shaped(2, width + SPARE, half), shaped(2, half, width)])(
        object_slices[0]
    )
    (own,) = kernel(seal_kernel, "seal", [VMEM, VMEM], [shaped(2, half + 16, half)])(tile, offsets)
    below = passed_along(below, "tile", 1)
    right = passed_along(right, "tile", row_tiles)
    own = passed_along(own, "tile", row_tiles + 1)
    far_right = crossed(right, "cuts", 2)
    far_own = crossed(own, "cuts", 2)
    level = shaped(half + 16, width)
    band, level = kernel(band_kernel, "band", [SMEM, VMEM, VMEM], [shaped(4, width, width), level])(counts, fresnel_taps, measured)
    level, right = lax.optimization_barrier((level, right))
    far_below = crossed(below, "cuts", 2)
    level = passed_along(level, "tile", row_tiles + 1)
    rows, columns, rows_back, columns_back = kernel(
        window_kernel,
        "window",
        [VMEM],
        [part, shaped(2, wide, width), shaped(2, wide, width), shaped(2 * width, wide)],
    )(own)
    first, second = kernel(extract_kernel, "near", [VMEM] * 6, [full, full])(rows, columns, tile, below, right, own)
    swapped = crossed(second, "cuts", 1)
    far_level = crossed(level, "cuts", 2)
    straight, far_second = kernel(extract_kernel, "far", [VMEM] * 6, [full, full])(rows, columns, far_tile, far_below, far_right, far_own)
    far_second, far_level = lax.optimization_barrier((far_second, far_level))
    diagonal = crossed(far_second, "cuts", 1)
    one, two = kernel(head_kernel, "head", [VMEM] * 4, [full, full])(probe, band, first, swapped)
    mine, other = kernel(chain_kernel, "chain", [VMEM] * 11, [full, full], [pltpu.VMEM((2 * width, width), jnp.bfloat16)] * 3)(
        probe, first, swapped, straight, diagonal, level, far_level, band, fourier, one, two
    )
    other = crossed(other, "cuts", 1)
    (strip,) = kernel(rows_kernel, "rows", [VMEM] * 2, [shaped(wide, 2 * width)])(rows_back, mine)
    total, below, right, own = kernel(
        scatter_kernel,
        "scatter",
        [VMEM] * 4,
        [shaped(2, width, width, dtype=jnp.float32), shaped(2, width, half), shaped(2, half, width), shaped(2, half, half)],
    )(rows_back, columns_back, strip, other)
    below = passed_along(below, "tile", -1)
    right = passed_along(right, "tile", -row_tiles)
    own = passed_along(own, "tile", -row_tiles - 1)
    whole = shaped(1, 2, width, width, dtype=jnp.float32)
    quarter = shaped(2, half, half, dtype=jnp.float32)
    out, quarter = kernel(total_kernel, "total", [VMEM] * 3, [whole, quarter])(total, below, right)
    out = pl.pallas_call(
        quarter_kernel,
        in_specs=[ANY, VMEM, VMEM],
        out_specs=ANY,
        out_shape=whole,
        input_output_aliases={0: 0},
        scratch_shapes=[pltpu.VMEM((2, half, half), jnp.float32), pltpu.SemaphoreType.DMA],
        compiler_params=PARAMS,
        name="quarter",
    )(out, quarter, own)
    return out


def solution(mesh):
    return jax.shard_map(
        local,
        mesh=mesh,
        in_specs=(
            P("cuts", None, "tile", None),
            P(),
            P(),
            P("tile", None),
            P("tile"),
            P("tile", None, None),
        ),
        out_specs=P("cuts", None, "tile", None),
        check_vma=False,
    )
```

```python
import jax
import jax.numpy as jnp
import numpy as np
from jax import lax
from jax.experimental import pallas as pl
from jax.experimental.pallas import tpu as pltpu
from jax.sharding import PartitionSpec as P


SPARE = 16


def passed_along(value, axis, steps):
    count = lax.axis_size(axis)
    pairs = [(source, (source + steps) % count) for source in range(count)]
    return lax.ppermute(value, axis, pairs)


def crossed(value, axis, mask):
    pairs = [(source, source ^ mask) for source in range(lax.axis_size(axis))]
    return lax.ppermute(value, axis, pairs)


def fourier_matrix(width):
    index = np.arange(width)
    angle = 2.0 * np.pi * (index[:, None] * index[None, :] % width) / width
    return np.stack([np.cos(angle), -np.sin(angle)]) / np.sqrt(width)


def dot(left, right):
    return jnp.dot(left, right, preferred_element_type=jnp.float32)


def sandwich(left_real, left_imag, field, right_real, right_imag):
    right = jnp.concatenate([right_real, right_imag], axis=0)
    top = dot(jnp.concatenate([left_real, -left_imag], axis=1), field).astype(jnp.bfloat16)
    bottom = dot(jnp.concatenate([left_imag, left_real], axis=1), field).astype(jnp.bfloat16)
    real = dot(jnp.concatenate([top, -bottom], axis=1), right)
    imag = dot(jnp.concatenate([bottom, top], axis=1), right)
    return jnp.concatenate([real, imag], axis=0)


def complex_mul(first, second, sign):
    width = first.shape[1]
    fr, fi = first[:width], first[width:]
    if sign < 0:
        fi = -fi
    sr, si = second[:width], second[width:]
    return jnp.concatenate([fr * sr - fi * si, fr * si + fi * sr], axis=0)


def band_kernel(counts_ref, taps_ref, measured_ref, band_ref, level_ref):
    width = band_ref.shape[1]
    half = taps_ref.shape[1] // 2
    core = lax.rem(lax.axis_index("cuts"), 2)
    rows = width // 2
    first = pl.multiple_of(lax.axis_index("cuts") // 2 * rows, rows)
    level_ref[:rows, :] = measured_ref[core, pl.ds(first, rows), :].astype(jnp.bfloat16)
    live = (core < counts_ref[0]).astype(jnp.float32)
    level_ref[rows:, :] = jnp.full((level_ref.shape[0] - rows, width), live, jnp.float32).astype(jnp.bfloat16)
    rows = lax.broadcasted_iota(jnp.int32, (width, width), 0)
    columns = lax.broadcasted_iota(jnp.int32, (width, width), 1)
    inside = jnp.abs(columns - rows) <= half
    for part in range(2):
        line = taps_ref[part : part + 1, :].astype(jnp.float32)
        filler = jnp.zeros((1, width - line.shape[1]), jnp.float32)
        line = jnp.concatenate([line, filler], axis=1)
        spread = jnp.broadcast_to(line, (width, width))
        turned = pltpu.roll(spread, width - half, 1, stride=1, stride_axis=0)
        band = jnp.where(inside, turned, 0.0)
        band_ref[part] = band.astype(jnp.bfloat16)
        band_ref[part + 2] = band.T.astype(jnp.bfloat16)


def cut_kernel(tile_ref, whole_ref, below_ref, right_ref):
    half = right_ref.shape[1]
    whole_ref[...] = tile_ref[...]
    below_ref[:, : 2 * half, :] = tile_ref[:, :, half:]
    below_ref[:, 2 * half :, :] = jnp.zeros((2, SPARE, half), jnp.bfloat16)
    right_ref[...] = tile_ref[:, half:, :]


def seal_kernel(tile_ref, offsets_ref, own_ref):
    half = tile_ref.shape[1] // 2
    own_ref[:, :half, :] = tile_ref[:, half:, half:]
    shape = (own_ref.shape[1] - half, half)
    line = lax.broadcasted_iota(jnp.int32, shape, 0)
    lines = jnp.zeros(shape, jnp.float32)
    for index in range(4):
        value = offsets_ref[index // 2 : index // 2 + 1, index % 2 : index % 2 + 1].astype(jnp.float32)
        lines = jnp.where(line == index, value, lines)
    for part in range(2):
        own_ref[part, half:, :] = lines.astype(jnp.bfloat16)


def window_kernel(own_ref, rows_ref, columns_ref, rows_back_ref, columns_back_ref):
    half = own_ref.shape[2]
    width = 2 * half
    core = lax.rem(lax.axis_index("cuts"), 2)
    lines = own_ref[0, half:, :].astype(jnp.float32).astype(jnp.int32) - half

    def placed(shape, axis, shift):
        i = lax.broadcasted_iota(jnp.int32, shape, axis)
        j = lax.broadcasted_iota(jnp.int32, shape, 1 - axis)
        shift = jnp.concatenate([shift] * (shape[1] // half), axis=1)
        return jnp.where(j - i == shift, 1.0, 0.0).astype(jnp.bfloat16)

    for place in range(2):
        second = core != place
        row = jnp.where(second, lines[2:3], lines[0:1])
        column = jnp.where(second, lines[3:4], lines[1:2])
        rows_ref[place * half : (place + 1) * half, :] = placed((half, width), 0, row)
        columns_ref[place] = placed((width + half, width), 1, column)
        rows_back_ref[place] = placed((width + half, width), 1, row)
        columns_back_ref[place * width : (place + 1) * width, :] = placed((width, width + half), 0, column)


def extract_kernel(rows_ref, columns_ref, tile_ref, below_ref, right_ref, own_ref, first_ref, second_ref):
    width = tile_ref.shape[1]
    half = width // 2
    wide = width + half
    blocks = []
    for part in range(2):
        upper = jnp.concatenate([own_ref[part, :half], right_ref[part]], axis=1)
        lower = jnp.concatenate([below_ref[part, :width], tile_ref[part]], axis=1)
        blocks.append(jnp.concatenate([upper, lower], axis=0))
    block = jnp.concatenate(blocks, axis=1)
    strips = [dot(rows_ref[...], block[top : top + width]).astype(jnp.bfloat16) for top in (0, half)]
    for place, out_ref in enumerate((first_ref, second_ref)):
        mine = [strip[place * half : (place + 1) * half, part * wide : (part + 1) * wide] for part in range(2) for strip in strips]
        out_ref[...] = dot(jnp.concatenate(mine, axis=0), columns_ref[place]).astype(jnp.bfloat16)


def ordered(first_ref, second_ref):
    odd = lax.rem(lax.axis_index("cuts"), 2) == 1
    first, second = first_ref[...], second_ref[...]
    return jnp.where(odd, second, first), jnp.where(odd, first, second)


def near_chip():
    return lax.axis_index("cuts") < 2


def spread_on(spread, patch, band_ref):
    wave = complex_mul(spread, patch, 1.0).astype(jnp.bfloat16)
    return sandwich(band_ref[0], band_ref[1], wave, band_ref[2], band_ref[3]).astype(jnp.bfloat16)


def back_on(back, patch, band_ref):
    carried = complex_mul(patch, back, -1.0).astype(jnp.bfloat16)
    return sandwich(band_ref[2], -band_ref[3], carried, band_ref[0], -band_ref[1]).astype(jnp.bfloat16)


def head_kernel(probe_ref, band_ref, p0_ref, p1_ref, one_ref, two_ref):
    @pl.when(near_chip())
    def _():
        patch_0, patch_1 = ordered(p0_ref, p1_ref)
        one_ref[...] = spread_on(probe_ref[...], patch_0, band_ref)
        two_ref[...] = spread_on(one_ref[...], patch_1, band_ref)


def chain_kernel(
    probe_ref, p0_ref, p1_ref, p2_ref, p3_ref, level_ref, far_level_ref, band_ref, fourier_ref, one_ref, two_ref, mine_ref, other_ref,
    keep_two_ref, keep_three_ref, wave_ref
):
    width = probe_ref.shape[1]

    @pl.when(near_chip())
    def _():
        patch_2, patch_3 = ordered(p2_ref, p3_ref)
        spread = spread_on(two_ref[...], patch_2, band_ref)
        wave_ref[...] = complex_mul(spread, patch_3, 1.0).astype(jnp.bfloat16)

    @pl.when(jnp.logical_not(near_chip()))
    def _():
        patch_0, patch_1 = ordered(p2_ref, p3_ref)
        patch_2, patch_3 = ordered(p0_ref, p1_ref)
        spread = spread_on(probe_ref[...], patch_0, band_ref)
        keep_two_ref[...] = spread_on(spread, patch_1, band_ref)
        keep_three_ref[...] = spread_on(keep_two_ref[...], patch_2, band_ref)
        wave_ref[...] = complex_mul(keep_three_ref[...], patch_3, 1.0).astype(jnp.bfloat16)

    fourier_r, fourier_i = fourier_ref[0], fourier_ref[1]
    far = sandwich(fourier_r, fourier_i, wave_ref[...], fourier_r, fourier_i)
    far_r, far_i = far[:width], far[width:]
    rows = width // 2
    level, far_level = level_ref[:rows, :].astype(jnp.float32), far_level_ref[:rows, :].astype(jnp.float32)
    level = jnp.concatenate([jnp.where(near_chip(), level, far_level), jnp.where(near_chip(), far_level, level)], axis=0)
    live = level_ref[rows : rows + 1, :].astype(jnp.float32)
    excess = 2.0 * live * (far_r * far_r + far_i * far_i - level)
    residual = jnp.concatenate([excess * far_r, excess * far_i], axis=0).astype(jnp.bfloat16)
    wave_ref[...] = sandwich(fourier_r, -fourier_i, residual, fourier_r, -fourier_i).astype(jnp.bfloat16)
    odd = lax.rem(lax.axis_index("cuts"), 2) == 1

    def out(low, high):
        mine_ref[...] = jnp.where(odd, high, low)
        other_ref[...] = jnp.where(odd, low, high)

    @pl.when(near_chip())
    def _():
        _, patch_1 = ordered(p0_ref, p1_ref)
        patch_2, patch_3 = ordered(p2_ref, p3_ref)
        back = back_on(wave_ref[...], patch_3, band_ref)
        back = back_on(back, patch_2, band_ref)
        high = complex_mul(one_ref[...], back, -1.0).astype(jnp.bfloat16)
        back = back_on(back, patch_1, band_ref)
        out(complex_mul(probe_ref[...], back, -1.0).astype(jnp.bfloat16), high)

    @pl.when(jnp.logical_not(near_chip()))
    def _():
        _, patch_3 = ordered(p0_ref, p1_ref)
        back = wave_ref[...]
        high = complex_mul(keep_three_ref[...], back, -1.0).astype(jnp.bfloat16)
        back = back_on(back, patch_3, band_ref)
        out(complex_mul(keep_two_ref[...], back, -1.0).astype(jnp.bfloat16), high)


def placed_rows(rows, ref):
    width = ref.shape[1]
    return dot(rows, jnp.concatenate([ref[:width, :], ref[width:, :]], axis=1)).astype(jnp.bfloat16)


def rows_kernel(rows_ref, mine_ref, strip_ref):
    strip_ref[...] = placed_rows(rows_ref[0], mine_ref)


def scatter_kernel(rows_ref, columns_ref, strip_ref, other_ref, tile_ref, below_ref, right_ref, own_ref):
    width = tile_ref.shape[1]
    half = width // 2
    strips = [strip_ref[...], placed_rows(rows_ref[1], other_ref)]
    for part in range(2):
        strip = jnp.concatenate([strip[:, part * width : (part + 1) * width] for strip in strips], axis=1)
        total = dot(strip, columns_ref[...])
        tile_ref[part] = total[half:, half:]
        below_ref[part] = total[half:, :half].astype(jnp.bfloat16)
        right_ref[part] = total[:half, half:].astype(jnp.bfloat16)
        own_ref[part] = total[:half, :half].astype(jnp.bfloat16)


def total_kernel(tile_ref, below_ref, right_ref, out_ref, quarter_ref):
    half = right_ref.shape[1]
    below = below_ref[...].astype(jnp.float32)
    right = right_ref[...].astype(jnp.float32)
    quarter = tile_ref[:, half:, half:] + below[:, half:] + right[:, :, half:]
    out_ref[0, :, :half, :half] = tile_ref[:, :half, :half]
    out_ref[0, :, :half, half:] = tile_ref[:, :half, half:] + below[:, :half]
    out_ref[0, :, half:, :half] = tile_ref[:, half:, :half] + right[:, :, :half]
    out_ref[0, :, half:, half:] = quarter
    quarter_ref[...] = quarter


def quarter_kernel(out_ref, quarter_ref, own_ref, same_ref, sum_ref, sem):
    half = quarter_ref.shape[1]
    sum_ref[...] = quarter_ref[...] + own_ref[...].astype(jnp.float32)
    copy = pltpu.make_async_copy(sum_ref, same_ref.at[0, :, pl.ds(half, half), pl.ds(half, half)], sem)
    copy.start()
    copy.wait()


VMEM = pl.BlockSpec(memory_space=pltpu.VMEM)
ANY = pl.BlockSpec(memory_space=pl.ANY)
SMEM = pl.BlockSpec(memory_space=pltpu.SMEM)
PARAMS = pltpu.CompilerParams(vmem_limit_bytes=48 * 1024 * 1024)


def shaped(*shape, dtype=jnp.bfloat16):
    return jax.ShapeDtypeStruct(shape, dtype)


def kernel(body, name, in_specs, out_shape, scratch=()):
    return pl.pallas_call(
        body, in_specs=in_specs, out_specs=[VMEM] * len(out_shape), out_shape=out_shape, scratch_shapes=scratch, compiler_params=PARAMS, name=name
    )


def local(object_slices, probe, fresnel_taps, offsets, counts, measured):
    width = probe.shape[1]
    half = width // 2
    wide = width + half
    full = shaped(2 * width, width)
    part = shaped(width, width)
    row_tiles = max(lax.axis_size("tile") // 16, 2)
    probe = probe.reshape(2 * width, width)
    fourier = jnp.asarray(fourier_matrix(width), jnp.bfloat16)

    far_tile = crossed(object_slices[0], "cuts", 2)
    tile, below, right = kernel(cut_kernel, "cut", [VMEM], [shaped(2, width, width), shaped(2, width + SPARE, half), shaped(2, half, width)])(
        object_slices[0]
    )
    (own,) = kernel(seal_kernel, "seal", [VMEM, VMEM], [shaped(2, half + 16, half)])(tile, offsets)
    below = passed_along(below, "tile", 1)
    right = passed_along(right, "tile", row_tiles)
    own = passed_along(own, "tile", row_tiles + 1)
    far_right = crossed(right, "cuts", 2)
    far_own = crossed(own, "cuts", 2)
    level = shaped(half + 16, width)
    band, level = kernel(band_kernel, "band", [SMEM, VMEM, VMEM], [shaped(4, width, width), level])(counts, fresnel_taps, measured)
    level, far_tile = lax.optimization_barrier((level, far_tile))
    below, far_tile = lax.optimization_barrier((below, far_tile))
    far_below = crossed(below, "cuts", 2)
    level = passed_along(level, "tile", row_tiles + 1)
    rows, columns, rows_back, columns_back = kernel(
        window_kernel,
        "window",
        [VMEM],
        [part, shaped(2, wide, width), shaped(2, wide, width), shaped(2 * width, wide)],
    )(own)
    first, second = kernel(extract_kernel, "near", [VMEM] * 6, [full, full])(rows, columns, tile, below, right, own)
    swapped = crossed(second, "cuts", 1)
    far_level = crossed(level, "cuts", 2)
    straight, far_second = kernel(extract_kernel, "far", [VMEM] * 6, [full, full])(rows, columns, far_tile, far_below, far_right, far_own)
    far_second, far_level = lax.optimization_barrier((far_second, far_level))
    diagonal = crossed(far_second, "cuts", 1)
    one, two = kernel(head_kernel, "head", [VMEM] * 4, [full, full])(probe, band, first, swapped)
    mine, other = kernel(chain_kernel, "chain", [VMEM] * 11, [full, full], [pltpu.VMEM((2 * width, width), jnp.bfloat16)] * 3)(
        probe, first, swapped, straight, diagonal, level, far_level, band, fourier, one, two
    )
    other = crossed(other, "cuts", 1)
    (strip,) = kernel(rows_kernel, "rows", [VMEM] * 2, [shaped(wide, 2 * width)])(rows_back, mine)
    total, below, right, own = kernel(
        scatter_kernel,
        "scatter",
        [VMEM] * 4,
        [shaped(2, width, width, dtype=jnp.float32), shaped(2, width, half), shaped(2, half, width), shaped(2, half, half)],
    )(rows_back, columns_back, strip, other)
    below = passed_along(below, "tile", -1)
    right = passed_along(right, "tile", -row_tiles)
    own = passed_along(own, "tile", -row_tiles - 1)
    whole = shaped(1, 2, width, width, dtype=jnp.float32)
    quarter = shaped(2, half, half, dtype=jnp.float32)
    out, quarter = kernel(total_kernel, "total", [VMEM] * 3, [whole, quarter])(total, below, right)
    out = pl.pallas_call(
        quarter_kernel,
        in_specs=[ANY, VMEM, VMEM],
        out_specs=ANY,
        out_shape=whole,
        input_output_aliases={0: 0},
        scratch_shapes=[pltpu.VMEM((2, half, half), jnp.float32), pltpu.SemaphoreType.DMA],
        compiler_params=PARAMS,
        name="quarter",
    )(out, quarter, own)
    return out


def solution(mesh):
    return jax.shard_map(
        local,
        mesh=mesh,
        in_specs=(
            P("cuts", None, "tile", None),
            P(),
            P(),
            P("tile", None),
            P("tile"),
            P("tile", None, None),
        ),
        out_specs=P("cuts", None, "tile", None),
        check_vma=False,
    )
```

```python
import jax
import jax.numpy as jnp
import numpy as np
from jax import lax
from jax.experimental import pallas as pl
from jax.experimental.pallas import tpu as pltpu
from jax.sharding import PartitionSpec as P


SPARE = 16


def passed_along(value, axis, steps):
    count = lax.axis_size(axis)
    pairs = [(source, (source + steps) % count) for source in range(count)]
    return lax.ppermute(value, axis, pairs)


def crossed(value, axis, mask):
    pairs = [(source, source ^ mask) for source in range(lax.axis_size(axis))]
    return lax.ppermute(value, axis, pairs)


def fourier_matrix(width):
    index = np.arange(width)
    angle = 2.0 * np.pi * (index[:, None] * index[None, :] % width) / width
    return np.stack([np.cos(angle), -np.sin(angle)]) / np.sqrt(width)


def dot(left, right):
    return jnp.dot(left, right, preferred_element_type=jnp.float32)


def sandwich(left_real, left_imag, field, right_real, right_imag):
    right = jnp.concatenate([right_real, right_imag], axis=0)
    top = dot(jnp.concatenate([left_real, -left_imag], axis=1), field).astype(jnp.bfloat16)
    bottom = dot(jnp.concatenate([left_imag, left_real], axis=1), field).astype(jnp.bfloat16)
    real = dot(jnp.concatenate([top, -bottom], axis=1), right)
    imag = dot(jnp.concatenate([bottom, top], axis=1), right)
    return jnp.concatenate([real, imag], axis=0)


def complex_mul(first, second, sign):
    width = first.shape[1]
    fr, fi = first[:width], first[width:]
    if sign < 0:
        fi = -fi
    sr, si = second[:width], second[width:]
    return jnp.concatenate([fr * sr - fi * si, fr * si + fi * sr], axis=0)


def band_kernel(counts_ref, taps_ref, measured_ref, band_ref, level_ref):
    width = band_ref.shape[1]
    half = taps_ref.shape[1] // 2
    core = lax.rem(lax.axis_index("cuts"), 2)
    rows = width // 2
    first = pl.multiple_of(lax.axis_index("cuts") // 2 * rows, rows)
    level_ref[:rows, :] = measured_ref[core, pl.ds(first, rows), :].astype(jnp.bfloat16)
    live = (core < counts_ref[0]).astype(jnp.float32)
    level_ref[rows:, :] = jnp.full((level_ref.shape[0] - rows, width), live, jnp.float32).astype(jnp.bfloat16)
    rows = lax.broadcasted_iota(jnp.int32, (width, width), 0)
    columns = lax.broadcasted_iota(jnp.int32, (width, width), 1)
    inside = jnp.abs(columns - rows) <= half
    for part in range(2):
        line = taps_ref[part : part + 1, :].astype(jnp.float32)
        filler = jnp.zeros((1, width - line.shape[1]), jnp.float32)
        line = jnp.concatenate([line, filler], axis=1)
        spread = jnp.broadcast_to(line, (width, width))
        turned = pltpu.roll(spread, width - half, 1, stride=1, stride_axis=0)
        band = jnp.where(inside, turned, 0.0)
        band_ref[part] = band.astype(jnp.bfloat16)
        band_ref[part + 2] = band.T.astype(jnp.bfloat16)


def cut_kernel(tile_ref, whole_ref, below_ref, right_ref):
    half = right_ref.shape[1]
    whole_ref[...] = tile_ref[...]
    below_ref[:, : 2 * half, :] = tile_ref[:, :, half:]
    below_ref[:, 2 * half :, :] = jnp.zeros((2, SPARE, half), jnp.bfloat16)
    right_ref[...] = tile_ref[:, half:, :]


def seal_kernel(tile_ref, offsets_ref, own_ref):
    half = tile_ref.shape[1] // 2
    own_ref[:, :half, :] = tile_ref[:, half:, half:]
    shape = (own_ref.shape[1] - half, half)
    line = lax.broadcasted_iota(jnp.int32, shape, 0)
    lines = jnp.zeros(shape, jnp.float32)
    for index in range(4):
        value = offsets_ref[index // 2 : index // 2 + 1, index % 2 : index % 2 + 1].astype(jnp.float32)
        lines = jnp.where(line == index, value, lines)
    for part in range(2):
        own_ref[part, half:, :] = lines.astype(jnp.bfloat16)


def window_kernel(own_ref, rows_ref, columns_ref, rows_back_ref, columns_back_ref):
    half = own_ref.shape[2]
    width = 2 * half
    core = lax.rem(lax.axis_index("cuts"), 2)
    lines = own_ref[0, half:, :].astype(jnp.float32).astype(jnp.int32) - half

    def placed(shape, axis, shift):
        i = lax.broadcasted_iota(jnp.int32, shape, axis)
        j = lax.broadcasted_iota(jnp.int32, shape, 1 - axis)
        shift = jnp.concatenate([shift] * (shape[1] // half), axis=1)
        return jnp.where(j - i == shift, 1.0, 0.0).astype(jnp.bfloat16)

    for place in range(2):
        second = core != place
        row = jnp.where(second, lines[2:3], lines[0:1])
        column = jnp.where(second, lines[3:4], lines[1:2])
        rows_ref[place * half : (place + 1) * half, :] = placed((half, width), 0, row)
        columns_ref[place] = placed((width + half, width), 1, column)
        rows_back_ref[place] = placed((width + half, width), 1, row)
        columns_back_ref[place * width : (place + 1) * width, :] = placed((width, width + half), 0, column)


def extract_kernel(rows_ref, columns_ref, tile_ref, below_ref, right_ref, own_ref, first_ref, second_ref):
    width = tile_ref.shape[1]
    half = width // 2
    wide = width + half
    blocks = []
    for part in range(2):
        upper = jnp.concatenate([own_ref[part, :half], right_ref[part]], axis=1)
        lower = jnp.concatenate([below_ref[part, :width], tile_ref[part]], axis=1)
        blocks.append(jnp.concatenate([upper, lower], axis=0))
    block = jnp.concatenate(blocks, axis=1)
    strips = [dot(rows_ref[...], block[top : top + width]).astype(jnp.bfloat16) for top in (0, half)]
    for place, out_ref in enumerate((first_ref, second_ref)):
        mine = [strip[place * half : (place + 1) * half, part * wide : (part + 1) * wide] for part in range(2) for strip in strips]
        out_ref[...] = dot(jnp.concatenate(mine, axis=0), columns_ref[place]).astype(jnp.bfloat16)


def ordered(first_ref, second_ref):
    odd = lax.rem(lax.axis_index("cuts"), 2) == 1
    first, second = first_ref[...], second_ref[...]
    return jnp.where(odd, second, first), jnp.where(odd, first, second)


def near_chip():
    return lax.axis_index("cuts") < 2


def spread_on(spread, patch, band_ref):
    wave = complex_mul(spread, patch, 1.0).astype(jnp.bfloat16)
    return sandwich(band_ref[0], band_ref[1], wave, band_ref[2], band_ref[3]).astype(jnp.bfloat16)


def back_on(back, patch, band_ref):
    carried = complex_mul(patch, back, -1.0).astype(jnp.bfloat16)
    return sandwich(band_ref[2], -band_ref[3], carried, band_ref[0], -band_ref[1]).astype(jnp.bfloat16)


def head_kernel(probe_ref, band_ref, p0_ref, p1_ref, one_ref, two_ref):
    @pl.when(near_chip())
    def _():
        patch_0, patch_1 = ordered(p0_ref, p1_ref)
        one_ref[...] = spread_on(probe_ref[...], patch_0, band_ref)
        two_ref[...] = spread_on(one_ref[...], patch_1, band_ref)


def chain_kernel(
    probe_ref, p0_ref, p1_ref, p2_ref, p3_ref, level_ref, far_level_ref, band_ref, fourier_ref, one_ref, two_ref, mine_ref, other_ref,
    keep_two_ref, keep_three_ref, wave_ref
):
    width = probe_ref.shape[1]

    @pl.when(near_chip())
    def _():
        patch_2, patch_3 = ordered(p2_ref, p3_ref)
        spread = spread_on(two_ref[...], patch_2, band_ref)
        wave_ref[...] = complex_mul(spread, patch_3, 1.0).astype(jnp.bfloat16)

    @pl.when(jnp.logical_not(near_chip()))
    def _():
        patch_0, patch_1 = ordered(p2_ref, p3_ref)
        patch_2, patch_3 = ordered(p0_ref, p1_ref)
        spread = spread_on(probe_ref[...], patch_0, band_ref)
        keep_two_ref[...] = spread_on(spread, patch_1, band_ref)
        keep_three_ref[...] = spread_on(keep_two_ref[...], patch_2, band_ref)
        wave_ref[...] = complex_mul(keep_three_ref[...], patch_3, 1.0).astype(jnp.bfloat16)

    fourier_r, fourier_i = fourier_ref[0], fourier_ref[1]
    far = sandwich(fourier_r, fourier_i, wave_ref[...], fourier_r, fourier_i)
    far_r, far_i = far[:width], far[width:]
    rows = width // 2
    level, far_level = level_ref[:rows, :].astype(jnp.float32), far_level_ref[:rows, :].astype(jnp.float32)
    level = jnp.concatenate([jnp.where(near_chip(), level, far_level), jnp.where(near_chip(), far_level, level)], axis=0)
    live = level_ref[rows : rows + 1, :].astype(jnp.float32)
    excess = 2.0 * live * (far_r * far_r + far_i * far_i - level)
    residual = jnp.concatenate([excess * far_r, excess * far_i], axis=0).astype(jnp.bfloat16)
    wave_ref[...] = sandwich(fourier_r, -fourier_i, residual, fourier_r, -fourier_i).astype(jnp.bfloat16)
    odd = lax.rem(lax.axis_index("cuts"), 2) == 1

    def out(low, high):
        mine_ref[...] = jnp.where(odd, high, low)
        other_ref[...] = jnp.where(odd, low, high)

    @pl.when(near_chip())
    def _():
        _, patch_1 = ordered(p0_ref, p1_ref)
        patch_2, patch_3 = ordered(p2_ref, p3_ref)
        back = back_on(wave_ref[...], patch_3, band_ref)
        back = back_on(back, patch_2, band_ref)
        high = complex_mul(one_ref[...], back, -1.0).astype(jnp.bfloat16)
        back = back_on(back, patch_1, band_ref)
        out(complex_mul(probe_ref[...], back, -1.0).astype(jnp.bfloat16), high)

    @pl.when(jnp.logical_not(near_chip()))
    def _():
        _, patch_3 = ordered(p0_ref, p1_ref)
        back = wave_ref[...]
        high = complex_mul(keep_three_ref[...], back, -1.0).astype(jnp.bfloat16)
        back = back_on(back, patch_3, band_ref)
        out(complex_mul(keep_two_ref[...], back, -1.0).astype(jnp.bfloat16), high)


def placed_rows(rows, ref):
    width = ref.shape[1]
    return dot(rows, jnp.concatenate([ref[:width, :], ref[width:, :]], axis=1)).astype(jnp.bfloat16)


def rows_kernel(rows_ref, mine_ref, strip_ref):
    strip_ref[...] = placed_rows(rows_ref[0], mine_ref)


def scatter_kernel(rows_ref, columns_ref, strip_ref, other_ref, tile_ref, below_ref, right_ref, own_ref):
    width = tile_ref.shape[1]
    half = width // 2
    strips = [strip_ref[...], placed_rows(rows_ref[1], other_ref)]
    for part in range(2):
        strip = jnp.concatenate([strip[:, part * width : (part + 1) * width] for strip in strips], axis=1)
        total = dot(strip, columns_ref[...])
        tile_ref[part] = total[half:, half:]
        below_ref[part] = total[half:, :half].astype(jnp.bfloat16)
        right_ref[part, :half, :] = total[:half, half:].astype(jnp.bfloat16)
        right_ref[part, half:, :] = jnp.zeros((SPARE, width), jnp.bfloat16)
        own_ref[part] = total[:half, :half].astype(jnp.bfloat16)


def total_kernel(tile_ref, below_ref, right_ref, out_ref, quarter_ref):
    half = right_ref.shape[2] // 2
    below = below_ref[...].astype(jnp.float32)
    right = right_ref[:, :half, :].astype(jnp.float32)
    quarter = tile_ref[:, half:, half:] + below[:, half:] + right[:, :, half:]
    out_ref[0, :, :half, :half] = tile_ref[:, :half, :half]
    out_ref[0, :, :half, half:] = tile_ref[:, :half, half:] + below[:, :half]
    out_ref[0, :, half:, :half] = tile_ref[:, half:, :half] + right[:, :, :half]
    out_ref[0, :, half:, half:] = quarter
    quarter_ref[...] = quarter


def quarter_kernel(out_ref, quarter_ref, own_ref, same_ref, sum_ref, sem):
    half = quarter_ref.shape[1]
    sum_ref[...] = quarter_ref[...] + own_ref[...].astype(jnp.float32)
    copy = pltpu.make_async_copy(sum_ref, same_ref.at[0, :, pl.ds(half, half), pl.ds(half, half)], sem)
    copy.start()
    copy.wait()


VMEM = pl.BlockSpec(memory_space=pltpu.VMEM)
ANY = pl.BlockSpec(memory_space=pl.ANY)
SMEM = pl.BlockSpec(memory_space=pltpu.SMEM)
PARAMS = pltpu.CompilerParams(vmem_limit_bytes=48 * 1024 * 1024)


def shaped(*shape, dtype=jnp.bfloat16):
    return jax.ShapeDtypeStruct(shape, dtype)


def kernel(body, name, in_specs, out_shape, scratch=()):
    return pl.pallas_call(
        body, in_specs=in_specs, out_specs=[VMEM] * len(out_shape), out_shape=out_shape, scratch_shapes=scratch, compiler_params=PARAMS, name=name
    )


def local(object_slices, probe, fresnel_taps, offsets, counts, measured):
    width = probe.shape[1]
    half = width // 2
    wide = width + half
    full = shaped(2 * width, width)
    part = shaped(width, width)
    row_tiles = max(lax.axis_size("tile") // 16, 2)
    probe = probe.reshape(2 * width, width)
    fourier = jnp.asarray(fourier_matrix(width), jnp.bfloat16)

    far_tile = crossed(object_slices[0], "cuts", 2)
    tile, below, right = kernel(cut_kernel, "cut", [VMEM], [shaped(2, width, width), shaped(2, width + SPARE, half), shaped(2, half, width)])(
        object_slices[0]
    )
    (own,) = kernel(seal_kernel, "seal", [VMEM, VMEM], [shaped(2, half + 16, half)])(tile, offsets)
    below = passed_along(below, "tile", 1)
    right = passed_along(right, "tile", row_tiles)
    own = passed_along(own, "tile", row_tiles + 1)
    far_right = crossed(right, "cuts", 2)
    far_own = crossed(own, "cuts", 2)
    level = shaped(half + 16, width)
    band, level = kernel(band_kernel, "band", [SMEM, VMEM, VMEM], [shaped(4, width, width), level])(counts, fresnel_taps, measured)
    level, far_tile = lax.optimization_barrier((level, far_tile))
    below, far_tile = lax.optimization_barrier((below, far_tile))
    far_below = crossed(below, "cuts", 2)
    level = passed_along(level, "tile", row_tiles + 1)
    rows, columns, rows_back, columns_back = kernel(
        window_kernel,
        "window",
        [VMEM],
        [part, shaped(2, wide, width), shaped(2, wide, width), shaped(2 * width, wide)],
    )(own)
    first, second = kernel(extract_kernel, "near", [VMEM] * 6, [full, full])(rows, columns, tile, below, right, own)
    swapped = crossed(second, "cuts", 1)
    far_level = crossed(level, "cuts", 2)
    straight, far_second = kernel(extract_kernel, "far", [VMEM] * 6, [full, full])(rows, columns, far_tile, far_below, far_right, far_own)
    far_second, far_level = lax.optimization_barrier((far_second, far_level))
    diagonal = crossed(far_second, "cuts", 1)
    one, two = kernel(head_kernel, "head", [VMEM] * 4, [full, full])(probe, band, first, swapped)
    mine, other = kernel(chain_kernel, "chain", [VMEM] * 11, [full, full], [pltpu.VMEM((2 * width, width), jnp.bfloat16)] * 3)(
        probe, first, swapped, straight, diagonal, level, far_level, band, fourier, one, two
    )
    other = crossed(other, "cuts", 1)
    (strip,) = kernel(rows_kernel, "rows", [VMEM] * 2, [shaped(wide, 2 * width)])(rows_back, mine)
    total, below, right, own = kernel(
        scatter_kernel,
        "scatter",
        [VMEM] * 4,
        [shaped(2, width, width, dtype=jnp.float32), shaped(2, width, half), shaped(2, half + SPARE, width), shaped(2, half, half)],
    )(rows_back, columns_back, strip, other)
    below = passed_along(below, "tile", -1)
    right = passed_along(right, "tile", -row_tiles)
    own = passed_along(own, "tile", -row_tiles - 1)
    whole = shaped(1, 2, width, width, dtype=jnp.float32)
    quarter = shaped(2, half, half, dtype=jnp.float32)
    out, quarter = kernel(total_kernel, "total", [VMEM] * 3, [whole, quarter])(total, below, right)
    out = pl.pallas_call(
        quarter_kernel,
        in_specs=[ANY, VMEM, VMEM],
        out_specs=ANY,
        out_shape=whole,
        input_output_aliases={0: 0},
        scratch_shapes=[pltpu.VMEM((2, half, half), jnp.float32), pltpu.SemaphoreType.DMA],
        compiler_params=PARAMS,
        name="quarter",
    )(out, quarter, own)
    return out


def solution(mesh):
    return jax.shard_map(
        local,
        mesh=mesh,
        in_specs=(
            P("cuts", None, "tile", None),
            P(),
            P(),
            P("tile", None),
            P("tile"),
            P("tile", None, None),
        ),
        out_specs=P("cuts", None, "tile", None),
        check_vma=False,
    )
```

```python
import jax
import jax.numpy as jnp
import numpy as np
from jax import lax
from jax.experimental import pallas as pl
from jax.experimental.pallas import tpu as pltpu
from jax.sharding import PartitionSpec as P


SPARE = 16


def passed_along(value, axis, steps):
    count = lax.axis_size(axis)
    pairs = [(source, (source + steps) % count) for source in range(count)]
    return lax.ppermute(value, axis, pairs)


def crossed(value, axis, mask):
    pairs = [(source, source ^ mask) for source in range(lax.axis_size(axis))]
    return lax.ppermute(value, axis, pairs)


def fourier_matrix(width):
    index = np.arange(width)
    angle = 2.0 * np.pi * (index[:, None] * index[None, :] % width) / width
    return np.stack([np.cos(angle), -np.sin(angle)]) / np.sqrt(width)


def dot(left, right):
    return jnp.dot(left, right, preferred_element_type=jnp.float32)


def sandwich(left_real, left_imag, field, right_real, right_imag):
    right = jnp.concatenate([right_real, right_imag], axis=0)
    top = dot(jnp.concatenate([left_real, -left_imag], axis=1), field).astype(jnp.bfloat16)
    bottom = dot(jnp.concatenate([left_imag, left_real], axis=1), field).astype(jnp.bfloat16)
    real = dot(jnp.concatenate([top, -bottom], axis=1), right)
    imag = dot(jnp.concatenate([bottom, top], axis=1), right)
    return jnp.concatenate([real, imag], axis=0)


def complex_mul(first, second, sign):
    width = first.shape[1]
    fr, fi = first[:width], first[width:]
    if sign < 0:
        fi = -fi
    sr, si = second[:width], second[width:]
    return jnp.concatenate([fr * sr - fi * si, fr * si + fi * sr], axis=0)


def band_kernel(counts_ref, taps_ref, measured_ref, band_ref, level_ref):
    width = band_ref.shape[1]
    half = taps_ref.shape[1] // 2
    core = lax.rem(lax.axis_index("cuts"), 2)
    rows = width // 2
    first = pl.multiple_of(lax.axis_index("cuts") // 2 * rows, rows)
    level_ref[:rows, :] = measured_ref[core, pl.ds(first, rows), :].astype(jnp.bfloat16)
    live = (core < counts_ref[0]).astype(jnp.float32)
    level_ref[rows:, :] = jnp.full((level_ref.shape[0] - rows, width), live, jnp.float32).astype(jnp.bfloat16)
    rows = lax.broadcasted_iota(jnp.int32, (width, width), 0)
    columns = lax.broadcasted_iota(jnp.int32, (width, width), 1)
    inside = jnp.abs(columns - rows) <= half
    for part in range(2):
        line = taps_ref[part : part + 1, :].astype(jnp.float32)
        filler = jnp.zeros((1, width - line.shape[1]), jnp.float32)
        line = jnp.concatenate([line, filler], axis=1)
        spread = jnp.broadcast_to(line, (width, width))
        turned = pltpu.roll(spread, width - half, 1, stride=1, stride_axis=0)
        band = jnp.where(inside, turned, 0.0)
        band_ref[part] = band.astype(jnp.bfloat16)
        band_ref[part + 2] = band.T.astype(jnp.bfloat16)


def cut_kernel(tile_ref, whole_ref, below_ref, right_ref):
    half = right_ref.shape[1]
    whole_ref[...] = tile_ref[...]
    below_ref[:, : 2 * half, :] = tile_ref[:, :, half:]
    below_ref[:, 2 * half :, :] = jnp.zeros((2, SPARE, half), jnp.bfloat16)
    right_ref[...] = tile_ref[:, half:, :]


def seal_kernel(tile_ref, offsets_ref, own_ref):
    half = tile_ref.shape[1] // 2
    own_ref[:, :half, :] = tile_ref[:, half:, half:]
    shape = (own_ref.shape[1] - half, half)
    line = lax.broadcasted_iota(jnp.int32, shape, 0)
    lines = jnp.zeros(shape, jnp.float32)
    for index in range(4):
        value = offsets_ref[index // 2 : index // 2 + 1, index % 2 : index % 2 + 1].astype(jnp.float32)
        lines = jnp.where(line == index, value, lines)
    for part in range(2):
        own_ref[part, half:, :] = lines.astype(jnp.bfloat16)


def window_kernel(own_ref, rows_ref, columns_ref, rows_back_ref, columns_back_ref):
    half = own_ref.shape[2]
    width = 2 * half
    core = lax.rem(lax.axis_index("cuts"), 2)
    lines = own_ref[0, half:, :].astype(jnp.float32).astype(jnp.int32) - half

    def placed(shape, axis, shift):
        i = lax.broadcasted_iota(jnp.int32, shape, axis)
        j = lax.broadcasted_iota(jnp.int32, shape, 1 - axis)
        shift = jnp.concatenate([shift] * (shape[1] // half), axis=1)
        return jnp.where(j - i == shift, 1.0, 0.0).astype(jnp.bfloat16)

    for place in range(2):
        second = core != place
        row = jnp.where(second, lines[2:3], lines[0:1])
        column = jnp.where(second, lines[3:4], lines[1:2])
        rows_ref[place * half : (place + 1) * half, :] = placed((half, width), 0, row)
        columns_ref[place] = placed((width + half, width), 1, column)
        rows_back_ref[place] = placed((width + half, width), 1, row)
        columns_back_ref[place * width : (place + 1) * width, :] = placed((width, width + half), 0, column)


def extract_kernel(rows_ref, columns_ref, tile_ref, below_ref, right_ref, own_ref, first_ref, second_ref):
    width = tile_ref.shape[1]
    half = width // 2
    wide = width + half
    blocks = []
    for part in range(2):
        upper = jnp.concatenate([own_ref[part, :half], right_ref[part]], axis=1)
        lower = jnp.concatenate([below_ref[part, :width], tile_ref[part]], axis=1)
        blocks.append(jnp.concatenate([upper, lower], axis=0))
    block = jnp.concatenate(blocks, axis=1)
    strips = [dot(rows_ref[...], block[top : top + width]).astype(jnp.bfloat16) for top in (0, half)]
    for place, out_ref in enumerate((first_ref, second_ref)):
        mine = [strip[place * half : (place + 1) * half, part * wide : (part + 1) * wide] for part in range(2) for strip in strips]
        out_ref[...] = dot(jnp.concatenate(mine, axis=0), columns_ref[place]).astype(jnp.bfloat16)


def ordered(first_ref, second_ref):
    odd = lax.rem(lax.axis_index("cuts"), 2) == 1
    first, second = first_ref[...], second_ref[...]
    return jnp.where(odd, second, first), jnp.where(odd, first, second)


def near_chip():
    return lax.axis_index("cuts") < 2


def spread_on(spread, patch, band_ref):
    wave = complex_mul(spread, patch, 1.0).astype(jnp.bfloat16)
    return sandwich(band_ref[0], band_ref[1], wave, band_ref[2], band_ref[3]).astype(jnp.bfloat16)


def back_on(back, patch, band_ref):
    carried = complex_mul(patch, back, -1.0).astype(jnp.bfloat16)
    return sandwich(band_ref[2], -band_ref[3], carried, band_ref[0], -band_ref[1]).astype(jnp.bfloat16)


def head_kernel(probe_ref, band_ref, p0_ref, p1_ref, one_ref, two_ref):
    @pl.when(near_chip())
    def _():
        patch_0, patch_1 = ordered(p0_ref, p1_ref)
        one_ref[...] = spread_on(probe_ref[...], patch_0, band_ref)
        two_ref[...] = spread_on(one_ref[...], patch_1, band_ref)


def chain_kernel(
    probe_ref, p0_ref, p1_ref, p2_ref, p3_ref, level_ref, far_level_ref, band_ref, fourier_ref, one_ref, two_ref, mine_ref, other_ref,
    keep_two_ref, keep_three_ref, wave_ref
):
    width = probe_ref.shape[1]

    @pl.when(near_chip())
    def _():
        patch_2, patch_3 = ordered(p2_ref, p3_ref)
        spread = spread_on(two_ref[...], patch_2, band_ref)
        wave_ref[...] = complex_mul(spread, patch_3, 1.0).astype(jnp.bfloat16)

    @pl.when(jnp.logical_not(near_chip()))
    def _():
        patch_0, patch_1 = ordered(p2_ref, p3_ref)
        patch_2, patch_3 = ordered(p0_ref, p1_ref)
        spread = spread_on(probe_ref[...], patch_0, band_ref)
        keep_two_ref[...] = spread_on(spread, patch_1, band_ref)
        keep_three_ref[...] = spread_on(keep_two_ref[...], patch_2, band_ref)
        wave_ref[...] = complex_mul(keep_three_ref[...], patch_3, 1.0).astype(jnp.bfloat16)

    fourier_r, fourier_i = fourier_ref[0], fourier_ref[1]
    far = sandwich(fourier_r, fourier_i, wave_ref[...], fourier_r, fourier_i)
    far_r, far_i = far[:width], far[width:]
    rows = width // 2
    level, far_level = level_ref[:rows, :].astype(jnp.float32), far_level_ref[:rows, :].astype(jnp.float32)
    level = jnp.concatenate([jnp.where(near_chip(), level, far_level), jnp.where(near_chip(), far_level, level)], axis=0)
    live = level_ref[rows : rows + 1, :].astype(jnp.float32)
    excess = 2.0 * live * (far_r * far_r + far_i * far_i - level)
    residual = jnp.concatenate([excess * far_r, excess * far_i], axis=0).astype(jnp.bfloat16)
    wave_ref[...] = sandwich(fourier_r, -fourier_i, residual, fourier_r, -fourier_i).astype(jnp.bfloat16)
    odd = lax.rem(lax.axis_index("cuts"), 2) == 1

    def out(low, high):
        mine_ref[...] = jnp.where(odd, high, low)
        other_ref[...] = jnp.where(odd, low, high)

    @pl.when(near_chip())
    def _():
        _, patch_1 = ordered(p0_ref, p1_ref)
        patch_2, patch_3 = ordered(p2_ref, p3_ref)
        back = back_on(wave_ref[...], patch_3, band_ref)
        back = back_on(back, patch_2, band_ref)
        high = complex_mul(one_ref[...], back, -1.0).astype(jnp.bfloat16)
        back = back_on(back, patch_1, band_ref)
        out(complex_mul(probe_ref[...], back, -1.0).astype(jnp.bfloat16), high)

    @pl.when(jnp.logical_not(near_chip()))
    def _():
        _, patch_3 = ordered(p0_ref, p1_ref)
        back = wave_ref[...]
        high = complex_mul(keep_three_ref[...], back, -1.0).astype(jnp.bfloat16)
        back = back_on(back, patch_3, band_ref)
        out(complex_mul(keep_two_ref[...], back, -1.0).astype(jnp.bfloat16), high)


def placed_rows(rows, ref):
    width = ref.shape[1]
    return jnp.concatenate([dot(rows, part).astype(jnp.bfloat16) for part in (ref[:width, :], ref[width:, :])], axis=1)


def rows_kernel(rows_ref, mine_ref, strip_ref):
    strip_ref[...] = placed_rows(rows_ref[0], mine_ref)


def scatter_kernel(rows_ref, columns_ref, strip_ref, other_ref, tile_ref, below_ref, right_ref, own_ref):
    width = tile_ref.shape[1]
    half = width // 2
    strips = [strip_ref[...], placed_rows(rows_ref[1], other_ref)]
    for part in range(2):
        strip = jnp.concatenate([strip[:, part * width : (part + 1) * width] for strip in strips], axis=1)
        total = dot(strip, columns_ref[...])
        tile_ref[part] = total[half:, half:]
        below_ref[part] = total[half:, :half].astype(jnp.bfloat16)
        right_ref[part] = total[:half, half:].astype(jnp.bfloat16)
        own_ref[part] = total[:half, :half].astype(jnp.bfloat16)


def total_kernel(tile_ref, below_ref, right_ref, out_ref, quarter_ref):
    half = right_ref.shape[1]
    below = below_ref[...].astype(jnp.float32)
    right = right_ref[...].astype(jnp.float32)
    quarter = tile_ref[:, half:, half:] + below[:, half:] + right[:, :, half:]
    out_ref[0, :, :half, :half] = tile_ref[:, :half, :half]
    out_ref[0, :, :half, half:] = tile_ref[:, :half, half:] + below[:, :half]
    out_ref[0, :, half:, :half] = tile_ref[:, half:, :half] + right[:, :, :half]
    out_ref[0, :, half:, half:] = quarter
    quarter_ref[...] = quarter


def quarter_kernel(out_ref, quarter_ref, own_ref, same_ref, sum_ref, sem):
    half = quarter_ref.shape[1]
    sum_ref[...] = quarter_ref[...] + own_ref[...].astype(jnp.float32)
    copy = pltpu.make_async_copy(sum_ref, same_ref.at[0, :, pl.ds(half, half), pl.ds(half, half)], sem)
    copy.start()
    copy.wait()


VMEM = pl.BlockSpec(memory_space=pltpu.VMEM)
ANY = pl.BlockSpec(memory_space=pl.ANY)
SMEM = pl.BlockSpec(memory_space=pltpu.SMEM)
PARAMS = pltpu.CompilerParams(vmem_limit_bytes=48 * 1024 * 1024)


def shaped(*shape, dtype=jnp.bfloat16):
    return jax.ShapeDtypeStruct(shape, dtype)


def kernel(body, name, in_specs, out_shape, scratch=()):
    return pl.pallas_call(
        body, in_specs=in_specs, out_specs=[VMEM] * len(out_shape), out_shape=out_shape, scratch_shapes=scratch, compiler_params=PARAMS, name=name
    )


def local(object_slices, probe, fresnel_taps, offsets, counts, measured):
    width = probe.shape[1]
    half = width // 2
    wide = width + half
    full = shaped(2 * width, width)
    part = shaped(width, width)
    row_tiles = max(lax.axis_size("tile") // 16, 2)
    probe = probe.reshape(2 * width, width)
    fourier = jnp.asarray(fourier_matrix(width), jnp.bfloat16)

    far_tile = crossed(object_slices[0], "cuts", 2)
    tile, below, right = kernel(cut_kernel, "cut", [VMEM], [shaped(2, width, width), shaped(2, width + SPARE, half), shaped(2, half, width)])(
        object_slices[0]
    )
    (own,) = kernel(seal_kernel, "seal", [VMEM, VMEM], [shaped(2, half + 16, half)])(tile, offsets)
    below = passed_along(below, "tile", 1)
    right = passed_along(right, "tile", row_tiles)
    own = passed_along(own, "tile", row_tiles + 1)
    far_right = crossed(right, "cuts", 2)
    far_own = crossed(own, "cuts", 2)
    level = shaped(half + 16, width)
    band, level = kernel(band_kernel, "band", [SMEM, VMEM, VMEM], [shaped(4, width, width), level])(counts, fresnel_taps, measured)
    level, far_tile = lax.optimization_barrier((level, far_tile))
    below, far_tile = lax.optimization_barrier((below, far_tile))
    far_below = crossed(below, "cuts", 2)
    level = passed_along(level, "tile", row_tiles + 1)
    rows, columns, rows_back, columns_back = kernel(
        window_kernel,
        "window",
        [VMEM],
        [part, shaped(2, wide, width), shaped(2, wide, width), shaped(2 * width, wide)],
    )(own)
    first, second = kernel(extract_kernel, "near", [VMEM] * 6, [full, full])(rows, columns, tile, below, right, own)
    swapped = crossed(second, "cuts", 1)
    far_level = crossed(level, "cuts", 2)
    straight, far_second = kernel(extract_kernel, "far", [VMEM] * 6, [full, full])(rows, columns, far_tile, far_below, far_right, far_own)
    far_second, far_level = lax.optimization_barrier((far_second, far_level))
    diagonal = crossed(far_second, "cuts", 1)
    one, two = kernel(head_kernel, "head", [VMEM] * 4, [full, full])(probe, band, first, swapped)
    mine, other = kernel(chain_kernel, "chain", [VMEM] * 11, [full, full], [pltpu.VMEM((2 * width, width), jnp.bfloat16)] * 3)(
        probe, first, swapped, straight, diagonal, level, far_level, band, fourier, one, two
    )
    other = crossed(other, "cuts", 1)
    (strip,) = kernel(rows_kernel, "rows", [VMEM] * 2, [shaped(wide, 2 * width)])(rows_back, mine)
    total, below, right, own = kernel(
        scatter_kernel,
        "scatter",
        [VMEM] * 4,
        [shaped(2, width, width, dtype=jnp.float32), shaped(2, width, half), shaped(2, half, width), shaped(2, half, half)],
    )(rows_back, columns_back, strip, other)
    below = passed_along(below, "tile", -1)
    right = passed_along(right, "tile", -row_tiles)
    own = passed_along(own, "tile", -row_tiles - 1)
    whole = shaped(1, 2, width, width, dtype=jnp.float32)
    quarter = shaped(2, half, half, dtype=jnp.float32)
    out, quarter = kernel(total_kernel, "total", [VMEM] * 3, [whole, quarter])(total, below, right)
    out = pl.pallas_call(
        quarter_kernel,
        in_specs=[ANY, VMEM, VMEM],
        out_specs=ANY,
        out_shape=whole,
        input_output_aliases={0: 0},
        scratch_shapes=[pltpu.VMEM((2, half, half), jnp.float32), pltpu.SemaphoreType.DMA],
        compiler_params=PARAMS,
        name="quarter",
    )(out, quarter, own)
    return out


def solution(mesh):
    return jax.shard_map(
        local,
        mesh=mesh,
        in_specs=(
            P("cuts", None, "tile", None),
            P(),
            P(),
            P("tile", None),
            P("tile"),
            P("tile", None, None),
        ),
        out_specs=P("cuts", None, "tile", None),
        check_vma=False,
    )
```

```python
import jax
import jax.numpy as jnp
import numpy as np
from jax import lax
from jax.experimental import pallas as pl
from jax.experimental.pallas import tpu as pltpu
from jax.sharding import PartitionSpec as P


SPARE = 16


def passed_along(value, axis, steps):
    count = lax.axis_size(axis)
    pairs = [(source, (source + steps) % count) for source in range(count)]
    return lax.ppermute(value, axis, pairs)


def crossed(value, axis, mask):
    pairs = [(source, source ^ mask) for source in range(lax.axis_size(axis))]
    return lax.ppermute(value, axis, pairs)


def fourier_matrix(width):
    index = np.arange(width)
    angle = 2.0 * np.pi * (index[:, None] * index[None, :] % width) / width
    return np.stack([np.cos(angle), -np.sin(angle)]) / np.sqrt(width)


def dot(left, right):
    return jnp.dot(left, right, preferred_element_type=jnp.float32)


def sandwich(left_real, left_imag, field, right_real, right_imag):
    right = jnp.concatenate([right_real, right_imag], axis=0)
    top = dot(jnp.concatenate([left_real, -left_imag], axis=1), field).astype(jnp.bfloat16)
    bottom = dot(jnp.concatenate([left_imag, left_real], axis=1), field).astype(jnp.bfloat16)
    real = dot(jnp.concatenate([top, -bottom], axis=1), right)
    imag = dot(jnp.concatenate([bottom, top], axis=1), right)
    return jnp.concatenate([real, imag], axis=0)


def complex_mul(first, second, sign):
    width = first.shape[1]
    fr, fi = first[:width], first[width:]
    if sign < 0:
        fi = -fi
    sr, si = second[:width], second[width:]
    return jnp.concatenate([fr * sr - fi * si, fr * si + fi * sr], axis=0)


def band_kernel(counts_ref, taps_ref, measured_ref, band_ref, level_ref):
    width = band_ref.shape[1]
    half = taps_ref.shape[1] // 2
    core = lax.rem(lax.axis_index("cuts"), 2)
    rows = width // 2
    first = pl.multiple_of(lax.axis_index("cuts") // 2 * rows, rows)
    level_ref[:rows, :] = measured_ref[core, pl.ds(first, rows), :].astype(jnp.bfloat16)
    live = (core < counts_ref[0]).astype(jnp.float32)
    level_ref[rows:, :] = jnp.full((level_ref.shape[0] - rows, width), live, jnp.float32).astype(jnp.bfloat16)
    rows = lax.broadcasted_iota(jnp.int32, (width, width), 0)
    columns = lax.broadcasted_iota(jnp.int32, (width, width), 1)
    inside = jnp.abs(columns - rows) <= half
    for part in range(2):
        line = taps_ref[part : part + 1, :].astype(jnp.float32)
        filler = jnp.zeros((1, width - line.shape[1]), jnp.float32)
        line = jnp.concatenate([line, filler], axis=1)
        spread = jnp.broadcast_to(line, (width, width))
        turned = pltpu.roll(spread, width - half, 1, stride=1, stride_axis=0)
        band = jnp.where(inside, turned, 0.0)
        band_ref[part] = band.astype(jnp.bfloat16)
        band_ref[part + 2] = band.T.astype(jnp.bfloat16)


def cut_kernel(tile_ref, whole_ref, below_ref, right_ref):
    half = right_ref.shape[1]
    whole_ref[...] = tile_ref[...]
    below_ref[:, : 2 * half, :] = tile_ref[:, :, half:]
    below_ref[:, 2 * half :, :] = jnp.zeros((2, SPARE, half), jnp.bfloat16)
    right_ref[...] = tile_ref[:, half:, :]


def seal_kernel(tile_ref, offsets_ref, own_ref):
    half = tile_ref.shape[1] // 2
    own_ref[:, :half, :] = tile_ref[:, half:, half:]
    shape = (own_ref.shape[1] - half, half)
    line = lax.broadcasted_iota(jnp.int32, shape, 0)
    lines = jnp.zeros(shape, jnp.float32)
    for index in range(4):
        value = offsets_ref[index // 2 : index // 2 + 1, index % 2 : index % 2 + 1].astype(jnp.float32)
        lines = jnp.where(line == index, value, lines)
    for part in range(2):
        own_ref[part, half:, :] = lines.astype(jnp.bfloat16)


def window_kernel(own_ref, rows_ref, columns_ref, rows_back_ref, columns_back_ref):
    half = own_ref.shape[2]
    width = 2 * half
    core = lax.rem(lax.axis_index("cuts"), 2)
    lines = own_ref[0, half:, :].astype(jnp.float32).astype(jnp.int32) - half

    def placed(shape, axis, shift):
        i = lax.broadcasted_iota(jnp.int32, shape, axis)
        j = lax.broadcasted_iota(jnp.int32, shape, 1 - axis)
        shift = jnp.concatenate([shift] * (shape[1] // half), axis=1)
        return jnp.where(j - i == shift, 1.0, 0.0).astype(jnp.bfloat16)

    for place in range(2):
        second = core != place
        row = jnp.where(second, lines[2:3], lines[0:1])
        column = jnp.where(second, lines[3:4], lines[1:2])
        rows_ref[place * half : (place + 1) * half, :] = placed((half, width), 0, row)
        columns_ref[place] = placed((width + half, width), 1, column)
        rows_back_ref[place] = placed((width + half, width), 1, row)
        columns_back_ref[place * width : (place + 1) * width, :] = placed((width, width + half), 0, column)


def extract_kernel(rows_ref, columns_ref, tile_ref, below_ref, right_ref, own_ref, first_ref, second_ref):
    width = tile_ref.shape[1]
    half = width // 2
    wide = width + half
    blocks = []
    for part in range(2):
        upper = jnp.concatenate([own_ref[part, :half], right_ref[part]], axis=1)
        lower = jnp.concatenate([below_ref[part, :width], tile_ref[part]], axis=1)
        blocks.append(jnp.concatenate([upper, lower], axis=0))
    block = jnp.concatenate(blocks, axis=1)
    strips = [dot(rows_ref[...], block[top : top + width]).astype(jnp.bfloat16) for top in (0, half)]
    for place, out_ref in enumerate((first_ref, second_ref)):
        mine = [strip[place * half : (place + 1) * half, part * wide : (part + 1) * wide] for part in range(2) for strip in strips]
        out_ref[...] = dot(jnp.concatenate(mine, axis=0), columns_ref[place]).astype(jnp.bfloat16)


def ordered(first_ref, second_ref):
    odd = lax.rem(lax.axis_index("cuts"), 2) == 1
    first, second = first_ref[...], second_ref[...]
    return jnp.where(odd, second, first), jnp.where(odd, first, second)


def near_chip():
    return lax.axis_index("cuts") < 2


def spread_on(spread, patch, band_ref):
    wave = complex_mul(spread, patch, 1.0).astype(jnp.bfloat16)
    return sandwich(band_ref[0], band_ref[1], wave, band_ref[2], band_ref[3]).astype(jnp.bfloat16)


def back_on(back, patch, band_ref):
    carried = complex_mul(patch, back, -1.0).astype(jnp.bfloat16)
    return sandwich(band_ref[2], -band_ref[3], carried, band_ref[0], -band_ref[1]).astype(jnp.bfloat16)


def head_kernel(probe_ref, band_ref, p0_ref, p1_ref, one_ref, two_ref):
    @pl.when(near_chip())
    def _():
        patch_0, patch_1 = ordered(p0_ref, p1_ref)
        one_ref[...] = spread_on(probe_ref[...], patch_0, band_ref)
        two_ref[...] = spread_on(one_ref[...], patch_1, band_ref)


def chain_kernel(
    probe_ref, p0_ref, p1_ref, p2_ref, p3_ref, level_ref, far_level_ref, band_ref, fourier_ref, one_ref, two_ref, mine_ref, other_ref,
    keep_two_ref, keep_three_ref, wave_ref
):
    width = probe_ref.shape[1]

    @pl.when(near_chip())
    def _():
        patch_2, patch_3 = ordered(p2_ref, p3_ref)
        spread = spread_on(two_ref[...], patch_2, band_ref)
        wave_ref[...] = complex_mul(spread, patch_3, 1.0).astype(jnp.bfloat16)

    @pl.when(jnp.logical_not(near_chip()))
    def _():
        patch_0, patch_1 = ordered(p2_ref, p3_ref)
        patch_2, patch_3 = ordered(p0_ref, p1_ref)
        spread = spread_on(probe_ref[...], patch_0, band_ref)
        keep_two_ref[...] = spread_on(spread, patch_1, band_ref)
        keep_three_ref[...] = spread_on(keep_two_ref[...], patch_2, band_ref)
        wave_ref[...] = complex_mul(keep_three_ref[...], patch_3, 1.0).astype(jnp.bfloat16)

    fourier_r, fourier_i = fourier_ref[0], fourier_ref[1]
    far = sandwich(fourier_r, fourier_i, wave_ref[...], fourier_r, fourier_i)
    far_r, far_i = far[:width], far[width:]
    rows = width // 2
    level, far_level = level_ref[:rows, :].astype(jnp.float32), far_level_ref[:rows, :].astype(jnp.float32)
    level = jnp.concatenate([jnp.where(near_chip(), level, far_level), jnp.where(near_chip(), far_level, level)], axis=0)
    live = level_ref[rows : rows + 1, :].astype(jnp.float32)
    excess = 2.0 * live * (far_r * far_r + far_i * far_i - level)
    residual = jnp.concatenate([excess * far_r, excess * far_i], axis=0).astype(jnp.bfloat16)
    wave_ref[...] = sandwich(fourier_r, -fourier_i, residual, fourier_r, -fourier_i).astype(jnp.bfloat16)
    odd = lax.rem(lax.axis_index("cuts"), 2) == 1

    def out(low, high):
        mine_ref[...] = jnp.where(odd, high, low)
        other_ref[...] = jnp.where(odd, low, high)

    @pl.when(near_chip())
    def _():
        _, patch_1 = ordered(p0_ref, p1_ref)
        patch_2, patch_3 = ordered(p2_ref, p3_ref)
        back = back_on(wave_ref[...], patch_3, band_ref)
        back = back_on(back, patch_2, band_ref)
        high = complex_mul(one_ref[...], back, -1.0).astype(jnp.bfloat16)
        back = back_on(back, patch_1, band_ref)
        out(complex_mul(probe_ref[...], back, -1.0).astype(jnp.bfloat16), high)

    @pl.when(jnp.logical_not(near_chip()))
    def _():
        _, patch_3 = ordered(p0_ref, p1_ref)
        back = wave_ref[...]
        high = complex_mul(keep_three_ref[...], back, -1.0).astype(jnp.bfloat16)
        back = back_on(back, patch_3, band_ref)
        out(complex_mul(keep_two_ref[...], back, -1.0).astype(jnp.bfloat16), high)


def placed_rows(rows, ref):
    width = ref.shape[1]
    return dot(rows, jnp.concatenate([ref[:width, :], ref[width:, :]], axis=1)).astype(jnp.bfloat16)


def rows_kernel(rows_ref, mine_ref, strip_ref):
    strip_ref[...] = placed_rows(rows_ref[0], mine_ref)


def scattered(first, last, rows_ref, columns_ref, strip_ref, other_ref):
    width = other_ref.shape[1]
    strips = [strip_ref[first:last, :], placed_rows(rows_ref[1, first:last, :], other_ref)]
    parts = []
    for part in range(2):
        strip = jnp.concatenate([strip[:, part * width : (part + 1) * width] for strip in strips], axis=1)
        parts.append(dot(strip, columns_ref[...]))
    return parts


def low_kernel(rows_ref, columns_ref, strip_ref, other_ref, tile_ref, below_ref):
    half = below_ref.shape[2]
    for part, total in enumerate(scattered(half, 3 * half, rows_ref, columns_ref, strip_ref, other_ref)):
        tile_ref[part] = total[:, half:]
        below_ref[part] = total[:, :half].astype(jnp.bfloat16)


def high_kernel(rows_ref, columns_ref, strip_ref, other_ref, right_ref, own_ref):
    half = own_ref.shape[1]
    for part, total in enumerate(scattered(0, half, rows_ref, columns_ref, strip_ref, other_ref)):
        right_ref[part] = total[:, half:].astype(jnp.bfloat16)
        own_ref[part] = total[:, :half].astype(jnp.bfloat16)


def total_kernel(tile_ref, below_ref, right_ref, out_ref, quarter_ref):
    half = right_ref.shape[1]
    below = below_ref[...].astype(jnp.float32)
    right = right_ref[...].astype(jnp.float32)
    quarter = tile_ref[:, half:, half:] + below[:, half:] + right[:, :, half:]
    out_ref[0, :, :half, :half] = tile_ref[:, :half, :half]
    out_ref[0, :, :half, half:] = tile_ref[:, :half, half:] + below[:, :half]
    out_ref[0, :, half:, :half] = tile_ref[:, half:, :half] + right[:, :, :half]
    out_ref[0, :, half:, half:] = quarter
    quarter_ref[...] = quarter


def quarter_kernel(out_ref, quarter_ref, own_ref, same_ref, sum_ref, sem):
    half = quarter_ref.shape[1]
    sum_ref[...] = quarter_ref[...] + own_ref[...].astype(jnp.float32)
    copy = pltpu.make_async_copy(sum_ref, same_ref.at[0, :, pl.ds(half, half), pl.ds(half, half)], sem)
    copy.start()
    copy.wait()


VMEM = pl.BlockSpec(memory_space=pltpu.VMEM)
ANY = pl.BlockSpec(memory_space=pl.ANY)
SMEM = pl.BlockSpec(memory_space=pltpu.SMEM)
PARAMS = pltpu.CompilerParams(vmem_limit_bytes=48 * 1024 * 1024)


def shaped(*shape, dtype=jnp.bfloat16):
    return jax.ShapeDtypeStruct(shape, dtype)


def kernel(body, name, in_specs, out_shape, scratch=()):
    return pl.pallas_call(
        body, in_specs=in_specs, out_specs=[VMEM] * len(out_shape), out_shape=out_shape, scratch_shapes=scratch, compiler_params=PARAMS, name=name
    )


def local(object_slices, probe, fresnel_taps, offsets, counts, measured):
    width = probe.shape[1]
    half = width // 2
    wide = width + half
    full = shaped(2 * width, width)
    part = shaped(width, width)
    row_tiles = max(lax.axis_size("tile") // 16, 2)
    probe = probe.reshape(2 * width, width)
    fourier = jnp.asarray(fourier_matrix(width), jnp.bfloat16)

    far_tile = crossed(object_slices[0], "cuts", 2)
    tile, below, right = kernel(cut_kernel, "cut", [VMEM], [shaped(2, width, width), shaped(2, width + SPARE, half), shaped(2, half, width)])(
        object_slices[0]
    )
    (own,) = kernel(seal_kernel, "seal", [VMEM, VMEM], [shaped(2, half + 16, half)])(tile, offsets)
    below = passed_along(below, "tile", 1)
    right = passed_along(right, "tile", row_tiles)
    own = passed_along(own, "tile", row_tiles + 1)
    far_right = crossed(right, "cuts", 2)
    far_own = crossed(own, "cuts", 2)
    level = shaped(half + 16, width)
    band, level = kernel(band_kernel, "band", [SMEM, VMEM, VMEM], [shaped(4, width, width), level])(counts, fresnel_taps, measured)
    level, far_tile = lax.optimization_barrier((level, far_tile))
    below, far_tile = lax.optimization_barrier((below, far_tile))
    far_below = crossed(below, "cuts", 2)
    level = passed_along(level, "tile", row_tiles + 1)
    rows, columns, rows_back, columns_back = kernel(
        window_kernel,
        "window",
        [VMEM],
        [part, shaped(2, wide, width), shaped(2, wide, width), shaped(2 * width, wide)],
    )(own)
    first, second = kernel(extract_kernel, "near", [VMEM] * 6, [full, full])(rows, columns, tile, below, right, own)
    swapped = crossed(second, "cuts", 1)
    far_level = crossed(level, "cuts", 2)
    straight, far_second = kernel(extract_kernel, "far", [VMEM] * 6, [full, full])(rows, columns, far_tile, far_below, far_right, far_own)
    far_second, far_level = lax.optimization_barrier((far_second, far_level))
    diagonal = crossed(far_second, "cuts", 1)
    one, two = kernel(head_kernel, "head", [VMEM] * 4, [full, full])(probe, band, first, swapped)
    mine, other = kernel(chain_kernel, "chain", [VMEM] * 11, [full, full], [pltpu.VMEM((2 * width, width), jnp.bfloat16)] * 3)(
        probe, first, swapped, straight, diagonal, level, far_level, band, fourier, one, two
    )
    other = crossed(other, "cuts", 1)
    (strip,) = kernel(rows_kernel, "rows", [VMEM] * 2, [shaped(wide, 2 * width)])(rows_back, mine)
    terms = rows_back, columns_back, strip, other
    total, below = kernel(low_kernel, "low", [VMEM] * 4, [shaped(2, width, width, dtype=jnp.float32), shaped(2, width, half)])(*terms)
    right, own = kernel(high_kernel, "high", [VMEM] * 4, [shaped(2, half, width), shaped(2, half, half)])(*terms)
    below = passed_along(below, "tile", -1)
    right = passed_along(right, "tile", -row_tiles)
    own = passed_along(own, "tile", -row_tiles - 1)
    whole = shaped(1, 2, width, width, dtype=jnp.float32)
    quarter = shaped(2, half, half, dtype=jnp.float32)
    out, quarter = kernel(total_kernel, "total", [VMEM] * 3, [whole, quarter])(total, below, right)
    out = pl.pallas_call(
        quarter_kernel,
        in_specs=[ANY, VMEM, VMEM],
        out_specs=ANY,
        out_shape=whole,
        input_output_aliases={0: 0},
        scratch_shapes=[pltpu.VMEM((2, half, half), jnp.float32), pltpu.SemaphoreType.DMA],
        compiler_params=PARAMS,
        name="quarter",
    )(out, quarter, own)
    return out


def solution(mesh):
    return jax.shard_map(
        local,
        mesh=mesh,
        in_specs=(
            P("cuts", None, "tile", None),
            P(),
            P(),
            P("tile", None),
            P("tile"),
            P("tile", None, None),
        ),
        out_specs=P("cuts", None, "tile", None),
        check_vma=False,
    )
```

```python
import jax
import jax.numpy as jnp
import numpy as np
from jax import lax
from jax.experimental import pallas as pl
from jax.experimental.pallas import tpu as pltpu
from jax.sharding import PartitionSpec as P


SPARE = 16


def passed_along(value, axis, steps):
    count = lax.axis_size(axis)
    pairs = [(source, (source + steps) % count) for source in range(count)]
    return lax.ppermute(value, axis, pairs)


def crossed(value, axis, mask):
    pairs = [(source, source ^ mask) for source in range(lax.axis_size(axis))]
    return lax.ppermute(value, axis, pairs)


def fourier_matrix(width):
    index = np.arange(width)
    angle = 2.0 * np.pi * (index[:, None] * index[None, :] % width) / width
    return np.stack([np.cos(angle), -np.sin(angle), np.sin(angle)]) / np.sqrt(width)


def dot(left, right):
    return jnp.dot(left, right, preferred_element_type=jnp.float32)


def sandwich(left_real, left_imag, left_less, field, right_real, right_imag):
    right = jnp.concatenate([right_real, right_imag], axis=0)
    top = dot(jnp.concatenate([left_real, left_less], axis=1), field).astype(jnp.bfloat16)
    bottom = dot(jnp.concatenate([left_imag, left_real], axis=1), field).astype(jnp.bfloat16)
    real = dot(jnp.concatenate([top, -bottom], axis=1), right)
    imag = dot(jnp.concatenate([bottom, top], axis=1), right)
    return jnp.concatenate([real, imag], axis=0)


def complex_mul(first, second, sign):
    width = first.shape[1]
    fr, fi = first[:width], first[width:]
    if sign < 0:
        fi = -fi
    sr, si = second[:width], second[width:]
    return jnp.concatenate([fr * sr - fi * si, fr * si + fi * sr], axis=0)


def band_kernel(counts_ref, taps_ref, measured_ref, band_ref, level_ref):
    width = band_ref.shape[1]
    half = taps_ref.shape[1] // 2
    core = lax.rem(lax.axis_index("cuts"), 2)
    rows = width // 2
    first = pl.multiple_of(lax.axis_index("cuts") // 2 * rows, rows)
    level_ref[:rows, :] = measured_ref[core, pl.ds(first, rows), :].astype(jnp.bfloat16)
    live = (core < counts_ref[0]).astype(jnp.float32)
    level_ref[rows:, :] = jnp.full((level_ref.shape[0] - rows, width), live, jnp.float32).astype(jnp.bfloat16)
    rows = lax.broadcasted_iota(jnp.int32, (width, width), 0)
    columns = lax.broadcasted_iota(jnp.int32, (width, width), 1)
    inside = jnp.abs(columns - rows) <= half
    for part in range(2):
        line = taps_ref[part : part + 1, :].astype(jnp.float32)
        filler = jnp.zeros((1, width - line.shape[1]), jnp.float32)
        line = jnp.concatenate([line, filler], axis=1)
        spread = jnp.broadcast_to(line, (width, width))
        turned = pltpu.roll(spread, width - half, 1, stride=1, stride_axis=0)
        band = jnp.where(inside, turned, 0.0)
        band_ref[part] = band.astype(jnp.bfloat16)
        band_ref[part + 2] = band.T.astype(jnp.bfloat16)
    band_ref[4] = -band_ref[1]
    band_ref[5] = -band_ref[3]


def cut_kernel(tile_ref, whole_ref, below_ref, right_ref):
    half = right_ref.shape[1]
    whole_ref[...] = tile_ref[...]
    below_ref[:, : 2 * half, :] = tile_ref[:, :, half:]
    below_ref[:, 2 * half :, :] = jnp.zeros((2, SPARE, half), jnp.bfloat16)
    right_ref[...] = tile_ref[:, half:, :]


def seal_kernel(tile_ref, offsets_ref, own_ref):
    half = tile_ref.shape[1] // 2
    own_ref[:, :half, :] = tile_ref[:, half:, half:]
    shape = (own_ref.shape[1] - half, half)
    line = lax.broadcasted_iota(jnp.int32, shape, 0)
    lines = jnp.zeros(shape, jnp.float32)
    for index in range(4):
        value = offsets_ref[index // 2 : index // 2 + 1, index % 2 : index % 2 + 1].astype(jnp.float32)
        lines = jnp.where(line == index, value, lines)
    for part in range(2):
        own_ref[part, half:, :] = lines.astype(jnp.bfloat16)


def window_kernel(own_ref, rows_ref, columns_ref, rows_back_ref, columns_back_ref):
    half = own_ref.shape[2]
    width = 2 * half
    core = lax.rem(lax.axis_index("cuts"), 2)
    lines = own_ref[0, half:, :].astype(jnp.float32).astype(jnp.int32) - half

    def placed(shape, axis, shift):
        i = lax.broadcasted_iota(jnp.int32, shape, axis)
        j = lax.broadcasted_iota(jnp.int32, shape, 1 - axis)
        shift = jnp.concatenate([shift] * (shape[1] // half), axis=1)
        return jnp.where(j - i == shift, 1.0, 0.0).astype(jnp.bfloat16)

    for place in range(2):
        second = core != place
        row = jnp.where(second, lines[2:3], lines[0:1])
        column = jnp.where(second, lines[3:4], lines[1:2])
        rows_ref[place * half : (place + 1) * half, :] = placed((half, width), 0, row)
        columns_ref[place] = placed((width + half, width), 1, column)
        rows_back_ref[place] = placed((width + half, width), 1, row)
        columns_back_ref[place * width : (place + 1) * width, :] = placed((width, width + half), 0, column)


def extract_kernel(rows_ref, columns_ref, tile_ref, below_ref, right_ref, own_ref, first_ref, second_ref):
    width = tile_ref.shape[1]
    half = width // 2
    wide = width + half
    blocks = []
    for part in range(2):
        upper = jnp.concatenate([own_ref[part, :half], right_ref[part]], axis=1)
        lower = jnp.concatenate([below_ref[part, :width], tile_ref[part]], axis=1)
        blocks.append(jnp.concatenate([upper, lower], axis=0))
    block = jnp.concatenate(blocks, axis=1)
    strips = [dot(rows_ref[...], block[top : top + width]).astype(jnp.bfloat16) for top in (0, half)]
    for place, out_ref in enumerate((first_ref, second_ref)):
        mine = [strip[place * half : (place + 1) * half, part * wide : (part + 1) * wide] for part in range(2) for strip in strips]
        out_ref[...] = dot(jnp.concatenate(mine, axis=0), columns_ref[place]).astype(jnp.bfloat16)


def ordered(first_ref, second_ref):
    odd = lax.rem(lax.axis_index("cuts"), 2) == 1
    first, second = first_ref[...], second_ref[...]
    return jnp.where(odd, second, first), jnp.where(odd, first, second)


def near_chip():
    return lax.axis_index("cuts") < 2


def spread_on(spread, patch, band_ref):
    wave = complex_mul(spread, patch, 1.0).astype(jnp.bfloat16)
    return sandwich(band_ref[0], band_ref[1], band_ref[4], wave, band_ref[2], band_ref[3]).astype(jnp.bfloat16)


def back_on(back, patch, band_ref):
    carried = complex_mul(patch, back, -1.0).astype(jnp.bfloat16)
    return sandwich(band_ref[2], band_ref[5], band_ref[3], carried, band_ref[0], band_ref[4]).astype(jnp.bfloat16)


def head_kernel(probe_ref, band_ref, p0_ref, p1_ref, one_ref, two_ref):
    @pl.when(near_chip())
    def _():
        patch_0, patch_1 = ordered(p0_ref, p1_ref)
        one_ref[...] = spread_on(probe_ref[...], patch_0, band_ref)
        two_ref[...] = spread_on(one_ref[...], patch_1, band_ref)


def chain_kernel(
    probe_ref, p0_ref, p1_ref, p2_ref, p3_ref, level_ref, far_level_ref, band_ref, fourier_ref, one_ref, two_ref, mine_ref, other_ref,
    keep_two_ref, keep_three_ref, wave_ref
):
    width = probe_ref.shape[1]

    @pl.when(near_chip())
    def _():
        patch_2, patch_3 = ordered(p2_ref, p3_ref)
        spread = spread_on(two_ref[...], patch_2, band_ref)
        wave_ref[...] = complex_mul(spread, patch_3, 1.0).astype(jnp.bfloat16)

    @pl.when(jnp.logical_not(near_chip()))
    def _():
        patch_0, patch_1 = ordered(p2_ref, p3_ref)
        patch_2, patch_3 = ordered(p0_ref, p1_ref)
        spread = spread_on(probe_ref[...], patch_0, band_ref)
        keep_two_ref[...] = spread_on(spread, patch_1, band_ref)
        keep_three_ref[...] = spread_on(keep_two_ref[...], patch_2, band_ref)
        wave_ref[...] = complex_mul(keep_three_ref[...], patch_3, 1.0).astype(jnp.bfloat16)

    fourier_r, fourier_i = fourier_ref[0], fourier_ref[1]
    far = sandwich(fourier_r, fourier_i, fourier_ref[2], wave_ref[...], fourier_r, fourier_i)
    far_r, far_i = far[:width], far[width:]
    rows = width // 2
    level, far_level = level_ref[:rows, :].astype(jnp.float32), far_level_ref[:rows, :].astype(jnp.float32)
    level = jnp.concatenate([jnp.where(near_chip(), level, far_level), jnp.where(near_chip(), far_level, level)], axis=0)
    live = level_ref[rows : rows + 1, :].astype(jnp.float32)
    excess = 2.0 * live * (far_r * far_r + far_i * far_i - level)
    residual = jnp.concatenate([excess * far_r, excess * far_i], axis=0).astype(jnp.bfloat16)
    wave_ref[...] = sandwich(fourier_r, fourier_ref[2], fourier_i, residual, fourier_r, fourier_ref[2]).astype(jnp.bfloat16)
    odd = lax.rem(lax.axis_index("cuts"), 2) == 1

    def out(low, high):
        mine_ref[...] = jnp.where(odd, high, low)
        other_ref[...] = jnp.where(odd, low, high)

    @pl.when(near_chip())
    def _():
        _, patch_1 = ordered(p0_ref, p1_ref)
        patch_2, patch_3 = ordered(p2_ref, p3_ref)
        back = back_on(wave_ref[...], patch_3, band_ref)
        back = back_on(back, patch_2, band_ref)
        high = complex_mul(one_ref[...], back, -1.0).astype(jnp.bfloat16)
        back = back_on(back, patch_1, band_ref)
        out(complex_mul(probe_ref[...], back, -1.0).astype(jnp.bfloat16), high)

    @pl.when(jnp.logical_not(near_chip()))
    def _():
        _, patch_3 = ordered(p0_ref, p1_ref)
        back = wave_ref[...]
        high = complex_mul(keep_three_ref[...], back, -1.0).astype(jnp.bfloat16)
        back = back_on(back, patch_3, band_ref)
        out(complex_mul(keep_two_ref[...], back, -1.0).astype(jnp.bfloat16), high)


def placed_rows(rows, ref):
    width = ref.shape[1]
    return dot(rows, jnp.concatenate([ref[:width, :], ref[width:, :]], axis=1)).astype(jnp.bfloat16)


def rows_kernel(rows_ref, mine_ref, strip_ref):
    strip_ref[...] = placed_rows(rows_ref[0], mine_ref)


def scattered(first, last, rows_ref, columns_ref, strip_ref, other_ref):
    width = other_ref.shape[1]
    strips = [strip_ref[first:last, :], placed_rows(rows_ref[1, first:last, :], other_ref)]
    parts = []
    for part in range(2):
        strip = jnp.concatenate([strip[:, part * width : (part + 1) * width] for strip in strips], axis=1)
        parts.append(dot(strip, columns_ref[...]))
    return parts


def low_kernel(rows_ref, columns_ref, strip_ref, other_ref, tile_ref, below_ref):
    half = below_ref.shape[2]
    for part, total in enumerate(scattered(half, 3 * half, rows_ref, columns_ref, strip_ref, other_ref)):
        tile_ref[part] = total[:, half:]
        below_ref[part] = total[:, :half].astype(jnp.bfloat16)


def high_kernel(rows_ref, columns_ref, strip_ref, other_ref, right_ref, own_ref):
    half = own_ref.shape[1]
    for part, total in enumerate(scattered(0, half, rows_ref, columns_ref, strip_ref, other_ref)):
        right_ref[part] = total[:, half:].astype(jnp.bfloat16)
        own_ref[part] = total[:, :half].astype(jnp.bfloat16)


def total_kernel(tile_ref, below_ref, right_ref, out_ref, quarter_ref):
    half = right_ref.shape[1]
    below = below_ref[...].astype(jnp.float32)
    right = right_ref[...].astype(jnp.float32)
    quarter = tile_ref[:, half:, half:] + below[:, half:] + right[:, :, half:]
    out_ref[0, :, :half, :half] = tile_ref[:, :half, :half]
    out_ref[0, :, :half, half:] = tile_ref[:, :half, half:] + below[:, :half]
    out_ref[0, :, half:, :half] = tile_ref[:, half:, :half] + right[:, :, :half]
    out_ref[0, :, half:, half:] = quarter
    quarter_ref[...] = quarter


def quarter_kernel(out_ref, quarter_ref, own_ref, same_ref, sum_ref, sem):
    half = quarter_ref.shape[1]
    sum_ref[...] = quarter_ref[...] + own_ref[...].astype(jnp.float32)
    copy = pltpu.make_async_copy(sum_ref, same_ref.at[0, :, pl.ds(half, half), pl.ds(half, half)], sem)
    copy.start()
    copy.wait()


VMEM = pl.BlockSpec(memory_space=pltpu.VMEM)
ANY = pl.BlockSpec(memory_space=pl.ANY)
SMEM = pl.BlockSpec(memory_space=pltpu.SMEM)
PARAMS = pltpu.CompilerParams(vmem_limit_bytes=48 * 1024 * 1024)


def shaped(*shape, dtype=jnp.bfloat16):
    return jax.ShapeDtypeStruct(shape, dtype)


def kernel(body, name, in_specs, out_shape, scratch=()):
    return pl.pallas_call(
        body, in_specs=in_specs, out_specs=[VMEM] * len(out_shape), out_shape=out_shape, scratch_shapes=scratch, compiler_params=PARAMS, name=name
    )


def local(object_slices, probe, fresnel_taps, offsets, counts, measured):
    width = probe.shape[1]
    half = width // 2
    wide = width + half
    full = shaped(2 * width, width)
    part = shaped(width, width)
    row_tiles = max(lax.axis_size("tile") // 16, 2)
    probe = probe.reshape(2 * width, width)
    fourier = jnp.asarray(fourier_matrix(width), jnp.bfloat16)

    far_tile = crossed(object_slices[0], "cuts", 2)
    tile, below, right = kernel(cut_kernel, "cut", [VMEM], [shaped(2, width, width), shaped(2, width + SPARE, half), shaped(2, half, width)])(
        object_slices[0]
    )
    (own,) = kernel(seal_kernel, "seal", [VMEM, VMEM], [shaped(2, half + 16, half)])(tile, offsets)
    below = passed_along(below, "tile", 1)
    right = passed_along(right, "tile", row_tiles)
    own = passed_along(own, "tile", row_tiles + 1)
    far_right = crossed(right, "cuts", 2)
    far_own = crossed(own, "cuts", 2)
    level = shaped(half + 16, width)
    band, level = kernel(band_kernel, "band", [SMEM, VMEM, VMEM], [shaped(6, width, width), level])(counts, fresnel_taps, measured)
    level, far_tile = lax.optimization_barrier((level, far_tile))
    below, far_tile = lax.optimization_barrier((below, far_tile))
    far_below = crossed(below, "cuts", 2)
    level = passed_along(level, "tile", row_tiles + 1)
    rows, columns, rows_back, columns_back = kernel(
        window_kernel,
        "window",
        [VMEM],
        [part, shaped(2, wide, width), shaped(2, wide, width), shaped(2 * width, wide)],
    )(own)
    first, second = kernel(extract_kernel, "near", [VMEM] * 6, [full, full])(rows, columns, tile, below, right, own)
    swapped = crossed(second, "cuts", 1)
    far_level = crossed(level, "cuts", 2)
    straight, far_second = kernel(extract_kernel, "far", [VMEM] * 6, [full, full])(rows, columns, far_tile, far_below, far_right, far_own)
    far_second, far_level = lax.optimization_barrier((far_second, far_level))
    diagonal = crossed(far_second, "cuts", 1)
    one, two = kernel(head_kernel, "head", [VMEM] * 4, [full, full])(probe, band, first, swapped)
    mine, other = kernel(chain_kernel, "chain", [VMEM] * 11, [full, full], [pltpu.VMEM((2 * width, width), jnp.bfloat16)] * 3)(
        probe, first, swapped, straight, diagonal, level, far_level, band, fourier, one, two
    )
    other = crossed(other, "cuts", 1)
    (strip,) = kernel(rows_kernel, "rows", [VMEM] * 2, [shaped(wide, 2 * width)])(rows_back, mine)
    terms = rows_back, columns_back, strip, other
    total, below = kernel(low_kernel, "low", [VMEM] * 4, [shaped(2, width, width, dtype=jnp.float32), shaped(2, width, half)])(*terms)
    right, own = kernel(high_kernel, "high", [VMEM] * 4, [shaped(2, half, width), shaped(2, half, half)])(*terms)
    below = passed_along(below, "tile", -1)
    right = passed_along(right, "tile", -row_tiles)
    own = passed_along(own, "tile", -row_tiles - 1)
    whole = shaped(1, 2, width, width, dtype=jnp.float32)
    quarter = shaped(2, half, half, dtype=jnp.float32)
    out, quarter = kernel(total_kernel, "total", [VMEM] * 3, [whole, quarter])(total, below, right)
    out = pl.pallas_call(
        quarter_kernel,
        in_specs=[ANY, VMEM, VMEM],
        out_specs=ANY,
        out_shape=whole,
        input_output_aliases={0: 0},
        scratch_shapes=[pltpu.VMEM((2, half, half), jnp.float32), pltpu.SemaphoreType.DMA],
        compiler_params=PARAMS,
        name="quarter",
    )(out, quarter, own)
    return out


def solution(mesh):
    return jax.shard_map(
        local,
        mesh=mesh,
        in_specs=(
            P("cuts", None, "tile", None),
            P(),
            P(),
            P("tile", None),
            P("tile"),
            P("tile", None, None),
        ),
        out_specs=P("cuts", None, "tile", None),
        check_vma=False,
    )
```

```python
import jax
import jax.numpy as jnp
import numpy as np
from jax import lax
from jax.experimental import pallas as pl
from jax.experimental.pallas import tpu as pltpu
from jax.sharding import PartitionSpec as P


SPARE = 16


def passed_along(value, axis, steps):
    count = lax.axis_size(axis)
    pairs = [(source, (source + steps) % count) for source in range(count)]
    return lax.ppermute(value, axis, pairs)


def crossed(value, axis, mask):
    pairs = [(source, source ^ mask) for source in range(lax.axis_size(axis))]
    return lax.ppermute(value, axis, pairs)


def fourier_matrix(width):
    index = np.arange(width)
    angle = 2.0 * np.pi * (index[:, None] * index[None, :] % width) / width
    return np.stack([np.cos(angle), -np.sin(angle)]) / np.sqrt(width)


def dot(left, right):
    return jnp.dot(left, right, preferred_element_type=jnp.float32)


def sandwich(left_real, left_imag, field, right_real, right_imag):
    right = jnp.concatenate([right_real, right_imag], axis=0)
    top = dot(jnp.concatenate([left_real, -left_imag], axis=1), field).astype(jnp.bfloat16)
    bottom = dot(jnp.concatenate([left_imag, left_real], axis=1), field).astype(jnp.bfloat16)
    real = dot(jnp.concatenate([top, -bottom], axis=1), right)
    imag = dot(jnp.concatenate([bottom, top], axis=1), right)
    return jnp.concatenate([real, imag], axis=0)


def complex_mul(first, second, sign):
    width = first.shape[1]
    fr, fi = first[:width], first[width:]
    if sign < 0:
        fi = -fi
    sr, si = second[:width], second[width:]
    return jnp.concatenate([fr * sr - fi * si, fr * si + fi * sr], axis=0)


def band_kernel(counts_ref, taps_ref, measured_ref, band_ref, level_ref):
    width = band_ref.shape[1]
    half = taps_ref.shape[1] // 2
    core = lax.rem(lax.axis_index("cuts"), 2)
    rows = width // 2
    first = pl.multiple_of(lax.axis_index("cuts") // 2 * rows, rows)
    level_ref[:rows, :] = measured_ref[core, pl.ds(first, rows), :].astype(jnp.bfloat16)
    live = (core < counts_ref[0]).astype(jnp.float32)
    level_ref[rows:, :] = jnp.full((level_ref.shape[0] - rows, width), live, jnp.float32).astype(jnp.bfloat16)
    rows = lax.broadcasted_iota(jnp.int32, (width, width), 0)
    columns = lax.broadcasted_iota(jnp.int32, (width, width), 1)
    inside = jnp.abs(columns - rows) <= half
    for part in range(2):
        line = taps_ref[part : part + 1, :].astype(jnp.float32)
        filler = jnp.zeros((1, width - line.shape[1]), jnp.float32)
        line = jnp.concatenate([line, filler], axis=1)
        spread = jnp.broadcast_to(line, (width, width))
        turned = pltpu.roll(spread, width - half, 1, stride=1, stride_axis=0)
        band = jnp.where(inside, turned, 0.0)
        band_ref[part] = band.astype(jnp.bfloat16)
        band_ref[part + 2] = band.T.astype(jnp.bfloat16)


def cut_kernel(tile_ref, whole_ref, below_ref, right_ref):
    half = right_ref.shape[1]
    whole_ref[...] = tile_ref[...]
    below_ref[:, : 2 * half, :] = tile_ref[:, :, half:]
    below_ref[:, 2 * half :, :] = jnp.zeros((2, SPARE, half), jnp.bfloat16)
    right_ref[...] = tile_ref[:, half:, :]


def seal_kernel(tile_ref, offsets_ref, own_ref):
    half = tile_ref.shape[1] // 2
    own_ref[:, :half, :] = tile_ref[:, half:, half:]
    shape = (own_ref.shape[1] - half, half)
    line = lax.broadcasted_iota(jnp.int32, shape, 0)
    lines = jnp.zeros(shape, jnp.float32)
    for index in range(4):
        value = offsets_ref[index // 2 : index // 2 + 1, index % 2 : index % 2 + 1].astype(jnp.float32)
        lines = jnp.where(line == index, value, lines)
    for part in range(2):
        own_ref[part, half:, :] = lines.astype(jnp.bfloat16)


def window_kernel(own_ref, rows_ref, columns_ref, rows_back_ref, columns_back_ref):
    half = own_ref.shape[2]
    width = 2 * half
    core = lax.rem(lax.axis_index("cuts"), 2)
    lines = own_ref[0, half:, :].astype(jnp.float32).astype(jnp.int32) - half

    def placed(shape, axis, shift):
        i = lax.broadcasted_iota(jnp.int32, shape, axis)
        j = lax.broadcasted_iota(jnp.int32, shape, 1 - axis)
        shift = jnp.concatenate([shift] * (shape[1] // half), axis=1)
        return jnp.where(j - i == shift, 1.0, 0.0).astype(jnp.bfloat16)

    for place in range(2):
        second = core != place
        row = jnp.where(second, lines[2:3], lines[0:1])
        column = jnp.where(second, lines[3:4], lines[1:2])
        rows_ref[place * half : (place + 1) * half, :] = placed((half, width), 0, row)
        columns_ref[place] = placed((width + half, width), 1, column)
        rows_back_ref[place] = placed((width + half, width), 1, row)
        columns_back_ref[place * width : (place + 1) * width, :] = placed((width, width + half), 0, column)


def extract_kernel(rows_ref, columns_ref, tile_ref, below_ref, right_ref, own_ref, first_ref, second_ref):
    width = tile_ref.shape[1]
    half = width // 2
    wide = width + half
    blocks = []
    for part in range(2):
        upper = jnp.concatenate([own_ref[part, :half], right_ref[part]], axis=1)
        lower = jnp.concatenate([below_ref[part, :width], tile_ref[part]], axis=1)
        blocks.append(jnp.concatenate([upper, lower], axis=0))
    block = jnp.concatenate(blocks, axis=1)
    strips = [dot(rows_ref[...], block[top : top + width]).astype(jnp.bfloat16) for top in (0, half)]
    for place, out_ref in enumerate((first_ref, second_ref)):
        mine = [strip[place * half : (place + 1) * half, part * wide : (part + 1) * wide] for part in range(2) for strip in strips]
        out_ref[...] = dot(jnp.concatenate(mine, axis=0), columns_ref[place]).astype(jnp.bfloat16)


def ordered(first_ref, second_ref):
    odd = lax.rem(lax.axis_index("cuts"), 2) == 1
    first, second = first_ref[...], second_ref[...]
    return jnp.where(odd, second, first), jnp.where(odd, first, second)


def near_chip():
    return lax.axis_index("cuts") < 2


def spread_on(spread, patch, band_ref):
    wave = complex_mul(spread, patch, 1.0).astype(jnp.bfloat16)
    return sandwich(band_ref[0], band_ref[1], wave, band_ref[2], band_ref[3]).astype(jnp.bfloat16)


def back_on(back, patch, band_ref):
    carried = complex_mul(patch, back, -1.0).astype(jnp.bfloat16)
    return sandwich(band_ref[2], -band_ref[3], carried, band_ref[0], -band_ref[1]).astype(jnp.bfloat16)


def head_kernel(probe_ref, band_ref, p0_ref, p1_ref, one_ref, two_ref):
    @pl.when(near_chip())
    def _():
        patch_0, patch_1 = ordered(p0_ref, p1_ref)
        one_ref[...] = spread_on(probe_ref[...], patch_0, band_ref)
        two_ref[...] = spread_on(one_ref[...], patch_1, band_ref)


def chain_kernel(
    probe_ref, p0_ref, p1_ref, p2_ref, p3_ref, level_ref, far_level_ref, band_ref, fourier_ref, one_ref, two_ref, mine_ref, other_ref,
    keep_two_ref, keep_three_ref, wave_ref
):
    width = probe_ref.shape[1]

    @pl.when(near_chip())
    def _():
        patch_2, patch_3 = ordered(p2_ref, p3_ref)
        spread = spread_on(two_ref[...], patch_2, band_ref)
        wave_ref[...] = complex_mul(spread, patch_3, 1.0).astype(jnp.bfloat16)

    @pl.when(jnp.logical_not(near_chip()))
    def _():
        patch_0, patch_1 = ordered(p2_ref, p3_ref)
        patch_2, patch_3 = ordered(p0_ref, p1_ref)
        spread = spread_on(probe_ref[...], patch_0, band_ref)
        keep_two_ref[...] = spread_on(spread, patch_1, band_ref)
        keep_three_ref[...] = spread_on(keep_two_ref[...], patch_2, band_ref)
        wave_ref[...] = complex_mul(keep_three_ref[...], patch_3, 1.0).astype(jnp.bfloat16)

    fourier_r, fourier_i = fourier_ref[0], fourier_ref[1]
    far = sandwich(fourier_r, fourier_i, wave_ref[...], fourier_r, fourier_i)
    far_r, far_i = far[:width], far[width:]
    rows = width // 2
    level, far_level = level_ref[:rows, :].astype(jnp.float32), far_level_ref[:rows, :].astype(jnp.float32)
    level = jnp.concatenate([jnp.where(near_chip(), level, far_level), jnp.where(near_chip(), far_level, level)], axis=0)
    live = level_ref[rows : rows + 1, :].astype(jnp.float32)
    excess = 2.0 * live * (far_r * far_r + far_i * far_i - level)
    residual = jnp.concatenate([excess * far_r, excess * far_i], axis=0).astype(jnp.bfloat16)
    wave_ref[...] = sandwich(fourier_r, -fourier_i, residual, fourier_r, -fourier_i).astype(jnp.bfloat16)
    odd = lax.rem(lax.axis_index("cuts"), 2) == 1

    def out(low, high):
        mine_ref[...] = jnp.where(odd, high, low)
        other_ref[...] = jnp.where(odd, low, high)

    @pl.when(near_chip())
    def _():
        _, patch_1 = ordered(p0_ref, p1_ref)
        patch_2, patch_3 = ordered(p2_ref, p3_ref)
        back = back_on(wave_ref[...], patch_3, band_ref)
        back = back_on(back, patch_2, band_ref)
        high = complex_mul(one_ref[...], back, -1.0).astype(jnp.bfloat16)
        back = back_on(back, patch_1, band_ref)
        out(complex_mul(probe_ref[...], back, -1.0).astype(jnp.bfloat16), high)

    @pl.when(jnp.logical_not(near_chip()))
    def _():
        _, patch_3 = ordered(p0_ref, p1_ref)
        back = wave_ref[...]
        high = complex_mul(keep_three_ref[...], back, -1.0).astype(jnp.bfloat16)
        back = back_on(back, patch_3, band_ref)
        out(complex_mul(keep_two_ref[...], back, -1.0).astype(jnp.bfloat16), high)


def placed_rows(rows, ref):
    width = ref.shape[1]
    return jnp.concatenate([dot(rows, part).astype(jnp.bfloat16) for part in (ref[:width, :], ref[width:, :])], axis=1)


def rows_kernel(rows_ref, mine_ref, strip_ref):
    strip_ref[...] = placed_rows(rows_ref[0], mine_ref)


def scattered(first, last, rows_ref, columns_ref, strip_ref, other_ref):
    width = other_ref.shape[1]
    strips = [strip_ref[first:last, :], placed_rows(rows_ref[1, first:last, :], other_ref)]
    parts = []
    for part in range(2):
        strip = jnp.concatenate([strip[:, part * width : (part + 1) * width] for strip in strips], axis=1)
        parts.append(dot(strip, columns_ref[...]))
    return parts


def low_kernel(rows_ref, columns_ref, strip_ref, other_ref, tile_ref, below_ref):
    half = below_ref.shape[2]
    for part, total in enumerate(scattered(half, 3 * half, rows_ref, columns_ref, strip_ref, other_ref)):
        tile_ref[part] = total[:, half:]
        below_ref[part] = total[:, :half].astype(jnp.bfloat16)


def high_kernel(rows_ref, columns_ref, strip_ref, other_ref, right_ref, own_ref):
    half = own_ref.shape[1]
    for part, total in enumerate(scattered(0, half, rows_ref, columns_ref, strip_ref, other_ref)):
        right_ref[part] = total[:, half:].astype(jnp.bfloat16)
        own_ref[part] = total[:, :half].astype(jnp.bfloat16)


def total_kernel(tile_ref, below_ref, right_ref, out_ref, quarter_ref):
    half = right_ref.shape[1]
    below = below_ref[...].astype(jnp.float32)
    right = right_ref[...].astype(jnp.float32)
    quarter = tile_ref[:, half:, half:] + below[:, half:] + right[:, :, half:]
    out_ref[0, :, :half, :half] = tile_ref[:, :half, :half]
    out_ref[0, :, :half, half:] = tile_ref[:, :half, half:] + below[:, :half]
    out_ref[0, :, half:, :half] = tile_ref[:, half:, :half] + right[:, :, :half]
    out_ref[0, :, half:, half:] = quarter
    quarter_ref[...] = quarter


def quarter_kernel(out_ref, quarter_ref, own_ref, same_ref, sum_ref, sem):
    half = quarter_ref.shape[1]
    sum_ref[...] = quarter_ref[...] + own_ref[...].astype(jnp.float32)
    copy = pltpu.make_async_copy(sum_ref, same_ref.at[0, :, pl.ds(half, half), pl.ds(half, half)], sem)
    copy.start()
    copy.wait()


VMEM = pl.BlockSpec(memory_space=pltpu.VMEM)
ANY = pl.BlockSpec(memory_space=pl.ANY)
SMEM = pl.BlockSpec(memory_space=pltpu.SMEM)
PARAMS = pltpu.CompilerParams(vmem_limit_bytes=48 * 1024 * 1024)


def shaped(*shape, dtype=jnp.bfloat16):
    return jax.ShapeDtypeStruct(shape, dtype)


def kernel(body, name, in_specs, out_shape, scratch=()):
    return pl.pallas_call(
        body, in_specs=in_specs, out_specs=[VMEM] * len(out_shape), out_shape=out_shape, scratch_shapes=scratch, compiler_params=PARAMS, name=name
    )


def local(object_slices, probe, fresnel_taps, offsets, counts, measured):
    width = probe.shape[1]
    half = width // 2
    wide = width + half
    full = shaped(2 * width, width)
    part = shaped(width, width)
    row_tiles = max(lax.axis_size("tile") // 16, 2)
    probe = probe.reshape(2 * width, width)
    fourier = jnp.asarray(fourier_matrix(width), jnp.bfloat16)

    far_tile = crossed(object_slices[0], "cuts", 2)
    tile, below, right = kernel(cut_kernel, "cut", [VMEM], [shaped(2, width, width), shaped(2, width + SPARE, half), shaped(2, half, width)])(
        object_slices[0]
    )
    (own,) = kernel(seal_kernel, "seal", [VMEM, VMEM], [shaped(2, half + 16, half)])(tile, offsets)
    below = passed_along(below, "tile", 1)
    right = passed_along(right, "tile", row_tiles)
    own = passed_along(own, "tile", row_tiles + 1)
    far_right = crossed(right, "cuts", 2)
    far_own = crossed(own, "cuts", 2)
    level = shaped(half + 16, width)
    band, level = kernel(band_kernel, "band", [SMEM, VMEM, VMEM], [shaped(4, width, width), level])(counts, fresnel_taps, measured)
    level, far_tile = lax.optimization_barrier((level, far_tile))
    below, far_tile = lax.optimization_barrier((below, far_tile))
    far_below = crossed(below, "cuts", 2)
    level = passed_along(level, "tile", row_tiles + 1)
    rows, columns, rows_back, columns_back = kernel(
        window_kernel,
        "window",
        [VMEM],
        [part, shaped(2, wide, width), shaped(2, wide, width), shaped(2 * width, wide)],
    )(own)
    first, second = kernel(extract_kernel, "near", [VMEM] * 6, [full, full])(rows, columns, tile, below, right, own)
    swapped = crossed(second, "cuts", 1)
    far_level = crossed(level, "cuts", 2)
    straight, far_second = kernel(extract_kernel, "far", [VMEM] * 6, [full, full])(rows, columns, far_tile, far_below, far_right, far_own)
    far_second, far_level = lax.optimization_barrier((far_second, far_level))
    diagonal = crossed(far_second, "cuts", 1)
    one, two = kernel(head_kernel, "head", [VMEM] * 4, [full, full])(probe, band, first, swapped)
    mine, other = kernel(chain_kernel, "chain", [VMEM] * 11, [full, full], [pltpu.VMEM((2 * width, width), jnp.bfloat16)] * 3)(
        probe, first, swapped, straight, diagonal, level, far_level, band, fourier, one, two
    )
    other = crossed(other, "cuts", 1)
    (strip,) = kernel(rows_kernel, "rows", [VMEM] * 2, [shaped(wide, 2 * width)])(rows_back, mine)
    terms = rows_back, columns_back, strip, other
    total, below = kernel(low_kernel, "low", [VMEM] * 4, [shaped(2, width, width, dtype=jnp.float32), shaped(2, width, half)])(*terms)
    right, own = kernel(high_kernel, "high", [VMEM] * 4, [shaped(2, half, width), shaped(2, half, half)])(*terms)
    below = passed_along(below, "tile", -1)
    right = passed_along(right, "tile", -row_tiles)
    own = passed_along(own, "tile", -row_tiles - 1)
    whole = shaped(1, 2, width, width, dtype=jnp.float32)
    quarter = shaped(2, half, half, dtype=jnp.float32)
    out, quarter = kernel(total_kernel, "total", [VMEM] * 3, [whole, quarter])(total, below, right)
    out = pl.pallas_call(
        quarter_kernel,
        in_specs=[ANY, VMEM, VMEM],
        out_specs=ANY,
        out_shape=whole,
        input_output_aliases={0: 0},
        scratch_shapes=[pltpu.VMEM((2, half, half), jnp.float32), pltpu.SemaphoreType.DMA],
        compiler_params=PARAMS,
        name="quarter",
    )(out, quarter, own)
    return out


def solution(mesh):
    return jax.shard_map(
        local,
        mesh=mesh,
        in_specs=(
            P("cuts", None, "tile", None),
            P(),
            P(),
            P("tile", None),
            P("tile"),
            P("tile", None, None),
        ),
        out_specs=P("cuts", None, "tile", None),
        check_vma=False,
    )
```
